32 devices in a mesh: dp: 16 (over z, y, core), grp: 2 (over x).
Axes of the slice: x: 2, y: 2, z: 4, core: 2. Of those that a mesh axis runs over, the one named last changes fastest.
Arguments:
- layer_input: bfloat16 [16, 2080, 512], P('dp', 'grp'), may hold values from -6 to 6
- lang_counts: int32 [16], P('dp'), may hold values from 5 to 77, as said below
- w_query: bfloat16 [512, 512], replicated, may hold values from -0.375 to 0.375
- w_key: bfloat16 [512, 512], replicated, may hold values from -0.375 to 0.375
- w_value: bfloat16 [512, 512], replicated, may hold values from -0.25 to 0.25
- w_output: bfloat16 [512, 512], replicated, may hold values from -1 to 1
- w_expand: bfloat16 [512, 2048], replicated, may hold values from -0.25 to 0.25
- w_reduce: bfloat16 [2048, 512], replicated, may hold values from -0.125 to 0.125
- b_query: float32 [512], replicated, may hold values from -3 to 3
- b_value: float32 [512], replicated, may hold values from -3 to 3
- b_output: float32 [512], replicated, may hold values from -3 to 3
- b_expand: float32 [2048], replicated, may hold values from -3 to 3
- b_reduce: float32 [512], replicated, may hold values from -3 to 3
- gain_attn: float32 [512], replicated, may hold values from 0.1 to 1.9
- shift_attn: float32 [512], replicated, may hold values from -2 to 2
- gain_mlp: float32 [512], replicated, may hold values from 0.1 to 1.9
- shift_mlp: float32 [512], replicated, may hold values from -2 to 2
- cotangent: bfloat16 [16, 2080, 512], P('dp', 'grp'), may hold values from -6 to 6
Outputs:
- layer_output: bfloat16 [16, 2080, 512], P('dp', 'grp')
- grad_input: float32 [16, 2080, 512], P('dp', 'grp')
- grad_wquery: float32 [512, 512], replicated
- grad_wkey: float32 [512, 512], replicated
- grad_wvalue: float32 [512, 512], replicated
- grad_woutput: float32 [512, 512], replicated
- grad_wexpand: float32 [512, 2048], replicated
- grad_wreduce: float32 [2048, 512], replicated
- grad_bquery: float32 [512], replicated
- grad_bvalue: float32 [512], replicated
- grad_boutput: float32 [512], replicated
- grad_bexpand: float32 [2048], replicated
- grad_breduce: float32 [512], replicated
- grad_gattn: float32 [512], replicated
- grad_sattn: float32 [512], replicated
- grad_gmlp: float32 [512], replicated
- grad_smlp: float32 [512], replicated
The draws below stay inside these ranges and needn't reach their ends.
Inputs may be any that keep to these rules, and one draw needn't show every extreme that they name: Language rows of an item at positions 2000 + lang_counts and later are padding; some item has exactly 77 and some exactly 5.
All inputs are finite; a program needn't handle non-finite values.
Results may differ from the reference program's by a relative error of at most 0.012.
The reference program's roundings to bfloat16 on the way count: a program that leaves them out, or rounds other values in their place, can miss the bound.
Values may be sent and summed in bfloat16 or wider, within the bound.
No kernel may reach another device: no remote copies, remote signals or barrier semaphores. Data moves between devices by JAX's collectives and lax.ppermute only.
A program may use at most 192 MiB of HBM per device.

```python
import math
import jax
import jax.numpy as jnp
from jax import lax

D = 512
HEADS = 8
HEAD_DIM = 64
FF = 2048
VIEWS = 5
PATCH = 400
LANG_MIN = 5
LANG_MAX = 77
SEQ = 2080
BATCH = 16


def draw_lang_counts(key, part):
    key = jax.random.fold_in(key, 11)
    split_keys = jax.random.split(key, 3)
    counts = jax.random.randint(split_keys[0], (BATCH,), LANG_MIN, LANG_MAX + 1)
    highest = jax.random.randint(split_keys[1], (), 0, BATCH)
    lowest = (highest + 1 + jax.random.randint(split_keys[2], (), 0, BATCH - 1)) % BATCH
    places = jnp.arange(BATCH)
    counts = jnp.where(places == highest, LANG_MAX, counts)
    counts = jnp.where(places == lowest, LANG_MIN, counts)
    return counts.astype(jnp.int32)


def level_of(own_key, extent, cuts, low, largest):
    loudness = 1.0
    for dim, blocks in cuts:
        draws = jax.random.uniform(jax.random.fold_in(jax.random.fold_in(own_key, 6), dim), (blocks,), jnp.float32, low / len(cuts), largest / len(cuts))
        loudness = loudness * jnp.repeat(jnp.exp(draws), extent[dim] // blocks).reshape((-1,) + (1,) * (len(extent) - 1 - dim))
    return loudness


def scatter_about(rng, extent, deviation, limit, cuts=(), kind=jnp.bfloat16):
    result = deviation * jax.random.normal(rng, extent, jnp.float32)
    if cuts:
        result = result * level_of(rng, extent, cuts, -0.22, 0.18)
    return jnp.clip(result, -limit, limit).astype(kind)


def setup_inputs(seed: int = 0) -> dict:
    key_of = jax.random.split(jax.random.key(seed), 19)
    return {
        "layer_input": scatter_about(key_of[0], (BATCH, SEQ, D), 1.0, 6.0, ((0, 16), (1, 2))),
        "lang_counts": draw_lang_counts(jax.random.fold_in(key_of[18], 71), 0),
        "w_query": scatter_about(key_of[2], (D, D), (D // 2) ** -0.5, 0.375),
        "w_key": scatter_about(key_of[3], (D, D), (D // 2) ** -0.5, 0.375),
        "w_value": scatter_about(key_of[4], (D, D), D ** -0.5, 0.25),
        "w_output": scatter_about(key_of[5], (D, D), (D // 16) ** -0.5, 1.0),
        "w_expand": scatter_about(key_of[6], (D, FF), D ** -0.5, 0.25),
        "w_reduce": scatter_about(key_of[7], (FF, D), FF ** -0.5, 0.125),
        "b_query": scatter_about(key_of[8], (D,), 0.5, 3.0, (), jnp.float32),
        "b_value": scatter_about(key_of[9], (D,), 0.5, 3.0, (), jnp.float32),
        "b_output": scatter_about(key_of[10], (D,), 0.5, 3.0, (), jnp.float32),
        "b_expand": scatter_about(key_of[11], (FF,), 0.5, 3.0, (), jnp.float32),
        "b_reduce": scatter_about(key_of[12], (D,), 0.5, 3.0, (), jnp.float32),
        "gain_attn": jnp.clip(1.0 + 0.18 * jax.random.normal(key_of[13], (D,), jnp.float32), 0.1, 1.9),
        "shift_attn": scatter_about(key_of[14], (D,), 0.3, 2.0, (), jnp.float32),
        "gain_mlp": jnp.clip(1.0 + 0.18 * jax.random.normal(key_of[15], (D,), jnp.float32), 0.1, 1.9),
        "shift_mlp": scatter_about(key_of[16], (D,), 0.3, 2.0, (), jnp.float32),
        "cotangent": scatter_about(key_of[17], (BATCH, SEQ, D), 1.0, 6.0, ((0, 16), (1, 2))),
    }


@jax.custom_vjp
def low(v):
    return lax.optimization_barrier(v.astype(jnp.bfloat16)).astype(jnp.float32)

@jax.custom_vjp
def low_back(v):
    return v

def low_keep(v):
    return (low(v), None)

def low_pass(kept, grad):
    return (grad,)

def back_keep(v):
    return (v, None)

def back_low(kept, grad):
    return (low(grad),)
low.defvjp(low_keep, low_pass)
low_back.defvjp(back_keep, back_low)
EPSILON = 1e-05
NEGATIVE = -1e+30
HIGHEST = lax.Precision.HIGHEST

def norm_rows(matrix, gain, shift):
    center = matrix - lax.optimization_barrier(jnp.mean(matrix, axis=-1, keepdims=True))
    spread = lax.optimization_barrier(jnp.mean(center * center, axis=-1, keepdims=True))
    return center * lax.rsqrt(spread + EPSILON) * gain + shift

def matmul(left, right):
    return jnp.dot(left, right, precision=HIGHEST)

def item_forward(params, item_rows, lang_count):
    w_query, w_key, w_value, w_output, w_expand, w_reduce, b_query, b_value, b_output, b_expand, b_reduce, gain_attn, shift_attn, gain_mlp, shift_mlp = params
    score_scale = 1.0 / math.sqrt(HEAD_DIM)
    normed = low(norm_rows(item_rows, gain_attn, shift_attn))
    queries = low(low_back(matmul(normed, w_query) + b_query)).reshape(SEQ, HEADS, HEAD_DIM)
    key_rows = low(low_back(matmul(normed, w_key))).reshape(SEQ, HEADS, HEAD_DIM)
    value_rows = low(low_back(matmul(normed, w_value) + b_value)).reshape(SEQ, HEADS, HEAD_DIM)
    scores = low_back(jnp.einsum('qhd,khd->hqk', queries, key_rows, precision=HIGHEST) * score_scale)
    valid = jnp.arange(SEQ) < VIEWS * PATCH + lang_count
    scores = jnp.where(valid[None, None, :], scores, NEGATIVE)
    row_max = lax.optimization_barrier(jnp.max(scores, axis=-1, keepdims=True))
    weights = jnp.exp(scores - row_max)
    probs = low(weights / lax.optimization_barrier(jnp.sum(weights, axis=-1, keepdims=True)))
    mixed = jnp.einsum('hqk,khd->qhd', probs, value_rows, precision=HIGHEST).reshape(SEQ, HEADS * HEAD_DIM)
    mixed = low(low_back(mixed))
    branch = low_back(matmul(mixed, w_output) + b_output)
    middle = item_rows + branch
    normed_mlp = low(norm_rows(middle, gain_mlp, shift_mlp))
    upper = low_back(matmul(normed_mlp, w_expand) + b_expand)
    active = low(jax.nn.gelu(upper, approximate=False))
    return middle + matmul(active, w_reduce) + b_reduce

def reference(layer_input, lang_counts, w_query, w_key, w_value, w_output, w_expand, w_reduce, b_query, b_value, b_output, b_expand, b_reduce, gain_attn, shift_attn, gain_mlp, shift_mlp, cotangent):
    params = tuple((p.astype(jnp.float32) for p in (w_query, w_key, w_value, w_output, w_expand, w_reduce, b_query, b_value, b_output, b_expand, b_reduce, gain_attn, shift_attn, gain_mlp, shift_mlp)))
    inputs = layer_input.astype(jnp.float32)
    saved_item = jax.checkpoint(item_forward)

    def forward(param_set, rows_all):

        def one_item(pair):
            return saved_item(param_set, pair[0], pair[1])
        return lax.map(one_item, (rows_all, lang_counts))
    output, backward = jax.vjp(forward, params, inputs)
    grads, grad_in = backward(cotangent.astype(jnp.float32))
    g_wq, g_wk, g_wv, g_wo, g_we, g_wr, g_bq, g_bv, g_bo, g_be, g_br, g_ga, g_sa, g_gm, g_sm = grads
    return (output.astype(jnp.bfloat16), grad_in, g_wq, g_wk, g_wv, g_wo, g_we, g_wr, g_bq, g_bv, g_bo, g_be, g_br, g_ga, g_sa, g_gm, g_sm)
```

```python
import functools
import math

import jax
import jax.numpy as jnp
from jax import lax
from jax.experimental import pallas as pl
from jax.experimental.pallas import tpu as pltpu
from jax.sharding import PartitionSpec as P

HEADS = 8
HEAD_DIM = 64
VIEWS = 5
PATCH = 400
PAIR = 2 * HEAD_DIM
PAIRS = HEADS // 2

EPSILON = 1e-05
NEGATIVE = -1e30
SCALE = 1.0 / math.sqrt(HEAD_DIM)

bf16 = jnp.bfloat16
f32 = jnp.float32


def dot_rows(left, right):
    return lax.dot_general(
        left, right, (((1,), (0,)), ((), ())), preferred_element_type=f32
    )


def dot_left(left, right):
    return lax.dot_general(
        left, right, (((0,), (0,)), ((), ())), preferred_element_type=f32
    )


def dot_right(left, right):
    return lax.dot_general(
        left, right, (((1,), (1,)), ((), ())), preferred_element_type=f32
    )


def chunk_of(rows, limit):
    best = 16
    for size in range(16, limit + 1, 16):
        if rows % size == 0:
            best = size
    return best


def hat_rows(matrix):
    center = matrix - jnp.mean(matrix, axis=-1, keepdims=True)
    spread = jnp.mean(center * center, axis=-1, keepdims=True)
    inverse = lax.rsqrt(spread + EPSILON)
    return center * inverse, inverse


def hat_back(grad_hat, hat, inverse):
    mean_grad = jnp.mean(grad_hat, axis=-1, keepdims=True)
    mean_cross = jnp.mean(grad_hat * hat, axis=-1, keepdims=True)
    return inverse * (grad_hat - mean_grad - hat * mean_cross)


def column_sums(matrix):
    return jnp.sum(matrix, axis=0, keepdims=True)


def params(limit_mib, axes):
    return pltpu.CompilerParams(
        dimension_semantics=("arbitrary",) * axes, vmem_limit_bytes=limit_mib << 20
    )


def cost(flops, bytes_accessed, transcendentals=0):
    return pl.CostEstimate(
        flops=int(flops), bytes_accessed=int(bytes_accessed), transcendentals=int(transcendentals)
    )


def whole(shape):
    return pl.BlockSpec(shape, lambda *_: (0,) * len(shape))


def project_kernel(with_query, x_ref, gain, shift, w_query, w_key, w_value, b_query, b_value, *outs):
    hat, _ = hat_rows(x_ref[...].astype(f32))
    normed = (hat * gain[...] + shift[...]).astype(bf16)
    if with_query:
        normed_ref, key_ref, value_ref, query_ref = outs
        query = (dot_rows(normed, w_query[...]) + b_query[...]).astype(bf16)
        query_ref[...] = (query.astype(f32) * SCALE).astype(bf16)
    else:
        normed_ref, key_ref, value_ref = outs
    normed_ref[...] = normed
    key_ref[...] = dot_rows(normed, w_key[...]).astype(bf16)
    value_ref[...] = (dot_rows(normed, w_value[...]) + b_value[...]).astype(bf16)


def project(x, gain, shift, w_query, w_key, w_value, b_query, b_value, with_query):
    rows, width = x.shape
    step = chunk_of(rows, 272)
    count = 4 if with_query else 3
    row_block = pl.BlockSpec((step, width), lambda i: (i, 0))
    return pl.pallas_call(
        functools.partial(project_kernel, with_query),
        grid=(rows // step,),
        in_specs=[row_block, whole((1, width)), whole((1, width))]
        + [whole((width, width))] * 3
        + [whole((1, width))] * 2,
        out_specs=[row_block] * count,
        out_shape=[jax.ShapeDtypeStruct((rows, width), bf16)] * count,
        compiler_params=params(32, 1),
        cost_estimate=cost(2 * rows * width * width * (count - 1), 2 * rows * width * (count + 1)),
        name="project",
    )(x, gain, shift, w_query, w_key, w_value, b_query, b_value)


def lanes_of(shape):
    return lax.broadcasted_iota(jnp.int32, shape, 1)


def forward_kernel(
    final, rows, blocks, step, limits, q_ref, k_ref, v_ref, *rest
):
    if final:
        acc_in, top_in, sum_in, out_ref, lse_ref, kt_ref, va_ref = rest
    else:
        acc_out, top_out, sum_out, kt_ref, va_ref = rest
    item = pl.program_id(0)
    key_count = rows * blocks
    query_rows = q_ref.shape[0]
    keys = k_ref[...].astype(f32)
    values = v_ref[...].astype(f32)
    first = lanes_of((key_count, PAIR)) < HEAD_DIM
    flipped = keys.T
    row_id = lax.broadcasted_iota(jnp.int32, (PAIR, key_count), 0)
    key_id = lax.broadcasted_iota(jnp.int32, (PAIR, key_count), 1)
    bias = jnp.zeros((PAIR, key_count), f32)
    for block in range(blocks):
        here = (key_id >= block * rows + limits[item, block]) & (key_id < (block + 1) * rows)
        bias = jnp.where(here, NEGATIVE, bias)
    spare = jnp.where((row_id & (HEAD_DIM - 1)) == 0, bias, 0.0)
    kt_ref[0] = jnp.where(row_id < HEAD_DIM, flipped, spare).astype(bf16)
    kt_ref[1] = jnp.where(row_id < HEAD_DIM, spare, flipped).astype(bf16)
    va_ref[0] = jnp.where(first, values, 1.0).astype(bf16)
    va_ref[1] = jnp.where(first, 1.0, values).astype(bf16)
    lanes = lanes_of((step, PAIR))
    head_first = lanes < HEAD_DIM
    one = jnp.where((lanes & (HEAD_DIM - 1)) == 0, 1.0, 0.0)

    def body(index, carry):
        place = pl.ds(pl.multiple_of(index * step, step), step)
        query = q_ref[place, :].astype(f32)
        outs, tops = [], []
        for head in range(2):
            mine = head_first if head == 0 else jnp.logical_not(head_first)
            query_head = jnp.where(mine, query, one).astype(bf16)
            scores = dot_rows(query_head, kt_ref[head])
            top = jnp.max(scores, axis=1, keepdims=True)
            weights = jnp.exp(scores - top).astype(bf16)
            outs.append(dot_rows(weights, va_ref[head]))
            tops.append(top)
        acc = jnp.where(head_first, outs[0], outs[1])
        total = pltpu.roll(jnp.where(head_first, outs[1], outs[0]), HEAD_DIM, 1)
        top = jnp.where(head_first, tops[0], tops[1])
        if final:
            other_top = top_in[place, :]
            new_top = jnp.maximum(top, other_top)
            scale_here = jnp.exp(top - new_top)
            scale_there = jnp.exp(other_top - new_top)
            total = total * scale_here + sum_in[place, :] * scale_there
            acc = acc * scale_here + acc_in[place, :] * scale_there
            out_ref[place, :] = acc / total
            lse_ref[place, :] = pltpu.roll(new_top + jnp.log(total), HEAD_DIM, 1)
        else:
            acc_out[place, :] = acc
            top_out[place, :] = top
            sum_out[place, :] = total
        return carry

    lax.fori_loop(0, query_rows // step, body, 0)


def attend(limits, queries, keys, values, rows, blocks, before):
    total, width = queries.shape
    items = total // rows
    key_count = rows * blocks
    step = chunk_of(rows, 208)
    query_block = pl.BlockSpec((rows, PAIR), lambda i, p, *_: (i, p))
    key_block = pl.BlockSpec((key_count, PAIR), lambda i, p, *_: (i, p))
    final = before is not None
    extra = list(before) if final else []
    outs = 2 if final else 3
    return pl.pallas_call(
        functools.partial(forward_kernel, final, rows, blocks, step),
        grid_spec=pltpu.PrefetchScalarGridSpec(
            num_scalar_prefetch=1,
            grid=(items, PAIRS),
            in_specs=[query_block, key_block, key_block] + [query_block] * len(extra),
            out_specs=[query_block] * outs,
            scratch_shapes=[
                pltpu.VMEM((2, PAIR, key_count), bf16),
                pltpu.VMEM((2, key_count, PAIR), bf16),
            ],
        ),
        out_shape=[jax.ShapeDtypeStruct((total, width), f32)] * outs,
        compiler_params=params(48, 2),
        cost_estimate=cost(
            16 * total * key_count * width, 12 * total * width, total * key_count * HEADS
        ),
        name="attend",
    )(limits, queries, keys, values, *extra)


def split_three(value):
    high = value.astype(bf16).astype(f32)
    rest = value - high
    middle = rest.astype(bf16).astype(f32)
    return high, middle, rest - middle


def backward_kernel(
    last, rows, blocks, step, limits, q_ref, k_ref, v_ref, g_ref, out_ref, lse_ref, *rest
):
    if last:
        before_ref, dq_ref, dk_ref, dv_ref, qt_ref, gt_ref, dqt_ref = rest
    else:
        dq_ref, dk_ref, dv_ref, qt_ref, gt_ref, dqt_ref = rest
    item = pl.program_id(0)
    query_rows = q_ref.shape[0]
    lanes = lanes_of((query_rows, PAIR))
    head_first = lanes < HEAD_DIM
    spare_lane = lanes & (HEAD_DIM - 1)

    def spare(parts, mask_one):
        high, middle, low = parts
        value = jnp.where(spare_lane == 0, high, 0.0)
        value = jnp.where(spare_lane == 1, middle, value)
        value = jnp.where(spare_lane == 2, low, value)
        return jnp.where(spare_lane == 3, mask_one, value)

    query = q_ref[...].astype(f32)
    grad = g_ref[...].astype(f32)
    product = grad * out_ref[...]
    delta_first = jnp.sum(jnp.where(head_first, product, 0.0), axis=1, keepdims=True)
    delta_second = jnp.sum(jnp.where(head_first, 0.0, product), axis=1, keepdims=True)
    delta = jnp.where(head_first, delta_second, delta_first)
    lse_spare = spare(split_three(-lse_ref[...]), 1.0)
    delta_spare = spare(split_three(-delta), 0.0)
    qt_ref[0] = jnp.where(head_first, query, lse_spare).T.astype(bf16)
    qt_ref[1] = jnp.where(head_first, lse_spare, query).T.astype(bf16)
    gt_ref[0] = jnp.where(head_first, grad, delta_spare).T.astype(bf16)
    gt_ref[1] = jnp.where(head_first, delta_spare, grad).T.astype(bf16)
    dqt_ref[...] = jnp.zeros_like(dqt_ref)

    key_lanes = lanes_of((step, PAIR))
    key_first = key_lanes < HEAD_DIM
    key_spare = key_lanes & (HEAD_DIM - 1)
    key_row = lax.broadcasted_iota(jnp.int32, (step, PAIR), 0)
    ones = jnp.where(key_spare < 3, 1.0, 0.0)
    per_block = rows // step

    def body(index, carry):
        place = pl.ds(pl.multiple_of(index * step, step), step)
        block = index // per_block
        limit = limits[item, block] - (index - block * per_block) * step
        bias = jnp.where(key_row >= limit, NEGATIVE, 0.0)
        key = k_ref[place, :].astype(f32)
        value = v_ref[place, :].astype(f32)
        key_aug = jnp.where(key_spare == 3, bias, ones)
        key_flipped = key.T.astype(bf16)
        dks, dvs = [], []
        for head in range(2):
            mine = key_first if head == 0 else jnp.logical_not(key_first)
            key_head = jnp.where(mine, key, key_aug).astype(bf16)
            value_head = jnp.where(mine, value, ones).astype(bf16)
            probs = jnp.exp(dot_rows(key_head, qt_ref[head]))
            grad_probs = dot_rows(value_head, gt_ref[head])
            grad_scores = (probs * grad_probs).astype(bf16)
            dvs.append(dot_rows(probs.astype(bf16), g_ref[...]))
            dks.append(dot_rows(grad_scores, q_ref[...]))
            own = pl.ds(head * HEAD_DIM, HEAD_DIM)
            half = key_flipped[head * HEAD_DIM:(head + 1) * HEAD_DIM]
            dqt_ref[own, :] += dot_rows(half, grad_scores)
        dk_ref[place, :] = jnp.where(key_first, dks[0], dks[1]).astype(bf16)
        dv_ref[place, :] = jnp.where(key_first, dvs[0], dvs[1]).astype(bf16)
        return carry

    lax.fori_loop(0, blocks * per_block, body, 0)
    result = dqt_ref[...].T
    if last:
        dq_ref[...] = ((result + before_ref[...]) * SCALE).astype(bf16)
    else:
        dq_ref[...] = result


def attend_back(limits, queries, keys, values, grads, outs, lse, rows, blocks, before):
    total, width = queries.shape
    items = total // rows
    key_count = rows * blocks
    step = chunk_of(rows, 208)
    query_block = pl.BlockSpec((rows, PAIR), lambda i, p, *_: (i, p))
    key_block = pl.BlockSpec((key_count, PAIR), lambda i, p, *_: (i, p))
    last = before is not None
    extra = [before] if last else []
    key_shape = jax.ShapeDtypeStruct((total * blocks, width), bf16)
    return pl.pallas_call(
        functools.partial(backward_kernel, last, rows, blocks, step),
        grid_spec=pltpu.PrefetchScalarGridSpec(
            num_scalar_prefetch=1,
            grid=(items, PAIRS),
            in_specs=[query_block, key_block, key_block]
            + [query_block] * (3 + len(extra)),
            out_specs=[query_block, key_block, key_block],
            scratch_shapes=[
                pltpu.VMEM((2, PAIR, rows), bf16),
                pltpu.VMEM((2, PAIR, rows), bf16),
                pltpu.VMEM((PAIR, rows), f32),
            ],
        ),
        out_shape=[
            jax.ShapeDtypeStruct((total, width), bf16 if last else f32),
            key_shape,
            key_shape,
        ],
        compiler_params=params(48, 2),
        cost_estimate=cost(
            40 * total * key_count * width, 16 * total * width, total * key_count * HEADS
        ),
        name="attend_back",
    )(limits, queries, keys, values, grads, outs, lse, *extra)


def feed_kernel(
    x_ref, mix_ref, dy_ref, w_output, w_expand, w_reduce, b_output, b_expand, b_reduce, gain, shift,
    y_ref, dmid_ref, dmix_ref, dwo_ref, dwe_ref, dwr_ref,
    dbo_ref, dbe_ref, dbr_ref, dgain_ref, dshift_ref,
    middle_ref, normed_ref, y_acc, grad_acc,
):
    part = pl.program_id(0)

    @pl.when(part == 0)
    def _():
        mixed = mix_ref[...].astype(bf16)
        middle = x_ref[...].astype(f32) + dot_rows(mixed, w_output[...]) + b_output[...]
        middle_ref[...] = middle
        hat, _ = hat_rows(middle)
        normed_ref[...] = (hat * gain[...] + shift[...]).astype(bf16)
        y_acc[...] = middle + b_reduce[...]
        grad_acc[...] = jnp.zeros_like(grad_acc)
        dbr_ref[...] = column_sums(dy_ref[...].astype(f32))

    normed = normed_ref[...]
    upper = dot_rows(normed, w_expand[...]) + b_expand[...]
    cumulative = 0.5 * lax.erf(upper * math.sqrt(0.5)) + 0.5
    density = jnp.exp(upper * upper * -0.5) * (1.0 / math.sqrt(2.0 * math.pi))
    active = (upper * cumulative).astype(bf16)
    slope = cumulative + upper * density
    y_acc[...] += dot_rows(active, w_reduce[...])
    dwr_ref[...] = dot_left(active, dy_ref[...]).astype(dwr_ref.dtype)
    grad_upper = (dot_right(dy_ref[...], w_reduce[...]) * slope).astype(bf16)
    dbe_ref[...] = column_sums(grad_upper.astype(f32))
    dwe_ref[...] = dot_left(normed, grad_upper).astype(dwe_ref.dtype)
    grad_acc[...] += dot_right(grad_upper, w_expand[...])

    @pl.when(part == pl.num_programs(0) - 1)
    def _():
        y_ref[...] = y_acc[...].astype(bf16)
        grad = grad_acc[...]
        hat, inverse = hat_rows(middle_ref[...])
        dgain_ref[...] = column_sums(grad * hat)
        dshift_ref[...] = column_sums(grad)
        dmid = hat_back(grad * gain[...], hat, inverse) + dy_ref[...].astype(f32)
        dmid_ref[...] = dmid
        branch = dmid.astype(bf16)
        dbo_ref[...] = column_sums(branch.astype(f32))
        dwo_ref[...] = dot_left(mix_ref[...].astype(bf16), branch).astype(dwo_ref.dtype)
        dmix_ref[...] = dot_right(branch, w_output[...]).astype(bf16)


def feed(x, mixed, dy, w_output, w_expand, w_reduce, b_output, b_expand, b_reduce, gain, shift):
    rows, width = x.shape
    hidden = w_expand.shape[1]
    part = 512
    row = whole((rows, width))
    line = whole((1, width))
    expand = pl.BlockSpec((width, part), lambda i: (0, i))
    reduce = pl.BlockSpec((part, width), lambda i: (i, 0))
    hidden_line = pl.BlockSpec((1, part), lambda i: (0, i))
    shape = jax.ShapeDtypeStruct
    return pl.pallas_call(
        feed_kernel,
        grid=(hidden // part,),
        in_specs=[row, row, row, whole((width, width)), expand, reduce, line, hidden_line, line, line, line],
        out_specs=[row, row, row, whole((width, width)), expand, reduce, line, hidden_line, line, line, line],
        out_shape=[
            shape((rows, width), bf16),
            shape((rows, width), f32),
            shape((rows, width), bf16),
            shape((width, width), bf16),
            shape((width, hidden), bf16),
            shape((hidden, width), bf16),
            shape((1, width), f32),
            shape((1, hidden), f32),
            shape((1, width), f32),
            shape((1, width), f32),
            shape((1, width), f32),
        ],
        scratch_shapes=[
            pltpu.VMEM((rows, width), f32),
            pltpu.VMEM((rows, width), bf16),
            pltpu.VMEM((rows, width), f32),
            pltpu.VMEM((rows, width), f32),
        ],
        compiler_params=params(56, 1),
        cost_estimate=cost(12 * rows * width * hidden + 6 * rows * width * width, 20 * rows * width, 2 * rows * hidden),
        name="feed",
    )(x, mixed, dy, w_output, w_expand, w_reduce, b_output, b_expand, b_reduce, gain, shift)


def other_kernel(
    x_ref, normed_ref, dk_ref, dv_ref, w_key, w_value,
    send_ref, dwk_ref, dwv_ref, dbv_ref, dgain_ref, dshift_ref, dwk_acc, dwv_acc,
):
    index = pl.program_id(0)
    dk, dv, normed = dk_ref[...], dv_ref[...], normed_ref[...]
    grad = dot_right(dk, w_key[...]) + dot_right(dv, w_value[...])
    send_ref[...] = grad.astype(bf16)
    hat, _ = hat_rows(x_ref[...].astype(f32))

    @pl.when(index == 0)
    def _():
        for ref in (dbv_ref, dgain_ref, dshift_ref, dwk_acc, dwv_acc):
            ref[...] = jnp.zeros_like(ref)

    dwk_acc[...] += dot_left(normed, dk)
    dwv_acc[...] += dot_left(normed, dv)
    dbv_ref[...] += column_sums(dv.astype(f32))
    dgain_ref[...] += column_sums(grad * hat)
    dshift_ref[...] += column_sums(grad)

    @pl.when(index == pl.num_programs(0) - 1)
    def _():
        dwk_ref[...] = dwk_acc[...]
        dwv_ref[...] = dwv_acc[...]


def other_grads(x, normed, dk, dv, w_key, w_value, rows):
    total, width = x.shape
    row = pl.BlockSpec((rows, width), lambda i: (i, 0))
    square, line = whole((width, width)), whole((1, width))
    shape = jax.ShapeDtypeStruct
    return pl.pallas_call(
        other_kernel,
        grid=(total // rows,),
        in_specs=[row] * 4 + [square] * 2,
        out_specs=[row, square, square, line, line, line],
        out_shape=[
            shape((total, width), bf16),
            shape((width, width), f32),
            shape((width, width), f32),
        ]
        + [shape((1, width), f32)] * 3,
        scratch_shapes=[pltpu.VMEM((width, width), f32)] * 2,
        compiler_params=params(48, 1),
        cost_estimate=cost(8 * total * width * width, 10 * total * width),
        name="other_grads",
    )(x, normed, dk, dv, w_key, w_value)


def own_kernel(
    x_ref, normed_ref, dq_ref, dk_ref, dv_ref, recv_ref, dmid_ref, w_query, w_key, w_value, gain,
    dwk_in, dwv_in, dbv_in, dgain_in, dshift_in,
    dx_ref, dwq_ref, dwk_ref, dwv_ref, dbq_ref, dbv_ref, dgain_ref, dshift_ref,
):
    dq, dk, dv, normed = dq_ref[...], dk_ref[...], dv_ref[...], normed_ref[...]
    dwq_ref[...] = dot_left(normed, dq).astype(dwq_ref.dtype)
    dwk_ref[...] = (dot_left(normed, dk) + dwk_in[...]).astype(dwk_ref.dtype)
    dwv_ref[...] = (dot_left(normed, dv) + dwv_in[...]).astype(dwv_ref.dtype)
    dbq_ref[...] = column_sums(dq.astype(f32))
    dbv_ref[...] = column_sums(dv.astype(f32)) + dbv_in[...]
    grad = dot_right(dq, w_query[...]) + dot_right(dk, w_key[...]) + dot_right(dv, w_value[...])
    hat, inverse = hat_rows(x_ref[...].astype(f32))
    dgain_ref[...] = column_sums(grad * hat) + dgain_in[...]
    dshift_ref[...] = column_sums(grad) + dshift_in[...]
    for index in range(recv_ref.shape[0]):
        grad = grad + recv_ref[index].astype(f32)
    dx_ref[...] = hat_back(grad * gain[...], hat, inverse) + dmid_ref[...]


def own_grads(x, normed, dq, dk, dv, recv, dmid, w_query, w_key, w_value, gain, sums):
    rows, width = x.shape
    row, square, line = whole((rows, width)), whole((width, width)), whole((1, width))
    shape = jax.ShapeDtypeStruct
    return pl.pallas_call(
        own_kernel,
        grid=(1,),
        in_specs=[row] * 5 + [whole(recv.shape), row] + [square] * 3 + [line]
        + [square] * 2 + [line] * 3,
        out_specs=[row] + [square] * 3 + [line] * 4,
        out_shape=[shape((rows, width), f32)]
        + [shape((width, width), bf16)] * 3
        + [shape((1, width), f32)] * 4,
        compiler_params=params(56, 1),
        cost_estimate=cost(12 * rows * width * width, 20 * rows * width),
        name="own_grads",
    )(x, normed, dq, dk, dv, recv, dmid, w_query, w_key, w_value, gain, *sums)


def body(
    layer_input,
    lang_counts,
    w_query,
    w_key,
    w_value,
    w_output,
    w_expand,
    w_reduce,
    b_query,
    b_value,
    b_output,
    b_expand,
    b_reduce,
    gain_attn,
    shift_attn,
    gain_mlp,
    shift_mlp,
    cotangent,
):
    items, own_rows, width = layer_input.shape
    group = lax.axis_size("grp")
    me = lax.axis_index("grp")
    rows = -(-own_rows // 16) * 16
    total = items * rows
    patch_rows = VIEWS * PATCH
    shifts = range(1, group)
    axes = ("dp", "grp")

    def padded(array):
        if rows != own_rows:
            array = jnp.pad(array, ((0, 0), (0, rows - own_rows), (0, 0)))
        return array.reshape(total, width)

    def unpadded(array):
        return array.reshape(items, rows, width)[:, :own_rows]

    def limit_of(owner):
        return jnp.clip(patch_rows + lang_counts - owner * own_rows, 0, own_rows)

    def line(vector):
        return vector.reshape(1, -1)

    def group_shift(array, shift):
        return lax.ppermute(array, "grp", [(i, (i + shift) % group) for i in range(group)])

    def joined(parts):
        if len(parts) == 1:
            return parts[0]
        return jnp.stack([p.reshape(items, rows, width) for p in parts], 1).reshape(-1, width)

    x = padded(layer_input)
    dy = padded(cotangent)
    others = [group_shift(x, -shift) for shift in shifts]
    own_limits = limit_of(me).reshape(items, 1)
    other_limits = jnp.stack([limit_of((me + shift) % group) for shift in shifts], 1)

    weights = (w_query, w_key, w_value, line(b_query), line(b_value))
    norms = (line(gain_attn), line(shift_attn))
    normed, keys, values, queries = project(x, *norms, *weights, with_query=True)
    first = attend(own_limits, queries, keys, values, rows, 1, None)
    x_other = joined(others)
    normed_other, keys_other, values_other = project(x_other, *norms, *weights, with_query=False)
    mixed, lse = attend(other_limits, queries, keys_other, values_other, rows, group - 1, first)

    (output, dmid, dmix, dwo, dwe, dwr, dbo, dbe, dbr, dgain_mlp, dshift_mlp) = feed(
        x, mixed, dy, w_output, w_expand, w_reduce, line(b_output), line(b_expand), line(b_reduce),
        line(gain_mlp), line(shift_mlp),
    )
    dwo, dwe, dwr = lax.psum((dwo, dwe, dwr), axes)

    dq_part, dk_other, dv_other = attend_back(
        other_limits, queries, keys_other, values_other, dmix, mixed, lse, rows, group - 1, None
    )
    send, *sums = other_grads(x_other, normed_other, dk_other, dv_other, w_key, w_value, rows)
    send = send.reshape(items, group - 1, rows, width)
    received = jnp.stack(
        [group_shift(send[:, shift - 1].reshape(total, width), shift) for shift in shifts]
    )
    dq, dk, dv = attend_back(own_limits, queries, keys, values, dmix, mixed, lse, rows, 1, dq_part)
    (dx, dwq, dwk, dwv, dbq, dbv, dgain, dshift) = own_grads(
        x, normed, dq, dk, dv, received, dmid, w_query, w_key, w_value, line(gain_attn), sums
    )
    (dwq, dwk, dwv), (dwo, dwe, dwr) = lax.optimization_barrier(((dwq, dwk, dwv), (dwo, dwe, dwr)))
    dwq, dwk, dwv = lax.psum((dwq, dwk, dwv), axes)
    small = lax.psum((dbq, dbv, dbo, dbe, dbr, dgain, dshift, dgain_mlp, dshift_mlp), axes)
    return (
        unpadded(output),
        unpadded(dx),
        *(w.astype(f32) for w in (dwq, dwk, dwv, dwo, dwe, dwr)),
        *(s.reshape(-1) for s in small),
    )


def solution(mesh):
    rows = P("dp", "grp", None)
    in_specs = (rows, P("dp")) + (P(),) * 15 + (rows,)
    out_specs = (rows, rows) + (P(),) * 15
    return jax.shard_map(body, mesh=mesh, in_specs=in_specs, out_specs=out_specs, check_vma=False)
```

```python
import functools
import math

import jax
import jax.numpy as jnp
from jax import lax
from jax.experimental import pallas as pl
from jax.experimental.pallas import tpu as pltpu
from jax.sharding import PartitionSpec as P

HEADS = 8
HEAD_DIM = 64
VIEWS = 5
PATCH = 400
PAIR = 2 * HEAD_DIM
PAIRS = HEADS // 2

GROUPS = ((0, 2), (2, 1), (3, 1))

EPSILON = 1e-05
NEGATIVE = -1e30
SCALE = 1.0 / math.sqrt(HEAD_DIM)

bf16 = jnp.bfloat16
f32 = jnp.float32


def dot_rows(left, right):
    return lax.dot_general(
        left, right, (((1,), (0,)), ((), ())), preferred_element_type=f32
    )


def dot_left(left, right):
    return lax.dot_general(
        left, right, (((0,), (0,)), ((), ())), preferred_element_type=f32
    )


def dot_right(left, right):
    return lax.dot_general(
        left, right, (((1,), (1,)), ((), ())), preferred_element_type=f32
    )


def chunk_of(rows, limit):
    best = 16
    for size in range(16, limit + 1, 16):
        if rows % size == 0:
            best = size
    return best


def hat_rows(matrix):
    center = matrix - jnp.mean(matrix, axis=-1, keepdims=True)
    spread = jnp.mean(center * center, axis=-1, keepdims=True)
    inverse = lax.rsqrt(spread + EPSILON)
    return center * inverse, inverse


def hat_back(grad_hat, hat, inverse):
    mean_grad = jnp.mean(grad_hat, axis=-1, keepdims=True)
    mean_cross = jnp.mean(grad_hat * hat, axis=-1, keepdims=True)
    return inverse * (grad_hat - mean_grad - hat * mean_cross)


def column_sums(matrix):
    return jnp.sum(matrix, axis=0, keepdims=True)


VMEM_MIB = 58


def params(axes):
    return pltpu.CompilerParams(
        dimension_semantics=("arbitrary",) * axes, vmem_limit_bytes=VMEM_MIB << 20
    )


def cost(flops, bytes_accessed, transcendentals=0):
    return pl.CostEstimate(
        flops=int(flops), bytes_accessed=int(bytes_accessed), transcendentals=int(transcendentals)
    )


def whole(shape):
    return pl.BlockSpec(shape, lambda *_: (0,) * len(shape))


def project_kernel(with_query, x_ref, gain, shift, w_query, w_key, w_value, b_query, b_value, *outs):
    hat, _ = hat_rows(x_ref[...].astype(f32))
    normed = (hat * gain[...] + shift[...]).astype(bf16)
    if with_query:
        normed_ref, key_ref, value_ref, query_ref = outs
        query = (dot_rows(normed, w_query[...]) + b_query[...]).astype(bf16)
        query_ref[...] = (query.astype(f32) * SCALE).astype(bf16)
    else:
        normed_ref, key_ref, value_ref = outs
    normed_ref[...] = normed
    key_ref[...] = dot_rows(normed, w_key[...]).astype(bf16)
    value_ref[...] = (dot_rows(normed, w_value[...]) + b_value[...]).astype(bf16)


def project(x, gain, shift, w_query, w_key, w_value, b_query, b_value, with_query):
    rows, width = x.shape
    step = chunk_of(rows, 272)
    count = 4 if with_query else 3
    row_block = pl.BlockSpec((step, width), lambda i: (i, 0))
    return pl.pallas_call(
        functools.partial(project_kernel, with_query),
        grid=(rows // step,),
        in_specs=[row_block, whole((1, width)), whole((1, width))]
        + [whole((width, width))] * 3
        + [whole((1, width))] * 2,
        out_specs=[row_block] * count,
        out_shape=[jax.ShapeDtypeStruct((rows, width), bf16)] * count,
        compiler_params=params(1),
        cost_estimate=cost(2 * rows * width * width * (count - 1), 2 * rows * width * (count + 1)),
        name="project",
    )(x, gain, shift, w_query, w_key, w_value, b_query, b_value)


def lanes_of(shape):
    return lax.broadcasted_iota(jnp.int32, shape, 1)


def forward_kernel(
    final, rows, blocks, step, limits, q_ref, k_ref, v_ref, *rest
):
    if final:
        acc_in, top_in, sum_in, out_ref, lse_ref, kt_ref, va_ref = rest
    else:
        acc_out, top_out, sum_out, kt_ref, va_ref = rest
    item = pl.program_id(0)
    key_count = rows * blocks
    query_rows = q_ref.shape[0]
    keys = k_ref[...].astype(f32)
    values = v_ref[...].astype(f32)
    first = lanes_of((key_count, PAIR)) < HEAD_DIM
    flipped = keys.T
    row_id = lax.broadcasted_iota(jnp.int32, (PAIR, key_count), 0)
    key_id = lax.broadcasted_iota(jnp.int32, (PAIR, key_count), 1)
    bias = jnp.zeros((PAIR, key_count), f32)
    for block in range(blocks):
        here = (key_id >= block * rows + limits[item, block]) & (key_id < (block + 1) * rows)
        bias = jnp.where(here, NEGATIVE, bias)
    spare = jnp.where((row_id & (HEAD_DIM - 1)) == 0, bias, 0.0)
    kt_ref[0] = jnp.where(row_id < HEAD_DIM, flipped, spare).astype(bf16)
    kt_ref[1] = jnp.where(row_id < HEAD_DIM, spare, flipped).astype(bf16)
    va_ref[0] = jnp.where(first, values, 1.0).astype(bf16)
    va_ref[1] = jnp.where(first, 1.0, values).astype(bf16)
    lanes = lanes_of((step, PAIR))
    head_first = lanes < HEAD_DIM
    one = jnp.where((lanes & (HEAD_DIM - 1)) == 0, 1.0, 0.0)

    def body(index, carry):
        place = pl.ds(pl.multiple_of(index * step, step), step)
        query = q_ref[place, :].astype(f32)
        outs, tops = [], []
        for head in range(2):
            mine = head_first if head == 0 else jnp.logical_not(head_first)
            query_head = jnp.where(mine, query, one).astype(bf16)
            scores = dot_rows(query_head, kt_ref[head])
            top = jnp.max(scores, axis=1, keepdims=True)
            weights = jnp.exp(scores - top).astype(bf16)
            outs.append(dot_rows(weights, va_ref[head]))
            tops.append(top)
        acc = jnp.where(head_first, outs[0], outs[1])
        total = pltpu.roll(jnp.where(head_first, outs[1], outs[0]), HEAD_DIM, 1)
        top = jnp.where(head_first, tops[0], tops[1])
        if final:
            other_top = top_in[place, :]
            new_top = jnp.maximum(top, other_top)
            scale_here = jnp.exp(top - new_top)
            scale_there = jnp.exp(other_top - new_top)
            total = total * scale_here + sum_in[place, :] * scale_there
            acc = acc * scale_here + acc_in[place, :] * scale_there
            out_ref[place, :] = acc / total
            lse_ref[place, :] = pltpu.roll(new_top + jnp.log(total), HEAD_DIM, 1)
        else:
            acc_out[place, :] = acc
            top_out[place, :] = top
            sum_out[place, :] = total
        return carry

    lax.fori_loop(0, query_rows // step, body, 0)


def attend(limits, queries, keys, values, rows, blocks, before):
    total, width = queries.shape
    items = total // rows
    key_count = rows * blocks
    step = chunk_of(rows, 208)
    query_block = pl.BlockSpec((rows, PAIR), lambda i, p, *_: (i, p))
    key_block = pl.BlockSpec((key_count, PAIR), lambda i, p, *_: (i, p))
    final = before is not None
    extra = list(before) if final else []
    outs = 2 if final else 3
    return pl.pallas_call(
        functools.partial(forward_kernel, final, rows, blocks, step),
        grid_spec=pltpu.PrefetchScalarGridSpec(
            num_scalar_prefetch=1,
            grid=(items, PAIRS),
            in_specs=[query_block, key_block, key_block] + [query_block] * len(extra),
            out_specs=[query_block] * outs,
            scratch_shapes=[
                pltpu.VMEM((2, PAIR, key_count), bf16),
                pltpu.VMEM((2, key_count, PAIR), bf16),
            ],
        ),
        out_shape=[jax.ShapeDtypeStruct((total, width), f32)] * outs,
        compiler_params=params(2),
        cost_estimate=cost(
            16 * total * key_count * width, 12 * total * width, total * key_count * HEADS
        ),
        name="attend",
    )(limits, queries, keys, values, *extra)


def split_three(value):
    high = value.astype(bf16).astype(f32)
    rest = value - high
    middle = rest.astype(bf16).astype(f32)
    return high, middle, rest - middle


def backward_kernel(
    last, rows, blocks, step, limits, q_ref, k_ref, v_ref, g_ref, out_ref, lse_ref, normed_ref, *rest
):
    if last:
        before_ref, dw_in, cat_ref, dw_ref, dw_acc, qt_ref, gt_ref, dqt_ref = rest
    else:
        dq_ref, cat_ref, dw_ref, dw_acc, qt_ref, gt_ref, dqt_ref = rest
    item = pl.program_id(1)
    query_rows = q_ref.shape[0]
    lanes = lanes_of((query_rows, PAIR))
    head_first = lanes < HEAD_DIM
    spare_lane = lanes & (HEAD_DIM - 1)

    def spare(parts, mask_one):
        high, middle, low = parts
        value = jnp.where(spare_lane == 0, high, 0.0)
        value = jnp.where(spare_lane == 1, middle, value)
        value = jnp.where(spare_lane == 2, low, value)
        return jnp.where(spare_lane == 3, mask_one, value)

    query = q_ref[...].astype(f32)
    grad = g_ref[...].astype(f32)
    product = grad * out_ref[...]
    delta_first = jnp.sum(jnp.where(head_first, product, 0.0), axis=1, keepdims=True)
    delta_second = jnp.sum(jnp.where(head_first, 0.0, product), axis=1, keepdims=True)
    delta = jnp.where(head_first, delta_second, delta_first)
    lse_spare = spare(split_three(-lse_ref[...]), 1.0)
    delta_spare = spare(split_three(-delta), 0.0)
    qt_ref[0] = jnp.where(head_first, query, lse_spare).T.astype(bf16)
    qt_ref[1] = jnp.where(head_first, lse_spare, query).T.astype(bf16)
    gt_ref[0] = jnp.where(head_first, grad, delta_spare).T.astype(bf16)
    gt_ref[1] = jnp.where(head_first, delta_spare, grad).T.astype(bf16)
    dqt_ref[...] = jnp.zeros_like(dqt_ref)

    key_lanes = lanes_of((step, PAIR))
    key_first = key_lanes < HEAD_DIM
    key_spare = key_lanes & (HEAD_DIM - 1)
    key_row = lax.broadcasted_iota(jnp.int32, (step, PAIR), 0)
    ones = jnp.where(key_spare < 3, 1.0, 0.0)
    per_block = rows // step

    def body(index, carry):
        place = pl.ds(pl.multiple_of(index * step, step), step)
        block = index // per_block
        limit = limits[item, block] - (index - block * per_block) * step
        bias = jnp.where(key_row >= limit, NEGATIVE, 0.0)
        key = k_ref[place, :].astype(f32)
        value = v_ref[place, :].astype(f32)
        key_aug = jnp.where(key_spare == 3, bias, ones)
        key_flipped = key.T.astype(bf16)
        dks, dvs = [], []
        for head in range(2):
            mine = key_first if head == 0 else jnp.logical_not(key_first)
            key_head = jnp.where(mine, key, key_aug).astype(bf16)
            value_head = jnp.where(mine, value, ones).astype(bf16)
            probs = jnp.exp(dot_rows(key_head, qt_ref[head]))
            grad_probs = dot_rows(value_head, gt_ref[head])
            grad_scores = (probs * grad_probs).astype(bf16)
            dvs.append(dot_rows(probs.astype(bf16), g_ref[...]))
            dks.append(dot_rows(grad_scores, q_ref[...]))
            own = pl.ds(head * HEAD_DIM, HEAD_DIM)
            half = key_flipped[head * HEAD_DIM:(head + 1) * HEAD_DIM]
            dqt_ref[own, :] += dot_rows(half, grad_scores)
        cat_ref[place, :PAIR] = jnp.where(key_first, dks[0], dks[1]).astype(bf16)
        cat_ref[place, PAIR:2 * PAIR] = jnp.where(key_first, dvs[0], dvs[1]).astype(bf16)
        return carry

    lax.fori_loop(0, blocks * per_block, body, 0)
    result = dqt_ref[...].T
    if last:
        cat_ref[:, 2 * PAIR:] = ((result + before_ref[...]) * SCALE).astype(bf16)
    else:
        dq_ref[...] = result
    added = dot_left(normed_ref[...], cat_ref[...])
    items = pl.num_programs(1)

    @pl.when(item == 0)
    def _():
        dw_acc[...] = added
        if last:
            dw_acc[:, :2 * PAIR] += dw_in[0]

    @pl.when(item > 0)
    def _():
        dw_acc[...] += added

    @pl.when(item == items - 1)
    def _():
        dw_ref[0] = dw_acc[...].astype(dw_ref.dtype)


def attend_back(
    limits, queries, keys, values, grads, outs, lse, normed, rows, blocks, first, count, before
):
    total, width = queries.shape
    items = total // rows
    key_count = rows * blocks
    step = chunk_of(rows, 208)
    last = before is not None
    cat = (3 if last else 2) * PAIR
    query_block = pl.BlockSpec((rows, PAIR), lambda p, i, *_: (i, first + p))
    key_block = pl.BlockSpec((key_count, PAIR), lambda p, i, *_: (i, first + p))
    normed_block = pl.BlockSpec((key_count, width), lambda p, i, *_: (i, 0))
    part_block = pl.BlockSpec((rows, PAIR), lambda p, i, *_: (i, p))
    cat_block = pl.BlockSpec((key_count, cat), lambda p, i, *_: (i, p))
    weight_block = pl.BlockSpec((1, width, cat), lambda p, i, *_: (p, 0, 0))
    weight_in = pl.BlockSpec((1, width, 2 * PAIR), lambda p, i, *_: (p, 0, 0))
    shape = jax.ShapeDtypeStruct
    cat_shape = shape((total * blocks, cat * count), bf16)
    if last:
        extra, extra_specs = list(before), [part_block, weight_in]
        out_shape = [cat_shape, shape((count, width, cat), bf16)]
        out_specs = [cat_block, weight_block]
    else:
        extra, extra_specs = [], []
        out_shape = [shape((total, PAIR * count), f32), cat_shape, shape((count, width, cat), f32)]
        out_specs = [part_block, cat_block, weight_block]
    return pl.pallas_call(
        functools.partial(backward_kernel, last, rows, blocks, step),
        grid_spec=pltpu.PrefetchScalarGridSpec(
            num_scalar_prefetch=1,
            grid=(count, items),
            in_specs=[query_block, key_block, key_block]
            + [query_block] * 3
            + [normed_block]
            + extra_specs,
            out_specs=out_specs,
            scratch_shapes=[
                pltpu.VMEM((width, cat), f32),
                pltpu.VMEM((2, PAIR, rows), bf16),
                pltpu.VMEM((2, PAIR, rows), bf16),
                pltpu.VMEM((PAIR, rows), f32),
            ],
        ),
        out_shape=out_shape,
        compiler_params=params(2),
        cost_estimate=cost(
            40 * total * key_count * PAIR * count,
            16 * total * PAIR * count,
            2 * total * key_count * count,
        ),
        name="attend_back",
    )(limits, queries, keys, values, grads, outs, lse, normed, *extra)


def feed_kernel(
    x_ref, mix_ref, dy_ref, w_output, w_expand, w_reduce, b_output, b_expand, b_reduce, gain, shift,
    y_ref, dmid_ref, dmix_ref, dw_ref, line_ref,
    middle_ref, normed_ref, y_acc, grad_acc,
):
    part = pl.program_id(0)

    @pl.when(part == 0)
    def _():
        mixed = mix_ref[...].astype(bf16)
        middle = x_ref[...].astype(f32) + dot_rows(mixed, w_output[...]) + b_output[...]
        middle_ref[...] = middle
        hat, _ = hat_rows(middle)
        normed_ref[...] = (hat * gain[...] + shift[...]).astype(bf16)
        y_acc[...] = middle + b_reduce[...]
        grad_acc[...] = jnp.zeros_like(grad_acc)
        line_ref[1:2, :] = column_sums(dy_ref[...].astype(f32))

    normed = normed_ref[...]
    upper = dot_rows(normed, w_expand[...]) + b_expand[...]
    cumulative = 0.5 * lax.erf(upper * math.sqrt(0.5)) + 0.5
    density = jnp.exp(upper * upper * -0.5) * (1.0 / math.sqrt(2.0 * math.pi))
    active = (upper * cumulative).astype(bf16)
    slope = cumulative + upper * density
    y_acc[...] += dot_rows(active, w_reduce[...])
    dw_ref[1 + 2 * part] = dot_left(active, dy_ref[...]).astype(bf16)
    grad_upper = (dot_right(dy_ref[...], w_reduce[...]) * slope).astype(bf16)
    line_ref[pl.ds(4 + part, 1), :] = column_sums(grad_upper.astype(f32))
    dw_ref[2 + 2 * part] = dot_left(normed, grad_upper).astype(bf16)
    grad_acc[...] += dot_right(grad_upper, w_expand[...])

    @pl.when(part == pl.num_programs(0) - 1)
    def _():
        y_ref[...] = y_acc[...].astype(bf16)
        grad = grad_acc[...]
        hat, inverse = hat_rows(middle_ref[...])
        line_ref[2:3, :] = column_sums(grad * hat)
        line_ref[3:4, :] = column_sums(grad)
        dmid = hat_back(grad * gain[...], hat, inverse) + dy_ref[...].astype(f32)
        dmid_ref[...] = dmid
        branch = dmid.astype(bf16)
        line_ref[0:1, :] = column_sums(branch.astype(f32))
        dw_ref[0] = dot_left(mix_ref[...].astype(bf16), branch).astype(bf16)
        dmix_ref[...] = dot_right(branch, w_output[...]).astype(bf16)


def feed(x, mixed, dy, w_output, w_expand, w_reduce, b_output, b_expand, b_reduce, gain, shift):
    rows, width = x.shape
    hidden = w_expand.shape[1]
    parts = hidden // width
    row = whole((rows, width))
    line = whole((1, width))
    expand = pl.BlockSpec((width, width), lambda i: (0, i))
    reduce = pl.BlockSpec((width, width), lambda i: (i, 0))
    hidden_line = pl.BlockSpec((1, width), lambda i: (0, i))
    weights = (1 + 2 * parts, width, width)
    lines = (4 + parts, width)
    shape = jax.ShapeDtypeStruct
    return pl.pallas_call(
        feed_kernel,
        grid=(parts,),
        in_specs=[row, row, row, whole((width, width)), expand, reduce, line, hidden_line, line, line, line],
        out_specs=[row, row, row, whole(weights), whole(lines)],
        out_shape=[
            shape((rows, width), bf16),
            shape((rows, width), f32),
            shape((rows, width), bf16),
            shape(weights, bf16),
            shape(lines, f32),
        ],
        scratch_shapes=[
            pltpu.VMEM((rows, width), f32),
            pltpu.VMEM((rows, width), bf16),
            pltpu.VMEM((rows, width), f32),
            pltpu.VMEM((rows, width), f32),
        ],
        compiler_params=params(1),
        cost_estimate=cost(12 * rows * width * hidden + 6 * rows * width * width, 20 * rows * width, 2 * rows * hidden),
        name="feed",
    )(x, mixed, dy, w_output, w_expand, w_reduce, b_output, b_expand, b_reduce, gain, shift)


def gather_parts(refs, part, parts):
    blocks = []
    for ref in refs:
        pairs = ref.shape[1] // (parts * PAIR)
        for pair in range(pairs):
            start = (pair * parts + part) * PAIR
            blocks.append(ref[:, start:start + PAIR])
    return jnp.concatenate(blocks, axis=1)


def other_kernel(cats, x_ref, w_key, w_value, *rest):
    cat_refs, (send_ref, line_ref) = rest[:cats], rest[cats:]
    dk = gather_parts(cat_refs, 0, 2)
    dv = gather_parts(cat_refs, 1, 2)
    grad = dot_right(dk, w_key[...]) + dot_right(dv, w_value[...])
    send_ref[...] = grad.astype(bf16)
    hat, _ = hat_rows(x_ref[...].astype(f32))

    @pl.when(pl.program_id(0) == 0)
    def _():
        line_ref[...] = jnp.zeros_like(line_ref)

    line_ref[1:2, :] += column_sums(dv.astype(f32))
    line_ref[2:3, :] += column_sums(grad * hat)
    line_ref[3:4, :] += column_sums(grad)


def other_grads(x, cats, w_key, w_value, rows):
    total, width = x.shape
    step = chunk_of(rows, 272)
    row = pl.BlockSpec((step, width), lambda i: (i, 0))
    square = whole((width, width))
    shape = jax.ShapeDtypeStruct
    return pl.pallas_call(
        functools.partial(other_kernel, len(cats)),
        grid=(total // step,),
        in_specs=[row] + [square] * 2
        + [pl.BlockSpec((step, c.shape[1]), lambda i: (i, 0)) for c in cats],
        out_specs=[row, whole((8, width))],
        out_shape=[shape((total, width), bf16), shape((8, width), f32)],
        compiler_params=params(1),
        cost_estimate=cost(4 * total * width * width, 8 * total * width),
        name="other_grads",
    )(x, w_key, w_value, *cats)


def own_kernel(cats, x_ref, recv_ref, dmid_ref, w_query, w_key, w_value, gain, line_in, *rest):
    cat_refs, (dx_ref, line_ref) = rest[:cats], rest[cats:]
    dk = gather_parts(cat_refs, 0, 3)
    dv = gather_parts(cat_refs, 1, 3)
    dq = gather_parts(cat_refs, 2, 3)
    grad = dot_right(dq, w_query[...]) + dot_right(dk, w_key[...]) + dot_right(dv, w_value[...])
    hat, inverse = hat_rows(x_ref[...].astype(f32))

    @pl.when(pl.program_id(0) == 0)
    def _():
        line_ref[...] = line_in[...]

    line_ref[0:1, :] += column_sums(dq.astype(f32))
    line_ref[1:2, :] += column_sums(dv.astype(f32))
    line_ref[2:3, :] += column_sums(grad * hat)
    line_ref[3:4, :] += column_sums(grad)
    for index in range(recv_ref.shape[0]):
        grad = grad + recv_ref[index].astype(f32)
    dx_ref[...] = hat_back(grad * gain[...], hat, inverse) + dmid_ref[...]


def own_grads(x, cats, recv, dmid, w_query, w_key, w_value, gain, lines):
    rows, width = x.shape
    step = chunk_of(rows, 272)
    row = pl.BlockSpec((step, width), lambda i: (i, 0))
    square = whole((width, width))
    shape = jax.ShapeDtypeStruct
    return pl.pallas_call(
        functools.partial(own_kernel, len(cats)),
        grid=(rows // step,),
        in_specs=[row, pl.BlockSpec((recv.shape[0], step, width), lambda i: (0, i, 0)), row]
        + [square] * 3
        + [whole((1, width)), whole((8, width))]
        + [pl.BlockSpec((step, c.shape[1]), lambda i: (i, 0)) for c in cats],
        out_specs=[row, whole((8, width))],
        out_shape=[shape((rows, width), f32), shape((8, width), f32)],
        compiler_params=params(1),
        cost_estimate=cost(6 * rows * width * width, 16 * rows * width),
        name="own_grads",
    )(x, recv, dmid, w_query, w_key, w_value, gain, lines, *cats)


class Slice:
    def __init__(self):
        group = lax.axis_size("grp")
        batch = lax.axis_size("dp")
        cores = 2 if batch % 2 == 0 else 1
        rest = batch // cores
        side = 2 if rest % 2 == 0 else 1
        self.group, self.batch, self.cores, self.side = group, batch, cores, side
        self.sizes = (cores, side * group, rest // side)
        self.places = self.coords(lax.axis_index("dp"), lax.axis_index("grp"))

    def coords(self, batch, member):
        core = batch % self.cores
        side = batch // self.cores % self.side
        return (core, side * self.group + member, batch // (self.cores * self.side))

    def linear(self, coords):
        core, plane, line = coords
        side, member = plane // self.group, plane % self.group
        batch = (line * self.side + side) * self.cores + core
        return batch * self.group + member

    def send(self, array, stage, shift):
        pairs = []
        for batch in range(self.batch):
            for member in range(self.group):
                coords = list(self.coords(batch, member))
                here = self.linear(coords)
                coords[stage] = (coords[stage] + shift) % self.sizes[stage]
                pairs.append((here, self.linear(coords)))
        return lax.ppermute(array, ("dp", "grp"), pairs)

    def scatter(self, array):
        rows, width = array.shape
        count = math.prod(self.sizes)
        chunk = -(-rows // (16 * count)) * 16
        if chunk * count != rows:
            array = jnp.pad(array, ((0, chunk * count - rows), (0, 0)))
        value = array.reshape(*self.sizes, chunk, width)
        for stage, size in enumerate(self.sizes):
            place = self.places[stage]
            came = [
                self.send(lax.dynamic_index_in_dim(value, (place + s) % size, 0, False), stage, s)
                for s in range(1, size)
            ]
            total = lax.dynamic_index_in_dim(value, place, 0, False).astype(f32)
            for part in came:
                total = total + part.astype(f32)
            value = total.astype(bf16)
        return value

    def gather(self, chunk):
        value = chunk[None]
        for stage in (2, 1, 0):
            parts = [value] + [self.send(value, stage, s) for s in range(1, self.sizes[stage])]
            value = jnp.concatenate(parts, 0)
        return value

    def origins(self):
        cores, planes, lines = self.sizes
        core = (self.places[0] - jnp.arange(cores)) % cores
        plane = (self.places[1] - jnp.arange(planes)) % planes
        line = (self.places[2] - jnp.arange(lines)) % lines
        index = (core[:, None, None] * planes + plane[None, :, None]) * lines + line[None, None, :]
        return index.reshape(-1).astype(jnp.int32)

    def total(self, array):
        for stage, size in enumerate(self.sizes):
            parts = [self.send(array, stage, s) for s in range(1, size)]
            for part in parts:
                array = array + part
        return array


def place_chunks(origins, in_ref, out_ref):
    count, chunk, _ = in_ref.shape
    for index in range(count):
        out_ref[index * chunk:(index + 1) * chunk, :] = in_ref[origins[index]]


def feed_weights_kernel(origins, in_ref, dwo_ref, dwe_ref, dwr_ref, flat):
    width = in_ref.shape[2]
    place_chunks(origins, in_ref, flat)
    dwo_ref[...] = flat[:width, :].astype(f32)
    for part in range(dwr_ref.shape[0] // width):
        start = (1 + 2 * part) * width
        span = slice(part * width, (part + 1) * width)
        dwr_ref[span, :] = flat[start:start + width, :].astype(f32)
        dwe_ref[:, span] = flat[start + width:start + 2 * width, :].astype(f32)


def feed_weights(origins, chunks, hidden):
    count, chunk, width = chunks.shape
    shape = jax.ShapeDtypeStruct
    shapes = [(width, width), (width, hidden), (hidden, width)]
    return pl.pallas_call(
        feed_weights_kernel,
        grid_spec=pltpu.PrefetchScalarGridSpec(
            num_scalar_prefetch=1,
            grid=(1,),
            in_specs=[whole(chunks.shape)],
            out_specs=[whole(s) for s in shapes],
            scratch_shapes=[pltpu.VMEM((count * chunk, width), bf16)],
        ),
        out_shape=[shape(s, f32) for s in shapes],
        compiler_params=params(1),
        cost_estimate=cost(0, 6 * chunks.size),
        name="feed_weights",
    )(origins, chunks)


def project_weights_kernel(pairs, origins, *refs):
    groups = len(pairs)
    ins, outs, flats = refs[:groups], refs[groups:groups + 3], refs[groups + 3:]
    dwq_ref, dwk_ref, dwv_ref = outs
    width = dwq_ref.shape[0]
    pair = 0
    for in_ref, flat, count in zip(ins, flats, pairs):
        place_chunks(origins, in_ref, flat)
        for index in range(count):
            block = flat[index * width:(index + 1) * width, :].astype(f32)
            span = slice(pair * PAIR, (pair + 1) * PAIR)
            dwk_ref[:, span] = block[:, :PAIR]
            dwv_ref[:, span] = block[:, PAIR:2 * PAIR]
            dwq_ref[:, span] = block[:, 2 * PAIR:]
            pair += 1


def project_weights(origins, chunks, pairs, width):
    shape = jax.ShapeDtypeStruct
    square = (width, width)
    return pl.pallas_call(
        functools.partial(project_weights_kernel, pairs),
        grid_spec=pltpu.PrefetchScalarGridSpec(
            num_scalar_prefetch=1,
            grid=(1,),
            in_specs=[whole(c.shape) for c in chunks],
            out_specs=[whole(square)] * 3,
            scratch_shapes=[
                pltpu.VMEM((c.shape[0] * c.shape[1], c.shape[2]), bf16) for c in chunks
            ],
        ),
        out_shape=[shape(square, f32)] * 3,
        compiler_params=params(1),
        cost_estimate=cost(0, 20 * width * width),
        name="project_weights",
    )(origins, *chunks)


def body(
    layer_input,
    lang_counts,
    w_query,
    w_key,
    w_value,
    w_output,
    w_expand,
    w_reduce,
    b_query,
    b_value,
    b_output,
    b_expand,
    b_reduce,
    gain_attn,
    shift_attn,
    gain_mlp,
    shift_mlp,
    cotangent,
):
    items, own_rows, width = layer_input.shape
    group = lax.axis_size("grp")
    me = lax.axis_index("grp")
    rows = -(-own_rows // 16) * 16
    total = items * rows
    patch_rows = VIEWS * PATCH
    shifts = range(1, group)
    axes = ("dp", "grp")

    def padded(array):
        if rows != own_rows:
            array = jnp.pad(array, ((0, 0), (0, rows - own_rows), (0, 0)))
        return array.reshape(total, width)

    def unpadded(array):
        return array.reshape(items, rows, width)[:, :own_rows]

    def limit_of(owner):
        return jnp.clip(patch_rows + lang_counts - owner * own_rows, 0, own_rows)

    def line(vector):
        return vector.reshape(1, -1)

    def group_shift(array, shift):
        return lax.ppermute(array, "grp", [(i, (i + shift) % group) for i in range(group)])

    def joined(parts):
        if len(parts) == 1:
            return parts[0]
        return jnp.stack([p.reshape(items, rows, width) for p in parts], 1).reshape(-1, width)

    x = padded(layer_input)
    dy = padded(cotangent)
    others = [group_shift(x, -shift) for shift in shifts]
    own_limits = limit_of(me).reshape(items, 1)
    other_limits = jnp.stack([limit_of((me + shift) % group) for shift in shifts], 1)

    weights = (w_query, w_key, w_value, line(b_query), line(b_value))
    norms = (line(gain_attn), line(shift_attn))
    normed, keys, values, queries = project(x, *norms, *weights, with_query=True)
    first = attend(own_limits, queries, keys, values, rows, 1, None)
    x_other = joined(others)
    normed_other, keys_other, values_other = project(x_other, *norms, *weights, with_query=False)
    mixed, lse = attend(other_limits, queries, keys_other, values_other, rows, group - 1, first)

    output, dmid, dmix, dw_feed, feed_lines = feed(
        x, mixed, dy, w_output, w_expand, w_reduce, line(b_output), line(b_expand), line(b_reduce),
        line(gain_mlp), line(shift_mlp),
    )
    devices = Slice()
    feed_chunk = devices.scatter(dw_feed.reshape(-1, width))

    parts, cats_other, dw_parts = [], [], []
    for start, count in GROUPS:
        part, cat, dw = attend_back(
            other_limits, queries, keys_other, values_other, dmix, mixed, lse, normed_other,
            rows, group - 1, start, count, None,
        )
        parts.append(part)
        cats_other.append(cat)
        dw_parts.append(dw)
    send, lines = other_grads(x_other, cats_other, w_key, w_value, rows)
    send = send.reshape(items, group - 1, rows, width)
    received = jnp.stack(
        [group_shift(send[:, shift - 1].reshape(total, width), shift) for shift in shifts]
    )
    cats, chunks = [], []
    for (start, count), part, dw_part in zip(GROUPS, parts, dw_parts):
        cat, dw = attend_back(
            own_limits, queries, keys, values, dmix, mixed, lse, normed,
            rows, 1, start, count, (part, dw_part),
        )
        cats.append(cat)
        chunks.append(devices.scatter(dw.reshape(-1, dw.shape[2])))
    dx, lines = own_grads(
        x, cats, received, dmid, w_query, w_key, w_value, line(gain_attn), lines
    )
    origins = devices.origins()
    dwo, dwe, dwr = feed_weights(origins, devices.gather(feed_chunk), w_expand.shape[1])
    dwq, dwk, dwv = project_weights(
        origins, [devices.gather(c) for c in chunks], [count for _, count in GROUPS], width
    )
    lines = devices.total(jnp.concatenate([lines[:4], feed_lines], 0))
    dbq, dbv, dgain, dshift, dbo, dbr, dgain_mlp, dshift_mlp = lines[:8]
    dbe = lines[8:].reshape(-1)
    return (
        unpadded(output),
        unpadded(dx),
        dwq, dwk, dwv, dwo, dwe, dwr,
        dbq, dbv, dbo, dbe, dbr, dgain, dshift, dgain_mlp, dshift_mlp,
    )


def solution(mesh):
    rows = P("dp", "grp", None)
    in_specs = (rows, P("dp")) + (P(),) * 15 + (rows,)
    out_specs = (rows, rows) + (P(),) * 15
    return jax.shard_map(body, mesh=mesh, in_specs=in_specs, out_specs=out_specs, check_vma=False)
```

```python
import functools
import math

import jax
import jax.numpy as jnp
from jax import lax
from jax.experimental import pallas as pl
from jax.experimental.pallas import tpu as pltpu
from jax.sharding import PartitionSpec as P

HEADS = 8
HEAD_DIM = 64
VIEWS = 5
PATCH = 400
PAIR = 2 * HEAD_DIM
PAIRS = HEADS // 2

EPSILON = 1e-05
NEGATIVE = -1e30
SCALE = 1.0 / math.sqrt(HEAD_DIM)

bf16 = jnp.bfloat16
f32 = jnp.float32


def dot_rows(left, right):
    return lax.dot_general(
        left, right, (((1,), (0,)), ((), ())), preferred_element_type=f32
    )


def dot_left(left, right):
    return lax.dot_general(
        left, right, (((0,), (0,)), ((), ())), preferred_element_type=f32
    )


def dot_right(left, right):
    return lax.dot_general(
        left, right, (((1,), (1,)), ((), ())), preferred_element_type=f32
    )


def chunk_of(rows, limit):
    best = 16
    for size in range(16, limit + 1, 16):
        if rows % size == 0:
            best = size
    return best


def hat_rows(matrix):
    center = matrix - jnp.mean(matrix, axis=-1, keepdims=True)
    spread = jnp.mean(center * center, axis=-1, keepdims=True)
    inverse = lax.rsqrt(spread + EPSILON)
    return center * inverse, inverse


def hat_back(grad_hat, hat, inverse):
    mean_grad = jnp.mean(grad_hat, axis=-1, keepdims=True)
    mean_cross = jnp.mean(grad_hat * hat, axis=-1, keepdims=True)
    return inverse * (grad_hat - mean_grad - hat * mean_cross)


def column_sums(matrix):
    return jnp.sum(matrix, axis=0, keepdims=True)


VMEM_MIB = 60
ANYWHERE = pl.BlockSpec(memory_space=pl.ANY)


def params(axes):
    return pltpu.CompilerParams(
        dimension_semantics=("arbitrary",) * axes, vmem_limit_bytes=VMEM_MIB << 20
    )


def cost(flops, bytes_accessed, transcendentals=0):
    return pl.CostEstimate(
        flops=int(flops), bytes_accessed=int(bytes_accessed), transcendentals=int(transcendentals)
    )


def whole(shape):
    return pl.BlockSpec(shape, lambda *_: (0,) * len(shape))


def project_kernel(with_query, x_ref, gain, shift, w_query, w_key, w_value, b_query, b_value, *outs):
    hat, _ = hat_rows(x_ref[...].astype(f32))
    normed = (hat * gain[...] + shift[...]).astype(bf16)
    if with_query:
        normed_ref, key_ref, value_ref, query_ref = outs
        query = (dot_rows(normed, w_query[...]) + b_query[...]).astype(bf16)
        query_ref[...] = (query.astype(f32) * SCALE).astype(bf16)
    else:
        normed_ref, key_ref, value_ref = outs
    normed_ref[...] = normed
    key_ref[...] = dot_rows(normed, w_key[...]).astype(bf16)
    value_ref[...] = (dot_rows(normed, w_value[...]) + b_value[...]).astype(bf16)


def project(x, gain, shift, w_query, w_key, w_value, b_query, b_value, with_query):
    rows, width = x.shape
    step = chunk_of(rows, 272)
    count = 4 if with_query else 3
    row_block = pl.BlockSpec((step, width), lambda i: (i, 0))
    return pl.pallas_call(
        functools.partial(project_kernel, with_query),
        grid=(rows // step,),
        in_specs=[row_block, whole((1, width)), whole((1, width))]
        + [whole((width, width))] * 3
        + [whole((1, width))] * 2,
        out_specs=[row_block] * count,
        out_shape=[jax.ShapeDtypeStruct((rows, width), bf16)] * count,
        compiler_params=params(1),
        cost_estimate=cost(2 * rows * width * width * (count - 1), 2 * rows * width * (count + 1)),
        name="project",
    )(x, gain, shift, w_query, w_key, w_value, b_query, b_value)


def lanes_of(shape):
    return lax.broadcasted_iota(jnp.int32, shape, 1)


def forward_kernel(
    final, rows, blocks, step, limits, q_ref, k_ref, v_ref, *rest
):
    if final:
        acc_in, top_in, sum_in, out_ref, lse_ref, kt_ref, va_ref = rest
    else:
        acc_out, top_out, sum_out, kt_ref, va_ref = rest
    item = pl.program_id(0)
    key_count = rows * blocks
    query_rows = q_ref.shape[0]
    keys = k_ref[...].astype(f32)
    values = v_ref[...].astype(f32)
    first = lanes_of((key_count, PAIR)) < HEAD_DIM
    flipped = keys.T
    row_id = lax.broadcasted_iota(jnp.int32, (PAIR, key_count), 0)
    key_id = lax.broadcasted_iota(jnp.int32, (PAIR, key_count), 1)
    bias = jnp.zeros((PAIR, key_count), f32)
    for block in range(blocks):
        here = (key_id >= block * rows + limits[item, block]) & (key_id < (block + 1) * rows)
        bias = jnp.where(here, NEGATIVE, bias)
    spare = jnp.where((row_id & (HEAD_DIM - 1)) == 0, bias, 0.0)
    kt_ref[0] = jnp.where(row_id < HEAD_DIM, flipped, spare).astype(bf16)
    kt_ref[1] = jnp.where(row_id < HEAD_DIM, spare, flipped).astype(bf16)
    va_ref[0] = jnp.where(first, values, 1.0).astype(bf16)
    va_ref[1] = jnp.where(first, 1.0, values).astype(bf16)
    lanes = lanes_of((step, PAIR))
    head_first = lanes < HEAD_DIM
    one = jnp.where((lanes & (HEAD_DIM - 1)) == 0, 1.0, 0.0)

    def body(index, carry):
        place = pl.ds(pl.multiple_of(index * step, step), step)
        query = q_ref[place, :].astype(f32)
        outs, tops = [], []
        for head in range(2):
            mine = head_first if head == 0 else jnp.logical_not(head_first)
            query_head = jnp.where(mine, query, one).astype(bf16)
            scores = dot_rows(query_head, kt_ref[head])
            top = jnp.max(scores, axis=1, keepdims=True)
            weights = jnp.exp(scores - top).astype(bf16)
            outs.append(dot_rows(weights, va_ref[head]))
            tops.append(top)
        acc = jnp.where(head_first, outs[0], outs[1])
        total = pltpu.roll(jnp.where(head_first, outs[1], outs[0]), HEAD_DIM, 1)
        top = jnp.where(head_first, tops[0], tops[1])
        if final:
            other_top = top_in[place, :]
            new_top = jnp.maximum(top, other_top)
            scale_here = jnp.exp(top - new_top)
            scale_there = jnp.exp(other_top - new_top)
            total = total * scale_here + sum_in[place, :] * scale_there
            acc = acc * scale_here + acc_in[place, :] * scale_there
            out_ref[place, :] = acc / total
            lse_ref[place, :] = pltpu.roll(new_top + jnp.log(total), HEAD_DIM, 1)
        else:
            acc_out[place, :] = acc
            top_out[place, :] = top
            sum_out[place, :] = total
        return carry

    lax.fori_loop(0, query_rows // step, body, 0)


def attend(limits, queries, keys, values, rows, blocks, before):
    total, width = queries.shape
    items = total // rows
    key_count = rows * blocks
    step = chunk_of(rows, 208)
    query_block = pl.BlockSpec((rows, PAIR), lambda i, p, *_: (i, p))
    key_block = pl.BlockSpec((key_count, PAIR), lambda i, p, *_: (i, p))
    final = before is not None
    extra = list(before) if final else []
    outs = 2 if final else 3
    return pl.pallas_call(
        functools.partial(forward_kernel, final, rows, blocks, step),
        grid_spec=pltpu.PrefetchScalarGridSpec(
            num_scalar_prefetch=1,
            grid=(items, PAIRS),
            in_specs=[query_block, key_block, key_block] + [query_block] * len(extra),
            out_specs=[query_block] * outs,
            scratch_shapes=[
                pltpu.VMEM((2, PAIR, key_count), bf16),
                pltpu.VMEM((2, key_count, PAIR), bf16),
            ],
        ),
        out_shape=[jax.ShapeDtypeStruct((total, width), f32)] * outs,
        compiler_params=params(2),
        cost_estimate=cost(
            16 * total * key_count * width, 12 * total * width, total * key_count * HEADS
        ),
        name="attend",
    )(limits, queries, keys, values, *extra)


def split_three(value):
    high = value.astype(bf16).astype(f32)
    rest = value - high
    middle = rest.astype(bf16).astype(f32)
    return high, middle, rest - middle


def halves(core, block):
    half = block.shape[0] // 2
    upper, lower = block[:half], block[half:]
    mine = jnp.where(core == 0, upper, lower)
    theirs = jnp.where(core == 0, lower, upper)
    return mine.astype(bf16), theirs.astype(bf16)


def backward_kernel(
    last, tokens, rows, blocks, step, limits, core,
    q_ref, k_ref, v_ref, g_ref, out_ref, lse_ref, normed_ref, *rest,
):
    if last:
        before_ref, dw_in, *rest = rest
        cat_ref, keep_ref, send_ref, dw_acc, qt_ref, gt_ref, dqt_ref = rest[tokens:]
    else:
        dq_ref, cat_ref, dw_ref, dw_acc, qt_ref, gt_ref, dqt_ref = rest[tokens:]
    item = pl.program_id(1)
    query_rows = q_ref.shape[0]
    lanes = lanes_of((query_rows, PAIR))
    head_first = lanes < HEAD_DIM
    spare_lane = lanes & (HEAD_DIM - 1)

    def spare(parts, mask_one):
        high, middle, low = parts
        value = jnp.where(spare_lane == 0, high, 0.0)
        value = jnp.where(spare_lane == 1, middle, value)
        value = jnp.where(spare_lane == 2, low, value)
        return jnp.where(spare_lane == 3, mask_one, value)

    query = q_ref[...].astype(f32)
    grad = g_ref[...].astype(f32)
    product = grad * out_ref[...]
    delta_first = jnp.sum(jnp.where(head_first, product, 0.0), axis=1, keepdims=True)
    delta_second = jnp.sum(jnp.where(head_first, 0.0, product), axis=1, keepdims=True)
    delta = jnp.where(head_first, delta_second, delta_first)
    lse_spare = spare(split_three(-lse_ref[...]), 1.0)
    delta_spare = spare(split_three(-delta), 0.0)
    qt_ref[0] = jnp.where(head_first, query, lse_spare).T.astype(bf16)
    qt_ref[1] = jnp.where(head_first, lse_spare, query).T.astype(bf16)
    gt_ref[0] = jnp.where(head_first, grad, delta_spare).T.astype(bf16)
    gt_ref[1] = jnp.where(head_first, delta_spare, grad).T.astype(bf16)
    dqt_ref[...] = jnp.zeros_like(dqt_ref)

    key_lanes = lanes_of((step, PAIR))
    key_first = key_lanes < HEAD_DIM
    key_spare = key_lanes & (HEAD_DIM - 1)
    key_row = lax.broadcasted_iota(jnp.int32, (step, PAIR), 0)
    ones = jnp.where(key_spare < 3, 1.0, 0.0)
    per_block = rows // step

    def body(index, carry):
        place = pl.ds(pl.multiple_of(index * step, step), step)
        block = index // per_block
        limit = limits[item, block] - (index - block * per_block) * step
        bias = jnp.where(key_row >= limit, NEGATIVE, 0.0)
        key = k_ref[place, :].astype(f32)
        value = v_ref[place, :].astype(f32)
        key_aug = jnp.where(key_spare == 3, bias, ones)
        key_flipped = key.T.astype(bf16)
        dks, dvs = [], []
        for head in range(2):
            mine = key_first if head == 0 else jnp.logical_not(key_first)
            key_head = jnp.where(mine, key, key_aug).astype(bf16)
            value_head = jnp.where(mine, value, ones).astype(bf16)
            probs = jnp.exp(dot_rows(key_head, qt_ref[head]))
            grad_probs = dot_rows(value_head, gt_ref[head])
            grad_scores = (probs * grad_probs).astype(bf16)
            dvs.append(dot_rows(probs.astype(bf16), g_ref[...]))
            dks.append(dot_rows(grad_scores, q_ref[...]))
            own = pl.ds(head * HEAD_DIM, HEAD_DIM)
            half = key_flipped[head * HEAD_DIM:(head + 1) * HEAD_DIM]
            dqt_ref[own, :] += dot_rows(half, grad_scores)
        cat_ref[place, :PAIR] = jnp.where(key_first, dks[0], dks[1]).astype(bf16)
        cat_ref[place, PAIR:2 * PAIR] = jnp.where(key_first, dvs[0], dvs[1]).astype(bf16)
        return carry

    lax.fori_loop(0, blocks * per_block, body, 0)
    result = dqt_ref[...].T
    if last:
        cat_ref[:, 2 * PAIR:] = ((result + before_ref[...]) * SCALE).astype(bf16)
    else:
        dq_ref[...] = result
    added = dot_left(normed_ref[...], cat_ref[...])
    items = pl.num_programs(1)

    @pl.when(item == 0)
    def _():
        dw_acc[...] = added
        if last:
            dw_acc[:, :2 * PAIR] += dw_in[0]

    @pl.when(item > 0)
    def _():
        dw_acc[...] += added

    @pl.when(item == items - 1)
    def _():
        if last:
            keep_ref[...], send_ref[...] = halves(core[0], dw_acc[...])
        else:
            dw_ref[0] = dw_acc[...]


def attend_back(
    limits, core, queries, keys, values, grads, outs, lse, normed, rows, blocks, first, count, before,
    tokens,
):
    total, width = queries.shape
    items = total // rows
    key_count = rows * blocks
    step = chunk_of(rows, 208)
    last = before is not None
    cat = (3 if last else 2) * PAIR
    query_block = pl.BlockSpec((rows, PAIR), lambda p, i, *_: (i, first + p))
    key_block = pl.BlockSpec((key_count, PAIR), lambda p, i, *_: (i, first + p))
    normed_block = pl.BlockSpec((key_count, width), lambda p, i, *_: (i, 0))
    part_block = pl.BlockSpec((rows, PAIR), lambda p, i, *_: (i, p))
    cat_block = pl.BlockSpec((key_count, cat), lambda p, i, *_: (i, p))
    half_block = pl.BlockSpec((width // 2, cat), lambda p, i, *_: (p, 0))
    weight_block = pl.BlockSpec((1, width, cat), lambda p, i, *_: (p, 0, 0))
    weight_in = pl.BlockSpec((1, width, 2 * PAIR), lambda p, i, *_: (p, 0, 0))
    shape = jax.ShapeDtypeStruct
    cat_shape = shape((total * blocks, cat * count), bf16)
    if last:
        extra, extra_specs = list(before), [part_block, weight_in]
        out_shape = [cat_shape] + [shape((count * width // 2, cat), bf16)] * 2
        out_specs = [cat_block, half_block, half_block]
    else:
        extra, extra_specs = [], []
        out_shape = [shape((total, PAIR * count), f32), cat_shape, shape((count, width, cat), f32)]
        out_specs = [part_block, cat_block, weight_block]
    return pl.pallas_call(
        functools.partial(backward_kernel, last, len(tokens), rows, blocks, step),
        grid_spec=pltpu.PrefetchScalarGridSpec(
            num_scalar_prefetch=2,
            grid=(count, items),
            in_specs=[query_block, key_block, key_block]
            + [query_block] * 3
            + [normed_block]
            + extra_specs
            + [ANYWHERE] * len(tokens),
            out_specs=out_specs,
            scratch_shapes=[
                pltpu.VMEM((width, cat), f32),
                pltpu.VMEM((2, PAIR, rows), bf16),
                pltpu.VMEM((2, PAIR, rows), bf16),
                pltpu.VMEM((PAIR, rows), f32),
            ],
        ),
        out_shape=out_shape,
        compiler_params=params(2),
        cost_estimate=cost(
            40 * total * key_count * PAIR * count,
            16 * total * PAIR * count,
            2 * total * key_count * count,
        ),
        name="attend_back",
    )(limits, core, queries, keys, values, grads, outs, lse, normed, *extra, *tokens)


def feed_kernel(
    core, x_ref, mix_ref, dy_ref, w_output, w_expand, w_reduce, b_output, b_expand, b_reduce, gain, shift,
    y_ref, dmid_ref, dmix_ref, keep_ref, send_ref, line_ref,
    middle_ref, normed_ref, y_acc, grad_acc,
):
    part = pl.program_id(0)

    def put(index, block):
        keep_ref[index], send_ref[index] = halves(core[0], block)

    @pl.when(part == 0)
    def _():
        mixed = mix_ref[...].astype(bf16)
        middle = x_ref[...].astype(f32) + dot_rows(mixed, w_output[...]) + b_output[...]
        middle_ref[...] = middle
        hat, _ = hat_rows(middle)
        normed_ref[...] = (hat * gain[...] + shift[...]).astype(bf16)
        y_acc[...] = middle + b_reduce[...]
        grad_acc[...] = jnp.zeros_like(grad_acc)
        line_ref[1:2, :] = column_sums(dy_ref[...].astype(f32))

    normed = normed_ref[...]
    upper = dot_rows(normed, w_expand[...]) + b_expand[...]
    cumulative = 0.5 * lax.erf(upper * math.sqrt(0.5)) + 0.5
    density = jnp.exp(upper * upper * -0.5) * (1.0 / math.sqrt(2.0 * math.pi))
    active = (upper * cumulative).astype(bf16)
    slope = cumulative + upper * density
    y_acc[...] += dot_rows(active, w_reduce[...])
    put(1 + 2 * part, dot_left(active, dy_ref[...]))
    grad_upper = (dot_right(dy_ref[...], w_reduce[...]) * slope).astype(bf16)
    line_ref[pl.ds(4 + part, 1), :] = column_sums(grad_upper.astype(f32))
    put(2 + 2 * part, dot_left(normed, grad_upper))
    grad_acc[...] += dot_right(grad_upper, w_expand[...])

    @pl.when(part == pl.num_programs(0) - 1)
    def _():
        y_ref[...] = y_acc[...].astype(bf16)
        grad = grad_acc[...]
        hat, inverse = hat_rows(middle_ref[...])
        line_ref[2:3, :] = column_sums(grad * hat)
        line_ref[3:4, :] = column_sums(grad)
        dmid = hat_back(grad * gain[...], hat, inverse) + dy_ref[...].astype(f32)
        dmid_ref[...] = dmid
        branch = dmid.astype(bf16)
        line_ref[0:1, :] = column_sums(branch.astype(f32))
        put(0, dot_left(mix_ref[...].astype(bf16), branch))
        dmix_ref[...] = dot_right(branch, w_output[...]).astype(bf16)


def feed(core, x, mixed, dy, w_output, w_expand, w_reduce, b_output, b_expand, b_reduce, gain, shift):
    rows, width = x.shape
    hidden = w_expand.shape[1]
    parts = hidden // width
    row = whole((rows, width))
    line = whole((1, width))
    expand = pl.BlockSpec((width, width), lambda i, *_: (0, i))
    reduce = pl.BlockSpec((width, width), lambda i, *_: (i, 0))
    hidden_line = pl.BlockSpec((1, width), lambda i, *_: (0, i))
    weights = (1 + 2 * parts, width // 2, width)
    lines = (4 + parts, width)
    shape = jax.ShapeDtypeStruct
    return pl.pallas_call(
        feed_kernel,
        grid_spec=pltpu.PrefetchScalarGridSpec(
            num_scalar_prefetch=1,
            grid=(parts,),
            in_specs=[row, row, row, whole((width, width)), expand, reduce, line, hidden_line, line, line, line],
            out_specs=[row, row, row, whole(weights), whole(weights), whole(lines)],
            scratch_shapes=[
                pltpu.VMEM((rows, width), f32),
                pltpu.VMEM((rows, width), bf16),
                pltpu.VMEM((rows, width), f32),
                pltpu.VMEM((rows, width), f32),
            ],
        ),
        out_shape=[
            shape((rows, width), bf16),
            shape((rows, width), f32),
            shape((rows, width), bf16),
            shape(weights, bf16),
            shape(weights, bf16),
            shape(lines, f32),
        ],
        compiler_params=params(1),
        cost_estimate=cost(12 * rows * width * hidden + 6 * rows * width * width, 20 * rows * width, 2 * rows * hidden),
        name="feed",
    )(core, x, mixed, dy, w_output, w_expand, w_reduce, b_output, b_expand, b_reduce, gain, shift)


def gather_parts(refs, part, parts):
    blocks = []
    for ref in refs:
        pairs = ref.shape[1] // (parts * PAIR)
        for pair in range(pairs):
            start = (pair * parts + part) * PAIR
            blocks.append(ref[:, start:start + PAIR])
    return jnp.concatenate(blocks, axis=1)


def other_kernel(cats, x_ref, w_key, w_value, *rest):
    cat_refs, (send_ref, line_ref) = rest[:cats], rest[cats:]
    dk = gather_parts(cat_refs, 0, 2)
    dv = gather_parts(cat_refs, 1, 2)
    grad = dot_right(dk, w_key[...]) + dot_right(dv, w_value[...])
    send_ref[...] = grad.astype(bf16)
    hat, _ = hat_rows(x_ref[...].astype(f32))

    @pl.when(pl.program_id(0) == 0)
    def _():
        line_ref[...] = jnp.zeros_like(line_ref)

    line_ref[1:2, :] += column_sums(dv.astype(f32))
    line_ref[2:3, :] += column_sums(grad * hat)
    line_ref[3:4, :] += column_sums(grad)


def other_grads(x, cats, w_key, w_value, rows):
    total, width = x.shape
    step = chunk_of(rows, 272)
    row = pl.BlockSpec((step, width), lambda i: (i, 0))
    square = whole((width, width))
    shape = jax.ShapeDtypeStruct
    return pl.pallas_call(
        functools.partial(other_kernel, len(cats)),
        grid=(total // step,),
        in_specs=[row] + [square] * 2
        + [pl.BlockSpec((step, c.shape[1]), lambda i: (i, 0)) for c in cats],
        out_specs=[row, whole((8, width))],
        out_shape=[shape((total, width), bf16), shape((8, width), f32)],
        compiler_params=params(1),
        cost_estimate=cost(4 * total * width * width, 8 * total * width),
        name="other_grads",
    )(x, w_key, w_value, *cats)


def own_kernel(cats, x_ref, recv_ref, dmid_ref, w_query, w_key, w_value, gain, line_in, *rest):
    cat_refs, (dx_ref, line_ref) = rest[:cats], rest[cats:]
    dk = gather_parts(cat_refs, 0, 3)
    dv = gather_parts(cat_refs, 1, 3)
    dq = gather_parts(cat_refs, 2, 3)
    grad = dot_right(dq, w_query[...]) + dot_right(dk, w_key[...]) + dot_right(dv, w_value[...])
    hat, inverse = hat_rows(x_ref[...].astype(f32))

    @pl.when(pl.program_id(0) == 0)
    def _():
        line_ref[...] = line_in[...]

    line_ref[0:1, :] += column_sums(dq.astype(f32))
    line_ref[1:2, :] += column_sums(dv.astype(f32))
    line_ref[2:3, :] += column_sums(grad * hat)
    line_ref[3:4, :] += column_sums(grad)
    for index in range(recv_ref.shape[0]):
        grad = grad + recv_ref[index].astype(f32)
    dx_ref[...] = hat_back(grad * gain[...], hat, inverse) + dmid_ref[...]


def own_grads(x, cats, recv, dmid, w_query, w_key, w_value, gain, lines):
    rows, width = x.shape
    step = chunk_of(rows, 272)
    row = pl.BlockSpec((step, width), lambda i: (i, 0))
    square = whole((width, width))
    shape = jax.ShapeDtypeStruct
    return pl.pallas_call(
        functools.partial(own_kernel, len(cats)),
        grid=(rows // step,),
        in_specs=[row, pl.BlockSpec((recv.shape[0], step, width), lambda i: (0, i, 0)), row]
        + [square] * 3
        + [whole((1, width)), whole((8, width))]
        + [pl.BlockSpec((step, c.shape[1]), lambda i: (i, 0)) for c in cats],
        out_specs=[row, whole((8, width))],
        out_shape=[shape((rows, width), f32), shape((8, width), f32)],
        compiler_params=params(1),
        cost_estimate=cost(6 * rows * width * width, 16 * rows * width),
        name="own_grads",
    )(x, recv, dmid, w_query, w_key, w_value, gain, lines, *cats)


class Slice:
    def __init__(self):
        group, batch = lax.axis_size("grp"), lax.axis_size("dp")
        rest = batch // 2
        side = 2 if rest % 2 == 0 else 1
        rest //= side
        high = 2 if rest % 2 == 0 else 1
        self.sizes = {"core": 2, "side": side, "member": group, "high": high, "low": rest // high}
        self.count = group * batch
        self.here = self.coords(lax.axis_index("dp") * group + lax.axis_index("grp"))

    def coords(self, linear):
        out = {}
        for name in ("member", "core", "side", "low", "high"):
            out[name] = linear % self.sizes[name]
            linear = linear // self.sizes[name]
        return out

    def linear(self, coords):
        total = 0
        for name in ("high", "low", "side", "core", "member"):
            total = total * self.sizes[name] + coords[name]
        return total

    def size(self, stage):
        return math.prod(self.sizes[name] for name in stage)

    def place(self, stage, coords=None):
        coords = self.here if coords is None else coords
        total = 0
        for name in stage:
            total = total * self.sizes[name] + coords[name]
        return total

    def send(self, array, stage, shift):
        pairs = []
        for source in range(self.count):
            coords = self.coords(source)
            place = (self.place(stage, coords) + shift) % self.size(stage)
            for name in reversed(stage):
                coords[name] = place % self.sizes[name]
                place //= self.sizes[name]
            pairs.append((source, self.linear(coords)))
        return lax.ppermute(array, ("dp", "grp"), pairs)

    def spread(self, parts, stage):
        return [parts[0]] + [self.send(part, stage, s) for s, part in enumerate(parts) if s > 0]

    def share(self, array, stage):
        return self.spread([array] * self.size(stage), stage)

    def origins(self, stage):
        size = self.size(stage)
        return ((self.place(stage) - jnp.arange(size)) % size).astype(jnp.int32)

    def in_order(self, parts, stage):
        if len(parts) <= 2:
            return parts
        stack = jnp.stack(parts)
        order = self.origins(stage)
        return [lax.dynamic_index_in_dim(stack, order[i], 0, False) for i in range(len(parts))]

    def total(self, array):
        for name in ("core", "member", "side", "low", "high"):
            first, *others = self.in_order(self.share(array, (name,)), (name,))
            for part in others:
                first = first + part
            array = first
        return array


def combine_kernel(groups, size, place, *refs):
    count = sum(groups)
    ins, outs = refs[:count], refs[len(refs) - size:]
    start, at = 0, 0
    for length in groups:
        parts = ins[at:at + length]
        at += length
        rows = parts[0].shape[0] // size
        for shift, out in enumerate(outs):
            if size == 1:
                span = slice(None)
            else:
                span = pl.ds(pl.multiple_of((place[0] + shift) % size * rows, rows), rows)
            total = parts[0][span, :].astype(f32)
            for part in parts[1:]:
                total = total + part[span, :].astype(f32)
            out[start:start + rows, :] = total.astype(bf16)
        start += rows


def combine(groups, place, size, after=()):
    width = groups[0][0].shape[1]
    rows = sum(group[0].shape[0] for group in groups) // size
    arrays = [array for group in groups for array in group]
    return pl.pallas_call(
        functools.partial(combine_kernel, [len(g) for g in groups], size),
        grid_spec=pltpu.PrefetchScalarGridSpec(
            num_scalar_prefetch=1,
            grid=(1,),
            in_specs=[whole(a.shape) for a in arrays] + [ANYWHERE] * len(after),
            out_specs=[whole((rows, width))] * size,
        ),
        out_shape=[jax.ShapeDtypeStruct((rows, width), bf16)] * size,
        compiler_params=params(1),
        cost_estimate=cost(rows * width, rows * width),
        name="combine",
    )(jnp.reshape(place, (1,)).astype(jnp.int32), *arrays, *after)


def join_kernel(count, *refs):
    out = refs[-1]
    at = 0
    for ref in refs[:count]:
        out[at:at + ref.shape[0]] = ref[...]
        at += ref.shape[0]


def join(parts, after=()):
    shape = (sum(p.shape[0] for p in parts),) + parts[0].shape[1:]
    return pl.pallas_call(
        functools.partial(join_kernel, len(parts)),
        grid=(1,),
        in_specs=[whole(p.shape) for p in parts] + [ANYWHERE] * len(after),
        out_specs=whole(shape),
        out_shape=jax.ShapeDtypeStruct(shape, bf16),
        compiler_params=params(1),
        cost_estimate=cost(0, 4 * math.prod(shape)),
        name="join",
    )(*parts, *after)


def place_halves(origins, core, ins, flat):
    for which, ref in enumerate(ins):
        target = core[0] if which == 0 else 1 - core[0]
        count, rows, _ = ref.shape
        for index in range(count):
            flat[target, index * rows:(index + 1) * rows, :] = ref[origins[index]]


def feed_weights_kernel(origins, core, own_ref, came_ref, dwo_ref, dwe_ref, dwr_ref, flat):
    width = own_ref.shape[2]
    half = width // 2
    place_halves(origins, core, (own_ref, came_ref), flat)
    for side in range(2):
        rows = slice(side * half, (side + 1) * half)
        dwo_ref[rows, :] = flat[side, :half, :].astype(f32)
        for part in range(dwr_ref.shape[0] // width):
            start = (1 + 2 * part) * half
            down = slice(part * width + side * half, part * width + (side + 1) * half)
            across = slice(part * width, (part + 1) * width)
            dwr_ref[down, :] = flat[side, start:start + half, :].astype(f32)
            dwe_ref[rows, across] = flat[side, start + half:start + width, :].astype(f32)


def feed_weights(origins, core, own, came, hidden):
    count, rows, width = own.shape
    shape = jax.ShapeDtypeStruct
    shapes = [(width, width), (width, hidden), (hidden, width)]
    return pl.pallas_call(
        feed_weights_kernel,
        grid_spec=pltpu.PrefetchScalarGridSpec(
            num_scalar_prefetch=2,
            grid=(1,),
            in_specs=[whole(own.shape)] * 2,
            out_specs=[whole(s) for s in shapes],
            scratch_shapes=[pltpu.VMEM((2, count * rows, width), bf16)],
        ),
        out_shape=[shape(s, f32) for s in shapes],
        compiler_params=params(1),
        cost_estimate=cost(0, 12 * own.size),
        name="feed_weights",
    )(origins, core, own, came)


def project_weights_kernel(pairs, origins, core, own_ref, came_ref, dwq_ref, dwk_ref, dwv_ref):
    half = dwq_ref.shape[0] // 2
    count = own_ref.shape[0]
    rows = half // count
    for which, ref in enumerate((own_ref, came_ref)):
        target = core[0] if which == 0 else 1 - core[0]
        for index in range(count):
            chunk = ref[origins[index]].astype(f32)
            place = pl.ds(pl.multiple_of(target * half + index * rows, rows), rows)
            for pair in range(pairs):
                block = chunk[pair * rows:(pair + 1) * rows]
                span = slice(pair * PAIR, (pair + 1) * PAIR)
                dwk_ref[place, span] = block[:, :PAIR]
                dwv_ref[place, span] = block[:, PAIR:2 * PAIR]
                dwq_ref[place, span] = block[:, 2 * PAIR:]


def project_weights(origins, core, own, came, width):
    shape = jax.ShapeDtypeStruct
    square = (width, width)
    return pl.pallas_call(
        functools.partial(project_weights_kernel, PAIRS),
        grid_spec=pltpu.PrefetchScalarGridSpec(
            num_scalar_prefetch=2,
            grid=(1,),
            in_specs=[whole(own.shape)] * 2,
            out_specs=[whole(square)] * 3,
        ),
        out_shape=[shape(square, f32)] * 3,
        compiler_params=params(1),
        cost_estimate=cost(0, 20 * width * width),
        name="project_weights",
    )(origins, core, own, came)


def body(
    layer_input,
    lang_counts,
    w_query,
    w_key,
    w_value,
    w_output,
    w_expand,
    w_reduce,
    b_query,
    b_value,
    b_output,
    b_expand,
    b_reduce,
    gain_attn,
    shift_attn,
    gain_mlp,
    shift_mlp,
    cotangent,
):
    items, own_rows, width = layer_input.shape
    group = lax.axis_size("grp")
    me = lax.axis_index("grp")
    rows = -(-own_rows // 16) * 16
    total = items * rows
    patch_rows = VIEWS * PATCH
    shifts = range(1, group)
    axes = ("dp", "grp")

    def padded(array):
        if rows != own_rows:
            array = jnp.pad(array, ((0, 0), (0, rows - own_rows), (0, 0)))
        return array.reshape(total, width)

    def unpadded(array):
        return array.reshape(items, rows, width)[:, :own_rows]

    def limit_of(owner):
        return jnp.clip(patch_rows + lang_counts - owner * own_rows, 0, own_rows)

    def line(vector):
        return vector.reshape(1, -1)

    def group_shift(array, shift):
        return lax.ppermute(array, "grp", [(i, (i + shift) % group) for i in range(group)])

    def joined(parts):
        if len(parts) == 1:
            return parts[0]
        return jnp.stack([p.reshape(items, rows, width) for p in parts], 1).reshape(-1, width)

    x = padded(layer_input)
    dy = padded(cotangent)
    others = [group_shift(x, -shift) for shift in shifts]
    own_limits = limit_of(me).reshape(items, 1)
    other_limits = jnp.stack([limit_of((me + shift) % group) for shift in shifts], 1)

    weights = (w_query, w_key, w_value, line(b_query), line(b_value))
    norms = (line(gain_attn), line(shift_attn))
    normed, keys, values, queries = project(x, *norms, *weights, with_query=True)
    first = attend(own_limits, queries, keys, values, rows, 1, None)
    x_other = joined(others)
    normed_other, keys_other, values_other = project(x_other, *norms, *weights, with_query=False)
    mixed, lse = attend(other_limits, queries, keys_other, values_other, rows, group - 1, first)

    devices = Slice()
    plane, high = ("side", "member"), ("high",)
    core = jnp.reshape(devices.here["core"], (1,)).astype(jnp.int32)
    output, dmid, dmix, keep, give, feed_lines = feed(
        core, x, mixed, dy, w_output, w_expand, w_reduce, line(b_output), line(b_expand), line(b_reduce),
        line(gain_mlp), line(shift_mlp),
    )

    def back(own, start, token, before=None):
        return attend_back(
            own_limits if own else other_limits, core, queries,
            keys if own else keys_other, values if own else values_other, dmix, mixed, lse,
            normed if own else normed_other, rows, 1 if own else group - 1, start, 1, before,
            [] if token is None else [token],
        )

    def stage_sum(parts, stage, after):
        if stage is None:
            return combine([parts], 0, 1, after)
        return combine([parts], devices.place(stage), devices.size(stage), after)

    value = devices.spread([keep.reshape(-1, width), give.reshape(-1, width)], ("core",))
    back_other = [back(False, 0, None)]
    parts = stage_sum(value, plane, back_other[0][1:2])
    value = devices.spread(parts, plane)
    back_other += [back(False, p, parts[0]) for p in range(1, PAIRS)]
    send, lines = other_grads(x_other, [b[1] for b in back_other], w_key, w_value, rows)
    split_high = parts[0].shape[0] % (16 * devices.size(high)) == 0
    parts = stage_sum(value, high if split_high else None, [send])
    send = send.reshape(items, group - 1, rows, width)
    received = jnp.stack(
        [group_shift(send[:, shift - 1].reshape(total, width), shift) for shift in shifts]
    )
    own_back, groups = [], []

    def next_back(token):
        pair = len(own_back)
        own_back.append(back(True, pair, token, (back_other[pair][0], back_other[pair][2])))
        sent = [received] if pair == 1 else []
        sent += [groups[-1][1]] if pair > 0 else []
        groups.append(devices.spread(list(own_back[-1][1:]), ("core",)))
        return [own_back[-1][0]] + sent

    if split_high:
        value = devices.spread(parts, high)
    else:
        value = devices.in_order(devices.share(parts[0], high), high)
    value = stage_sum(value, None, next_back(parts[0]))[0]
    low = ("low",)
    parts = devices.in_order(devices.share(value, low), low)
    value = stage_sum(parts, None, next_back(value))[0]
    if split_high:
        value = join(devices.share(value, high), next_back(value))
    else:
        next_back(value)
    parts = devices.share(value, plane)
    next_back(value)
    scattered = combine(groups, devices.place(plane), devices.size(plane), [groups[2][1]])
    value = join(parts, scattered[:1])
    value = value.reshape(devices.size(plane) * (devices.size(high) if split_high else 1), -1, width)
    feed_own, feed_came = devices.share(value, ("core",))

    dx, lines = own_grads(
        x, [b[0] for b in own_back], received, dmid, w_query, w_key, w_value, line(gain_attn), lines
    )
    value = combine([devices.spread(scattered, plane)], 0, 1)[0]
    for stage in (low, high):
        value = combine([devices.in_order(devices.share(value, stage), stage)], 0, 1)[0]
    value = join(devices.share(value[None], plane))
    project_own, project_came = devices.share(value, ("core",))

    plane_origins = devices.origins(plane)
    if split_high:
        count = devices.size(high)
        feed_origins = (plane_origins[:, None] * count + devices.origins(high)[None]).reshape(-1)
    else:
        feed_origins = plane_origins
    dwo, dwe, dwr = feed_weights(feed_origins, core, feed_own, feed_came, w_expand.shape[1])
    dwq, dwk, dwv = project_weights(plane_origins, core, project_own, project_came, width)
    lines = devices.total(jnp.concatenate([lines[:4], feed_lines], 0))
    dbq, dbv, dgain, dshift, dbo, dbr, dgain_mlp, dshift_mlp = lines[:8]
    dbe = lines[8:].reshape(-1)
    return (
        unpadded(output),
        unpadded(dx),
        dwq, dwk, dwv, dwo, dwe, dwr,
        dbq, dbv, dbo, dbe, dbr, dgain, dshift, dgain_mlp, dshift_mlp,
    )


def solution(mesh):
    rows = P("dp", "grp", None)
    in_specs = (rows, P("dp")) + (P(),) * 15 + (rows,)
    out_specs = (rows, rows) + (P(),) * 15
    return jax.shard_map(body, mesh=mesh, in_specs=in_specs, out_specs=out_specs, check_vma=False)
```

```python
import functools
import math

import jax
import jax.numpy as jnp
from jax import lax
from jax.experimental import pallas as pl
from jax.experimental.pallas import tpu as pltpu
from jax.sharding import PartitionSpec as P

HEADS = 8
HEAD_DIM = 64
VIEWS = 5
PATCH = 400
PAIR = 2 * HEAD_DIM
PAIRS = HEADS // 2

EPSILON = 1e-05
NEGATIVE = -1e30
SCALE = 1.0 / math.sqrt(HEAD_DIM)

bf16 = jnp.bfloat16
f32 = jnp.float32


def dot_rows(left, right):
    return lax.dot_general(
        left, right, (((1,), (0,)), ((), ())), preferred_element_type=f32
    )


def dot_left(left, right):
    return lax.dot_general(
        left, right, (((0,), (0,)), ((), ())), preferred_element_type=f32
    )


def dot_right(left, right):
    return lax.dot_general(
        left, right, (((1,), (1,)), ((), ())), preferred_element_type=f32
    )


def chunk_of(rows, limit):
    best = 16
    for size in range(16, limit + 1, 16):
        if rows % size == 0:
            best = size
    return best


def hat_rows(matrix):
    center = matrix - jnp.mean(matrix, axis=-1, keepdims=True)
    spread = jnp.mean(center * center, axis=-1, keepdims=True)
    inverse = lax.rsqrt(spread + EPSILON)
    return center * inverse, inverse


def hat_back(grad_hat, hat, inverse):
    mean_grad = jnp.mean(grad_hat, axis=-1, keepdims=True)
    mean_cross = jnp.mean(grad_hat * hat, axis=-1, keepdims=True)
    return inverse * (grad_hat - mean_grad - hat * mean_cross)


def column_sums(matrix):
    return jnp.sum(matrix, axis=0, keepdims=True)


ALL = ("rest", "core", "grp")
VMEM_MIB = 60
ANYWHERE = pl.BlockSpec(memory_space=pl.ANY)


def params(axes):
    return pltpu.CompilerParams(
        dimension_semantics=("arbitrary",) * axes, vmem_limit_bytes=VMEM_MIB << 20
    )


def cost(flops, bytes_accessed, transcendentals=0):
    return pl.CostEstimate(
        flops=int(flops), bytes_accessed=int(bytes_accessed), transcendentals=int(transcendentals)
    )


def whole(shape):
    return pl.BlockSpec(shape, lambda *_: (0,) * len(shape))


def project_kernel(with_query, x_ref, gain, shift, w_query, w_key, w_value, b_query, b_value, *outs):
    hat, _ = hat_rows(x_ref[...].astype(f32))
    normed = (hat * gain[...] + shift[...]).astype(bf16)
    if with_query:
        normed_ref, key_ref, value_ref, query_ref = outs
        query = (dot_rows(normed, w_query[...]) + b_query[...]).astype(bf16)
        query_ref[...] = (query.astype(f32) * SCALE).astype(bf16)
    else:
        normed_ref, key_ref, value_ref = outs
    normed_ref[...] = normed
    key_ref[...] = dot_rows(normed, w_key[...]).astype(bf16)
    value_ref[...] = (dot_rows(normed, w_value[...]) + b_value[...]).astype(bf16)


def project(x, gain, shift, w_query, w_key, w_value, b_query, b_value, with_query):
    rows, width = x.shape
    step = chunk_of(rows, 272)
    count = 4 if with_query else 3
    row_block = pl.BlockSpec((step, width), lambda i: (i, 0))
    return pl.pallas_call(
        functools.partial(project_kernel, with_query),
        grid=(rows // step,),
        in_specs=[row_block, whole((1, width)), whole((1, width))]
        + [whole((width, width))] * 3
        + [whole((1, width))] * 2,
        out_specs=[row_block] * count,
        out_shape=[jax.ShapeDtypeStruct((rows, width), bf16)] * count,
        compiler_params=params(1),
        cost_estimate=cost(2 * rows * width * width * (count - 1), 2 * rows * width * (count + 1)),
        name="project",
    )(x, gain, shift, w_query, w_key, w_value, b_query, b_value)


def lanes_of(shape):
    return lax.broadcasted_iota(jnp.int32, shape, 1)


def forward_kernel(
    final, rows, blocks, step, limits, q_ref, k_ref, v_ref, *rest
):
    if final:
        acc_in, top_in, sum_in, out_ref, lse_ref, kt_ref, va_ref = rest
    else:
        acc_out, top_out, sum_out, kt_ref, va_ref = rest
    item = pl.program_id(0)
    key_count = rows * blocks
    query_rows = q_ref.shape[0]
    keys = k_ref[...].astype(f32)
    values = v_ref[...].astype(f32)
    first = lanes_of((key_count, PAIR)) < HEAD_DIM
    flipped = keys.T
    row_id = lax.broadcasted_iota(jnp.int32, (PAIR, key_count), 0)
    key_id = lax.broadcasted_iota(jnp.int32, (PAIR, key_count), 1)
    bias = jnp.zeros((PAIR, key_count), f32)
    for block in range(blocks):
        here = (key_id >= block * rows + limits[item, block]) & (key_id < (block + 1) * rows)
        bias = jnp.where(here, NEGATIVE, bias)
    spare = jnp.where((row_id & (HEAD_DIM - 1)) == 0, bias, 0.0)
    kt_ref[0] = jnp.where(row_id < HEAD_DIM, flipped, spare).astype(bf16)
    kt_ref[1] = jnp.where(row_id < HEAD_DIM, spare, flipped).astype(bf16)
    va_ref[0] = jnp.where(first, values, 1.0).astype(bf16)
    va_ref[1] = jnp.where(first, 1.0, values).astype(bf16)
    lanes = lanes_of((step, PAIR))
    head_first = lanes < HEAD_DIM
    one = jnp.where((lanes & (HEAD_DIM - 1)) == 0, 1.0, 0.0)

    def body(index, carry):
        place = pl.ds(pl.multiple_of(index * step, step), step)
        query = q_ref[place, :].astype(f32)
        outs, tops = [], []
        for head in range(2):
            mine = head_first if head == 0 else jnp.logical_not(head_first)
            query_head = jnp.where(mine, query, one).astype(bf16)
            scores = dot_rows(query_head, kt_ref[head])
            top = jnp.max(scores, axis=1, keepdims=True)
            weights = jnp.exp(scores - top).astype(bf16)
            outs.append(dot_rows(weights, va_ref[head]))
            tops.append(top)
        acc = jnp.where(head_first, outs[0], outs[1])
        total = pltpu.roll(jnp.where(head_first, outs[1], outs[0]), HEAD_DIM, 1)
        top = jnp.where(head_first, tops[0], tops[1])
        if final:
            other_top = top_in[place, :]
            new_top = jnp.maximum(top, other_top)
            scale_here = jnp.exp(top - new_top)
            scale_there = jnp.exp(other_top - new_top)
            total = total * scale_here + sum_in[place, :] * scale_there
            acc = acc * scale_here + acc_in[place, :] * scale_there
            out_ref[place, :] = acc / total
            lse_ref[place, :] = pltpu.roll(new_top + jnp.log(total), HEAD_DIM, 1)
        else:
            acc_out[place, :] = acc
            top_out[place, :] = top
            sum_out[place, :] = total
        return carry

    lax.fori_loop(0, query_rows // step, body, 0)


def attend(limits, queries, keys, values, rows, blocks, before):
    total, width = queries.shape
    items = total // rows
    key_count = rows * blocks
    step = chunk_of(rows, 208)
    query_block = pl.BlockSpec((rows, PAIR), lambda i, p, *_: (i, p))
    key_block = pl.BlockSpec((key_count, PAIR), lambda i, p, *_: (i, p))
    final = before is not None
    extra = list(before) if final else []
    outs = 2 if final else 3
    return pl.pallas_call(
        functools.partial(forward_kernel, final, rows, blocks, step),
        grid_spec=pltpu.PrefetchScalarGridSpec(
            num_scalar_prefetch=1,
            grid=(items, PAIRS),
            in_specs=[query_block, key_block, key_block] + [query_block] * len(extra),
            out_specs=[query_block] * outs,
            scratch_shapes=[
                pltpu.VMEM((2, PAIR, key_count), bf16),
                pltpu.VMEM((2, key_count, PAIR), bf16),
            ],
        ),
        out_shape=[jax.ShapeDtypeStruct((total, width), f32)] * outs,
        compiler_params=params(2),
        cost_estimate=cost(
            16 * total * key_count * width, 12 * total * width, total * key_count * HEADS
        ),
        name="attend",
    )(limits, queries, keys, values, *extra)


def split_three(value):
    high = value.astype(bf16).astype(f32)
    rest = value - high
    middle = rest.astype(bf16).astype(f32)
    return high, middle, rest - middle


def halves(core, block):
    half = block.shape[0] // 2
    upper, lower = block[:half], block[half:]
    mine = jnp.where(core == 0, upper, lower)
    theirs = jnp.where(core == 0, lower, upper)
    return mine.astype(bf16), theirs.astype(bf16)


def backward_kernel(
    last, tokens, rows, blocks, step, limits, core,
    q_ref, k_ref, v_ref, g_ref, out_ref, lse_ref, normed_ref, *rest,
):
    if last:
        before_ref, dw_in, *rest = rest
        cat_ref, keep_ref, send_ref, dw_acc, qt_ref, gt_ref, dqt_ref = rest[tokens:]
    else:
        dq_ref, cat_ref, dw_ref, dw_acc, qt_ref, gt_ref, dqt_ref = rest[tokens:]
    item = pl.program_id(1)
    query_rows = q_ref.shape[0]
    lanes = lanes_of((query_rows, PAIR))
    head_first = lanes < HEAD_DIM
    spare_lane = lanes & (HEAD_DIM - 1)

    def spare(parts, mask_one):
        high, middle, low = parts
        value = jnp.where(spare_lane == 0, high, 0.0)
        value = jnp.where(spare_lane == 1, middle, value)
        value = jnp.where(spare_lane == 2, low, value)
        return jnp.where(spare_lane == 3, mask_one, value)

    query = q_ref[...].astype(f32)
    grad = g_ref[...].astype(f32)
    product = grad * out_ref[...]
    delta_first = jnp.sum(jnp.where(head_first, product, 0.0), axis=1, keepdims=True)
    delta_second = jnp.sum(jnp.where(head_first, 0.0, product), axis=1, keepdims=True)
    delta = jnp.where(head_first, delta_second, delta_first)
    lse_spare = spare(split_three(-lse_ref[...]), 1.0)
    delta_spare = spare(split_three(-delta), 0.0)
    qt_ref[0] = jnp.where(head_first, query, lse_spare).T.astype(bf16)
    qt_ref[1] = jnp.where(head_first, lse_spare, query).T.astype(bf16)
    gt_ref[0] = jnp.where(head_first, grad, delta_spare).T.astype(bf16)
    gt_ref[1] = jnp.where(head_first, delta_spare, grad).T.astype(bf16)
    dqt_ref[...] = jnp.zeros_like(dqt_ref)

    key_lanes = lanes_of((step, PAIR))
    key_first = key_lanes < HEAD_DIM
    key_spare = key_lanes & (HEAD_DIM - 1)
    key_row = lax.broadcasted_iota(jnp.int32, (step, PAIR), 0)
    ones = jnp.where(key_spare < 3, 1.0, 0.0)
    per_block = rows // step

    def body(index, carry):
        place = pl.ds(pl.multiple_of(index * step, step), step)
        block = index // per_block
        limit = limits[item, block] - (index - block * per_block) * step
        bias = jnp.where(key_row >= limit, NEGATIVE, 0.0)
        key = k_ref[place, :].astype(f32)
        value = v_ref[place, :].astype(f32)
        key_aug = jnp.where(key_spare == 3, bias, ones)
        key_flipped = key.T.astype(bf16)
        dks, dvs = [], []
        for head in range(2):
            mine = key_first if head == 0 else jnp.logical_not(key_first)
            key_head = jnp.where(mine, key, key_aug).astype(bf16)
            value_head = jnp.where(mine, value, ones).astype(bf16)
            probs = jnp.exp(dot_rows(key_head, qt_ref[head]))
            grad_probs = dot_rows(value_head, gt_ref[head])
            grad_scores = (probs * grad_probs).astype(bf16)
            dvs.append(dot_rows(probs.astype(bf16), g_ref[...]))
            dks.append(dot_rows(grad_scores, q_ref[...]))
            own = pl.ds(head * HEAD_DIM, HEAD_DIM)
            half = key_flipped[head * HEAD_DIM:(head + 1) * HEAD_DIM]
            dqt_ref[own, :] += dot_rows(half, grad_scores)
        cat_ref[place, :PAIR] = jnp.where(key_first, dks[0], dks[1]).astype(bf16)
        cat_ref[place, PAIR:2 * PAIR] = jnp.where(key_first, dvs[0], dvs[1]).astype(bf16)
        return carry

    lax.fori_loop(0, blocks * per_block, body, 0)
    result = dqt_ref[...].T
    if last:
        cat_ref[:, 2 * PAIR:] = ((result + before_ref[...]) * SCALE).astype(bf16)
    else:
        dq_ref[...] = result
    added = dot_left(normed_ref[...], cat_ref[...])
    items = pl.num_programs(1)

    @pl.when(item == 0)
    def _():
        dw_acc[...] = added
        if last:
            dw_acc[:, :2 * PAIR] += dw_in[0]

    @pl.when(item > 0)
    def _():
        dw_acc[...] += added

    @pl.when(item == items - 1)
    def _():
        if last:
            keep_ref[...], send_ref[...] = halves(core[0], dw_acc[...])
        else:
            dw_ref[0] = dw_acc[...]


def attend_back(
    limits, core, queries, keys, values, grads, outs, lse, normed, rows, blocks, first, count, before,
    tokens,
):
    total, width = queries.shape
    items = total // rows
    key_count = rows * blocks
    step = chunk_of(rows, 208)
    last = before is not None
    cat = (3 if last else 2) * PAIR
    query_block = pl.BlockSpec((rows, PAIR), lambda p, i, *_: (i, first + p))
    key_block = pl.BlockSpec((key_count, PAIR), lambda p, i, *_: (i, first + p))
    normed_block = pl.BlockSpec((key_count, width), lambda p, i, *_: (i, 0))
    part_block = pl.BlockSpec((rows, PAIR), lambda p, i, *_: (i, p))
    cat_block = pl.BlockSpec((key_count, cat), lambda p, i, *_: (i, p))
    half_block = pl.BlockSpec((width // 2, cat), lambda p, i, *_: (p, 0))
    weight_block = pl.BlockSpec((1, width, cat), lambda p, i, *_: (p, 0, 0))
    weight_in = pl.BlockSpec((1, width, 2 * PAIR), lambda p, i, *_: (p, 0, 0))
    shape = jax.ShapeDtypeStruct
    cat_shape = shape((total * blocks, cat * count), bf16)
    if last:
        extra, extra_specs = list(before), [part_block, weight_in]
        out_shape = [cat_shape] + [shape((count * width // 2, cat), bf16)] * 2
        out_specs = [cat_block, half_block, half_block]
    else:
        extra, extra_specs = [], []
        out_shape = [shape((total, PAIR * count), f32), cat_shape, shape((count, width, cat), f32)]
        out_specs = [part_block, cat_block, weight_block]
    return pl.pallas_call(
        functools.partial(backward_kernel, last, len(tokens), rows, blocks, step),
        grid_spec=pltpu.PrefetchScalarGridSpec(
            num_scalar_prefetch=2,
            grid=(count, items),
            in_specs=[query_block, key_block, key_block]
            + [query_block] * 3
            + [normed_block]
            + extra_specs
            + [ANYWHERE] * len(tokens),
            out_specs=out_specs,
            scratch_shapes=[
                pltpu.VMEM((width, cat), f32),
                pltpu.VMEM((2, PAIR, rows), bf16),
                pltpu.VMEM((2, PAIR, rows), bf16),
                pltpu.VMEM((PAIR, rows), f32),
            ],
        ),
        out_shape=out_shape,
        compiler_params=params(2),
        cost_estimate=cost(
            40 * total * key_count * PAIR * count,
            16 * total * PAIR * count,
            2 * total * key_count * count,
        ),
        name="attend_back",
    )(limits, core, queries, keys, values, grads, outs, lse, normed, *extra, *tokens)


def feed_kernel(
    core, x_ref, mix_ref, dy_ref, w_output, w_expand, w_reduce, b_output, b_expand, b_reduce, gain, shift,
    y_ref, dmid_ref, dmix_ref, keep_ref, send_ref, line_ref,
    middle_ref, normed_ref, y_acc, grad_acc,
):
    part = pl.program_id(0)

    def put(index, block):
        keep_ref[index], send_ref[index] = halves(core[0], block)

    @pl.when(part == 0)
    def _():
        mixed = mix_ref[...].astype(bf16)
        middle = x_ref[...].astype(f32) + dot_rows(mixed, w_output[...]) + b_output[...]
        middle_ref[...] = middle
        hat, _ = hat_rows(middle)
        normed_ref[...] = (hat * gain[...] + shift[...]).astype(bf16)
        y_acc[...] = middle + b_reduce[...]
        grad_acc[...] = jnp.zeros_like(grad_acc)
        line_ref[1:2, :] = column_sums(dy_ref[...].astype(f32))

    normed = normed_ref[...]
    upper = dot_rows(normed, w_expand[...]) + b_expand[...]
    cumulative = 0.5 * lax.erf(upper * math.sqrt(0.5)) + 0.5
    density = jnp.exp(upper * upper * -0.5) * (1.0 / math.sqrt(2.0 * math.pi))
    active = (upper * cumulative).astype(bf16)
    slope = cumulative + upper * density
    y_acc[...] += dot_rows(active, w_reduce[...])
    put(1 + 2 * part, dot_left(active, dy_ref[...]))
    grad_upper = (dot_right(dy_ref[...], w_reduce[...]) * slope).astype(bf16)
    line_ref[pl.ds(4 + part, 1), :] = column_sums(grad_upper.astype(f32))
    put(2 + 2 * part, dot_left(normed, grad_upper))
    grad_acc[...] += dot_right(grad_upper, w_expand[...])

    @pl.when(part == pl.num_programs(0) - 1)
    def _():
        y_ref[...] = y_acc[...].astype(bf16)
        grad = grad_acc[...]
        hat, inverse = hat_rows(middle_ref[...])
        line_ref[2:3, :] = column_sums(grad * hat)
        line_ref[3:4, :] = column_sums(grad)
        dmid = hat_back(grad * gain[...], hat, inverse) + dy_ref[...].astype(f32)
        dmid_ref[...] = dmid
        branch = dmid.astype(bf16)
        line_ref[0:1, :] = column_sums(branch.astype(f32))
        put(0, dot_left(mix_ref[...].astype(bf16), branch))
        dmix_ref[...] = dot_right(branch, w_output[...]).astype(bf16)


def feed(core, x, mixed, dy, w_output, w_expand, w_reduce, b_output, b_expand, b_reduce, gain, shift):
    rows, width = x.shape
    hidden = w_expand.shape[1]
    parts = hidden // width
    row = whole((rows, width))
    line = whole((1, width))
    expand = pl.BlockSpec((width, width), lambda i, *_: (0, i))
    reduce = pl.BlockSpec((width, width), lambda i, *_: (i, 0))
    hidden_line = pl.BlockSpec((1, width), lambda i, *_: (0, i))
    weights = (1 + 2 * parts, width // 2, width)
    lines = (4 + parts, width)
    shape = jax.ShapeDtypeStruct
    return pl.pallas_call(
        feed_kernel,
        grid_spec=pltpu.PrefetchScalarGridSpec(
            num_scalar_prefetch=1,
            grid=(parts,),
            in_specs=[row, row, row, whole((width, width)), expand, reduce, line, hidden_line, line, line, line],
            out_specs=[row, row, row, whole(weights), whole(weights), whole(lines)],
            scratch_shapes=[
                pltpu.VMEM((rows, width), f32),
                pltpu.VMEM((rows, width), bf16),
                pltpu.VMEM((rows, width), f32),
                pltpu.VMEM((rows, width), f32),
            ],
        ),
        out_shape=[
            shape((rows, width), bf16),
            shape((rows, width), f32),
            shape((rows, width), bf16),
            shape(weights, bf16),
            shape(weights, bf16),
            shape(lines, f32),
        ],
        compiler_params=params(1),
        cost_estimate=cost(12 * rows * width * hidden + 6 * rows * width * width, 20 * rows * width, 2 * rows * hidden),
        name="feed",
    )(core, x, mixed, dy, w_output, w_expand, w_reduce, b_output, b_expand, b_reduce, gain, shift)


def gather_parts(refs, part, parts):
    blocks = []
    for ref in refs:
        pairs = ref.shape[1] // (parts * PAIR)
        for pair in range(pairs):
            start = (pair * parts + part) * PAIR
            blocks.append(ref[:, start:start + PAIR])
    return jnp.concatenate(blocks, axis=1)


def other_kernel(cats, x_ref, w_key, w_value, *rest):
    cat_refs, (send_ref, line_ref) = rest[:cats], rest[cats:]
    dk = gather_parts(cat_refs, 0, 2)
    dv = gather_parts(cat_refs, 1, 2)
    grad = dot_right(dk, w_key[...]) + dot_right(dv, w_value[...])
    send_ref[...] = grad.astype(bf16)
    hat, _ = hat_rows(x_ref[...].astype(f32))

    @pl.when(pl.program_id(0) == 0)
    def _():
        line_ref[...] = jnp.zeros_like(line_ref)

    line_ref[1:2, :] += column_sums(dv.astype(f32))
    line_ref[2:3, :] += column_sums(grad * hat)
    line_ref[3:4, :] += column_sums(grad)


def other_grads(x, cats, w_key, w_value, rows):
    total, width = x.shape
    step = chunk_of(rows, 272)
    row = pl.BlockSpec((step, width), lambda i: (i, 0))
    square = whole((width, width))
    shape = jax.ShapeDtypeStruct
    return pl.pallas_call(
        functools.partial(other_kernel, len(cats)),
        grid=(total // step,),
        in_specs=[row] + [square] * 2
        + [pl.BlockSpec((step, c.shape[1]), lambda i: (i, 0)) for c in cats],
        out_specs=[row, whole((8, width))],
        out_shape=[shape((total, width), bf16), shape((8, width), f32)],
        compiler_params=params(1),
        cost_estimate=cost(4 * total * width * width, 8 * total * width),
        name="other_grads",
    )(x, w_key, w_value, *cats)


def own_kernel(cats, x_ref, recv_ref, dmid_ref, w_query, w_key, w_value, gain, line_in, *rest):
    cat_refs, (dx_ref, line_ref) = rest[:cats], rest[-2:]
    dk = gather_parts(cat_refs, 0, 3)
    dv = gather_parts(cat_refs, 1, 3)
    dq = gather_parts(cat_refs, 2, 3)
    grad = dot_right(dq, w_query[...]) + dot_right(dk, w_key[...]) + dot_right(dv, w_value[...])
    hat, inverse = hat_rows(x_ref[...].astype(f32))

    @pl.when(pl.program_id(0) == 0)
    def _():
        line_ref[...] = line_in[...]

    line_ref[0:1, :] += column_sums(dq.astype(f32))
    line_ref[1:2, :] += column_sums(dv.astype(f32))
    line_ref[2:3, :] += column_sums(grad * hat)
    line_ref[3:4, :] += column_sums(grad)
    for index in range(recv_ref.shape[0]):
        grad = grad + recv_ref[index].astype(f32)
    dx_ref[...] = hat_back(grad * gain[...], hat, inverse) + dmid_ref[...]


def own_grads(x, cats, recv, dmid, w_query, w_key, w_value, gain, lines, after):
    rows, width = x.shape
    step = chunk_of(rows, 272)
    row = pl.BlockSpec((step, width), lambda i: (i, 0))
    square = whole((width, width))
    shape = jax.ShapeDtypeStruct
    return pl.pallas_call(
        functools.partial(own_kernel, len(cats)),
        grid=(rows // step,),
        in_specs=[row, pl.BlockSpec((recv.shape[0], step, width), lambda i: (0, i, 0)), row]
        + [square] * 3
        + [whole((1, width)), whole((8, width))]
        + [pl.BlockSpec((step, c.shape[1]), lambda i: (i, 0)) for c in cats]
        + [ANYWHERE] * len(after),
        out_specs=[row, whole((8, width))],
        out_shape=[shape((rows, width), f32), shape((8, width), f32)],
        compiler_params=params(1),
        cost_estimate=cost(6 * rows * width * width, 16 * rows * width),
        name="own_grads",
    )(x, recv, dmid, w_query, w_key, w_value, gain, lines, *cats, *after)


class Slice:
    def __init__(self):
        group, rest = lax.axis_size("grp"), lax.axis_size("rest")
        batch = rest * lax.axis_size("core")
        side = 2 if rest % 2 == 0 else 1
        rest //= side
        high = 2 if rest % 2 == 0 else 1
        self.sizes = {"core": 2, "side": side, "member": group, "high": high, "low": rest // high}
        self.count = group * batch
        self.here = self.coords(lax.axis_index(ALL))

    def coords(self, linear):
        out = {}
        for name in ("member", "core", "side", "low", "high"):
            out[name] = linear % self.sizes[name]
            linear = linear // self.sizes[name]
        return out

    def linear(self, coords):
        total = 0
        for name in ("high", "low", "side", "core", "member"):
            total = total * self.sizes[name] + coords[name]
        return total

    def size(self, stage):
        return math.prod(self.sizes[name] for name in stage)

    def place(self, stage, coords=None):
        coords = self.here if coords is None else coords
        total = 0
        for name in stage:
            total = total * self.sizes[name] + coords[name]
        return total

    def send(self, array, stage, shift):
        pairs = []
        for source in range(self.count):
            coords = self.coords(source)
            place = (self.place(stage, coords) + shift) % self.size(stage)
            for name in reversed(stage):
                coords[name] = place % self.sizes[name]
                place //= self.sizes[name]
            pairs.append((source, self.linear(coords)))
        return lax.ppermute(array, ALL, pairs)

    def spread(self, parts, stage):
        return [parts[0]] + [self.send(part, stage, s) for s, part in enumerate(parts) if s > 0]

    def share(self, array, stage):
        return self.spread([array] * self.size(stage), stage)

    def origins(self, stage):
        size = self.size(stage)
        return ((self.place(stage) - jnp.arange(size)) % size).astype(jnp.int32)

    def in_order(self, parts, stage):
        if len(parts) <= 2:
            return parts
        stack = jnp.stack(parts)
        order = self.origins(stage)
        return [lax.dynamic_index_in_dim(stack, order[i], 0, False) for i in range(len(parts))]

    def total(self, array, name):
        first, *others = self.in_order(self.share(array, (name,)), (name,))
        for part in others:
            first = first + part
        return first


def behind(array, *others):
    return lax.optimization_barrier((array, *others))[0]


def combine_kernel(groups, size, place, *refs):
    count = sum(groups)
    ins, outs = refs[:count], refs[len(refs) - size:]
    start, at = 0, 0
    for length in groups:
        parts = ins[at:at + length]
        at += length
        rows = parts[0].shape[0] // size
        for shift, out in enumerate(outs):
            if size == 1:
                span = slice(None)
            else:
                span = pl.ds(pl.multiple_of((place[0] + shift) % size * rows, rows), rows)
            total = parts[0][span, :].astype(f32)
            for part in parts[1:]:
                total = total + part[span, :].astype(f32)
            out[start:start + rows, :] = total.astype(bf16)
        start += rows


def combine(groups, place, size, after=()):
    width = groups[0][0].shape[1]
    rows = sum(group[0].shape[0] for group in groups) // size
    arrays = [array for group in groups for array in group]
    return pl.pallas_call(
        functools.partial(combine_kernel, [len(g) for g in groups], size),
        grid_spec=pltpu.PrefetchScalarGridSpec(
            num_scalar_prefetch=1,
            grid=(1,),
            in_specs=[whole(a.shape) for a in arrays] + [ANYWHERE] * len(after),
            out_specs=[whole((rows, width))] * size,
        ),
        out_shape=[jax.ShapeDtypeStruct((rows, width), bf16)] * size,
        compiler_params=params(1),
        cost_estimate=cost(rows * width, rows * width),
        name="combine",
    )(jnp.reshape(place, (1,)).astype(jnp.int32), *arrays, *after)


def join_kernel(count, *refs):
    out = refs[-1]
    at = 0
    for ref in refs[:count]:
        out[at:at + ref.shape[0]] = ref[...]
        at += ref.shape[0]


def join(parts, after=()):
    shape = (sum(p.shape[0] for p in parts),) + parts[0].shape[1:]
    return pl.pallas_call(
        functools.partial(join_kernel, len(parts)),
        grid=(1,),
        in_specs=[whole(p.shape) for p in parts] + [ANYWHERE] * len(after),
        out_specs=whole(shape),
        out_shape=jax.ShapeDtypeStruct(shape, bf16),
        compiler_params=params(1),
        cost_estimate=cost(0, 4 * math.prod(shape)),
        name="join",
    )(*parts, *after)


def place_halves(origins, core, ins, flat):
    for which, ref in enumerate(ins):
        target = core[0] if which == 0 else 1 - core[0]
        count, rows, _ = ref.shape
        for index in range(count):
            flat[target, index * rows:(index + 1) * rows, :] = ref[origins[index]]


def feed_weights_kernel(core, own_ref, came_ref, dwo_ref, dwe_ref, dwr_ref):
    width = own_ref.shape[1]
    half = width // 2
    for side in range(2):
        rows = slice(side * half, (side + 1) * half)

        def block(index):
            span = slice(index * half, (index + 1) * half)
            return jnp.where(core[0] == side, own_ref[span, :].astype(f32), came_ref[span, :].astype(f32))

        dwo_ref[rows, :] = block(0)
        for part in range(dwr_ref.shape[0] // width):
            down = slice(part * width + side * half, part * width + (side + 1) * half)
            across = slice(part * width, (part + 1) * width)
            dwr_ref[down, :] = block(1 + 2 * part)
            dwe_ref[rows, across] = block(2 + 2 * part)


def feed_weights(core, own, came, hidden):
    width = own.shape[1]
    shape = jax.ShapeDtypeStruct
    shapes = [(width, width), (width, hidden), (hidden, width)]
    return pl.pallas_call(
        feed_weights_kernel,
        grid_spec=pltpu.PrefetchScalarGridSpec(
            num_scalar_prefetch=1,
            grid=(1,),
            in_specs=[whole(own.shape)] * 2,
            out_specs=[whole(s) for s in shapes],
        ),
        out_shape=[shape(s, f32) for s in shapes],
        compiler_params=params(1),
        cost_estimate=cost(0, 12 * own.size),
        name="feed_weights",
    )(core, own, came)


def project_weights_kernel(origins, core, own_ref, came_ref, dwq_ref, dwk_ref, dwv_ref, flat):
    half = dwq_ref.shape[0] // 2
    place_halves(origins, core, (own_ref, came_ref), flat)
    for side in range(2):
        rows = slice(side * half, (side + 1) * half)
        for pair in range(PAIRS):
            block = flat[side, pair * half:(pair + 1) * half, :].astype(f32)
            span = slice(pair * PAIR, (pair + 1) * PAIR)
            dwk_ref[rows, span] = block[:, :PAIR]
            dwv_ref[rows, span] = block[:, PAIR:2 * PAIR]
            dwq_ref[rows, span] = block[:, 2 * PAIR:]


def project_weights(origins, core, own, came, width):
    shape = jax.ShapeDtypeStruct
    square = (width, width)
    return pl.pallas_call(
        project_weights_kernel,
        grid_spec=pltpu.PrefetchScalarGridSpec(
            num_scalar_prefetch=2,
            grid=(1,),
            in_specs=[whole(own.shape)] * 2,
            out_specs=[whole(square)] * 3,
            scratch_shapes=[pltpu.VMEM((2, own.shape[0] * own.shape[1], own.shape[2]), bf16)],
        ),
        out_shape=[shape(square, f32)] * 3,
        compiler_params=params(1),
        cost_estimate=cost(0, 20 * width * width),
        name="project_weights",
    )(origins, core, own, came)


def body(
    layer_input,
    lang_counts,
    w_query,
    w_key,
    w_value,
    w_output,
    w_expand,
    w_reduce,
    b_query,
    b_value,
    b_output,
    b_expand,
    b_reduce,
    gain_attn,
    shift_attn,
    gain_mlp,
    shift_mlp,
    cotangent,
):
    items, own_rows, width = layer_input.shape
    group = lax.axis_size("grp")
    me = lax.axis_index("grp")
    rows = -(-own_rows // 16) * 16
    total = items * rows
    patch_rows = VIEWS * PATCH
    shifts = range(1, group)

    def padded(array):
        if rows != own_rows:
            array = jnp.pad(array, ((0, 0), (0, rows - own_rows), (0, 0)))
        return array.reshape(total, width)

    def unpadded(array):
        return array.reshape(items, rows, width)[:, :own_rows]

    def limit_of(owner):
        return jnp.clip(patch_rows + lang_counts - owner * own_rows, 0, own_rows)

    def line(vector):
        return vector.reshape(1, -1)

    def group_shift(array, shift):
        return lax.ppermute(array, "grp", [(i, (i + shift) % group) for i in range(group)])

    def joined(parts):
        if len(parts) == 1:
            return parts[0]
        return jnp.stack([p.reshape(items, rows, width) for p in parts], 1).reshape(-1, width)

    x = padded(layer_input)
    dy = padded(cotangent)
    others = [group_shift(x, -shift) for shift in shifts]
    own_limits = limit_of(me).reshape(items, 1)
    other_limits = jnp.stack([limit_of((me + shift) % group) for shift in shifts], 1)

    weights = (w_query, w_key, w_value, line(b_query), line(b_value))
    norms = (line(gain_attn), line(shift_attn))
    normed, keys, values, queries = project(x, *norms, *weights, with_query=True)
    first = attend(own_limits, queries, keys, values, rows, 1, None)
    x_other = joined(others)
    normed_other, keys_other, values_other = project(x_other, *norms, *weights, with_query=False)
    mixed, lse = attend(other_limits, queries, keys_other, values_other, rows, group - 1, first)

    devices = Slice()
    plane, high = ("side", "member"), ("high",)
    core = jnp.reshape(devices.here["core"], (1,)).astype(jnp.int32)
    output, dmid, dmix, keep, give, feed_lines = feed(
        core, x, mixed, dy, w_output, w_expand, w_reduce, line(b_output), line(b_expand), line(b_reduce),
        line(gain_mlp), line(shift_mlp),
    )

    def back(own, start, count, token, before=None):
        return attend_back(
            own_limits if own else other_limits, core, queries,
            keys if own else keys_other, values if own else values_other, dmix, mixed, lse,
            normed if own else normed_other, rows, 1 if own else group - 1, start, count, before,
            token,
        )

    halves_feed = devices.spread([keep.reshape(-1, width), give.reshape(-1, width)], ("core",))
    part, cat_other, dw_other = back(False, 0, PAIRS, [])
    feed_half = combine([halves_feed], 0, 1, [cat_other])[0]
    cat_other = behind(cat_other, feed_half)
    feed_half = lax.psum(feed_half, ("rest", "grp"))
    send, lines = other_grads(x_other, [cat_other], w_key, w_value, rows)
    send = send.reshape(items, group - 1, rows, width)
    received = jnp.stack(
        [group_shift(send[:, shift - 1].reshape(total, width), shift) for shift in shifts]
    )
    cat, *halves_project = back(True, 0, PAIRS, [], (part, dw_other))
    value = devices.spread(halves_project, ("core",))
    value = devices.spread(combine([value], devices.place(plane), devices.size(plane)), plane)
    dx, lines = own_grads(
        x, [cat], received, dmid, w_query, w_key, w_value, line(gain_attn), lines, value[:1]
    )
    lines = jnp.concatenate([lines[:4], feed_lines], 0)
    value = combine([value], 0, 1, [dx])[0]
    for stage, small in (("low", "core"), ("high", "member")):
        lines = devices.total(lines, small)
        value = devices.in_order(devices.share(value, (stage,)), (stage,))
        value = combine([value], 0, 1, [lines])[0]
    lines = devices.total(lines, "side")
    value = join(devices.share(value[None], plane), [lines])
    project_own, project_came = devices.share(value, ("core",))
    lines = devices.total(devices.total(lines, "low"), "high")
    feed_half = behind(feed_half, value)
    feed_own, feed_came = devices.share(feed_half, ("core",))

    plane_origins = devices.origins(plane)
    dwo, dwe, dwr = feed_weights(core, feed_own, feed_came, w_expand.shape[1])
    dwq, dwk, dwv = project_weights(plane_origins, core, project_own, project_came, width)
    dbq, dbv, dgain, dshift, dbo, dbr, dgain_mlp, dshift_mlp = lines[:8]
    dbe = lines[8:].reshape(-1)
    return (
        unpadded(output),
        unpadded(dx),
        dwq, dwk, dwv, dwo, dwe, dwr,
        dbq, dbv, dbo, dbe, dbr, dgain, dshift, dgain_mlp, dshift_mlp,
    )


def solution(mesh):
    batch, group = mesh.shape["dp"], mesh.shape["grp"]
    mesh = jax.sharding.Mesh(mesh.devices.reshape(batch // 2, 2, group), ALL)
    items = ("rest", "core")
    rows = P(items, "grp", None)
    in_specs = (rows, P(items)) + (P(),) * 15 + (rows,)
    out_specs = (rows, rows) + (P(),) * 15
    return jax.shard_map(body, mesh=mesh, in_specs=in_specs, out_specs=out_specs, check_vma=False)
```

```python
import functools
import math

import jax
import jax.numpy as jnp
from jax import lax
from jax.experimental import pallas as pl
from jax.experimental.pallas import tpu as pltpu
from jax.sharding import PartitionSpec as P

HEADS = 8
HEAD_DIM = 64
VIEWS = 5
PATCH = 400
PAIR = 2 * HEAD_DIM
PAIRS = HEADS // 2
TILE = 256

EPSILON = 1e-05
NEGATIVE = -1e30
SCALE = 1.0 / math.sqrt(HEAD_DIM)

bf16 = jnp.bfloat16
f32 = jnp.float32


def dot_rows(left, right):
    return lax.dot_general(
        left, right, (((1,), (0,)), ((), ())), preferred_element_type=f32
    )


def dot_left(left, right):
    return lax.dot_general(
        left, right, (((0,), (0,)), ((), ())), preferred_element_type=f32
    )


def dot_right(left, right):
    return lax.dot_general(
        left, right, (((1,), (1,)), ((), ())), preferred_element_type=f32
    )


def chunk_of(rows, limit):
    best = 16
    for size in range(16, limit + 1, 16):
        if rows % size == 0:
            best = size
    return best


def hat_rows(matrix):
    center = matrix - jnp.mean(matrix, axis=-1, keepdims=True)
    spread = jnp.mean(center * center, axis=-1, keepdims=True)
    inverse = lax.rsqrt(spread + EPSILON)
    return center * inverse, inverse


def hat_back(grad_hat, hat, inverse):
    mean_grad = jnp.mean(grad_hat, axis=-1, keepdims=True)
    mean_cross = jnp.mean(grad_hat * hat, axis=-1, keepdims=True)
    return inverse * (grad_hat - mean_grad - hat * mean_cross)


def column_sums(matrix):
    return jnp.sum(matrix, axis=0, keepdims=True)


ALL = ("rest", "core", "grp")
VMEM_MIB = 60
ANYWHERE = pl.BlockSpec(memory_space=pl.ANY)


def params(axes):
    return pltpu.CompilerParams(
        dimension_semantics=("arbitrary",) * axes, vmem_limit_bytes=VMEM_MIB << 20
    )


def cost(flops, bytes_accessed, transcendentals=0):
    return pl.CostEstimate(
        flops=int(flops), bytes_accessed=int(bytes_accessed), transcendentals=int(transcendentals)
    )


def whole(shape):
    return pl.BlockSpec(shape, lambda *_: (0,) * len(shape))


def project_kernel(with_query, x_ref, gain, shift, w_query, w_key, w_value, b_query, b_value, *outs):
    hat, _ = hat_rows(x_ref[...].astype(f32))
    normed = (hat * gain[...] + shift[...]).astype(bf16)
    if with_query:
        normed_ref, key_ref, value_ref, query_ref = outs
        query = (dot_rows(normed, w_query[...]) + b_query[...]).astype(bf16)
        query_ref[...] = (query.astype(f32) * SCALE).astype(bf16)
    else:
        normed_ref, key_ref, value_ref = outs
    normed_ref[...] = normed
    key_ref[...] = dot_rows(normed, w_key[...]).astype(bf16)
    value_ref[...] = (dot_rows(normed, w_value[...]) + b_value[...]).astype(bf16)


def project(x, gain, shift, w_query, w_key, w_value, b_query, b_value, with_query):
    rows, width = x.shape
    step = chunk_of(rows, 272)
    count = 4 if with_query else 3
    row_block = pl.BlockSpec((step, width), lambda i: (i, 0))
    return pl.pallas_call(
        functools.partial(project_kernel, with_query),
        grid=(rows // step,),
        in_specs=[row_block, whole((1, width)), whole((1, width))]
        + [whole((width, width))] * 3
        + [whole((1, width))] * 2,
        out_specs=[row_block] * count,
        out_shape=[jax.ShapeDtypeStruct((rows, width), bf16)] * count,
        compiler_params=params(1),
        cost_estimate=cost(2 * rows * width * width * (count - 1), 2 * rows * width * (count + 1)),
        name="project",
    )(x, gain, shift, w_query, w_key, w_value, b_query, b_value)


def lanes_of(shape):
    return lax.broadcasted_iota(jnp.int32, shape, 1)


def forward_kernel(
    final, rows, blocks, step, limits, q_ref, k_ref, v_ref, *rest
):
    if final:
        acc_in, top_in, sum_in, out_ref, lse_ref, kt_ref, va_ref, *score_refs = rest
    else:
        acc_out, top_out, sum_out, kt_ref, va_ref, *score_refs = rest
    item = pl.program_id(0)
    key_count = rows * blocks
    query_rows = q_ref.shape[0]
    keys = k_ref[...].astype(f32)
    values = v_ref[...].astype(f32)
    first = lanes_of((key_count, PAIR)) < HEAD_DIM
    flipped = keys.T
    row_id = lax.broadcasted_iota(jnp.int32, (PAIR, key_count), 0)
    key_id = lax.broadcasted_iota(jnp.int32, (PAIR, key_count), 1)
    bias = jnp.zeros((PAIR, key_count), f32)
    for block in range(blocks):
        here = (key_id >= block * rows + limits[item, block]) & (key_id < (block + 1) * rows)
        bias = jnp.where(here, NEGATIVE, bias)
    spare = jnp.where((row_id & (HEAD_DIM - 1)) == 0, bias, 0.0)
    kt_ref[0] = jnp.where(row_id < HEAD_DIM, flipped, spare).astype(bf16)
    kt_ref[1] = jnp.where(row_id < HEAD_DIM, spare, flipped).astype(bf16)
    va_ref[0] = jnp.where(first, values, 1.0).astype(bf16)
    va_ref[1] = jnp.where(first, 1.0, values).astype(bf16)
    lanes = lanes_of((step, PAIR))
    head_first = lanes < HEAD_DIM
    one = jnp.where((lanes & (HEAD_DIM - 1)) == 0, 1.0, 0.0)
    tiles = [slice(t, min(t + TILE, key_count)) for t in range(0, key_count, TILE)]

    def query_of(unit):
        chunk, head = divmod(unit, 2)
        query = q_ref[chunk * step:(chunk + 1) * step, :].astype(f32)
        mine = head_first if head == 0 else jnp.logical_not(head_first)
        return jnp.where(mine, query, one).astype(bf16)

    units = 2 * (query_rows // step)
    outs, tops = [], []
    for unit in range(-1, units):
        query = query_of(unit + 1) if unit + 1 < units else None
        out, best = None, None
        for tile in tiles:
            if query is not None:
                scores = dot_rows(query, kt_ref[(unit + 1) % 2, :, tile])
                score_refs[(unit + 1) % 2][:, tile] = scores
                high = jnp.max(scores, axis=1, keepdims=True)
                best = high if best is None else jnp.maximum(best, high)
            if unit >= 0:
                weights = jnp.exp(score_refs[unit % 2][:, tile] - tops[unit]).astype(bf16)
                added = dot_rows(weights, va_ref[unit % 2, tile, :])
                out = added if out is None else out + added
        if best is not None:
            tops.append(best)
        if out is not None:
            outs.append(out)
        if unit % 2 == 0 or unit < 0:
            continue
        chunk = unit // 2
        place = slice(chunk * step, (chunk + 1) * step)
        acc = jnp.where(head_first, outs[unit - 1], outs[unit])
        total = pltpu.roll(jnp.where(head_first, outs[unit], outs[unit - 1]), HEAD_DIM, 1)
        top = jnp.where(head_first, tops[unit - 1], tops[unit])
        if final:
            other_top = top_in[place, :]
            new_top = jnp.maximum(top, other_top)
            scale_here = jnp.exp(top - new_top)
            scale_there = jnp.exp(other_top - new_top)
            total = total * scale_here + sum_in[place, :] * scale_there
            acc = acc * scale_here + acc_in[place, :] * scale_there
            out_ref[place, :] = acc / total
            lse_ref[place, :] = pltpu.roll(new_top + jnp.log(total), HEAD_DIM, 1)
        else:
            acc_out[place, :] = acc
            top_out[place, :] = top
            sum_out[place, :] = total


def attend(limits, queries, keys, values, rows, blocks, before):
    total, width = queries.shape
    items = total // rows
    key_count = rows * blocks
    step = chunk_of(rows, 208)
    query_block = pl.BlockSpec((rows, PAIR), lambda i, p, *_: (i, p))
    key_block = pl.BlockSpec((key_count, PAIR), lambda i, p, *_: (i, p))
    final = before is not None
    extra = list(before) if final else []
    outs = 2 if final else 3
    return pl.pallas_call(
        functools.partial(forward_kernel, final, rows, blocks, step),
        grid_spec=pltpu.PrefetchScalarGridSpec(
            num_scalar_prefetch=1,
            grid=(items, PAIRS),
            in_specs=[query_block, key_block, key_block] + [query_block] * len(extra),
            out_specs=[query_block] * outs,
            scratch_shapes=[
                pltpu.VMEM((2, PAIR, key_count), bf16),
                pltpu.VMEM((2, key_count, PAIR), bf16),
                pltpu.VMEM((step, key_count), f32),
                pltpu.VMEM((step, key_count), f32),
            ],
        ),
        out_shape=[jax.ShapeDtypeStruct((total, width), f32)] * outs,
        compiler_params=params(2),
        cost_estimate=cost(
            16 * total * key_count * width, 12 * total * width, total * key_count * HEADS
        ),
        name="attend",
    )(limits, queries, keys, values, *extra)


def split_three(value):
    high = value.astype(bf16).astype(f32)
    rest = value - high
    middle = rest.astype(bf16).astype(f32)
    return high, middle, rest - middle


def halves(core, block):
    half = block.shape[0] // 2
    upper, lower = block[:half], block[half:]
    mine = jnp.where(core == 0, upper, lower)
    theirs = jnp.where(core == 0, lower, upper)
    return mine.astype(bf16), theirs.astype(bf16)


def backward_kernel(
    last, tokens, rows, blocks, step, limits, core,
    q_ref, k_ref, v_ref, g_ref, out_ref, lse_ref, normed_ref, *rest,
):
    if last:
        before_ref, dw_in, *rest = rest
        cat_ref, keep_ref, send_ref, dw_acc, qt_ref, gt_ref, dqt_ref = rest[tokens:]
    else:
        dq_ref, cat_ref, dw_ref, dw_acc, qt_ref, gt_ref, dqt_ref = rest[tokens:]
    item = pl.program_id(1)
    query_rows = q_ref.shape[0]
    lanes = lanes_of((query_rows, PAIR))
    head_first = lanes < HEAD_DIM
    spare_lane = lanes & (HEAD_DIM - 1)

    def spare(parts, mask_one):
        high, middle, low = parts
        value = jnp.where(spare_lane == 0, high, 0.0)
        value = jnp.where(spare_lane == 1, middle, value)
        value = jnp.where(spare_lane == 2, low, value)
        return jnp.where(spare_lane == 3, mask_one, value)

    query = q_ref[...].astype(f32)
    grad = g_ref[...].astype(f32)
    product = grad * out_ref[...]
    delta_first = jnp.sum(jnp.where(head_first, product, 0.0), axis=1, keepdims=True)
    delta_second = jnp.sum(jnp.where(head_first, 0.0, product), axis=1, keepdims=True)
    delta = jnp.where(head_first, delta_second, delta_first)
    lse_spare = spare(split_three(-lse_ref[...]), 1.0)
    delta_spare = spare(split_three(-delta), 0.0)
    qt_ref[0] = jnp.where(head_first, query, lse_spare).T.astype(bf16)
    qt_ref[1] = jnp.where(head_first, lse_spare, query).T.astype(bf16)
    gt_ref[0] = jnp.where(head_first, grad, delta_spare).T.astype(bf16)
    gt_ref[1] = jnp.where(head_first, delta_spare, grad).T.astype(bf16)
    dqt_ref[...] = jnp.zeros_like(dqt_ref)

    key_lanes = lanes_of((step, PAIR))
    key_first = key_lanes < HEAD_DIM
    key_spare = key_lanes & (HEAD_DIM - 1)
    key_row = lax.broadcasted_iota(jnp.int32, (step, PAIR), 0)
    ones = jnp.where(key_spare < 3, 1.0, 0.0)
    per_block = rows // step

    def body(index, carry):
        place = pl.ds(pl.multiple_of(index * step, step), step)
        block = index // per_block
        limit = limits[item, block] - (index - block * per_block) * step
        bias = jnp.where(key_row >= limit, NEGATIVE, 0.0)
        key = k_ref[place, :].astype(f32)
        value = v_ref[place, :].astype(f32)
        key_aug = jnp.where(key_spare == 3, bias, ones)
        key_flipped = key.T.astype(bf16)
        dks, dvs = [], []
        for head in range(2):
            mine = key_first if head == 0 else jnp.logical_not(key_first)
            key_head = jnp.where(mine, key, key_aug).astype(bf16)
            value_head = jnp.where(mine, value, ones).astype(bf16)
            probs = jnp.exp(dot_rows(key_head, qt_ref[head]))
            grad_probs = dot_rows(value_head, gt_ref[head])
            grad_scores = (probs * grad_probs).astype(bf16)
            dvs.append(dot_rows(probs.astype(bf16), g_ref[...]))
            dks.append(dot_rows(grad_scores, q_ref[...]))
            own = pl.ds(head * HEAD_DIM, HEAD_DIM)
            half = key_flipped[head * HEAD_DIM:(head + 1) * HEAD_DIM]
            dqt_ref[own, :] += dot_rows(half, grad_scores)
        cat_ref[place, :PAIR] = jnp.where(key_first, dks[0], dks[1]).astype(bf16)
        cat_ref[place, PAIR:2 * PAIR] = jnp.where(key_first, dvs[0], dvs[1]).astype(bf16)
        return carry

    lax.fori_loop(0, blocks * per_block, body, 0)
    result = dqt_ref[...].T
    if last:
        cat_ref[:, 2 * PAIR:] = ((result + before_ref[...]) * SCALE).astype(bf16)
    else:
        dq_ref[...] = result
    added = dot_left(normed_ref[...], cat_ref[...])
    items = pl.num_programs(1)

    @pl.when(item == 0)
    def _():
        dw_acc[...] = added
        if last:
            dw_acc[:, :2 * PAIR] += dw_in[0]

    @pl.when(item > 0)
    def _():
        dw_acc[...] += added

    @pl.when(item == items - 1)
    def _():
        if last:
            keep_ref[...], send_ref[...] = halves(core[0], dw_acc[...])
        else:
            dw_ref[0] = dw_acc[...]


def attend_back(
    limits, core, queries, keys, values, grads, outs, lse, normed, rows, blocks, first, count, before,
    tokens,
):
    total, width = queries.shape
    items = total // rows
    key_count = rows * blocks
    step = chunk_of(rows, 208)
    last = before is not None
    cat = (3 if last else 2) * PAIR
    query_block = pl.BlockSpec((rows, PAIR), lambda p, i, *_: (i, first + p))
    key_block = pl.BlockSpec((key_count, PAIR), lambda p, i, *_: (i, first + p))
    normed_block = pl.BlockSpec((key_count, width), lambda p, i, *_: (i, 0))
    part_block = pl.BlockSpec((rows, PAIR), lambda p, i, *_: (i, p))
    cat_block = pl.BlockSpec((key_count, cat), lambda p, i, *_: (i, p))
    half_block = pl.BlockSpec((width // 2, cat), lambda p, i, *_: (p, 0))
    weight_block = pl.BlockSpec((1, width, cat), lambda p, i, *_: (p, 0, 0))
    weight_in = pl.BlockSpec((1, width, 2 * PAIR), lambda p, i, *_: (p, 0, 0))
    shape = jax.ShapeDtypeStruct
    cat_shape = shape((total * blocks, cat * count), bf16)
    if last:
        extra, extra_specs = list(before), [part_block, weight_in]
        out_shape = [cat_shape] + [shape((count * width // 2, cat), bf16)] * 2
        out_specs = [cat_block, half_block, half_block]
    else:
        extra, extra_specs = [], []
        out_shape = [shape((total, PAIR * count), f32), cat_shape, shape((count, width, cat), f32)]
        out_specs = [part_block, cat_block, weight_block]
    return pl.pallas_call(
        functools.partial(backward_kernel, last, len(tokens), rows, blocks, step),
        grid_spec=pltpu.PrefetchScalarGridSpec(
            num_scalar_prefetch=2,
            grid=(count, items),
            in_specs=[query_block, key_block, key_block]
            + [query_block] * 3
            + [normed_block]
            + extra_specs
            + [ANYWHERE] * len(tokens),
            out_specs=out_specs,
            scratch_shapes=[
                pltpu.VMEM((width, cat), f32),
                pltpu.VMEM((2, PAIR, rows), bf16),
                pltpu.VMEM((2, PAIR, rows), bf16),
                pltpu.VMEM((PAIR, rows), f32),
            ],
        ),
        out_shape=out_shape,
        compiler_params=params(2),
        cost_estimate=cost(total * PAIR, total * PAIR),
        name="attend_back",
    )(limits, core, queries, keys, values, grads, outs, lse, normed, *extra, *tokens)


def feed_kernel(
    x_ref, mix_ref, dy_ref, w_output, w_expand, w_reduce, b_output, b_expand, b_reduce, gain, shift,
    y_ref, dmid_ref, dmix_ref, dw_ref, line_ref,
    middle_ref, normed_ref, y_acc, grad_acc,
):
    part = pl.program_id(0)

    def put(index, block):
        dw_ref[index] = block.astype(bf16)

    @pl.when(part == 0)
    def _():
        mixed = mix_ref[...].astype(bf16)
        middle = x_ref[...].astype(f32) + dot_rows(mixed, w_output[...]) + b_output[...]
        middle_ref[...] = middle
        hat, _ = hat_rows(middle)
        normed_ref[...] = (hat * gain[...] + shift[...]).astype(bf16)
        y_acc[...] = middle + b_reduce[...]
        grad_acc[...] = jnp.zeros_like(grad_acc)
        line_ref[1:2, :] = column_sums(dy_ref[...].astype(f32))

    normed = normed_ref[...]
    upper = dot_rows(normed, w_expand[...]) + b_expand[...]
    cumulative = 0.5 * lax.erf(upper * math.sqrt(0.5)) + 0.5
    density = jnp.exp(upper * upper * -0.5) * (1.0 / math.sqrt(2.0 * math.pi))
    active = (upper * cumulative).astype(bf16)
    slope = cumulative + upper * density
    y_acc[...] += dot_rows(active, w_reduce[...])
    put(1 + 2 * part, dot_left(active, dy_ref[...]))
    grad_upper = (dot_right(dy_ref[...], w_reduce[...]) * slope).astype(bf16)
    line_ref[pl.ds(4 + part, 1), :] = column_sums(grad_upper.astype(f32))
    put(2 + 2 * part, dot_left(normed, grad_upper))
    grad_acc[...] += dot_right(grad_upper, w_expand[...])

    @pl.when(part == pl.num_programs(0) - 1)
    def _():
        y_ref[...] = y_acc[...].astype(bf16)
        grad = grad_acc[...]
        hat, inverse = hat_rows(middle_ref[...])
        line_ref[2:3, :] = column_sums(grad * hat)
        line_ref[3:4, :] = column_sums(grad)
        dmid = hat_back(grad * gain[...], hat, inverse) + dy_ref[...].astype(f32)
        dmid_ref[...] = dmid
        branch = dmid.astype(bf16)
        line_ref[0:1, :] = column_sums(branch.astype(f32))
        put(0, dot_left(mix_ref[...].astype(bf16), branch))
        dmix_ref[...] = dot_right(branch, w_output[...]).astype(bf16)


def feed(x, mixed, dy, w_output, w_expand, w_reduce, b_output, b_expand, b_reduce, gain, shift):
    rows, width = x.shape
    hidden = w_expand.shape[1]
    parts = hidden // width
    row = whole((rows, width))
    line = whole((1, width))
    expand = pl.BlockSpec((width, width), lambda i, *_: (0, i))
    reduce = pl.BlockSpec((width, width), lambda i, *_: (i, 0))
    hidden_line = pl.BlockSpec((1, width), lambda i, *_: (0, i))
    weights = (1 + 2 * parts, width, width)
    lines = (4 + parts, width)
    shape = jax.ShapeDtypeStruct
    return pl.pallas_call(
        feed_kernel,
        grid=(parts,),
        in_specs=[row, row, row, whole((width, width)), expand, reduce, line, hidden_line, line, line, line],
        out_specs=[row, row, row, whole(weights), whole(lines)],
        scratch_shapes=[
            pltpu.VMEM((rows, width), f32),
            pltpu.VMEM((rows, width), bf16),
            pltpu.VMEM((rows, width), f32),
            pltpu.VMEM((rows, width), f32),
        ],
        out_shape=[
            shape((rows, width), bf16),
            shape((rows, width), f32),
            shape((rows, width), bf16),
            shape(weights, bf16),
            shape(lines, f32),
        ],
        compiler_params=params(1),
        cost_estimate=cost(12 * rows * width * hidden + 6 * rows * width * width, 20 * rows * width, 2 * rows * hidden),
        name="feed",
    )(x, mixed, dy, w_output, w_expand, w_reduce, b_output, b_expand, b_reduce, gain, shift)


def gather_parts(refs, part, parts):
    blocks = []
    for ref in refs:
        pairs = ref.shape[1] // (parts * PAIR)
        for pair in range(pairs):
            start = (pair * parts + part) * PAIR
            blocks.append(ref[:, start:start + PAIR])
    return jnp.concatenate(blocks, axis=1)


def other_kernel(cats, x_ref, w_key, w_value, *rest):
    cat_refs, (send_ref, line_ref) = rest[:cats], rest[cats:]
    dk = gather_parts(cat_refs, 0, 2)
    dv = gather_parts(cat_refs, 1, 2)
    grad = dot_right(dk, w_key[...]) + dot_right(dv, w_value[...])
    send_ref[...] = grad.astype(bf16)
    hat, _ = hat_rows(x_ref[...].astype(f32))

    @pl.when(pl.program_id(0) == 0)
    def _():
        line_ref[...] = jnp.zeros_like(line_ref)

    line_ref[1:2, :] += column_sums(dv.astype(f32))
    line_ref[2:3, :] += column_sums(grad * hat)
    line_ref[3:4, :] += column_sums(grad)


def other_grads(x, cats, w_key, w_value, rows):
    total, width = x.shape
    step = chunk_of(rows, 272)
    row = pl.BlockSpec((step, width), lambda i: (i, 0))
    square = whole((width, width))
    shape = jax.ShapeDtypeStruct
    return pl.pallas_call(
        functools.partial(other_kernel, len(cats)),
        grid=(total // step,),
        in_specs=[row] + [square] * 2
        + [pl.BlockSpec((step, c.shape[1]), lambda i: (i, 0)) for c in cats],
        out_specs=[row, whole((8, width))],
        out_shape=[shape((total, width), bf16), shape((8, width), f32)],
        compiler_params=params(1),
        cost_estimate=cost(4 * total * width * width, 8 * total * width),
        name="other_grads",
    )(x, w_key, w_value, *cats)


def own_kernel(cats, x_ref, recv_ref, dmid_ref, w_query, w_key, w_value, gain, line_in, *rest):
    cat_refs, (dx_ref, line_ref) = rest[:cats], rest[-2:]
    dk = gather_parts(cat_refs, 0, 3)
    dv = gather_parts(cat_refs, 1, 3)
    dq = gather_parts(cat_refs, 2, 3)
    grad = dot_right(dq, w_query[...]) + dot_right(dk, w_key[...]) + dot_right(dv, w_value[...])
    hat, inverse = hat_rows(x_ref[...].astype(f32))

    @pl.when(pl.program_id(0) == 0)
    def _():
        line_ref[...] = line_in[...]

    line_ref[0:1, :] += column_sums(dq.astype(f32))
    line_ref[1:2, :] += column_sums(dv.astype(f32))
    line_ref[2:3, :] += column_sums(grad * hat)
    line_ref[3:4, :] += column_sums(grad)
    for index in range(recv_ref.shape[0]):
        grad = grad + recv_ref[index].astype(f32)
    dx_ref[...] = hat_back(grad * gain[...], hat, inverse) + dmid_ref[...]


def own_grads(x, cats, recv, dmid, w_query, w_key, w_value, gain, lines, after):
    rows, width = x.shape
    step = chunk_of(rows, 272)
    row = pl.BlockSpec((step, width), lambda i: (i, 0))
    square = whole((width, width))
    shape = jax.ShapeDtypeStruct
    return pl.pallas_call(
        functools.partial(own_kernel, len(cats)),
        grid=(rows // step,),
        in_specs=[row, pl.BlockSpec((recv.shape[0], step, width), lambda i: (0, i, 0)), row]
        + [square] * 3
        + [whole((1, width)), whole((8, width))]
        + [pl.BlockSpec((step, c.shape[1]), lambda i: (i, 0)) for c in cats]
        + [ANYWHERE] * len(after),
        out_specs=[row, whole((8, width))],
        out_shape=[shape((rows, width), f32), shape((8, width), f32)],
        compiler_params=params(1),
        cost_estimate=cost(6 * rows * width * width, 16 * rows * width),
        name="own_grads",
    )(x, recv, dmid, w_query, w_key, w_value, gain, lines, *cats, *after)


class Slice:
    def __init__(self):
        group, rest = lax.axis_size("grp"), lax.axis_size("rest")
        batch = rest * lax.axis_size("core")
        side = 2 if rest % 2 == 0 else 1
        rest //= side
        high = 2 if rest % 2 == 0 else 1
        self.sizes = {"core": 2, "side": side, "member": group, "high": high, "low": rest // high}
        self.count = group * batch
        self.here = self.coords(lax.axis_index(ALL))

    def coords(self, linear):
        out = {}
        for name in ("member", "core", "side", "low", "high"):
            out[name] = linear % self.sizes[name]
            linear = linear // self.sizes[name]
        return out

    def linear(self, coords):
        total = 0
        for name in ("high", "low", "side", "core", "member"):
            total = total * self.sizes[name] + coords[name]
        return total

    def size(self, stage):
        return math.prod(self.sizes[name] for name in stage)

    def place(self, stage, coords=None):
        coords = self.here if coords is None else coords
        total = 0
        for name in stage:
            total = total * self.sizes[name] + coords[name]
        return total

    def send(self, array, stage, shift):
        pairs = []
        for source in range(self.count):
            coords = self.coords(source)
            place = (self.place(stage, coords) + shift) % self.size(stage)
            for name in reversed(stage):
                coords[name] = place % self.sizes[name]
                place //= self.sizes[name]
            pairs.append((source, self.linear(coords)))
        return lax.ppermute(array, ALL, pairs)

    def spread(self, parts, stage):
        return [parts[0]] + [self.send(part, stage, s) for s, part in enumerate(parts) if s > 0]

    def share(self, array, stage):
        return self.spread([array] * self.size(stage), stage)

    def origins(self, stage):
        size = self.size(stage)
        return ((self.place(stage) - jnp.arange(size)) % size).astype(jnp.int32)

    def in_order(self, parts, stage):
        if len(parts) <= 2:
            return parts
        stack = jnp.stack(parts)
        order = self.origins(stage)
        return [lax.dynamic_index_in_dim(stack, order[i], 0, False) for i in range(len(parts))]

    def total(self, array, name):
        first, *others = self.in_order(self.share(array, (name,)), (name,))
        for part in others:
            first = first + part
        return first


def behind(array, *others):
    return lax.optimization_barrier((array, *others))[0]


def cut_kernel(size, place, keep_ref, came_ref, *outs):
    rows = keep_ref.shape[0] // size
    for shift, out in enumerate(outs):
        span = pl.ds(pl.multiple_of((place[0] + shift) % size * rows, rows), rows)
        out[...] = (keep_ref[span, :].astype(f32) + came_ref[span, :].astype(f32)).astype(bf16)


def cut(keep, came, place, size):
    rows, width = keep.shape
    part = (rows // size, width)
    return pl.pallas_call(
        functools.partial(cut_kernel, size),
        grid_spec=pltpu.PrefetchScalarGridSpec(
            num_scalar_prefetch=1,
            grid=(1,),
            in_specs=[whole(keep.shape)] * 2,
            out_specs=[whole(part)] * size,
        ),
        out_shape=[jax.ShapeDtypeStruct(part, bf16)] * size,
        compiler_params=params(1),
        cost_estimate=cost(rows * width, rows * width),
        name="cut",
    )(jnp.reshape(place, (1,)).astype(jnp.int32), keep, came)


def add_up(parts):
    total = parts[0].astype(f32)
    for part in parts[1:]:
        total = total + part.astype(f32)
    return total.astype(bf16)


def feed_weights(summed, hidden):
    width = summed.shape[1]
    parts = hidden // width
    blocks = [summed[index].astype(f32) for index in range(1 + 2 * parts)]
    expand = jnp.concatenate(blocks[2::2], 1)
    reduce = jnp.concatenate(blocks[1::2], 0)
    return blocks[0], expand, reduce


def project_weights_kernel(size, places, core, *refs):
    ins, (dwq_ref, dwk_ref, dwv_ref, flat) = refs[:2 * size], refs[2 * size:]
    half = dwq_ref.shape[0] // 2
    rows = PAIRS * half // size
    for which in range(2):
        target = core[0] if which == 0 else 1 - core[0]
        for index in range(size):
            span = pl.ds(pl.multiple_of(places[index] * rows, rows), rows)
            flat[target, span, :] = ins[which * size + index][...]
    for side in range(2):
        for pair in range(PAIRS):
            block = flat[side, pair * half:(pair + 1) * half, :].astype(f32)
            down = slice(side * half, (side + 1) * half)
            span = slice(pair * PAIR, (pair + 1) * PAIR)
            dwk_ref[down, span] = block[:, :PAIR]
            dwv_ref[down, span] = block[:, PAIR:2 * PAIR]
            dwq_ref[down, span] = block[:, 2 * PAIR:]


def project_weights(places, core, own, came, width):
    shape = jax.ShapeDtypeStruct
    square = (width, width)
    size = len(own)
    rows, cat = own[0].shape
    return pl.pallas_call(
        functools.partial(project_weights_kernel, size),
        grid_spec=pltpu.PrefetchScalarGridSpec(
            num_scalar_prefetch=2,
            grid=(1,),
            in_specs=[whole((rows, cat))] * (2 * size),
            out_specs=[whole(square)] * 3,
            scratch_shapes=[pltpu.VMEM((2, size * rows, cat), bf16)],
        ),
        out_shape=[shape(square, f32)] * 3,
        compiler_params=params(1),
        cost_estimate=cost(0, 20 * width * width),
        name="project_weights",
    )(places, core, *own, *came)


def body(
    layer_input,
    lang_counts,
    w_query,
    w_key,
    w_value,
    w_output,
    w_expand,
    w_reduce,
    b_query,
    b_value,
    b_output,
    b_expand,
    b_reduce,
    gain_attn,
    shift_attn,
    gain_mlp,
    shift_mlp,
    cotangent,
):
    items, own_rows, width = layer_input.shape
    group = lax.axis_size("grp")
    me = lax.axis_index("grp")
    rows = -(-own_rows // 16) * 16
    total = items * rows
    patch_rows = VIEWS * PATCH
    shifts = range(1, group)

    def padded(array):
        if rows != own_rows:
            array = jnp.pad(array, ((0, 0), (0, rows - own_rows), (0, 0)))
        return array.reshape(total, width)

    def unpadded(array):
        return array.reshape(items, rows, width)[:, :own_rows]

    def limit_of(owner):
        return jnp.clip(patch_rows + lang_counts - owner * own_rows, 0, own_rows)

    def line(vector):
        return vector.reshape(1, -1)

    def group_shift(array, shift):
        return lax.ppermute(array, "grp", [(i, (i + shift) % group) for i in range(group)])

    def joined(parts):
        if len(parts) == 1:
            return parts[0]
        return jnp.stack([p.reshape(items, rows, width) for p in parts], 1).reshape(-1, width)

    x = padded(layer_input)
    dy = padded(cotangent)
    others = [group_shift(x, -shift) for shift in shifts]
    own_limits = limit_of(me).reshape(items, 1)
    other_limits = jnp.stack([limit_of((me + shift) % group) for shift in shifts], 1)

    weights = (w_query, w_key, w_value, line(b_query), line(b_value))
    norms = (line(gain_attn), line(shift_attn))
    normed, keys, values, queries = project(x, *norms, *weights, with_query=True)
    first = attend(own_limits, queries, keys, values, rows, 1, None)
    x_other = joined(others)
    normed_other, keys_other, values_other = project(x_other, *norms, *weights, with_query=False)
    mixed, lse = attend(other_limits, queries, keys_other, values_other, rows, group - 1, first)

    devices = Slice()
    plane = ("side", "member")
    core = jnp.reshape(devices.here["core"], (1,)).astype(jnp.int32)
    output, dmid, dmix, dw_feed, feed_lines = feed(
        x, mixed, dy, w_output, w_expand, w_reduce, line(b_output), line(b_expand), line(b_reduce),
        line(gain_mlp), line(shift_mlp),
    )
    dw_feed = lax.psum(dw_feed, ALL)

    part, cat_other, dw_other = attend_back(
        other_limits, core, queries, keys_other, values_other, dmix, mixed, lse, normed_other,
        rows, group - 1, 0, PAIRS, None, [],
    )
    send, lines = other_grads(x_other, [cat_other], w_key, w_value, rows)
    send = send.reshape(items, group - 1, rows, width)
    received = jnp.stack(
        [group_shift(send[:, shift - 1].reshape(total, width), shift) for shift in shifts]
    )
    cat, keep, give = attend_back(
        own_limits, core, queries, keys, values, dmix, mixed, lse, normed,
        rows, 1, 0, PAIRS, (part, dw_other), [],
    )
    keep, came = devices.spread([keep, give], ("core",))
    parts = devices.spread(cut(keep, came, devices.place(plane), devices.size(plane)), plane)
    dx, lines = own_grads(
        x, [cat], received, dmid, w_query, w_key, w_value, line(gain_attn), lines, parts[:1]
    )
    lines = jnp.concatenate([lines[:4], feed_lines], 0)
    value = behind(add_up(parts), dx)
    for stage, small in (("low", "core"), ("high", "member")):
        lines = devices.total(lines, small)
        value = devices.in_order(devices.share(value, (stage,)), (stage,))
        value = behind(add_up(value), lines)
    lines = devices.total(lines, "side")
    project_own = devices.share(value, plane)
    project_came = [devices.send(piece, ("core",), 1) for piece in project_own]
    lines = devices.total(devices.total(behind(lines, *project_own), "low"), "high")
    dwq, dwk, dwv = project_weights(devices.origins(plane), core, project_own, project_came, width)
    dwo, dwe, dwr = feed_weights(behind(dw_feed, dwq), w_expand.shape[1])
    dbq, dbv, dgain, dshift, dbo, dbr, dgain_mlp, dshift_mlp = lines[:8]
    dbe = lines[8:].reshape(-1)
    return (
        unpadded(output),
        unpadded(dx),
        dwq, dwk, dwv, dwo, dwe, dwr,
        dbq, dbv, dbo, dbe, dbr, dgain, dshift, dgain_mlp, dshift_mlp,
    )


def solution(mesh):
    batch, group = mesh.shape["dp"], mesh.shape["grp"]
    mesh = jax.sharding.Mesh(mesh.devices.reshape(batch // 2, 2, group), ALL)
    items = ("rest", "core")
    rows = P(items, "grp", None)
    in_specs = (rows, P(items)) + (P(),) * 15 + (rows,)
    out_specs = (rows, rows) + (P(),) * 15
    return jax.shard_map(body, mesh=mesh, in_specs=in_specs, out_specs=out_specs, check_vma=False)
```

```python
import functools
import math

import jax
import jax.numpy as jnp
from jax import lax
from jax.experimental import pallas as pl
from jax.experimental.pallas import tpu as pltpu
from jax.sharding import PartitionSpec as P

HEADS = 8
HEAD_DIM = 64
VIEWS = 5
PATCH = 400
PAIR = 2 * HEAD_DIM
PAIRS = HEADS // 2
TILE = 256

EPSILON = 1e-05
NEGATIVE = -1e30
SCALE = 1.0 / math.sqrt(HEAD_DIM)

bf16 = jnp.bfloat16
f32 = jnp.float32


def dot_rows(left, right):
    return lax.dot_general(
        left, right, (((1,), (0,)), ((), ())), preferred_element_type=f32
    )


def dot_left(left, right):
    return lax.dot_general(
        left, right, (((0,), (0,)), ((), ())), preferred_element_type=f32
    )


def dot_right(left, right):
    return lax.dot_general(
        left, right, (((1,), (1,)), ((), ())), preferred_element_type=f32
    )


def chunk_of(rows, limit):
    best = 16
    for size in range(16, limit + 1, 16):
        if rows % size == 0:
            best = size
    return best


def hat_rows(matrix):
    center = matrix - jnp.mean(matrix, axis=-1, keepdims=True)
    spread = jnp.mean(center * center, axis=-1, keepdims=True)
    inverse = lax.rsqrt(spread + EPSILON)
    return center * inverse, inverse


def hat_back(grad_hat, hat, inverse):
    mean_grad = jnp.mean(grad_hat, axis=-1, keepdims=True)
    mean_cross = jnp.mean(grad_hat * hat, axis=-1, keepdims=True)
    return inverse * (grad_hat - mean_grad - hat * mean_cross)


def column_sums(matrix):
    return jnp.sum(matrix, axis=0, keepdims=True)


ALL = ("rest", "core", "grp")
VMEM_MIB = 60
ANYWHERE = pl.BlockSpec(memory_space=pl.ANY)


def params(axes):
    return pltpu.CompilerParams(
        dimension_semantics=("arbitrary",) * axes, vmem_limit_bytes=VMEM_MIB << 20
    )


def cost(flops, bytes_accessed, transcendentals=0):
    return pl.CostEstimate(
        flops=int(flops), bytes_accessed=int(bytes_accessed), transcendentals=int(transcendentals)
    )


def whole(shape):
    return pl.BlockSpec(shape, lambda *_: (0,) * len(shape))


def project_kernel(with_query, x_ref, gain, shift, w_query, w_key, w_value, b_query, b_value, *outs):
    hat, _ = hat_rows(x_ref[...].astype(f32))
    normed = (hat * gain[...] + shift[...]).astype(bf16)
    if with_query:
        normed_ref, key_ref, value_ref, query_ref = outs
        query = (dot_rows(normed, w_query[...]) + b_query[...]).astype(bf16)
        query_ref[...] = (query.astype(f32) * SCALE).astype(bf16)
    else:
        normed_ref, key_ref, value_ref = outs
    normed_ref[...] = normed
    key_ref[...] = dot_rows(normed, w_key[...]).astype(bf16)
    value_ref[...] = (dot_rows(normed, w_value[...]) + b_value[...]).astype(bf16)


def project(x, gain, shift, w_query, w_key, w_value, b_query, b_value, with_query):
    rows, width = x.shape
    step = chunk_of(rows, 272)
    count = 4 if with_query else 3
    row_block = pl.BlockSpec((step, width), lambda i: (i, 0))
    return pl.pallas_call(
        functools.partial(project_kernel, with_query),
        grid=(rows // step,),
        in_specs=[row_block, whole((1, width)), whole((1, width))]
        + [whole((width, width))] * 3
        + [whole((1, width))] * 2,
        out_specs=[row_block] * count,
        out_shape=[jax.ShapeDtypeStruct((rows, width), bf16)] * count,
        compiler_params=params(1),
        cost_estimate=cost(2 * rows * width * width * (count - 1), 2 * rows * width * (count + 1)),
        name="project",
    )(x, gain, shift, w_query, w_key, w_value, b_query, b_value)


def lanes_of(shape):
    return lax.broadcasted_iota(jnp.int32, shape, 1)


def forward_kernel(
    final, rows, blocks, step, limits, q_ref, k_ref, v_ref, *rest
):
    if final:
        acc_in, top_in, sum_in, out_ref, lse_ref, kt_ref, va_ref, *score_refs = rest
    else:
        acc_out, top_out, sum_out, kt_ref, va_ref, *score_refs = rest
    item = pl.program_id(0)
    key_count = rows * blocks
    query_rows = q_ref.shape[0]
    keys = k_ref[...].astype(f32)
    values = v_ref[...].astype(f32)
    first = lanes_of((key_count, PAIR)) < HEAD_DIM
    flipped = keys.T
    row_id = lax.broadcasted_iota(jnp.int32, (PAIR, key_count), 0)
    key_id = lax.broadcasted_iota(jnp.int32, (PAIR, key_count), 1)
    bias = jnp.zeros((PAIR, key_count), f32)
    for block in range(blocks):
        here = (key_id >= block * rows + limits[item, block]) & (key_id < (block + 1) * rows)
        bias = jnp.where(here, NEGATIVE, bias)
    spare = jnp.where((row_id & (HEAD_DIM - 1)) == 0, bias, 0.0)
    kt_ref[0] = jnp.where(row_id < HEAD_DIM, flipped, spare).astype(bf16)
    kt_ref[1] = jnp.where(row_id < HEAD_DIM, spare, flipped).astype(bf16)
    va_ref[0] = jnp.where(first, values, 1.0).astype(bf16)
    va_ref[1] = jnp.where(first, 1.0, values).astype(bf16)
    lanes = lanes_of((step, PAIR))
    head_first = lanes < HEAD_DIM
    one = jnp.where((lanes & (HEAD_DIM - 1)) == 0, 1.0, 0.0)
    tiles = [slice(t, min(t + TILE, key_count)) for t in range(0, key_count, TILE)]

    def query_of(unit):
        chunk, head = divmod(unit, 2)
        query = q_ref[chunk * step:(chunk + 1) * step, :].astype(f32)
        mine = head_first if head == 0 else jnp.logical_not(head_first)
        return jnp.where(mine, query, one).astype(bf16)

    units = 2 * (query_rows // step)
    outs, tops = [], []
    for unit in range(-1, units):
        query = query_of(unit + 1) if unit + 1 < units else None
        out, best = None, None
        for tile in tiles:
            if query is not None:
                scores = dot_rows(query, kt_ref[(unit + 1) % 2, :, tile])
                score_refs[(unit + 1) % 2][:, tile] = scores
                high = jnp.max(scores, axis=1, keepdims=True)
                best = high if best is None else jnp.maximum(best, high)
            if unit >= 0:
                weights = jnp.exp(score_refs[unit % 2][:, tile] - tops[unit]).astype(bf16)
                added = dot_rows(weights, va_ref[unit % 2, tile, :])
                out = added if out is None else out + added
        if best is not None:
            tops.append(best)
        if out is not None:
            outs.append(out)
        if unit % 2 == 0 or unit < 0:
            continue
        chunk = unit // 2
        place = slice(chunk * step, (chunk + 1) * step)
        acc = jnp.where(head_first, outs[unit - 1], outs[unit])
        total = pltpu.roll(jnp.where(head_first, outs[unit], outs[unit - 1]), HEAD_DIM, 1)
        top = jnp.where(head_first, tops[unit - 1], tops[unit])
        if final:
            other_top = top_in[place, :]
            new_top = jnp.maximum(top, other_top)
            scale_here = jnp.exp(top - new_top)
            scale_there = jnp.exp(other_top - new_top)
            total = total * scale_here + sum_in[place, :] * scale_there
            acc = acc * scale_here + acc_in[place, :] * scale_there
            out_ref[place, :] = acc / total
            lse_ref[place, :] = pltpu.roll(new_top + jnp.log(total), HEAD_DIM, 1)
        else:
            acc_out[place, :] = acc
            top_out[place, :] = top
            sum_out[place, :] = total


def attend(limits, queries, keys, values, rows, blocks, before):
    total, width = queries.shape
    items = total // rows
    key_count = rows * blocks
    step = chunk_of(rows, 208)
    query_block = pl.BlockSpec((rows, PAIR), lambda i, p, *_: (i, p))
    key_block = pl.BlockSpec((key_count, PAIR), lambda i, p, *_: (i, p))
    final = before is not None
    extra = list(before) if final else []
    outs = 2 if final else 3
    return pl.pallas_call(
        functools.partial(forward_kernel, final, rows, blocks, step),
        grid_spec=pltpu.PrefetchScalarGridSpec(
            num_scalar_prefetch=1,
            grid=(items, PAIRS),
            in_specs=[query_block, key_block, key_block] + [query_block] * len(extra),
            out_specs=[query_block] * outs,
            scratch_shapes=[
                pltpu.VMEM((2, PAIR, key_count), bf16),
                pltpu.VMEM((2, key_count, PAIR), bf16),
                pltpu.VMEM((step, key_count), f32),
                pltpu.VMEM((step, key_count), f32),
            ],
        ),
        out_shape=[jax.ShapeDtypeStruct((total, width), f32)] * outs,
        compiler_params=params(2),
        cost_estimate=cost(
            16 * total * key_count * width, 12 * total * width, total * key_count * HEADS
        ),
        name="attend",
    )(limits, queries, keys, values, *extra)


def split_three(value):
    high = value.astype(bf16).astype(f32)
    rest = value - high
    middle = rest.astype(bf16).astype(f32)
    return high, middle, rest - middle


def halves(core, block):
    half = block.shape[0] // 2
    upper, lower = block[:half], block[half:]
    mine = jnp.where(core == 0, upper, lower)
    theirs = jnp.where(core == 0, lower, upper)
    return mine.astype(bf16), theirs.astype(bf16)


def backward_kernel(
    last, tokens, rows, blocks, step, limits, core,
    q_ref, k_ref, v_ref, g_ref, out_ref, lse_ref, normed_ref, *rest,
):
    if last:
        before_ref, dw_in, *rest = rest
        cat_ref, keep_ref, send_ref, dw_acc, qt_ref, gt_ref, dqt_ref, *wide = rest[tokens:]
    else:
        dq_ref, cat_ref, dw_ref, dw_acc, qt_ref, gt_ref, dqt_ref, *wide = rest[tokens:]
    prob_refs, score_refs = wide[:2], wide[2:]
    item = pl.program_id(1)
    query_rows = q_ref.shape[0]
    lanes = lanes_of((query_rows, PAIR))
    head_first = lanes < HEAD_DIM
    spare_lane = lanes & (HEAD_DIM - 1)

    def spare(parts, mask_one):
        high, middle, low = parts
        value = jnp.where(spare_lane == 0, high, 0.0)
        value = jnp.where(spare_lane == 1, middle, value)
        value = jnp.where(spare_lane == 2, low, value)
        return jnp.where(spare_lane == 3, mask_one, value)

    query = q_ref[...].astype(f32)
    grad = g_ref[...].astype(f32)
    product = grad * out_ref[...]
    delta_first = jnp.sum(jnp.where(head_first, product, 0.0), axis=1, keepdims=True)
    delta_second = jnp.sum(jnp.where(head_first, 0.0, product), axis=1, keepdims=True)
    delta = jnp.where(head_first, delta_second, delta_first)
    lse_spare = spare(split_three(-lse_ref[...]), 1.0)
    delta_spare = spare(split_three(-delta), 0.0)
    qt_ref[0] = jnp.where(head_first, query, lse_spare).T.astype(bf16)
    qt_ref[1] = jnp.where(head_first, lse_spare, query).T.astype(bf16)
    gt_ref[0] = jnp.where(head_first, grad, delta_spare).T.astype(bf16)
    gt_ref[1] = jnp.where(head_first, delta_spare, grad).T.astype(bf16)
    dqt_ref[...] = jnp.zeros_like(dqt_ref)

    key_lanes = lanes_of((step, PAIR))
    key_first = key_lanes < HEAD_DIM
    key_spare = key_lanes & (HEAD_DIM - 1)
    key_row = lax.broadcasted_iota(jnp.int32, (step, PAIR), 0)
    ones = jnp.where(key_spare < 3, 1.0, 0.0)
    per_block = rows // step
    tiles = [slice(t, min(t + TILE, query_rows)) for t in range(0, query_rows, TILE)]

    def operands(unit):
        chunk, head = divmod(unit, 2)
        place = slice(chunk * step, (chunk + 1) * step)
        block = chunk // per_block
        limit = limits[item, block] - (chunk - block * per_block) * step
        bias = jnp.where(key_row >= limit, NEGATIVE, 0.0)
        key = k_ref[place, :].astype(f32)
        value = v_ref[place, :].astype(f32)
        mine = key_first if head == 0 else jnp.logical_not(key_first)
        key_head = jnp.where(mine, key, jnp.where(key_spare == 3, bias, ones)).astype(bf16)
        value_head = jnp.where(mine, value, ones).astype(bf16)
        half = key.T[head * HEAD_DIM:(head + 1) * HEAD_DIM].astype(bf16)
        return key_head, value_head, half

    units = 2 * blocks * per_block
    dks, dvs, half = [], [], None
    for unit in range(-1, units):
        more = unit + 1 < units
        if more:
            key_head, value_head, next_half = operands(unit + 1)
            which = (unit + 1) % 2
        dk, dv = None, None
        for tile in tiles:
            if more:
                probs = jnp.exp(dot_rows(key_head, qt_ref[which, :, tile]))
                grad_probs = dot_rows(value_head, gt_ref[which, :, tile])
                prob_refs[which][:, tile] = probs.astype(bf16)
                score_refs[which][:, tile] = (probs * grad_probs).astype(bf16)
            if unit >= 0:
                grad_scores = score_refs[unit % 2][:, tile]
                dv_part = dot_rows(prob_refs[unit % 2][:, tile], g_ref[tile, :])
                dk_part = dot_rows(grad_scores, q_ref[tile, :])
                dv = dv_part if dv is None else dv + dv_part
                dk = dk_part if dk is None else dk + dk_part
                own = slice(unit % 2 * HEAD_DIM, (unit % 2 + 1) * HEAD_DIM)
                dqt_ref[own, tile] += dot_rows(half, grad_scores)
        half = next_half if more else None
        if unit >= 0:
            dks.append(dk)
            dvs.append(dv)
        if unit >= 0 and unit % 2 == 1:
            place = slice(unit // 2 * step, (unit // 2 + 1) * step)
            cat_ref[place, :PAIR] = jnp.where(key_first, dks[-2], dks[-1]).astype(bf16)
            cat_ref[place, PAIR:2 * PAIR] = jnp.where(key_first, dvs[-2], dvs[-1]).astype(bf16)

    result = dqt_ref[...].T
    if last:
        cat_ref[:, 2 * PAIR:] = ((result + before_ref[...]) * SCALE).astype(bf16)
    else:
        dq_ref[...] = result
    added = dot_left(normed_ref[...], cat_ref[...])
    items = pl.num_programs(1)

    @pl.when(item == 0)
    def _():
        dw_acc[...] = added
        if last:
            dw_acc[:, :2 * PAIR] += dw_in[0]

    @pl.when(item > 0)
    def _():
        dw_acc[...] += added

    @pl.when(item == items - 1)
    def _():
        if last:
            keep_ref[...], send_ref[...] = halves(core[0], dw_acc[...])
        else:
            dw_ref[0] = dw_acc[...]


def attend_back(
    limits, core, queries, keys, values, grads, outs, lse, normed, rows, blocks, first, count, before,
    tokens,
):
    total, width = queries.shape
    items = total // rows
    key_count = rows * blocks
    step = chunk_of(rows, 208)
    last = before is not None
    cat = (3 if last else 2) * PAIR
    query_block = pl.BlockSpec((rows, PAIR), lambda p, i, *_: (i, first + p))
    key_block = pl.BlockSpec((key_count, PAIR), lambda p, i, *_: (i, first + p))
    normed_block = pl.BlockSpec((key_count, width), lambda p, i, *_: (i, 0))
    part_block = pl.BlockSpec((rows, PAIR), lambda p, i, *_: (i, p))
    cat_block = pl.BlockSpec((key_count, cat), lambda p, i, *_: (i, p))
    half_block = pl.BlockSpec((width // 2, cat), lambda p, i, *_: (p, 0))
    weight_block = pl.BlockSpec((1, width, cat), lambda p, i, *_: (p, 0, 0))
    weight_in = pl.BlockSpec((1, width, 2 * PAIR), lambda p, i, *_: (p, 0, 0))
    shape = jax.ShapeDtypeStruct
    cat_shape = shape((total * blocks, cat * count), bf16)
    if last:
        extra, extra_specs = list(before), [part_block, weight_in]
        out_shape = [cat_shape] + [shape((count * width // 2, cat), bf16)] * 2
        out_specs = [cat_block, half_block, half_block]
    else:
        extra, extra_specs = [], []
        out_shape = [shape((total, PAIR * count), f32), cat_shape, shape((count, width, cat), f32)]
        out_specs = [part_block, cat_block, weight_block]
    return pl.pallas_call(
        functools.partial(backward_kernel, last, len(tokens), rows, blocks, step),
        grid_spec=pltpu.PrefetchScalarGridSpec(
            num_scalar_prefetch=2,
            grid=(count, items),
            in_specs=[query_block, key_block, key_block]
            + [query_block] * 3
            + [normed_block]
            + extra_specs
            + [ANYWHERE] * len(tokens),
            out_specs=out_specs,
            scratch_shapes=[
                pltpu.VMEM((width, cat), f32),
                pltpu.VMEM((2, PAIR, rows), bf16),
                pltpu.VMEM((2, PAIR, rows), bf16),
                pltpu.VMEM((PAIR, rows), f32),
            ]
            + [pltpu.VMEM((step, rows), bf16)] * 4,
        ),
        out_shape=out_shape,
        compiler_params=params(2),
        cost_estimate=cost(total * PAIR, total * PAIR),
        name="attend_back",
    )(limits, core, queries, keys, values, grads, outs, lse, normed, *extra, *tokens)


def feed_kernel(
    x_ref, mix_ref, dy_ref, w_output, w_expand, w_reduce, b_output, b_expand, b_reduce, gain, shift,
    y_ref, dmid_ref, dmix_ref, dwo_ref, dw_ref, line_ref,
    middle_ref, normed_ref, y_acc, grad_acc, reduce_acc, expand_acc,
):
    part = pl.program_id(0)

    @pl.when(part == 0)
    def _():
        mixed = mix_ref[...].astype(bf16)
        middle = x_ref[...].astype(f32) + dot_rows(mixed, w_output[...]) + b_output[...]
        middle_ref[...] = middle
        hat, _ = hat_rows(middle)
        normed_ref[...] = (hat * gain[...] + shift[...]).astype(bf16)
        y_acc[...] = middle + b_reduce[...]
        grad_acc[...] = jnp.zeros_like(grad_acc)
        line_ref[1:2, :] = column_sums(dy_ref[...].astype(f32))

    rows = x_ref.shape[0]
    step = chunk_of(rows, 272)
    chunks = rows // step
    reduce_sum, expand_sum, lines, before = None, None, None, None
    for chunk in range(chunks + 1):
        if chunk < chunks:
            place = slice(chunk * step, (chunk + 1) * step)
            normed, dy = normed_ref[place, :], dy_ref[place, :]
            upper = dot_rows(normed, w_expand[...]) + b_expand[...]
            grad_active = dot_right(dy, w_reduce[...])
        if before is not None:
            old, old_normed, old_dy, active, grad_upper = before
            y_acc[old, :] += dot_rows(active, w_reduce[...])
            grad_acc[old, :] += dot_right(grad_upper, w_expand[...])
            reduce_part = dot_left(active, old_dy)
            expand_part = dot_left(old_normed, grad_upper)
            if chunk == 1:
                reduce_acc[...], expand_acc[...] = reduce_part, expand_part
            elif chunk < chunks:
                reduce_acc[...] += reduce_part
                expand_acc[...] += expand_part
            else:
                dw_ref[0, 0] = (reduce_acc[...] + reduce_part).astype(bf16)
                dw_ref[0, 1] = (expand_acc[...] + expand_part).astype(bf16)
        if chunk < chunks:
            cumulative = 0.5 * lax.erf(upper * math.sqrt(0.5)) + 0.5
            density = jnp.exp(upper * upper * -0.5) * (1.0 / math.sqrt(2.0 * math.pi))
            active = (upper * cumulative).astype(bf16)
            grad_upper = (grad_active * (cumulative + upper * density)).astype(bf16)
            line = column_sums(grad_upper.astype(f32))
            lines = line if lines is None else lines + line
            before = place, normed, dy, active, grad_upper
    line_ref[pl.ds(4 + part, 1), :] = lines

    @pl.when(part == pl.num_programs(0) - 1)
    def _():
        y_ref[...] = y_acc[...].astype(bf16)
        grad = grad_acc[...]
        hat, inverse = hat_rows(middle_ref[...])
        line_ref[2:3, :] = column_sums(grad * hat)
        line_ref[3:4, :] = column_sums(grad)
        dmid = hat_back(grad * gain[...], hat, inverse) + dy_ref[...].astype(f32)
        dmid_ref[...] = dmid
        branch = dmid.astype(bf16)
        line_ref[0:1, :] = column_sums(branch.astype(f32))
        dwo_ref[...] = dot_left(mix_ref[...].astype(bf16), branch).astype(bf16)
        dmix_ref[...] = dot_right(branch, w_output[...]).astype(bf16)


def feed(x, mixed, dy, w_output, w_expand, w_reduce, b_output, b_expand, b_reduce, gain, shift):
    rows, width = x.shape
    hidden = w_expand.shape[1]
    parts = hidden // width
    row = whole((rows, width))
    line = whole((1, width))
    expand = pl.BlockSpec((width, width), lambda i, *_: (0, i))
    reduce = pl.BlockSpec((width, width), lambda i, *_: (i, 0))
    hidden_line = pl.BlockSpec((1, width), lambda i, *_: (0, i))
    weights = (parts, 2, width, width)
    weight_block = pl.BlockSpec((1, 2, width, width), lambda i: (i, 0, 0, 0))
    lines = (4 + parts, width)
    shape = jax.ShapeDtypeStruct
    return pl.pallas_call(
        feed_kernel,
        grid=(parts,),
        in_specs=[row, row, row, whole((width, width)), expand, reduce, line, hidden_line, line, line, line],
        out_specs=[row, row, row, whole((width, width)), weight_block, whole(lines)],
        scratch_shapes=[
            pltpu.VMEM((rows, width), f32),
            pltpu.VMEM((rows, width), bf16),
            pltpu.VMEM((rows, width), f32),
            pltpu.VMEM((rows, width), f32),
            pltpu.VMEM((width, width), f32),
            pltpu.VMEM((width, width), f32),
        ],
        out_shape=[
            shape((rows, width), bf16),
            shape((rows, width), f32),
            shape((rows, width), bf16),
            shape((width, width), bf16),
            shape(weights, bf16),
            shape(lines, f32),
        ],
        compiler_params=params(1),
        cost_estimate=cost(12 * rows * width * hidden + 6 * rows * width * width, 20 * rows * width, 2 * rows * hidden),
        name="feed",
    )(x, mixed, dy, w_output, w_expand, w_reduce, b_output, b_expand, b_reduce, gain, shift)


def gather_parts(refs, part, parts):
    blocks = []
    for ref in refs:
        pairs = ref.shape[1] // (parts * PAIR)
        for pair in range(pairs):
            start = (pair * parts + part) * PAIR
            blocks.append(ref[:, start:start + PAIR])
    return jnp.concatenate(blocks, axis=1)


def other_kernel(cats, x_ref, w_key, w_value, *rest):
    cat_refs, (send_ref, line_ref) = rest[:cats], rest[cats:]
    dk = gather_parts(cat_refs, 0, 2)
    dv = gather_parts(cat_refs, 1, 2)
    grad = dot_right(dk, w_key[...]) + dot_right(dv, w_value[...])
    send_ref[...] = grad.astype(bf16)
    hat, _ = hat_rows(x_ref[...].astype(f32))

    @pl.when(pl.program_id(0) == 0)
    def _():
        line_ref[...] = jnp.zeros_like(line_ref)

    line_ref[1:2, :] += column_sums(dv.astype(f32))
    line_ref[2:3, :] += column_sums(grad * hat)
    line_ref[3:4, :] += column_sums(grad)


def other_grads(x, cats, w_key, w_value, rows):
    total, width = x.shape
    step = chunk_of(rows, 272)
    row = pl.BlockSpec((step, width), lambda i: (i, 0))
    square = whole((width, width))
    shape = jax.ShapeDtypeStruct
    return pl.pallas_call(
        functools.partial(other_kernel, len(cats)),
        grid=(total // step,),
        in_specs=[row] + [square] * 2
        + [pl.BlockSpec((step, c.shape[1]), lambda i: (i, 0)) for c in cats],
        out_specs=[row, whole((8, width))],
        out_shape=[shape((total, width), bf16), shape((8, width), f32)],
        compiler_params=params(1),
        cost_estimate=cost(total * width, total * width),
        name="other_grads",
    )(x, w_key, w_value, *cats)


def own_kernel(cats, x_ref, recv_ref, dmid_ref, w_query, w_key, w_value, gain, line_in, *rest):
    cat_refs, (dx_ref, line_ref) = rest[:cats], rest[-2:]
    dk = gather_parts(cat_refs, 0, 3)
    dv = gather_parts(cat_refs, 1, 3)
    dq = gather_parts(cat_refs, 2, 3)
    grad = dot_right(dq, w_query[...]) + dot_right(dk, w_key[...]) + dot_right(dv, w_value[...])
    hat, inverse = hat_rows(x_ref[...].astype(f32))

    @pl.when(pl.program_id(0) == 0)
    def _():
        line_ref[...] = line_in[...]

    line_ref[0:1, :] += column_sums(dq.astype(f32))
    line_ref[1:2, :] += column_sums(dv.astype(f32))
    line_ref[2:3, :] += column_sums(grad * hat)
    line_ref[3:4, :] += column_sums(grad)
    for index in range(recv_ref.shape[0]):
        grad = grad + recv_ref[index].astype(f32)
    dx_ref[...] = hat_back(grad * gain[...], hat, inverse) + dmid_ref[...]


def own_grads(x, cats, recv, dmid, w_query, w_key, w_value, gain, lines, after):
    rows, width = x.shape
    step = chunk_of(rows, 272)
    row = pl.BlockSpec((step, width), lambda i: (i, 0))
    square = whole((width, width))
    shape = jax.ShapeDtypeStruct
    return pl.pallas_call(
        functools.partial(own_kernel, len(cats)),
        grid=(rows // step,),
        in_specs=[row, pl.BlockSpec((recv.shape[0], step, width), lambda i: (0, i, 0)), row]
        + [square] * 3
        + [whole((1, width)), whole((8, width))]
        + [pl.BlockSpec((step, c.shape[1]), lambda i: (i, 0)) for c in cats]
        + [ANYWHERE] * len(after),
        out_specs=[row, whole((8, width))],
        out_shape=[shape((rows, width), f32), shape((8, width), f32)],
        compiler_params=params(1),
        cost_estimate=cost(6 * rows * width * width, 16 * rows * width),
        name="own_grads",
    )(x, recv, dmid, w_query, w_key, w_value, gain, lines, *cats, *after)


class Slice:
    def __init__(self):
        group, rest = lax.axis_size("grp"), lax.axis_size("rest")
        batch = rest * lax.axis_size("core")
        side = 2 if rest % 2 == 0 else 1
        rest //= side
        high = 2 if rest % 2 == 0 else 1
        self.sizes = {"core": 2, "side": side, "member": group, "high": high, "low": rest // high}
        self.count = group * batch
        self.here = self.coords(lax.axis_index(ALL))

    def coords(self, linear):
        out = {}
        for name in ("member", "core", "side", "low", "high"):
            out[name] = linear % self.sizes[name]
            linear = linear // self.sizes[name]
        return out

    def linear(self, coords):
        total = 0
        for name in ("high", "low", "side", "core", "member"):
            total = total * self.sizes[name] + coords[name]
        return total

    def size(self, stage):
        return math.prod(self.sizes[name] for name in stage)

    def place(self, stage, coords=None):
        coords = self.here if coords is None else coords
        total = 0
        for name in stage:
            total = total * self.sizes[name] + coords[name]
        return total

    def send(self, array, stage, shift):
        pairs = []
        for source in range(self.count):
            coords = self.coords(source)
            place = (self.place(stage, coords) + shift) % self.size(stage)
            for name in reversed(stage):
                coords[name] = place % self.sizes[name]
                place //= self.sizes[name]
            pairs.append((source, self.linear(coords)))
        return lax.ppermute(array, ALL, pairs)

    def spread(self, parts, stage):
        return [parts[0]] + [self.send(part, stage, s) for s, part in enumerate(parts) if s > 0]

    def share(self, array, stage):
        return self.spread([array] * self.size(stage), stage)

    def origins(self, stage):
        size = self.size(stage)
        return ((self.place(stage) - jnp.arange(size)) % size).astype(jnp.int32)

    def in_order(self, parts, stage):
        if len(parts) <= 2:
            return parts
        stack = jnp.stack(parts)
        order = self.origins(stage)
        return [lax.dynamic_index_in_dim(stack, order[i], 0, False) for i in range(len(parts))]

    def total(self, array, name):
        first, *others = self.in_order(self.share(array, (name,)), (name,))
        for part in others:
            first = first + part
        return first


def behind(array, *others):
    return lax.optimization_barrier((array, *others))[0]


def cut_kernel(size, place, keep_ref, came_ref, *outs):
    rows = keep_ref.shape[0] // size
    for shift, out in enumerate(outs):
        span = pl.ds(pl.multiple_of((place[0] + shift) % size * rows, rows), rows)
        out[...] = (keep_ref[span, :].astype(f32) + came_ref[span, :].astype(f32)).astype(bf16)


def cut(keep, came, place, size):
    rows, width = keep.shape
    part = (rows // size, width)
    return pl.pallas_call(
        functools.partial(cut_kernel, size),
        grid_spec=pltpu.PrefetchScalarGridSpec(
            num_scalar_prefetch=1,
            grid=(1,),
            in_specs=[whole(keep.shape)] * 2,
            out_specs=[whole(part)] * size,
        ),
        out_shape=[jax.ShapeDtypeStruct(part, bf16)] * size,
        compiler_params=params(1),
        cost_estimate=cost(rows * width, rows * width),
        name="cut",
    )(jnp.reshape(place, (1,)).astype(jnp.int32), keep, came)


def add_up(parts):
    total = parts[0].astype(f32)
    for part in parts[1:]:
        total = total + part.astype(f32)
    return total.astype(bf16)


def feed_weights(summed):
    blocks = summed.astype(f32)
    expand = jnp.concatenate([blocks[index, 1] for index in range(summed.shape[0])], 1)
    return expand, blocks[:, 0].reshape(-1, summed.shape[-1])


def project_weights_kernel(size, places, core, *refs):
    ins, (dwq_ref, dwk_ref, dwv_ref, flat) = refs[:2 * size], refs[2 * size:]
    half = dwq_ref.shape[0] // 2
    rows = PAIRS * half // size
    for which in range(2):
        target = core[0] if which == 0 else 1 - core[0]
        for index in range(size):
            span = pl.ds(pl.multiple_of(places[index] * rows, rows), rows)
            flat[target, span, :] = ins[which * size + index][...]
    for side in range(2):
        for pair in range(PAIRS):
            block = flat[side, pair * half:(pair + 1) * half, :].astype(f32)
            down = slice(side * half, (side + 1) * half)
            span = slice(pair * PAIR, (pair + 1) * PAIR)
            dwk_ref[down, span] = block[:, :PAIR]
            dwv_ref[down, span] = block[:, PAIR:2 * PAIR]
            dwq_ref[down, span] = block[:, 2 * PAIR:]


def project_weights(places, core, own, came, width):
    shape = jax.ShapeDtypeStruct
    square = (width, width)
    size = len(own)
    rows, cat = own[0].shape
    return pl.pallas_call(
        functools.partial(project_weights_kernel, size),
        grid_spec=pltpu.PrefetchScalarGridSpec(
            num_scalar_prefetch=2,
            grid=(1,),
            in_specs=[whole((rows, cat))] * (2 * size),
            out_specs=[whole(square)] * 3,
            scratch_shapes=[pltpu.VMEM((2, size * rows, cat), bf16)],
        ),
        out_shape=[shape(square, f32)] * 3,
        compiler_params=params(1),
        cost_estimate=cost(0, 20 * width * width),
        name="project_weights",
    )(places, core, *own, *came)


def body(
    layer_input,
    lang_counts,
    w_query,
    w_key,
    w_value,
    w_output,
    w_expand,
    w_reduce,
    b_query,
    b_value,
    b_output,
    b_expand,
    b_reduce,
    gain_attn,
    shift_attn,
    gain_mlp,
    shift_mlp,
    cotangent,
):
    items, own_rows, width = layer_input.shape
    group = lax.axis_size("grp")
    me = lax.axis_index("grp")
    rows = -(-own_rows // 16) * 16
    total = items * rows
    patch_rows = VIEWS * PATCH
    shifts = range(1, group)

    def padded(array):
        if rows != own_rows:
            array = jnp.pad(array, ((0, 0), (0, rows - own_rows), (0, 0)))
        return array.reshape(total, width)

    def unpadded(array):
        return array.reshape(items, rows, width)[:, :own_rows]

    def limit_of(owner):
        return jnp.clip(patch_rows + lang_counts - owner * own_rows, 0, own_rows)

    def line(vector):
        return vector.reshape(1, -1)

    def group_shift(array, shift):
        return lax.ppermute(array, "grp", [(i, (i + shift) % group) for i in range(group)])

    def joined(parts):
        if len(parts) == 1:
            return parts[0]
        return jnp.stack([p.reshape(items, rows, width) for p in parts], 1).reshape(-1, width)

    x = padded(layer_input)
    dy = padded(cotangent)
    others = [group_shift(x, -shift) for shift in shifts]
    own_limits = limit_of(me).reshape(items, 1)
    other_limits = jnp.stack([limit_of((me + shift) % group) for shift in shifts], 1)

    weights = (w_query, w_key, w_value, line(b_query), line(b_value))
    norms = (line(gain_attn), line(shift_attn))
    normed, keys, values, queries = project(x, *norms, *weights, with_query=True)
    first = attend(own_limits, queries, keys, values, rows, 1, None)
    x_other = joined(others)
    normed_other, keys_other, values_other = project(x_other, *norms, *weights, with_query=False)
    mixed, lse = attend(other_limits, queries, keys_other, values_other, rows, group - 1, first)

    devices = Slice()
    plane = ("side", "member")
    core = jnp.reshape(devices.here["core"], (1,)).astype(jnp.int32)
    output, dmid, dmix, dwo, dw_feed, feed_lines = feed(
        x, mixed, dy, w_output, w_expand, w_reduce, line(b_output), line(b_expand), line(b_reduce),
        line(gain_mlp), line(shift_mlp),
    )
    dwo, dw_feed = lax.psum((dwo, dw_feed), ALL)

    part, cat_other, dw_other = attend_back(
        other_limits, core, queries, keys_other, values_other, dmix, mixed, lse, normed_other,
        rows, group - 1, 0, PAIRS, None, [],
    )
    send, lines = other_grads(x_other, [cat_other], w_key, w_value, rows)
    send = send.reshape(items, group - 1, rows, width)
    received = jnp.stack(
        [group_shift(send[:, shift - 1].reshape(total, width), shift) for shift in shifts]
    )
    cat, keep, give = attend_back(
        own_limits, core, queries, keys, values, dmix, mixed, lse, normed,
        rows, 1, 0, PAIRS, (part, dw_other), [],
    )
    keep, came = devices.spread([keep, give], ("core",))
    parts = devices.spread(cut(keep, came, devices.place(plane), devices.size(plane)), plane)
    dx, lines = own_grads(
        x, [cat], received, dmid, w_query, w_key, w_value, line(gain_attn), lines, parts[:1]
    )
    lines = jnp.concatenate([lines[:4], feed_lines], 0)
    value = behind(add_up(parts), dx)
    for stage, small in (("low", "core"), ("high", "member")):
        lines = devices.total(lines, small)
        value = devices.in_order(devices.share(value, (stage,)), (stage,))
        value = behind(add_up(value), lines)
    lines = devices.total(lines, "side")
    project_own = devices.share(value, plane)
    project_came = [devices.send(piece, ("core",), 1) for piece in project_own]
    lines = behind(lines, dwo, *project_own)
    lines = devices.total(devices.total(lines, "low"), "high")
    dwq, dwk, dwv = project_weights(devices.origins(plane), core, project_own, project_came, width)
    dwe, dwr = feed_weights(dw_feed)
    dwo = dwo.astype(f32)
    dbq, dbv, dgain, dshift, dbo, dbr, dgain_mlp, dshift_mlp = lines[:8]
    dbe = lines[8:].reshape(-1)
    return (
        unpadded(output),
        unpadded(dx),
        dwq, dwk, dwv, dwo, dwe, dwr,
        dbq, dbv, dbo, dbe, dbr, dgain, dshift, dgain_mlp, dshift_mlp,
    )


def solution(mesh):
    batch, group = mesh.shape["dp"], mesh.shape["grp"]
    mesh = jax.sharding.Mesh(mesh.devices.reshape(batch // 2, 2, group), ALL)
    items = ("rest", "core")
    rows = P(items, "grp", None)
    in_specs = (rows, P(items)) + (P(),) * 15 + (rows,)
    out_specs = (rows, rows) + (P(),) * 15
    return jax.shard_map(body, mesh=mesh, in_specs=in_specs, out_specs=out_specs, check_vma=False)
```

```python
import functools
import math

import jax
import jax.numpy as jnp
from jax import lax
from jax.experimental import pallas as pl
from jax.experimental.pallas import tpu as pltpu
from jax.sharding import PartitionSpec as P

HEADS = 8
HEAD_DIM = 64
VIEWS = 5
PATCH = 400
PAIR = 2 * HEAD_DIM
PAIRS = HEADS // 2
CALLS = (PAIRS // 2, PAIRS - PAIRS // 2)
TILE = 256

EPSILON = 1e-05
NEGATIVE = -1e30
SCALE = 1.0 / math.sqrt(HEAD_DIM)

bf16 = jnp.bfloat16
f32 = jnp.float32


def dot_rows(left, right):
    return lax.dot_general(
        left, right, (((1,), (0,)), ((), ())), preferred_element_type=f32
    )


def dot_left(left, right):
    return lax.dot_general(
        left, right, (((0,), (0,)), ((), ())), preferred_element_type=f32
    )


def dot_right(left, right):
    return lax.dot_general(
        left, right, (((1,), (1,)), ((), ())), preferred_element_type=f32
    )


def chunk_of(rows, limit):
    best = 16
    for size in range(16, limit + 1, 16):
        if rows % size == 0:
            best = size
    return best


def hat_rows(matrix):
    center = matrix - jnp.mean(matrix, axis=-1, keepdims=True)
    spread = jnp.mean(center * center, axis=-1, keepdims=True)
    inverse = lax.rsqrt(spread + EPSILON)
    return center * inverse, inverse


def hat_back(grad_hat, hat, inverse):
    mean_grad = jnp.mean(grad_hat, axis=-1, keepdims=True)
    mean_cross = jnp.mean(grad_hat * hat, axis=-1, keepdims=True)
    return inverse * (grad_hat - mean_grad - hat * mean_cross)


def column_sums(matrix):
    return jnp.sum(matrix, axis=0, keepdims=True)


ALL = ("rest", "core", "grp")
VMEM_MIB = 60
ANYWHERE = pl.BlockSpec(memory_space=pl.ANY)


def params(axes):
    return pltpu.CompilerParams(
        dimension_semantics=("arbitrary",) * axes, vmem_limit_bytes=VMEM_MIB << 20
    )


def cost(flops, bytes_accessed, transcendentals=0):
    return pl.CostEstimate(
        flops=int(flops), bytes_accessed=int(bytes_accessed), transcendentals=int(transcendentals)
    )


def whole(shape):
    return pl.BlockSpec(shape, lambda *_: (0,) * len(shape))


def project_kernel(with_query, x_ref, gain, shift, w_query, w_key, w_value, b_query, b_value, *outs):
    hat, _ = hat_rows(x_ref[...].astype(f32))
    normed = (hat * gain[...] + shift[...]).astype(bf16)
    if with_query:
        normed_ref, key_ref, value_ref, query_ref = outs
        query = (dot_rows(normed, w_query[...]) + b_query[...]).astype(bf16)
        query_ref[...] = (query.astype(f32) * SCALE).astype(bf16)
    else:
        normed_ref, key_ref, value_ref = outs
    normed_ref[...] = normed
    key_ref[...] = dot_rows(normed, w_key[...]).astype(bf16)
    value_ref[...] = (dot_rows(normed, w_value[...]) + b_value[...]).astype(bf16)


def project(x, gain, shift, w_query, w_key, w_value, b_query, b_value, with_query):
    rows, width = x.shape
    step = chunk_of(rows, 272)
    count = 4 if with_query else 3
    row_block = pl.BlockSpec((step, width), lambda i: (i, 0))
    return pl.pallas_call(
        functools.partial(project_kernel, with_query),
        grid=(rows // step,),
        in_specs=[row_block, whole((1, width)), whole((1, width))]
        + [whole((width, width))] * 3
        + [whole((1, width))] * 2,
        out_specs=[row_block] * count,
        out_shape=[jax.ShapeDtypeStruct((rows, width), bf16)] * count,
        compiler_params=params(1),
        cost_estimate=cost(2 * rows * width * width * (count - 1), 2 * rows * width * (count + 1)),
        name="project",
    )(x, gain, shift, w_query, w_key, w_value, b_query, b_value)


def lanes_of(shape):
    return lax.broadcasted_iota(jnp.int32, shape, 1)


def forward_kernel(
    final, rows, blocks, step, limits, q_ref, k_ref, v_ref, *rest
):
    if final:
        acc_in, top_in, sum_in, out_ref, lse_ref, kt_ref, va_ref, *score_refs = rest
    else:
        acc_out, top_out, sum_out, kt_ref, va_ref, *score_refs = rest
    item = pl.program_id(0)
    key_count = rows * blocks
    query_rows = q_ref.shape[0]
    keys = k_ref[...].astype(f32)
    values = v_ref[...].astype(f32)
    first = lanes_of((key_count, PAIR)) < HEAD_DIM
    flipped = keys.T
    row_id = lax.broadcasted_iota(jnp.int32, (PAIR, key_count), 0)
    key_id = lax.broadcasted_iota(jnp.int32, (PAIR, key_count), 1)
    bias = jnp.zeros((PAIR, key_count), f32)
    for block in range(blocks):
        here = (key_id >= block * rows + limits[item, block]) & (key_id < (block + 1) * rows)
        bias = jnp.where(here, NEGATIVE, bias)
    spare = jnp.where((row_id & (HEAD_DIM - 1)) == 0, bias, 0.0)
    kt_ref[0] = jnp.where(row_id < HEAD_DIM, flipped, spare).astype(bf16)
    kt_ref[1] = jnp.where(row_id < HEAD_DIM, spare, flipped).astype(bf16)
    va_ref[0] = jnp.where(first, values, 1.0).astype(bf16)
    va_ref[1] = jnp.where(first, 1.0, values).astype(bf16)
    lanes = lanes_of((step, PAIR))
    head_first = lanes < HEAD_DIM
    one = jnp.where((lanes & (HEAD_DIM - 1)) == 0, 1.0, 0.0)
    tiles = [slice(t, min(t + TILE, key_count)) for t in range(0, key_count, TILE)]

    def query_of(unit):
        chunk, head = divmod(unit, 2)
        query = q_ref[chunk * step:(chunk + 1) * step, :].astype(f32)
        mine = head_first if head == 0 else jnp.logical_not(head_first)
        return jnp.where(mine, query, one).astype(bf16)

    units = 2 * (query_rows // step)
    outs, tops = [], []
    for unit in range(-1, units):
        query = query_of(unit + 1) if unit + 1 < units else None
        out, best = None, None
        for tile in tiles:
            if query is not None:
                scores = dot_rows(query, kt_ref[(unit + 1) % 2, :, tile])
                score_refs[(unit + 1) % 2][:, tile] = scores
                high = jnp.max(scores, axis=1, keepdims=True)
                best = high if best is None else jnp.maximum(best, high)
            if unit >= 0:
                weights = jnp.exp(score_refs[unit % 2][:, tile] - tops[unit]).astype(bf16)
                added = dot_rows(weights, va_ref[unit % 2, tile, :])
                out = added if out is None else out + added
        if best is not None:
            tops.append(best)
        if out is not None:
            outs.append(out)
        if unit % 2 == 0 or unit < 0:
            continue
        chunk = unit // 2
        place = slice(chunk * step, (chunk + 1) * step)
        acc = jnp.where(head_first, outs[unit - 1], outs[unit])
        total = pltpu.roll(jnp.where(head_first, outs[unit], outs[unit - 1]), HEAD_DIM, 1)
        top = jnp.where(head_first, tops[unit - 1], tops[unit])
        if final:
            other_top = top_in[place, :]
            new_top = jnp.maximum(top, other_top)
            scale_here = jnp.exp(top - new_top)
            scale_there = jnp.exp(other_top - new_top)
            total = total * scale_here + sum_in[place, :] * scale_there
            acc = acc * scale_here + acc_in[place, :] * scale_there
            out_ref[place, :] = acc / total
            lse_ref[place, :] = pltpu.roll(new_top + jnp.log(total), HEAD_DIM, 1)
        else:
            acc_out[place, :] = acc
            top_out[place, :] = top
            sum_out[place, :] = total


def attend(limits, queries, keys, values, rows, blocks, before):
    total, width = queries.shape
    items = total // rows
    key_count = rows * blocks
    step = chunk_of(rows, 208)
    query_block = pl.BlockSpec((rows, PAIR), lambda i, p, *_: (i, p))
    key_block = pl.BlockSpec((key_count, PAIR), lambda i, p, *_: (i, p))
    final = before is not None
    extra = list(before) if final else []
    outs = 2 if final else 3
    return pl.pallas_call(
        functools.partial(forward_kernel, final, rows, blocks, step),
        grid_spec=pltpu.PrefetchScalarGridSpec(
            num_scalar_prefetch=1,
            grid=(items, PAIRS),
            in_specs=[query_block, key_block, key_block] + [query_block] * len(extra),
            out_specs=[query_block] * outs,
            scratch_shapes=[
                pltpu.VMEM((2, PAIR, key_count), bf16),
                pltpu.VMEM((2, key_count, PAIR), bf16),
                pltpu.VMEM((step, key_count), f32),
                pltpu.VMEM((step, key_count), f32),
            ],
        ),
        out_shape=[jax.ShapeDtypeStruct((total, width), f32)] * outs,
        compiler_params=params(2),
        cost_estimate=cost(
            16 * total * key_count * width, 12 * total * width, total * key_count * HEADS
        ),
        name="attend",
    )(limits, queries, keys, values, *extra)


def split_three(value):
    high = value.astype(bf16).astype(f32)
    rest = value - high
    middle = rest.astype(bf16).astype(f32)
    return high, middle, rest - middle


def halves(core, block):
    half = block.shape[0] // 2
    upper, lower = block[:half], block[half:]
    mine = jnp.where(core == 0, upper, lower)
    theirs = jnp.where(core == 0, lower, upper)
    return mine.astype(bf16), theirs.astype(bf16)


def backward_kernel(
    last, tokens, rows, blocks, step, limits, core,
    q_ref, k_ref, v_ref, g_ref, out_ref, lse_ref, normed_ref, *rest,
):
    if last:
        before_ref, dw_in, *rest = rest
        cat_ref, keep_ref, send_ref, dw_acc, qt_ref, gt_ref, dqt_ref, *wide = rest[tokens:]
    else:
        dq_ref, cat_ref, dw_ref, dw_acc, qt_ref, gt_ref, dqt_ref, *wide = rest[tokens:]
    prob_refs, score_refs = wide[:2], wide[2:]
    item = pl.program_id(1)
    query_rows = q_ref.shape[0]
    lanes = lanes_of((query_rows, PAIR))
    head_first = lanes < HEAD_DIM
    spare_lane = lanes & (HEAD_DIM - 1)

    def spare(parts, mask_one):
        high, middle, low = parts
        value = jnp.where(spare_lane == 0, high, 0.0)
        value = jnp.where(spare_lane == 1, middle, value)
        value = jnp.where(spare_lane == 2, low, value)
        return jnp.where(spare_lane == 3, mask_one, value)

    query = q_ref[...].astype(f32)
    grad = g_ref[...].astype(f32)
    product = grad * out_ref[...]
    delta_first = jnp.sum(jnp.where(head_first, product, 0.0), axis=1, keepdims=True)
    delta_second = jnp.sum(jnp.where(head_first, 0.0, product), axis=1, keepdims=True)
    delta = jnp.where(head_first, delta_second, delta_first)
    lse_spare = spare(split_three(-lse_ref[...]), 1.0)
    delta_spare = spare(split_three(-delta), 0.0)
    qt_ref[0] = jnp.where(head_first, query, lse_spare).T.astype(bf16)
    qt_ref[1] = jnp.where(head_first, lse_spare, query).T.astype(bf16)
    gt_ref[0] = jnp.where(head_first, grad, delta_spare).T.astype(bf16)
    gt_ref[1] = jnp.where(head_first, delta_spare, grad).T.astype(bf16)
    dqt_ref[...] = jnp.zeros_like(dqt_ref)

    key_lanes = lanes_of((step, PAIR))
    key_first = key_lanes < HEAD_DIM
    key_spare = key_lanes & (HEAD_DIM - 1)
    key_row = lax.broadcasted_iota(jnp.int32, (step, PAIR), 0)
    ones = jnp.where(key_spare < 3, 1.0, 0.0)
    per_block = rows // step
    tiles = [slice(t, min(t + TILE, query_rows)) for t in range(0, query_rows, TILE)]

    def operands(unit):
        chunk, head = divmod(unit, 2)
        place = slice(chunk * step, (chunk + 1) * step)
        block = chunk // per_block
        limit = limits[item, block] - (chunk - block * per_block) * step
        bias = jnp.where(key_row >= limit, NEGATIVE, 0.0)
        key = k_ref[place, :].astype(f32)
        value = v_ref[place, :].astype(f32)
        mine = key_first if head == 0 else jnp.logical_not(key_first)
        key_head = jnp.where(mine, key, jnp.where(key_spare == 3, bias, ones)).astype(bf16)
        value_head = jnp.where(mine, value, ones).astype(bf16)
        half = key.T[head * HEAD_DIM:(head + 1) * HEAD_DIM].astype(bf16)
        return key_head, value_head, half

    units = 2 * blocks * per_block
    dks, dvs, half = [], [], None
    for unit in range(-1, units):
        more = unit + 1 < units
        if more:
            key_head, value_head, next_half = operands(unit + 1)
            which = (unit + 1) % 2
        dk, dv = None, None
        for tile in tiles:
            if more:
                probs = jnp.exp(dot_rows(key_head, qt_ref[which, :, tile]))
                grad_probs = dot_rows(value_head, gt_ref[which, :, tile])
                prob_refs[which][:, tile] = probs.astype(bf16)
                score_refs[which][:, tile] = (probs * grad_probs).astype(bf16)
            if unit >= 0:
                grad_scores = score_refs[unit % 2][:, tile]
                dv_part = dot_rows(prob_refs[unit % 2][:, tile], g_ref[tile, :])
                dk_part = dot_rows(grad_scores, q_ref[tile, :])
                dv = dv_part if dv is None else dv + dv_part
                dk = dk_part if dk is None else dk + dk_part
                own = slice(unit % 2 * HEAD_DIM, (unit % 2 + 1) * HEAD_DIM)
                dqt_ref[own, tile] += dot_rows(half, grad_scores)
        half = next_half if more else None
        if unit >= 0:
            dks.append(dk)
            dvs.append(dv)
        if unit >= 0 and unit % 2 == 1:
            place = slice(unit // 2 * step, (unit // 2 + 1) * step)
            cat_ref[place, :PAIR] = jnp.where(key_first, dks[-2], dks[-1]).astype(bf16)
            cat_ref[place, PAIR:2 * PAIR] = jnp.where(key_first, dvs[-2], dvs[-1]).astype(bf16)

    result = dqt_ref[...].T
    if last:
        cat_ref[:, 2 * PAIR:] = ((result + before_ref[...]) * SCALE).astype(bf16)
    else:
        dq_ref[...] = result
    added = dot_left(normed_ref[...], cat_ref[...])
    items = pl.num_programs(1)

    @pl.when(item == 0)
    def _():
        dw_acc[...] = added
        if last:
            dw_acc[:, :2 * PAIR] += dw_in[0]

    @pl.when(item > 0)
    def _():
        dw_acc[...] += added

    @pl.when(item == items - 1)
    def _():
        if last:
            keep_ref[...], send_ref[...] = halves(core[0], dw_acc[...])
        else:
            dw_ref[0] = dw_acc[...]


def attend_back(
    limits, core, queries, keys, values, grads, outs, lse, normed, rows, blocks, first, count, before,
    tokens,
):
    total, width = queries.shape
    items = total // rows
    key_count = rows * blocks
    step = chunk_of(rows, 208)
    last = before is not None
    cat = (3 if last else 2) * PAIR
    query_block = pl.BlockSpec((rows, PAIR), lambda p, i, *_: (i, first + p))
    key_block = pl.BlockSpec((key_count, PAIR), lambda p, i, *_: (i, first + p))
    normed_block = pl.BlockSpec((key_count, width), lambda p, i, *_: (i, 0))
    part_block = pl.BlockSpec((rows, PAIR), lambda p, i, *_: (i, p))
    cat_block = pl.BlockSpec((key_count, cat), lambda p, i, *_: (i, p))
    half_block = pl.BlockSpec((width // 2, cat), lambda p, i, *_: (p, 0))
    weight_block = pl.BlockSpec((1, width, cat), lambda p, i, *_: (p, 0, 0))
    weight_in = pl.BlockSpec((1, width, 2 * PAIR), lambda p, i, *_: (p, 0, 0))
    shape = jax.ShapeDtypeStruct
    cat_shape = shape((total * blocks, cat * count), bf16)
    if last:
        extra, extra_specs = list(before), [part_block, weight_in]
        out_shape = [cat_shape] + [shape((count * width // 2, cat), bf16)] * 2
        out_specs = [cat_block, half_block, half_block]
    else:
        extra, extra_specs = [], []
        out_shape = [shape((total, PAIR * count), f32), cat_shape, shape((count, width, cat), f32)]
        out_specs = [part_block, cat_block, weight_block]
    return pl.pallas_call(
        functools.partial(backward_kernel, last, len(tokens), rows, blocks, step),
        grid_spec=pltpu.PrefetchScalarGridSpec(
            num_scalar_prefetch=2,
            grid=(count, items),
            in_specs=[query_block, key_block, key_block]
            + [query_block] * 3
            + [normed_block]
            + extra_specs
            + [ANYWHERE] * len(tokens),
            out_specs=out_specs,
            scratch_shapes=[
                pltpu.VMEM((width, cat), f32),
                pltpu.VMEM((2, PAIR, rows), bf16),
                pltpu.VMEM((2, PAIR, rows), bf16),
                pltpu.VMEM((PAIR, rows), f32),
            ]
            + [pltpu.VMEM((step, rows), bf16)] * 4,
        ),
        out_shape=out_shape,
        compiler_params=params(2),
        cost_estimate=cost(
            40 * total * key_count * PAIR * count,
            16 * total * PAIR * count,
            2 * total * key_count * count,
        ),
        name="attend_back",
    )(limits, core, queries, keys, values, grads, outs, lse, normed, *extra, *tokens)


def feed_kernel(
    core, x_ref, mix_ref, dy_ref, w_output, w_expand, w_reduce, b_output, b_expand, b_reduce, gain, shift,
    y_ref, dmid_ref, dmix_ref, keep_ref, send_ref, line_ref,
    middle_ref, normed_ref, y_acc, grad_acc,
):
    part = pl.program_id(0)

    def put(index, block):
        keep_ref[index], send_ref[index] = halves(core[0], block)

    @pl.when(part == 0)
    def _():
        mixed = mix_ref[...].astype(bf16)
        middle = x_ref[...].astype(f32) + dot_rows(mixed, w_output[...]) + b_output[...]
        middle_ref[...] = middle
        hat, _ = hat_rows(middle)
        normed_ref[...] = (hat * gain[...] + shift[...]).astype(bf16)
        y_acc[...] = middle + b_reduce[...]
        grad_acc[...] = jnp.zeros_like(grad_acc)
        line_ref[1:2, :] = column_sums(dy_ref[...].astype(f32))

    normed = normed_ref[...]
    upper = dot_rows(normed, w_expand[...]) + b_expand[...]
    cumulative = 0.5 * lax.erf(upper * math.sqrt(0.5)) + 0.5
    density = jnp.exp(upper * upper * -0.5) * (1.0 / math.sqrt(2.0 * math.pi))
    active = (upper * cumulative).astype(bf16)
    slope = cumulative + upper * density
    y_acc[...] += dot_rows(active, w_reduce[...])
    put(1 + 2 * part, dot_left(active, dy_ref[...]))
    grad_upper = (dot_right(dy_ref[...], w_reduce[...]) * slope).astype(bf16)
    line_ref[pl.ds(4 + part, 1), :] = column_sums(grad_upper.astype(f32))
    put(2 + 2 * part, dot_left(normed, grad_upper))
    grad_acc[...] += dot_right(grad_upper, w_expand[...])

    @pl.when(part == pl.num_programs(0) - 1)
    def _():
        y_ref[...] = y_acc[...].astype(bf16)
        grad = grad_acc[...]
        hat, inverse = hat_rows(middle_ref[...])
        line_ref[2:3, :] = column_sums(grad * hat)
        line_ref[3:4, :] = column_sums(grad)
        dmid = hat_back(grad * gain[...], hat, inverse) + dy_ref[...].astype(f32)
        dmid_ref[...] = dmid
        branch = dmid.astype(bf16)
        line_ref[0:1, :] = column_sums(branch.astype(f32))
        put(0, dot_left(mix_ref[...].astype(bf16), branch))
        dmix_ref[...] = dot_right(branch, w_output[...]).astype(bf16)


def feed(core, x, mixed, dy, w_output, w_expand, w_reduce, b_output, b_expand, b_reduce, gain, shift):
    rows, width = x.shape
    hidden = w_expand.shape[1]
    parts = hidden // width
    row = whole((rows, width))
    line = whole((1, width))
    expand = pl.BlockSpec((width, width), lambda i, *_: (0, i))
    reduce = pl.BlockSpec((width, width), lambda i, *_: (i, 0))
    hidden_line = pl.BlockSpec((1, width), lambda i, *_: (0, i))
    weights = (1 + 2 * parts, width // 2, width)
    lines = (4 + parts, width)
    shape = jax.ShapeDtypeStruct
    return pl.pallas_call(
        feed_kernel,
        grid_spec=pltpu.PrefetchScalarGridSpec(
            num_scalar_prefetch=1,
            grid=(parts,),
            in_specs=[row, row, row, whole((width, width)), expand, reduce, line, hidden_line, line, line, line],
            out_specs=[row, row, row, whole(weights), whole(weights), whole(lines)],
            scratch_shapes=[
                pltpu.VMEM((rows, width), f32),
                pltpu.VMEM((rows, width), bf16),
                pltpu.VMEM((rows, width), f32),
                pltpu.VMEM((rows, width), f32),
            ],
        ),
        out_shape=[
            shape((rows, width), bf16),
            shape((rows, width), f32),
            shape((rows, width), bf16),
            shape(weights, bf16),
            shape(weights, bf16),
            shape(lines, f32),
        ],
        compiler_params=params(1),
        cost_estimate=cost(12 * rows * width * hidden + 6 * rows * width * width, 20 * rows * width, 2 * rows * hidden),
        name="feed",
    )(core, x, mixed, dy, w_output, w_expand, w_reduce, b_output, b_expand, b_reduce, gain, shift)


def gather_parts(refs, part, parts):
    blocks = []
    for ref in refs:
        pairs = ref.shape[1] // (parts * PAIR)
        for pair in range(pairs):
            start = (pair * parts + part) * PAIR
            blocks.append(ref[:, start:start + PAIR])
    return jnp.concatenate(blocks, axis=1)


def other_kernel(cats, x_ref, w_key, w_value, *rest):
    cat_refs, (send_ref, line_ref) = rest[:cats], rest[cats:]
    dk = gather_parts(cat_refs, 0, 2)
    dv = gather_parts(cat_refs, 1, 2)
    grad = dot_right(dk, w_key[...]) + dot_right(dv, w_value[...])
    send_ref[...] = grad.astype(bf16)
    hat, _ = hat_rows(x_ref[...].astype(f32))

    @pl.when(pl.program_id(0) == 0)
    def _():
        line_ref[...] = jnp.zeros_like(line_ref)

    line_ref[1:2, :] += column_sums(dv.astype(f32))
    line_ref[2:3, :] += column_sums(grad * hat)
    line_ref[3:4, :] += column_sums(grad)


def other_grads(x, cats, w_key, w_value, rows):
    total, width = x.shape
    step = chunk_of(rows, 272)
    row = pl.BlockSpec((step, width), lambda i: (i, 0))
    square = whole((width, width))
    shape = jax.ShapeDtypeStruct
    return pl.pallas_call(
        functools.partial(other_kernel, len(cats)),
        grid=(total // step,),
        in_specs=[row] + [square] * 2
        + [pl.BlockSpec((step, c.shape[1]), lambda i: (i, 0)) for c in cats],
        out_specs=[row, whole((8, width))],
        out_shape=[shape((total, width), bf16), shape((8, width), f32)],
        compiler_params=params(1),
        cost_estimate=cost(4 * total * width * width, 8 * total * width),
        name="other_grads",
    )(x, w_key, w_value, *cats)


def own_kernel(cats, x_ref, recv_ref, dmid_ref, w_query, w_key, w_value, gain, line_in, *rest):
    cat_refs, (dx_ref, line_ref) = rest[:cats], rest[-2:]
    dk = gather_parts(cat_refs, 0, 3)
    dv = gather_parts(cat_refs, 1, 3)
    dq = gather_parts(cat_refs, 2, 3)
    grad = dot_right(dq, w_query[...]) + dot_right(dk, w_key[...]) + dot_right(dv, w_value[...])
    hat, inverse = hat_rows(x_ref[...].astype(f32))

    @pl.when(pl.program_id(0) == 0)
    def _():
        line_ref[...] = line_in[...]

    line_ref[0:1, :] += column_sums(dq.astype(f32))
    line_ref[1:2, :] += column_sums(dv.astype(f32))
    line_ref[2:3, :] += column_sums(grad * hat)
    line_ref[3:4, :] += column_sums(grad)
    for index in range(recv_ref.shape[0]):
        grad = grad + recv_ref[index].astype(f32)
    dx_ref[...] = hat_back(grad * gain[...], hat, inverse) + dmid_ref[...]


def own_grads(x, cats, recv, dmid, w_query, w_key, w_value, gain, lines, after):
    rows, width = x.shape
    step = chunk_of(rows, 272)
    row = pl.BlockSpec((step, width), lambda i: (i, 0))
    square = whole((width, width))
    shape = jax.ShapeDtypeStruct
    return pl.pallas_call(
        functools.partial(own_kernel, len(cats)),
        grid=(rows // step,),
        in_specs=[row, pl.BlockSpec((recv.shape[0], step, width), lambda i: (0, i, 0)), row]
        + [square] * 3
        + [whole((1, width)), whole((8, width))]
        + [pl.BlockSpec((step, c.shape[1]), lambda i: (i, 0)) for c in cats]
        + [ANYWHERE] * len(after),
        out_specs=[row, whole((8, width))],
        out_shape=[shape((rows, width), f32), shape((8, width), f32)],
        compiler_params=params(1),
        cost_estimate=cost(6 * rows * width * width, 16 * rows * width),
        name="own_grads",
    )(x, recv, dmid, w_query, w_key, w_value, gain, lines, *cats, *after)


class Slice:
    def __init__(self):
        group, rest = lax.axis_size("grp"), lax.axis_size("rest")
        batch = rest * lax.axis_size("core")
        side = 2 if rest % 2 == 0 else 1
        rest //= side
        high = 2 if rest % 2 == 0 else 1
        self.sizes = {"core": 2, "side": side, "member": group, "high": high, "low": rest // high}
        self.count = group * batch
        self.here = self.coords(lax.axis_index(ALL))

    def coords(self, linear):
        out = {}
        for name in ("member", "core", "side", "low", "high"):
            out[name] = linear % self.sizes[name]
            linear = linear // self.sizes[name]
        return out

    def linear(self, coords):
        total = 0
        for name in ("high", "low", "side", "core", "member"):
            total = total * self.sizes[name] + coords[name]
        return total

    def size(self, stage):
        return math.prod(self.sizes[name] for name in stage)

    def place(self, stage, coords=None):
        coords = self.here if coords is None else coords
        total = 0
        for name in stage:
            total = total * self.sizes[name] + coords[name]
        return total

    def send(self, array, stage, shift):
        pairs = []
        for source in range(self.count):
            coords = self.coords(source)
            place = (self.place(stage, coords) + shift) % self.size(stage)
            for name in reversed(stage):
                coords[name] = place % self.sizes[name]
                place //= self.sizes[name]
            pairs.append((source, self.linear(coords)))
        return lax.ppermute(array, ALL, pairs)

    def spread(self, parts, stage):
        return [parts[0]] + [self.send(part, stage, s) for s, part in enumerate(parts) if s > 0]

    def share(self, array, stage):
        return self.spread([array] * self.size(stage), stage)

    def origins(self, stage):
        size = self.size(stage)
        return ((self.place(stage) - jnp.arange(size)) % size).astype(jnp.int32)

    def in_order(self, parts, stage):
        if len(parts) <= 2:
            return parts
        stack = jnp.stack(parts)
        order = self.origins(stage)
        return [lax.dynamic_index_in_dim(stack, order[i], 0, False) for i in range(len(parts))]

    def total(self, array, name):
        first, *others = self.in_order(self.share(array, (name,)), (name,))
        for part in others:
            first = first + part
        return first


def behind(array, *others):
    return lax.optimization_barrier((array, *others))[0]


def cut_kernel(size, groups, place, *refs):
    ins, outs = refs[:2 * groups], refs[len(refs) - size:]
    for shift, out in enumerate(outs):

        @pl.when(pl.program_id(0) == shift)
        def _():
            start = 0
            for index in range(groups):
                keep, came = ins[2 * index], ins[2 * index + 1]
                rows = keep.shape[0]
                total = keep[...].astype(f32) + came[...].astype(f32)
                out[start:start + rows, :] = total.astype(bf16)
                start += rows


def cut(pairs, place, size, after=()):
    arrays = [array for pair in pairs for array in pair]
    width = arrays[0].shape[1]
    part = (sum(keep.shape[0] for keep, _ in pairs) // size, width)
    return pl.pallas_call(
        functools.partial(cut_kernel, size, len(pairs)),
        grid_spec=pltpu.PrefetchScalarGridSpec(
            num_scalar_prefetch=1,
            grid=(size,),
            in_specs=[
                pl.BlockSpec((a.shape[0] // size, width), lambda s, place: ((place[0] + s) % size, 0))
                for a in arrays
            ]
            + [ANYWHERE] * len(after),
            out_specs=[whole(part)] * size,
        ),
        out_shape=[jax.ShapeDtypeStruct(part, bf16)] * size,
        compiler_params=params(1),
        cost_estimate=cost(size * part[0] * width, 6 * size * part[0] * width),
        name="cut",
    )(jnp.reshape(place, (1,)).astype(jnp.int32), *arrays, *after)


def add_up(parts):
    total = parts[0].astype(f32)
    for part in parts[1:]:
        total = total + part.astype(f32)
    return total.astype(bf16)


def place_pieces(places, core, pieces, flat):
    size = len(pieces) // 2
    for which in range(2):
        target = core[0] if which == 0 else 1 - core[0]
        for index in range(size):
            piece = pieces[which * size + index]
            rows = piece.shape[0]
            span = pl.ds(pl.multiple_of(places[index] * rows, rows), rows)
            flat[target, span, :] = piece[...]


def feed_weights_kernel(places, core, *refs):
    pieces, (dwo_ref, dwe_ref, dwr_ref, flat) = refs[:-4], refs[-4:]
    place_pieces(places, core, pieces, flat)
    width = dwo_ref.shape[0]
    half = width // 2
    for side in range(2):
        rows = slice(side * half, (side + 1) * half)
        dwo_ref[rows, :] = flat[side, :half, :].astype(f32)
        for part in range(dwr_ref.shape[0] // width):
            start = (1 + 2 * part) * half
            down = slice(part * width + side * half, part * width + (side + 1) * half)
            across = slice(part * width, (part + 1) * width)
            dwr_ref[down, :] = flat[side, start:start + half, :].astype(f32)
            dwe_ref[rows, across] = flat[side, start + half:start + width, :].astype(f32)


def feed_weights(places, core, own, came, hidden):
    rows, width = own[0].shape
    shapes = [(width, width), (width, hidden), (hidden, width)]
    return pl.pallas_call(
        feed_weights_kernel,
        grid_spec=pltpu.PrefetchScalarGridSpec(
            num_scalar_prefetch=2,
            grid=(1,),
            in_specs=[whole((rows, width))] * (2 * len(own)),
            out_specs=[whole(s) for s in shapes],
            scratch_shapes=[pltpu.VMEM((2, len(own) * rows, width), bf16)],
        ),
        out_shape=[jax.ShapeDtypeStruct(s, f32) for s in shapes],
        compiler_params=params(1),
        cost_estimate=cost(0, 12 * len(own) * rows * width),
        name="feed_weights",
    )(places, core, *own, *came)


def project_weights_kernel(calls, places, core, *refs):
    pieces, (dwq_ref, dwk_ref, dwv_ref, flat) = refs[:-4], refs[-4:]
    half = dwq_ref.shape[0] // 2
    place_pieces(places, core, pieces, flat)
    size = len(pieces) // 2
    share = half // size
    rows = pieces[0].shape[0]
    for side in range(2):
        for index in range(size):
            at = index * rows
            first = 0
            for count in calls:
                for part in range(count):
                    row = (index * count + part) * share
                    pair, down = first + row // half, side * half + row % half
                    block = flat[side, at:at + share, :].astype(f32)
                    place, span = slice(down, down + share), slice(pair * PAIR, (pair + 1) * PAIR)
                    dwk_ref[place, span] = block[:, :PAIR]
                    dwv_ref[place, span] = block[:, PAIR:2 * PAIR]
                    dwq_ref[place, span] = block[:, 2 * PAIR:]
                    at += share
                first += count


def project_weights(places, core, own, came, width, calls):
    square = (width, width)
    rows, cat = own[0].shape
    return pl.pallas_call(
        functools.partial(project_weights_kernel, calls),
        grid_spec=pltpu.PrefetchScalarGridSpec(
            num_scalar_prefetch=2,
            grid=(1,),
            in_specs=[whole((rows, cat))] * (2 * len(own)),
            out_specs=[whole(square)] * 3,
            scratch_shapes=[pltpu.VMEM((2, len(own) * rows, cat), bf16)],
        ),
        out_shape=[jax.ShapeDtypeStruct(square, f32)] * 3,
        compiler_params=params(1),
        cost_estimate=cost(0, 20 * width * width),
        name="project_weights",
    )(places, core, *own, *came)


def body(
    layer_input,
    lang_counts,
    w_query,
    w_key,
    w_value,
    w_output,
    w_expand,
    w_reduce,
    b_query,
    b_value,
    b_output,
    b_expand,
    b_reduce,
    gain_attn,
    shift_attn,
    gain_mlp,
    shift_mlp,
    cotangent,
):
    items, own_rows, width = layer_input.shape
    group = lax.axis_size("grp")
    me = lax.axis_index("grp")
    rows = -(-own_rows // 16) * 16
    total = items * rows
    patch_rows = VIEWS * PATCH
    shifts = range(1, group)

    def padded(array):
        if rows != own_rows:
            array = jnp.pad(array, ((0, 0), (0, rows - own_rows), (0, 0)))
        return array.reshape(total, width)

    def unpadded(array):
        return array.reshape(items, rows, width)[:, :own_rows]

    def limit_of(owner):
        return jnp.clip(patch_rows + lang_counts - owner * own_rows, 0, own_rows)

    def line(vector):
        return vector.reshape(1, -1)

    def group_shift(array, shift):
        return lax.ppermute(array, "grp", [(i, (i + shift) % group) for i in range(group)])

    def joined(parts):
        if len(parts) == 1:
            return parts[0]
        return jnp.stack([p.reshape(items, rows, width) for p in parts], 1).reshape(-1, width)

    x = padded(layer_input)
    dy = padded(cotangent)
    others = [group_shift(x, -shift) for shift in shifts]
    own_limits = limit_of(me).reshape(items, 1)
    other_limits = jnp.stack([limit_of((me + shift) % group) for shift in shifts], 1)

    weights = (w_query, w_key, w_value, line(b_query), line(b_value))
    norms = (line(gain_attn), line(shift_attn))
    normed, keys, values, queries = project(x, *norms, *weights, with_query=True)
    first = attend(own_limits, queries, keys, values, rows, 1, None)
    x_other = joined(others)
    normed_other, keys_other, values_other = project(x_other, *norms, *weights, with_query=False)
    mixed, lse = attend(other_limits, queries, keys_other, values_other, rows, group - 1, first)

    devices = Slice()
    plane = ("side", "member")
    core = jnp.reshape(devices.here["core"], (1,)).astype(jnp.int32)
    output, dmid, dmix, keep, give, feed_lines = feed(
        core, x, mixed, dy, w_output, w_expand, w_reduce, line(b_output), line(b_expand), line(b_reduce),
        line(gain_mlp), line(shift_mlp),
    )
    plane_place, plane_size = devices.place(plane), devices.size(plane)

    def summed(value, stage):
        return add_up(devices.in_order(devices.share(value, (stage,)), (stage,)))

    feed_pair = devices.spread([keep.reshape(-1, width), give.reshape(-1, width)], ("core",))

    def back_other(start, count, tokens):
        return attend_back(
            other_limits, core, queries, keys_other, values_other, dmix, mixed, lse, normed_other,
            rows, group - 1, start, count, None, tokens,
        )

    def back_own(start, count, before, tokens):
        return attend_back(
            own_limits, core, queries, keys, values, dmix, mixed, lse, normed,
            rows, 1, start, count, before, tokens,
        )

    (one, two) = CALLS
    first_part, first_cat, first_dw = back_other(0, one, [])
    parts = cut([feed_pair], plane_place, plane_size, [first_cat])
    second_part, second_cat, second_dw = back_other(one, two, parts[:1])
    parts = devices.spread(parts, plane)
    send, lines = other_grads(x_other, [first_cat, second_cat], w_key, w_value, rows)
    feed_sum = behind(add_up(parts), send)
    send = send.reshape(items, group - 1, rows, width)
    received = jnp.stack(
        [group_shift(send[:, shift - 1].reshape(total, width), shift) for shift in shifts]
    )
    first_cat, *first_pair = back_own(0, one, (first_part, first_dw), [feed_sum])
    feed_sum = behind(summed(feed_sum, "low"), first_cat)
    second_cat, *second_pair = back_own(one, two, (second_part, second_dw), [feed_sum])
    pairs = [devices.spread(pair, ("core",)) for pair in (first_pair, second_pair)]
    parts = devices.spread(cut(pairs, plane_place, plane_size), plane)
    dx, lines = own_grads(
        x, [first_cat, second_cat], received, dmid, w_query, w_key, w_value, line(gain_attn), lines, parts[:1]
    )
    feed_sum = behind(summed(feed_sum, "high"), dx)
    value = behind(add_up(parts), feed_sum)
    feed_own = devices.share(feed_sum, plane)
    lines = jnp.concatenate([lines[:4], feed_lines], 0)
    lines = devices.total(lines, "core")
    value = behind(summed(value, "low"), lines)
    lines = devices.total(lines, "member")
    value = behind(summed(value, "high"), lines, *feed_own)
    project_own = devices.share(value, plane)
    feed_came = [devices.send(piece, ("core",), 1) for piece in feed_own]
    lines = devices.total(lines, "side")
    places = devices.origins(plane)
    dwo, dwe, dwr = feed_weights(places, core, feed_own, feed_came, w_expand.shape[1])
    project_own = [project_own[0]] + [behind(piece, dwo) for piece in project_own[1:]]
    project_came = [devices.send(piece, ("core",), 1) for piece in project_own]
    lines = devices.total(devices.total(behind(lines, *project_own), "low"), "high")
    dwq, dwk, dwv = project_weights(places, core, project_own, project_came, width, CALLS)
    dbq, dbv, dgain, dshift, dbo, dbr, dgain_mlp, dshift_mlp = lines[:8]
    dbe = lines[8:].reshape(-1)
    return (
        unpadded(output),
        unpadded(dx),
        dwq, dwk, dwv, dwo, dwe, dwr,
        dbq, dbv, dbo, dbe, dbr, dgain, dshift, dgain_mlp, dshift_mlp,
    )


def solution(mesh):
    batch, group = mesh.shape["dp"], mesh.shape["grp"]
    mesh = jax.sharding.Mesh(mesh.devices.reshape(batch // 2, 2, group), ALL)
    items = ("rest", "core")
    rows = P(items, "grp", None)
    in_specs = (rows, P(items)) + (P(),) * 15 + (rows,)
    out_specs = (rows, rows) + (P(),) * 15
    return jax.shard_map(body, mesh=mesh, in_specs=in_specs, out_specs=out_specs, check_vma=False)
```

```python
import functools
import math

import jax
import jax.numpy as jnp
from jax import lax
from jax.experimental import pallas as pl
from jax.experimental.pallas import tpu as pltpu
from jax.sharding import PartitionSpec as P

HEADS = 8
HEAD_DIM = 64
VIEWS = 5
PATCH = 400
PAIR = 2 * HEAD_DIM
PAIRS = HEADS // 2
TILE = 256

EPSILON = 1e-05
NEGATIVE = -1e30
SCALE = 1.0 / math.sqrt(HEAD_DIM)

bf16 = jnp.bfloat16
f32 = jnp.float32


def dot_rows(left, right):
    return lax.dot_general(
        left, right, (((1,), (0,)), ((), ())), preferred_element_type=f32
    )


def dot_left(left, right):
    return lax.dot_general(
        left, right, (((0,), (0,)), ((), ())), preferred_element_type=f32
    )


def dot_right(left, right):
    return lax.dot_general(
        left, right, (((1,), (1,)), ((), ())), preferred_element_type=f32
    )


def chunk_of(rows, limit):
    best = 16
    for size in range(16, limit + 1, 16):
        if rows % size == 0:
            best = size
    return best


def hat_rows(matrix):
    center = matrix - jnp.mean(matrix, axis=-1, keepdims=True)
    spread = jnp.mean(center * center, axis=-1, keepdims=True)
    inverse = lax.rsqrt(spread + EPSILON)
    return center * inverse, inverse


def hat_back(grad_hat, hat, inverse):
    mean_grad = jnp.mean(grad_hat, axis=-1, keepdims=True)
    mean_cross = jnp.mean(grad_hat * hat, axis=-1, keepdims=True)
    return inverse * (grad_hat - mean_grad - hat * mean_cross)


def column_sums(matrix):
    return jnp.sum(matrix, axis=0, keepdims=True)


ALL = ("rest", "core", "grp")
VMEM_MIB = 60
ANYWHERE = pl.BlockSpec(memory_space=pl.ANY)


def params(axes):
    return pltpu.CompilerParams(
        dimension_semantics=("arbitrary",) * axes, vmem_limit_bytes=VMEM_MIB << 20
    )


def cost(flops, bytes_accessed, transcendentals=0):
    return pl.CostEstimate(
        flops=int(flops), bytes_accessed=int(bytes_accessed), transcendentals=int(transcendentals)
    )


def whole(shape):
    return pl.BlockSpec(shape, lambda *_: (0,) * len(shape))


def project_kernel(with_query, x_ref, gain, shift, w_query, w_key, w_value, b_query, b_value, *outs):
    hat, _ = hat_rows(x_ref[...].astype(f32))
    normed = (hat * gain[...] + shift[...]).astype(bf16)
    if with_query:
        hat_ref, key_ref, value_ref, query_ref = outs
        query = (dot_rows(normed, w_query[...]) + b_query[...]).astype(bf16)
        query_ref[...] = (query.astype(f32) * SCALE).astype(bf16)
    else:
        hat_ref, key_ref, value_ref = outs
    hat_ref[...] = hat.astype(bf16)
    key_ref[...] = dot_rows(normed, w_key[...]).astype(bf16)
    value_ref[...] = (dot_rows(normed, w_value[...]) + b_value[...]).astype(bf16)


def project(x, gain, shift, w_query, w_key, w_value, b_query, b_value, with_query):
    rows, width = x.shape
    step = chunk_of(rows, 272)
    count = 4 if with_query else 3
    row_block = pl.BlockSpec((step, width), lambda i: (i, 0))
    return pl.pallas_call(
        functools.partial(project_kernel, with_query),
        grid=(rows // step,),
        in_specs=[row_block, whole((1, width)), whole((1, width))]
        + [whole((width, width))] * 3
        + [whole((1, width))] * 2,
        out_specs=[row_block] * count,
        out_shape=[jax.ShapeDtypeStruct((rows, width), bf16)] * count,
        compiler_params=params(1),
        cost_estimate=cost(2 * rows * width * width * (count - 1), 2 * rows * width * (count + 1)),
        name="project",
    )(x, gain, shift, w_query, w_key, w_value, b_query, b_value)


def lanes_of(shape):
    return lax.broadcasted_iota(jnp.int32, shape, 1)


def forward_kernel(
    final, rows, blocks, step, limits, q_ref, k_ref, v_ref, *rest
):
    if final:
        acc_in, top_in, sum_in, out_ref, lse_ref, kt_ref, va_ref, *score_refs = rest
    else:
        acc_out, top_out, sum_out, kt_ref, va_ref, *score_refs = rest
    item = pl.program_id(0)
    key_count = rows * blocks
    query_rows = q_ref.shape[0]
    keys = k_ref[...].astype(f32)
    values = v_ref[...].astype(f32)
    first = lanes_of((key_count, PAIR)) < HEAD_DIM
    flipped = keys.T
    row_id = lax.broadcasted_iota(jnp.int32, (PAIR, key_count), 0)
    key_id = lax.broadcasted_iota(jnp.int32, (PAIR, key_count), 1)
    bias = jnp.zeros((PAIR, key_count), f32)
    for block in range(blocks):
        here = (key_id >= block * rows + limits[item, block]) & (key_id < (block + 1) * rows)
        bias = jnp.where(here, NEGATIVE, bias)
    spare = jnp.where((row_id & (HEAD_DIM - 1)) == 0, bias, 0.0)
    kt_ref[0] = jnp.where(row_id < HEAD_DIM, flipped, spare).astype(bf16)
    kt_ref[1] = jnp.where(row_id < HEAD_DIM, spare, flipped).astype(bf16)
    va_ref[0] = jnp.where(first, values, 1.0).astype(bf16)
    va_ref[1] = jnp.where(first, 1.0, values).astype(bf16)
    lanes = lanes_of((step, PAIR))
    head_first = lanes < HEAD_DIM
    one = jnp.where((lanes & (HEAD_DIM - 1)) == 0, 1.0, 0.0)
    tiles = [slice(t, min(t + TILE, key_count)) for t in range(0, key_count, TILE)]

    def query_of(unit):
        chunk, head = divmod(unit, 2)
        query = q_ref[chunk * step:(chunk + 1) * step, :].astype(f32)
        mine = head_first if head == 0 else jnp.logical_not(head_first)
        return jnp.where(mine, query, one).astype(bf16)

    units = 2 * (query_rows // step)
    outs, tops = [], []
    for unit in range(-1, units):
        query = query_of(unit + 1) if unit + 1 < units else None
        out, best = None, None
        for tile in tiles:
            if query is not None:
                scores = dot_rows(query, kt_ref[(unit + 1) % 2, :, tile])
                score_refs[(unit + 1) % 2][:, tile] = scores
                high = jnp.max(scores, axis=1, keepdims=True)
                best = high if best is None else jnp.maximum(best, high)
            if unit >= 0:
                weights = jnp.exp(score_refs[unit % 2][:, tile] - tops[unit]).astype(bf16)
                added = dot_rows(weights, va_ref[unit % 2, tile, :])
                out = added if out is None else out + added
        if best is not None:
            tops.append(best)
        if out is not None:
            outs.append(out)
        if unit % 2 == 0 or unit < 0:
            continue
        chunk = unit // 2
        place = slice(chunk * step, (chunk + 1) * step)
        acc = jnp.where(head_first, outs[unit - 1], outs[unit])
        total = pltpu.roll(jnp.where(head_first, outs[unit], outs[unit - 1]), HEAD_DIM, 1)
        top = jnp.where(head_first, tops[unit - 1], tops[unit])
        if final:
            other_top = top_in[place, :]
            new_top = jnp.maximum(top, other_top)
            scale_here = jnp.exp(top - new_top)
            scale_there = jnp.exp(other_top - new_top)
            total = total * scale_here + sum_in[place, :] * scale_there
            acc = acc * scale_here + acc_in[place, :] * scale_there
            out_ref[place, :] = acc / total
            lse_ref[place, :] = pltpu.roll(new_top + jnp.log(total), HEAD_DIM, 1)
        else:
            acc_out[place, :] = acc
            top_out[place, :] = top
            sum_out[place, :] = total


def attend(limits, queries, keys, values, rows, blocks, before):
    total, width = queries.shape
    items = total // rows
    key_count = rows * blocks
    step = chunk_of(rows, 208)
    query_block = pl.BlockSpec((rows, PAIR), lambda i, p, *_: (i, p))
    key_block = pl.BlockSpec((key_count, PAIR), lambda i, p, *_: (i, p))
    final = before is not None
    extra = list(before) if final else []
    outs = 2 if final else 3
    return pl.pallas_call(
        functools.partial(forward_kernel, final, rows, blocks, step),
        grid_spec=pltpu.PrefetchScalarGridSpec(
            num_scalar_prefetch=1,
            grid=(items, PAIRS),
            in_specs=[query_block, key_block, key_block] + [query_block] * len(extra),
            out_specs=[query_block] * outs,
            scratch_shapes=[
                pltpu.VMEM((2, PAIR, key_count), bf16),
                pltpu.VMEM((2, key_count, PAIR), bf16),
                pltpu.VMEM((step, key_count), f32),
                pltpu.VMEM((step, key_count), f32),
            ],
        ),
        out_shape=[jax.ShapeDtypeStruct((total, width), f32)] * outs,
        compiler_params=params(2),
        cost_estimate=cost(
            16 * total * key_count * width, 12 * total * width, total * key_count * HEADS
        ),
        name="attend",
    )(limits, queries, keys, values, *extra)


def split_three(value):
    high = value.astype(bf16).astype(f32)
    rest = value - high
    middle = rest.astype(bf16).astype(f32)
    return high, middle, rest - middle


def halves(core, block):
    half = block.shape[0] // 2
    upper, lower = block[:half], block[half:]
    mine = jnp.where(core == 0, upper, lower)
    theirs = jnp.where(core == 0, lower, upper)
    return mine.astype(bf16), theirs.astype(bf16)


def backward_kernel(
    last, tokens, rows, blocks, step, limits, core,
    q_ref, k_ref, v_ref, g_ref, out_ref, lse_ref, hat_ref, *rest,
):
    if last:
        before_ref, dw_in, sums_in, *rest = rest
        cat_ref, keep_ref, send_ref, dw_acc, sums_acc, qt_ref, gt_ref, dqt_ref, *wide = rest[tokens:]
    else:
        dq_ref, cat_ref, dw_ref, sums_ref, dw_acc, sums_acc, qt_ref, gt_ref, dqt_ref, *wide = rest[tokens:]
    prob_refs, score_refs = wide[:2], wide[2:]
    pair = pl.program_id(0)
    item = pl.program_id(1)
    query_rows = q_ref.shape[0]
    lanes = lanes_of((query_rows, PAIR))
    head_first = lanes < HEAD_DIM
    spare_lane = lanes & (HEAD_DIM - 1)

    def spare(parts, mask_one):
        high, middle, low = parts
        value = jnp.where(spare_lane == 0, high, 0.0)
        value = jnp.where(spare_lane == 1, middle, value)
        value = jnp.where(spare_lane == 2, low, value)
        return jnp.where(spare_lane == 3, mask_one, value)

    query = q_ref[...].astype(f32)
    grad = g_ref[...].astype(f32)
    product = grad * out_ref[...]
    delta_first = jnp.sum(jnp.where(head_first, product, 0.0), axis=1, keepdims=True)
    delta_second = jnp.sum(jnp.where(head_first, 0.0, product), axis=1, keepdims=True)
    delta = jnp.where(head_first, delta_second, delta_first)
    lse_spare = spare(split_three(-lse_ref[...]), 1.0)
    delta_spare = spare(split_three(-delta), 0.0)
    qt_ref[0] = jnp.where(head_first, query, lse_spare).T.astype(bf16)
    qt_ref[1] = jnp.where(head_first, lse_spare, query).T.astype(bf16)
    gt_ref[0] = jnp.where(head_first, grad, delta_spare).T.astype(bf16)
    gt_ref[1] = jnp.where(head_first, delta_spare, grad).T.astype(bf16)
    dqt_ref[...] = jnp.zeros_like(dqt_ref)

    key_lanes = lanes_of((step, PAIR))
    key_first = key_lanes < HEAD_DIM
    key_spare = key_lanes & (HEAD_DIM - 1)
    key_row = lax.broadcasted_iota(jnp.int32, (step, PAIR), 0)
    ones = jnp.where(key_spare < 3, 1.0, 0.0)
    per_block = rows // step
    tiles = [slice(t, min(t + TILE, query_rows)) for t in range(0, query_rows, TILE)]

    def operands(unit):
        chunk, head = divmod(unit, 2)
        place = slice(chunk * step, (chunk + 1) * step)
        block = chunk // per_block
        limit = limits[item, block] - (chunk - block * per_block) * step
        bias = jnp.where(key_row >= limit, NEGATIVE, 0.0)
        key = k_ref[place, :].astype(f32)
        value = v_ref[place, :].astype(f32)
        mine = key_first if head == 0 else jnp.logical_not(key_first)
        key_head = jnp.where(mine, key, jnp.where(key_spare == 3, bias, ones)).astype(bf16)
        value_head = jnp.where(mine, value, ones).astype(bf16)
        half = key.T[head * HEAD_DIM:(head + 1) * HEAD_DIM].astype(bf16)
        return key_head, value_head, half

    units = 2 * blocks * per_block
    dks, dvs, half = [], [], None
    for unit in range(-1, units):
        more = unit + 1 < units
        if more:
            key_head, value_head, next_half = operands(unit + 1)
            which = (unit + 1) % 2
        dk, dv = None, None
        for tile in tiles:
            if more:
                probs = jnp.exp(dot_rows(key_head, qt_ref[which, :, tile]))
                grad_probs = dot_rows(value_head, gt_ref[which, :, tile])
                prob_refs[which][:, tile] = probs.astype(bf16)
                score_refs[which][:, tile] = (probs * grad_probs).astype(bf16)
            if unit >= 0:
                grad_scores = score_refs[unit % 2][:, tile]
                dv_part = dot_rows(prob_refs[unit % 2][:, tile], g_ref[tile, :])
                dk_part = dot_rows(grad_scores, q_ref[tile, :])
                dv = dv_part if dv is None else dv + dv_part
                dk = dk_part if dk is None else dk + dk_part
                own = slice(unit % 2 * HEAD_DIM, (unit % 2 + 1) * HEAD_DIM)
                dqt_ref[own, tile] += dot_rows(half, grad_scores)
        half = next_half if more else None
        if unit >= 0:
            dks.append(dk)
            dvs.append(dv)
        if unit >= 0 and unit % 2 == 1:
            place = slice(unit // 2 * step, (unit // 2 + 1) * step)
            cat_ref[place, :PAIR] = jnp.where(key_first, dks[-2], dks[-1]).astype(bf16)
            cat_ref[place, PAIR:2 * PAIR] = jnp.where(key_first, dvs[-2], dvs[-1]).astype(bf16)

    result = dqt_ref[...].T
    if last:
        cat_ref[:, 2 * PAIR:] = ((result + before_ref[...]) * SCALE).astype(bf16)
    else:
        dq_ref[...] = result
    added = dot_left(hat_ref[...], cat_ref[...])
    sums = column_sums(cat_ref[...].astype(f32))
    items = pl.num_programs(1)
    here = pl.ds(pair, 1)

    @pl.when((item == 0) & (pair == 0))
    def _():
        sums_acc[...] = jnp.zeros_like(sums_acc)

    @pl.when(item == 0)
    def _():
        dw_acc[...] = added
        if last:
            dw_acc[:, :2 * PAIR] += dw_in[0]
            sums_acc[here, :2 * PAIR] = sums_in[0, :1, :]

    @pl.when(item > 0)
    def _():
        dw_acc[...] += added

    sums_acc[here, :] += sums

    @pl.when(item == items - 1)
    def _():
        if last:
            half = dw_acc.shape[0] // 2
            place = pl.ds(pl.multiple_of(pair * half, half), half)
            keep_ref[place, :], send_ref[place, :] = halves(core[0], dw_acc[...])
        else:
            dw_ref[0] = dw_acc[...]
            sums_ref[0] = jnp.broadcast_to(sums_acc[here, :], sums_ref.shape[1:])

    if last:

        @pl.when((item == items - 1) & (pair == pl.num_programs(0) - 1))
        def _():
            end = slice(keep_ref.shape[0] - sums_acc.shape[0] // 2, None)
            keep_ref[end, :], send_ref[end, :] = halves(core[0], sums_acc[...])


def attend_back(
    limits, core, queries, keys, values, grads, outs, lse, hat, rows, blocks, first, count, before,
    spare, tokens,
):
    total, width = queries.shape
    items = total // rows
    key_count = rows * blocks
    step = chunk_of(rows, 208)
    last = before is not None
    cat = (3 if last else 2) * PAIR
    query_block = pl.BlockSpec((rows, PAIR), lambda p, i, *_: (i, first + p))
    key_block = pl.BlockSpec((key_count, PAIR), lambda p, i, *_: (i, first + p))
    hat_block = pl.BlockSpec((key_count, width), lambda p, i, *_: (i, 0))
    cat_block = pl.BlockSpec((key_count, cat), lambda p, i, *_: (i, p))
    shape = jax.ShapeDtypeStruct
    cat_shape = shape((total * blocks, cat * count), bf16)
    if last:
        (part, _, dw_part, sums_part), skip = before
        extra = [part, dw_part, sums_part]
        extra_specs = [
            pl.BlockSpec((rows, PAIR), lambda p, i, *_: (i, skip + p)),
            pl.BlockSpec((1, width, 2 * PAIR), lambda p, i, *_: (skip + p, 0, 0)),
            pl.BlockSpec((1, 8, 2 * PAIR), lambda p, i, *_: (skip + p, 0, 0)),
        ]
        half = (count * width // 2 + spare, cat)
        out_shape = [cat_shape] + [shape(half, bf16)] * 2
        out_specs = [cat_block] + [whole(half)] * 2
    else:
        extra, extra_specs = [], []
        out_shape = [
            shape((total, PAIR * count), f32),
            cat_shape,
            shape((count, width, cat), f32),
            shape((count, 8, cat), f32),
        ]
        out_specs = [
            pl.BlockSpec((rows, PAIR), lambda p, i, *_: (i, p)),
            cat_block,
            pl.BlockSpec((1, width, cat), lambda p, i, *_: (p, 0, 0)),
            pl.BlockSpec((1, 8, cat), lambda p, i, *_: (p, 0, 0)),
        ]
    return pl.pallas_call(
        functools.partial(backward_kernel, last, len(tokens), rows, blocks, step),
        grid_spec=pltpu.PrefetchScalarGridSpec(
            num_scalar_prefetch=2,
            grid=(count, items),
            in_specs=[query_block, key_block, key_block]
            + [query_block] * 3
            + [hat_block]
            + extra_specs
            + [ANYWHERE] * len(tokens),
            out_specs=out_specs,
            scratch_shapes=[
                pltpu.VMEM((width, cat), f32),
                pltpu.VMEM((2 * spare, cat), f32),
                pltpu.VMEM((2, PAIR, rows), bf16),
                pltpu.VMEM((2, PAIR, rows), bf16),
                pltpu.VMEM((PAIR, rows), f32),
            ]
            + [pltpu.VMEM((step, rows), bf16)] * 4,
        ),
        out_shape=out_shape,
        compiler_params=params(2),
        cost_estimate=cost(
            40 * total * key_count * PAIR * count,
            16 * total * PAIR * count,
            2 * total * key_count * count,
        ),
        name="attend_back",
    )(limits, core, queries, keys, values, grads, outs, lse, hat, *extra, *tokens)


def feed_kernel(
    core, x_ref, mix_ref, dy_ref, w_output, w_expand, w_reduce, b_output, b_expand, b_reduce, gain, shift,
    y_ref, dmid_ref, dmix_ref, keep_ref, send_ref,
    middle_ref, normed_ref, y_acc, grad_acc, line_ref,
):
    part = pl.program_id(0)

    half = w_output.shape[0] // 2

    def put(index, block):
        place = pl.ds(pl.multiple_of(index * half, half), half)
        keep_ref[place, :], send_ref[place, :] = halves(core[0], block)

    @pl.when(part == 0)
    def _():
        mixed = mix_ref[...].astype(bf16)
        middle = x_ref[...].astype(f32) + dot_rows(mixed, w_output[...]) + b_output[...]
        middle_ref[...] = middle
        hat, _ = hat_rows(middle)
        normed_ref[...] = (hat * gain[...] + shift[...]).astype(bf16)
        y_acc[...] = middle + b_reduce[...]
        grad_acc[...] = jnp.zeros_like(grad_acc)
        line_ref[...] = jnp.zeros_like(line_ref)
        line_ref[1:2, :] = column_sums(dy_ref[...].astype(f32))

    normed = normed_ref[...]
    upper = dot_rows(normed, w_expand[...]) + b_expand[...]
    cumulative = 0.5 * lax.erf(upper * math.sqrt(0.5)) + 0.5
    density = jnp.exp(upper * upper * -0.5) * (1.0 / math.sqrt(2.0 * math.pi))
    active = (upper * cumulative).astype(bf16)
    slope = cumulative + upper * density
    y_acc[...] += dot_rows(active, w_reduce[...])
    put(1 + 2 * part, dot_left(active, dy_ref[...]))
    grad_upper = (dot_right(dy_ref[...], w_reduce[...]) * slope).astype(bf16)
    line_ref[pl.ds(4 + part, 1), :] = column_sums(grad_upper.astype(f32))
    put(2 + 2 * part, dot_left(normed, grad_upper))
    grad_acc[...] += dot_right(grad_upper, w_expand[...])

    @pl.when(part == pl.num_programs(0) - 1)
    def _():
        y_ref[...] = y_acc[...].astype(bf16)
        grad = grad_acc[...]
        hat, inverse = hat_rows(middle_ref[...])
        line_ref[2:3, :] = column_sums(grad * hat)
        line_ref[3:4, :] = column_sums(grad)
        dmid = hat_back(grad * gain[...], hat, inverse) + dy_ref[...].astype(f32)
        dmid_ref[...] = dmid
        branch = dmid.astype(bf16)
        line_ref[0:1, :] = column_sums(branch.astype(f32))
        put(0, dot_left(mix_ref[...].astype(bf16), branch))
        end = slice(keep_ref.shape[0] - line_ref.shape[0] // 2, None)
        keep_ref[end, :], send_ref[end, :] = halves(core[0], line_ref[...])
        dmix_ref[...] = dot_right(branch, w_output[...]).astype(bf16)


def feed(core, spare, x, mixed, dy, w_output, w_expand, w_reduce, b_output, b_expand, b_reduce, gain, shift):
    rows, width = x.shape
    hidden = w_expand.shape[1]
    parts = hidden // width
    row = whole((rows, width))
    line = whole((1, width))
    expand = pl.BlockSpec((width, width), lambda i, *_: (0, i))
    reduce = pl.BlockSpec((width, width), lambda i, *_: (i, 0))
    hidden_line = pl.BlockSpec((1, width), lambda i, *_: (0, i))
    weights = ((1 + 2 * parts) * width // 2 + spare, width)
    shape = jax.ShapeDtypeStruct
    return pl.pallas_call(
        feed_kernel,
        grid_spec=pltpu.PrefetchScalarGridSpec(
            num_scalar_prefetch=1,
            grid=(parts,),
            in_specs=[row, row, row, whole((width, width)), expand, reduce, line, hidden_line, line, line, line],
            out_specs=[row, row, row, whole(weights), whole(weights)],
            scratch_shapes=[
                pltpu.VMEM((rows, width), f32),
                pltpu.VMEM((rows, width), bf16),
                pltpu.VMEM((rows, width), f32),
                pltpu.VMEM((rows, width), f32),
                pltpu.VMEM((2 * spare, width), f32),
            ],
        ),
        out_shape=[
            shape((rows, width), bf16),
            shape((rows, width), f32),
            shape((rows, width), bf16),
            shape(weights, bf16),
            shape(weights, bf16),
        ],
        compiler_params=params(1),
        cost_estimate=cost(12 * rows * width * hidden + 6 * rows * width * width, 20 * rows * width, 2 * rows * hidden),
        name="feed",
    )(core, x, mixed, dy, w_output, w_expand, w_reduce, b_output, b_expand, b_reduce, gain, shift)


def gather_parts(refs, part, parts):
    blocks = []
    for ref in refs:
        pairs = ref.shape[1] // (parts * PAIR)
        for pair in range(pairs):
            start = (pair * parts + part) * PAIR
            blocks.append(ref[:, start:start + PAIR])
    return jnp.concatenate(blocks, axis=1)


def other_kernel(cats, w_key, w_value, *rest):
    cat_refs, send_ref = rest[:cats], rest[-1]
    dk = gather_parts(cat_refs, 0, 2)
    dv = gather_parts(cat_refs, 1, 2)
    send_ref[...] = (dot_right(dk, w_key[...]) + dot_right(dv, w_value[...])).astype(bf16)


def other_grads(cats, w_key, w_value, rows, after):
    total, width = cats[0].shape[0], w_key.shape[0]
    step = chunk_of(rows, 272)
    return pl.pallas_call(
        functools.partial(other_kernel, len(cats)),
        grid=(total // step,),
        in_specs=[whole((width, width))] * 2
        + [pl.BlockSpec((step, c.shape[1]), lambda i: (i, 0)) for c in cats]
        + [ANYWHERE] * len(after),
        out_specs=pl.BlockSpec((step, width), lambda i: (i, 0)),
        out_shape=jax.ShapeDtypeStruct((total, width), bf16),
        compiler_params=params(1),
        cost_estimate=cost(4 * total * width * width, 8 * total * width),
        name="other_grads",
    )(w_key, w_value, *cats, *after)


def own_kernel(cats, x_ref, recv_ref, dmid_ref, w_query, w_key, w_value, gain, *rest):
    cat_refs, dx_ref = rest[:cats], rest[-1]
    dk = gather_parts(cat_refs, 0, 3)
    dv = gather_parts(cat_refs, 1, 3)
    dq = gather_parts(cat_refs, 2, 3)
    grad = dot_right(dq, w_query[...]) + dot_right(dk, w_key[...]) + dot_right(dv, w_value[...])
    for index in range(recv_ref.shape[0]):
        grad = grad + recv_ref[index].astype(f32)
    hat, inverse = hat_rows(x_ref[...].astype(f32))
    dx_ref[...] = hat_back(grad * gain[...], hat, inverse) + dmid_ref[...]


def own_grads(x, cats, recv, dmid, w_query, w_key, w_value, gain, after):
    rows, width = x.shape
    step = chunk_of(rows, 272)
    row = pl.BlockSpec((step, width), lambda i: (i, 0))
    return pl.pallas_call(
        functools.partial(own_kernel, len(cats)),
        grid=(rows // step,),
        in_specs=[row, pl.BlockSpec((recv.shape[0], step, width), lambda i: (0, i, 0)), row]
        + [whole((width, width))] * 3
        + [whole((1, width))]
        + [pl.BlockSpec((step, c.shape[1]), lambda i: (i, 0)) for c in cats]
        + [ANYWHERE] * len(after),
        out_specs=row,
        out_shape=jax.ShapeDtypeStruct((rows, width), f32),
        compiler_params=params(1),
        cost_estimate=cost(6 * rows * width * width, 16 * rows * width),
        name="own_grads",
    )(x, recv, dmid, w_query, w_key, w_value, gain, *cats, *after)


class Slice:
    def __init__(self):
        group, rest = lax.axis_size("grp"), lax.axis_size("rest")
        batch = rest * lax.axis_size("core")
        side = 2 if rest % 2 == 0 else 1
        rest //= side
        high = 2 if rest % 2 == 0 else 1
        self.sizes = {"core": 2, "side": side, "member": group, "high": high, "low": rest // high}
        self.count = group * batch
        self.here = self.coords(lax.axis_index(ALL))

    def coords(self, linear):
        out = {}
        for name in ("member", "core", "side", "low", "high"):
            out[name] = linear % self.sizes[name]
            linear = linear // self.sizes[name]
        return out

    def linear(self, coords):
        total = 0
        for name in ("high", "low", "side", "core", "member"):
            total = total * self.sizes[name] + coords[name]
        return total

    def size(self, stage):
        return math.prod(self.sizes[name] for name in stage)

    def place(self, stage, coords=None):
        coords = self.here if coords is None else coords
        total = 0
        for name in stage:
            total = total * self.sizes[name] + coords[name]
        return total

    def send(self, array, stage, shift):
        pairs = []
        for source in range(self.count):
            coords = self.coords(source)
            place = (self.place(stage, coords) + shift) % self.size(stage)
            for name in reversed(stage):
                coords[name] = place % self.sizes[name]
                place //= self.sizes[name]
            pairs.append((source, self.linear(coords)))
        return lax.ppermute(array, ALL, pairs)

    def spread(self, parts, stage):
        return [parts[0]] + [self.send(part, stage, s) for s, part in enumerate(parts) if s > 0]

    def share(self, array, stage):
        return self.spread([array] * self.size(stage), stage)

    def origins(self, stage):
        size = self.size(stage)
        return ((self.place(stage) - jnp.arange(size)) % size).astype(jnp.int32)

    def in_order(self, parts, stage):
        if len(parts) <= 2:
            return parts
        stack = jnp.stack(parts)
        order = self.origins(stage)
        return [lax.dynamic_index_in_dim(stack, order[i], 0, False) for i in range(len(parts))]


def behind(array, *others):
    return lax.optimization_barrier((array, *others))[0]


def cut_kernel(size, groups, place, *refs):
    ins, outs = refs[:2 * groups], refs[len(refs) - size:]
    for shift, out in enumerate(outs):

        @pl.when(pl.program_id(0) == shift)
        def _():
            start = 0
            for index in range(groups):
                keep, came = ins[2 * index], ins[2 * index + 1]
                rows = keep.shape[0]
                total = keep[...].astype(f32) + came[...].astype(f32)
                out[start:start + rows, :] = total.astype(bf16)
                start += rows


def cut(pairs, place, size, after=()):
    arrays = [array for pair in pairs for array in pair]
    width = arrays[0].shape[1]
    part = (sum(keep.shape[0] for keep, _ in pairs) // size, width)
    return pl.pallas_call(
        functools.partial(cut_kernel, size, len(pairs)),
        grid_spec=pltpu.PrefetchScalarGridSpec(
            num_scalar_prefetch=1,
            grid=(size,),
            in_specs=[
                pl.BlockSpec((a.shape[0] // size, width), lambda s, place: ((place[0] + s) % size, 0))
                for a in arrays
            ]
            + [ANYWHERE] * len(after),
            out_specs=[whole(part)] * size,
        ),
        out_shape=[jax.ShapeDtypeStruct(part, bf16)] * size,
        compiler_params=params(1),
        cost_estimate=cost(size * part[0] * width, 6 * size * part[0] * width),
        name="cut",
    )(jnp.reshape(place, (1,)).astype(jnp.int32), *arrays, *after)


def add_up(parts):
    total = parts[0].astype(f32)
    for part in parts[1:]:
        total = total + part.astype(f32)
    return total.astype(bf16)


def place_pieces(places, core, pieces, flats):
    size = len(pieces) // 2
    for which in range(2):
        target = core[0] if which == 0 else 1 - core[0]
        for index in range(size):
            piece, at = pieces[which * size + index], 0
            for flat in flats:
                rows = flat.shape[1] // size
                span = pl.ds(pl.multiple_of(places[index] * rows, 16), rows)
                flat[target, span, :] = piece[at:at + rows, :]
                at += rows


def feed_weights_kernel(places, core, *refs):
    pieces, (dwo_ref, dwe_ref, dwr_ref, line_ref, flat) = refs[:-5], refs[-5:]
    place_pieces(places, core, pieces, [flat])
    width = dwo_ref.shape[0]
    half = width // 2
    parts = dwr_ref.shape[0] // width
    for side in range(2):
        rows = slice(side * half, (side + 1) * half)
        dwo_ref[rows, :] = flat[side, :half, :].astype(f32)
        for part in range(parts):
            start = (1 + 2 * part) * half
            down = slice(part * width + side * half, part * width + (side + 1) * half)
            across = slice(part * width, (part + 1) * width)
            dwr_ref[down, :] = flat[side, start:start + half, :].astype(f32)
            dwe_ref[rows, across] = flat[side, start + half:start + width, :].astype(f32)
    start = (1 + 2 * parts) * half
    line_ref[...] = flat[0, start:start + 16, :].astype(f32)


def feed_weights(places, core, own, came, hidden):
    rows, width = own[0].shape
    shapes = [(width, width), (width, hidden), (hidden, width), (16, width)]
    return pl.pallas_call(
        feed_weights_kernel,
        grid_spec=pltpu.PrefetchScalarGridSpec(
            num_scalar_prefetch=2,
            grid=(1,),
            in_specs=[whole((rows, width))] * (2 * len(own)),
            out_specs=[whole(s) for s in shapes],
            scratch_shapes=[pltpu.VMEM((2, len(own) * rows, width), bf16)],
        ),
        out_shape=[jax.ShapeDtypeStruct(s, f32) for s in shapes],
        compiler_params=params(1),
        cost_estimate=cost(0, 12 * len(own) * rows * width),
        name="feed_weights",
    )(places, core, *own, *came)


def project_weights_kernel(calls, places, core, *refs):
    count = len(calls)
    flats, refs = refs[len(refs) - count:], refs[:len(refs) - count]
    dwq_ref, dwk_ref, dwv_ref, dgain_ref, dshift_ref, dbq_ref, dbv_ref = refs[-7:]
    w_query, w_key, w_value, gain, shift = refs[-12:-7]
    place_pieces(places, core, refs[:-12], flats)
    half = dwq_ref.shape[0] // 2
    for side in range(2):
        down = slice(side * half, (side + 1) * half)
        gains, shifts = gain[down, :], shift[down, :]
        cross = jnp.zeros((half, PAIR), f32)
        plain = jnp.zeros((half, PAIR), f32)
        pair = 0
        for flat, pairs in zip(flats, calls):
            sums = flat[0, pairs * half:pairs * half + 16, :].astype(f32)
            for index in range(pairs):
                span = slice(pair * PAIR, (pair + 1) * PAIR)
                block = flat[side, index * half:(index + 1) * half, :].astype(f32)
                outs = ((dwk_ref, w_key), (dwv_ref, w_value), (dwq_ref, w_query))
                for which, (out, weight) in enumerate(outs):
                    lanes = slice(which * PAIR, (which + 1) * PAIR)
                    part, line = block[:, lanes], sums[index:index + 1, lanes]
                    out[down, span] = gains * part + shifts * line
                    own = weight[down, span].astype(f32)
                    cross += own * part
                    plain += own * line
                if side == 0:
                    dbv_ref[:, span] = sums[index:index + 1, PAIR:2 * PAIR]
                    dbq_ref[:, span] = sums[index:index + 1, 2 * PAIR:]
                pair += 1
        dgain_ref[down, :] = jnp.broadcast_to(jnp.sum(cross, axis=1, keepdims=True), (half, PAIR))
        dshift_ref[down, :] = jnp.broadcast_to(jnp.sum(plain, axis=1, keepdims=True), (half, PAIR))


def project_weights(places, core, own, came, w_query, w_key, w_value, gain, shift, calls, spare):
    width = w_query.shape[0]
    square, column, line = (width, width), (width, PAIR), (1, width)
    rows, cat = own[0].shape
    shapes = [square] * 3 + [column] * 2 + [line] * 2
    return pl.pallas_call(
        functools.partial(project_weights_kernel, calls),
        grid_spec=pltpu.PrefetchScalarGridSpec(
            num_scalar_prefetch=2,
            grid=(1,),
            in_specs=[whole((rows, cat))] * (2 * len(own)) + [whole(square)] * 3 + [whole(column)] * 2,
            out_specs=[whole(s) for s in shapes],
            scratch_shapes=[
                pltpu.VMEM((2, count * width // 2 + spare, cat), bf16) for count in calls
            ],
        ),
        out_shape=[jax.ShapeDtypeStruct(s, f32) for s in shapes],
        compiler_params=params(1),
        cost_estimate=cost(0, 20 * width * width),
        name="project_weights",
    )(places, core, *own, *came, w_query, w_key, w_value, gain, shift)


def body(
    layer_input,
    lang_counts,
    w_query,
    w_key,
    w_value,
    w_output,
    w_expand,
    w_reduce,
    b_query,
    b_value,
    b_output,
    b_expand,
    b_reduce,
    gain_attn,
    shift_attn,
    gain_mlp,
    shift_mlp,
    cotangent,
):
    items, own_rows, width = layer_input.shape
    group = lax.axis_size("grp")
    me = lax.axis_index("grp")
    rows = -(-own_rows // 16) * 16
    total = items * rows
    patch_rows = VIEWS * PATCH
    shifts = range(1, group)

    def padded(array):
        if rows != own_rows:
            array = jnp.pad(array, ((0, 0), (0, rows - own_rows), (0, 0)))
        return array.reshape(total, width)

    def unpadded(array):
        return array.reshape(items, rows, width)[:, :own_rows]

    def limit_of(owner):
        return jnp.clip(patch_rows + lang_counts - owner * own_rows, 0, own_rows)

    def line(vector):
        return vector.reshape(1, -1)

    def group_shift(array, shift):
        return lax.ppermute(array, "grp", [(i, (i + shift) % group) for i in range(group)])

    def joined(parts):
        if len(parts) == 1:
            return parts[0]
        return jnp.stack([p.reshape(items, rows, width) for p in parts], 1).reshape(-1, width)

    x = padded(layer_input)
    dy = padded(cotangent)
    others = [group_shift(x, -shift) for shift in shifts]
    own_limits = limit_of(me).reshape(items, 1)
    other_limits = jnp.stack([limit_of((me + shift) % group) for shift in shifts], 1)

    weights = (w_query, w_key, w_value, line(b_query), line(b_value))
    norms = (line(gain_attn), line(shift_attn))
    hat, keys, values, queries = project(x, *norms, *weights, with_query=True)
    first = attend(own_limits, queries, keys, values, rows, 1, None)
    x_other = joined(others)
    hat_other, keys_other, values_other = project(x_other, *norms, *weights, with_query=False)
    mixed, lse = attend(other_limits, queries, keys_other, values_other, rows, group - 1, first)

    devices = Slice()
    plane = ("side", "member")
    core = jnp.reshape(devices.here["core"], (1,)).astype(jnp.int32)
    plane_place, plane_size = devices.place(plane), devices.size(plane)
    spare = 16 * plane_size
    output, dmid, dmix, keep, give = feed(
        core, spare, x, mixed, dy, w_output, w_expand, w_reduce, line(b_output), line(b_expand),
        line(b_reduce), line(gain_mlp), line(shift_mlp),
    )

    def summed(value, stage):
        return add_up(devices.in_order(devices.share(value, (stage,)), (stage,)))

    def back_other(first, count, tokens):
        return attend_back(
            other_limits, core, queries, keys_other, values_other, dmix, mixed, lse, hat_other,
            rows, group - 1, first, count, None, spare, tokens,
        )

    def back_own(first, count, before, tokens):
        return attend_back(
            own_limits, core, queries, keys, values, dmix, mixed, lse, hat,
            rows, 1, first, count, before, spare, tokens,
        )

    feed_pair = devices.spread([keep, give], ("core",))
    other_first = back_other(0, 1, [])
    parts = cut([feed_pair], plane_place, plane_size, other_first[1:2])
    other_rest = back_other(1, PAIRS - 1, parts[:1])
    feed_sum = behind(add_up(devices.spread(parts, plane)), other_rest[1])
    cat_first, *pair_first = back_own(0, 1, (other_first, 0), [feed_sum])
    feed_sum = behind(summed(feed_sum, "low"), cat_first)
    send = other_grads([other_first[1], other_rest[1]], w_key, w_value, rows, [feed_sum])
    cat_middle, *pair_middle = back_own(1, PAIRS - 2, (other_rest, 0), [feed_sum, send])
    send = send.reshape(items, group - 1, rows, width)
    received = jnp.stack(
        [group_shift(send[:, shift - 1].reshape(total, width), shift) for shift in shifts]
    )
    pair_first = devices.spread(pair_first, ("core",))
    feed_sum = behind(summed(feed_sum, "high"), cat_middle, pair_first[1])
    cat_last, *pair_last = back_own(PAIRS - 1, 1, (other_rest, PAIRS - 2), [feed_sum])
    feed_own = devices.share(feed_sum, plane)
    pairs = [pair_first] + [devices.spread(pair, ("core",)) for pair in (pair_middle, pair_last)]
    parts = devices.spread(cut(pairs, plane_place, plane_size), plane)
    dx = own_grads(
        x, [cat_first, cat_middle, cat_last], received, dmid, w_query, w_key, w_value, line(gain_attn), parts[:1]
    )
    value = behind(add_up(parts), dx)
    value = summed(summed(value, "low"), "high")
    feed_came = [devices.send(behind(piece, value), ("core",), 1) for piece in feed_own]
    project_own = devices.share(value, plane)
    places = devices.origins(plane)
    dwo, dwe, dwr, feed_lines = feed_weights(places, core, feed_own, feed_came, w_expand.shape[1])
    project_own = [project_own[0]] + [behind(piece, dwo) for piece in project_own[1:]]
    project_came = [devices.send(piece, ("core",), 1) for piece in project_own]
    columns = [jnp.broadcast_to(vector[:, None], (width, PAIR)) for vector in (gain_attn, shift_attn)]
    dwq, dwk, dwv, dgain, dshift, dbq, dbv = project_weights(
        places, core, project_own, project_came, w_query, w_key, w_value, *columns, (1, PAIRS - 2, 1), spare
    )
    dbo, dbr, dgain_mlp, dshift_mlp = feed_lines[:4]
    dbe = feed_lines[4:4 + w_expand.shape[1] // width].reshape(-1)
    return (
        unpadded(output),
        unpadded(dx),
        dwq, dwk, dwv, dwo, dwe, dwr,
        dbq.reshape(-1), dbv.reshape(-1), dbo, dbe, dbr, dgain[:, 0], dshift[:, 0], dgain_mlp, dshift_mlp,
    )


def solution(mesh):
    batch, group = mesh.shape["dp"], mesh.shape["grp"]
    mesh = jax.sharding.Mesh(mesh.devices.reshape(batch // 2, 2, group), ALL)
    items = ("rest", "core")
    rows = P(items, "grp", None)
    in_specs = (rows, P(items)) + (P(),) * 15 + (rows,)
    out_specs = (rows, rows) + (P(),) * 15
    return jax.shard_map(body, mesh=mesh, in_specs=in_specs, out_specs=out_specs, check_vma=False)
```

```python
import functools
import math

import jax
import jax.numpy as jnp
from jax import lax
from jax.experimental import pallas as pl
from jax.experimental.pallas import tpu as pltpu
from jax.sharding import PartitionSpec as P

HEADS = 8
HEAD_DIM = 64
VIEWS = 5
PATCH = 400
PAIR = 2 * HEAD_DIM
PAIRS = HEADS // 2
TILE = 256

EPSILON = 1e-05
NEGATIVE = -1e30
SCALE = 1.0 / math.sqrt(HEAD_DIM)

bf16 = jnp.bfloat16
f32 = jnp.float32


def dot_rows(left, right):
    return lax.dot_general(
        left, right, (((1,), (0,)), ((), ())), preferred_element_type=f32
    )


def dot_left(left, right):
    return lax.dot_general(
        left, right, (((0,), (0,)), ((), ())), preferred_element_type=f32
    )


def dot_right(left, right):
    return lax.dot_general(
        left, right, (((1,), (1,)), ((), ())), preferred_element_type=f32
    )


def chunk_of(rows, limit):
    best = 16
    for size in range(16, limit + 1, 16):
        if rows % size == 0:
            best = size
    return best


def hat_rows(matrix):
    center = matrix - jnp.mean(matrix, axis=-1, keepdims=True)
    spread = jnp.mean(center * center, axis=-1, keepdims=True)
    inverse = lax.rsqrt(spread + EPSILON)
    return center * inverse, inverse


def hat_back(grad_hat, hat, inverse):
    mean_grad = jnp.mean(grad_hat, axis=-1, keepdims=True)
    mean_cross = jnp.mean(grad_hat * hat, axis=-1, keepdims=True)
    return inverse * (grad_hat - mean_grad - hat * mean_cross)


def column_sums(matrix):
    return jnp.sum(matrix, axis=0, keepdims=True)


ALL = ("rest", "core", "grp")
VMEM_MIB = 64
ANYWHERE = pl.BlockSpec(memory_space=pl.ANY)


def params(axes):
    return pltpu.CompilerParams(
        dimension_semantics=("arbitrary",) * axes, vmem_limit_bytes=VMEM_MIB << 20
    )


def cost(flops, bytes_accessed, transcendentals=0):
    return pl.CostEstimate(
        flops=int(flops), bytes_accessed=int(bytes_accessed), transcendentals=int(transcendentals)
    )


def whole(shape):
    return pl.BlockSpec(shape, lambda *_: (0,) * len(shape))


def project_kernel(with_query, x_ref, gain, shift, w_query, w_key, w_value, b_query, b_value, *outs):
    hat, _ = hat_rows(x_ref[...].astype(f32))
    normed = (hat * gain[...] + shift[...]).astype(bf16)
    if with_query:
        hat_ref, key_ref, value_ref, query_ref = outs
        query = (dot_rows(normed, w_query[...]) + b_query[...]).astype(bf16)
        query_ref[...] = (query.astype(f32) * SCALE).astype(bf16)
    else:
        hat_ref, key_ref, value_ref = outs
    hat_ref[...] = hat.astype(bf16)
    key_ref[...] = dot_rows(normed, w_key[...]).astype(bf16)
    value_ref[...] = (dot_rows(normed, w_value[...]) + b_value[...]).astype(bf16)


def project(x, gain, shift, w_query, w_key, w_value, b_query, b_value, with_query):
    rows, width = x.shape
    step = chunk_of(rows, 272)
    count = 4 if with_query else 3
    row_block = pl.BlockSpec((step, width), lambda i: (i, 0))
    return pl.pallas_call(
        functools.partial(project_kernel, with_query),
        grid=(rows // step,),
        in_specs=[row_block, whole((1, width)), whole((1, width))]
        + [whole((width, width))] * 3
        + [whole((1, width))] * 2,
        out_specs=[row_block] * count,
        out_shape=[jax.ShapeDtypeStruct((rows, width), bf16)] * count,
        compiler_params=params(1),
        cost_estimate=cost(2 * rows * width * width * (count - 1), 2 * rows * width * (count + 1)),
        name="project",
    )(x, gain, shift, w_query, w_key, w_value, b_query, b_value)


def lanes_of(shape):
    return lax.broadcasted_iota(jnp.int32, shape, 1)


def forward_kernel(
    final, rows, blocks, step, limits, q_ref, k_ref, v_ref, *rest
):
    if final:
        acc_in, top_in, sum_in, out_ref, lse_ref, kt_ref, va_ref, *score_refs = rest
    else:
        acc_out, top_out, sum_out, kt_ref, va_ref, *score_refs = rest
    item = pl.program_id(0)
    key_count = rows * blocks
    query_rows = q_ref.shape[0]
    keys = k_ref[...].astype(f32)
    values = v_ref[...].astype(f32)
    first = lanes_of((key_count, PAIR)) < HEAD_DIM
    flipped = keys.T.astype(bf16)
    key_id = lax.broadcasted_iota(jnp.int32, (8, key_count), 1)
    bias = jnp.zeros((8, key_count), f32)
    for block in range(blocks):
        here = (key_id >= block * rows + limits[item, block]) & (key_id < (block + 1) * rows)
        bias = jnp.where(here, NEGATIVE, bias)
    bias = jnp.where(lax.broadcasted_iota(jnp.int32, (8, key_count), 0) == 0, bias, 0.0)
    spare = jnp.concatenate([bias, jnp.zeros((HEAD_DIM - 8, key_count), f32)], 0).astype(bf16)
    kt_ref[0, :HEAD_DIM, :] = flipped[:HEAD_DIM]
    kt_ref[0, HEAD_DIM:, :] = spare
    kt_ref[1, :HEAD_DIM, :] = spare
    kt_ref[1, HEAD_DIM:, :] = flipped[HEAD_DIM:]
    va_ref[0] = jnp.where(first, values, 1.0).astype(bf16)
    va_ref[1] = jnp.where(first, 1.0, values).astype(bf16)
    lanes = lanes_of((step, PAIR))
    head_first = lanes < HEAD_DIM
    one = jnp.where((lanes & (HEAD_DIM - 1)) == 0, 1.0, 0.0)
    tiles = [slice(t, min(t + TILE, key_count)) for t in range(0, key_count, TILE)]

    def query_of(unit):
        chunk, head = divmod(unit, 2)
        query = q_ref[chunk * step:(chunk + 1) * step, :].astype(f32)
        mine = head_first if head == 0 else jnp.logical_not(head_first)
        return jnp.where(mine, query, one).astype(bf16)

    units = 2 * (query_rows // step)
    outs, tops = [], []
    for unit in range(-1, units):
        query = query_of(unit + 1) if unit + 1 < units else None
        out, best = None, None
        for tile in tiles:
            if query is not None:
                scores = dot_rows(query, kt_ref[(unit + 1) % 2, :, tile])
                score_refs[(unit + 1) % 2][:, tile] = scores
                high = jnp.max(scores, axis=1, keepdims=True)
                best = high if best is None else jnp.maximum(best, high)
            if unit >= 0:
                weights = jnp.exp(score_refs[unit % 2][:, tile] - tops[unit]).astype(bf16)
                added = dot_rows(weights, va_ref[unit % 2, tile, :])
                out = added if out is None else out + added
        if best is not None:
            tops.append(best)
        if out is not None:
            outs.append(out)
        if unit % 2 == 0 or unit < 0:
            continue
        chunk = unit // 2
        place = slice(chunk * step, (chunk + 1) * step)
        acc = jnp.where(head_first, outs[unit - 1], outs[unit])
        total = pltpu.roll(jnp.where(head_first, outs[unit], outs[unit - 1]), HEAD_DIM, 1)
        top = jnp.where(head_first, tops[unit - 1], tops[unit])
        if final:
            other_top = top_in[place, :]
            new_top = jnp.maximum(top, other_top)
            scale_here = jnp.exp(top - new_top)
            scale_there = jnp.exp(other_top - new_top)
            total = total * scale_here + sum_in[place, :] * scale_there
            acc = acc * scale_here + acc_in[place, :] * scale_there
            out_ref[place, :] = acc / total
            lse_ref[place, :] = pltpu.roll(new_top + jnp.log(total), HEAD_DIM, 1)
        else:
            acc_out[place, :] = acc
            top_out[place, :] = top
            sum_out[place, :] = total


def attend(limits, queries, keys, values, rows, blocks, before):
    total, width = queries.shape
    items = total // rows
    key_count = rows * blocks
    step = chunk_of(rows, 208)
    query_block = pl.BlockSpec((rows, PAIR), lambda i, p, *_: (i, p))
    key_block = pl.BlockSpec((key_count, PAIR), lambda i, p, *_: (i, p))
    final = before is not None
    extra = list(before) if final else []
    outs = 2 if final else 3
    return pl.pallas_call(
        functools.partial(forward_kernel, final, rows, blocks, step),
        grid_spec=pltpu.PrefetchScalarGridSpec(
            num_scalar_prefetch=1,
            grid=(items, PAIRS),
            in_specs=[query_block, key_block, key_block] + [query_block] * len(extra),
            out_specs=[query_block] * outs,
            scratch_shapes=[
                pltpu.VMEM((2, PAIR, key_count), bf16),
                pltpu.VMEM((2, key_count, PAIR), bf16),
                pltpu.VMEM((step, key_count), f32),
                pltpu.VMEM((step, key_count), f32),
            ],
        ),
        out_shape=[jax.ShapeDtypeStruct((total, width), f32)] * outs,
        compiler_params=params(2),
        cost_estimate=cost(
            16 * total * key_count * width, 12 * total * width, total * key_count * HEADS
        ),
        name="attend",
    )(limits, queries, keys, values, *extra)


def split_three(value):
    high = value.astype(bf16).astype(f32)
    rest = value - high
    middle = rest.astype(bf16).astype(f32)
    return high, middle, rest - middle


def halves(core, block):
    half = block.shape[0] // 2
    upper, lower = block[:half], block[half:]
    mine = jnp.where(core == 0, upper, lower)
    theirs = jnp.where(core == 0, lower, upper)
    return mine.astype(bf16), theirs.astype(bf16)


def backward_kernel(
    last, tokens, rows, blocks, step, limits, core,
    q_ref, k_ref, v_ref, g_ref, out_ref, lse_ref, hat_ref, *rest,
):
    if last:
        before_ref, dw_in, sums_in, *rest = rest
        cat_ref, keep_ref, send_ref, dw_acc, sums_acc, qt_ref, gt_ref, dqt_ref, *wide = rest[tokens:]
    else:
        dq_ref, cat_ref, dw_ref, sums_ref, dw_acc, sums_acc, qt_ref, gt_ref, dqt_ref, *wide = rest[tokens:]
    prob_refs, score_refs = wide[:2], wide[2:]
    pair = pl.program_id(0)
    item = pl.program_id(1)
    query_rows = q_ref.shape[0]
    lanes = lanes_of((query_rows, PAIR))
    head_first = lanes < HEAD_DIM
    spare_lane = lanes & (HEAD_DIM - 1)

    def spare(parts, mask_one):
        high, middle, low = parts
        value = jnp.where(spare_lane == 0, high, 0.0)
        value = jnp.where(spare_lane == 1, middle, value)
        value = jnp.where(spare_lane == 2, low, value)
        return jnp.where(spare_lane == 3, mask_one, value)

    query = q_ref[...].astype(f32)
    grad = g_ref[...].astype(f32)
    product = grad * out_ref[...]
    delta_first = jnp.sum(jnp.where(head_first, product, 0.0), axis=1, keepdims=True)
    delta_second = jnp.sum(jnp.where(head_first, 0.0, product), axis=1, keepdims=True)
    delta = jnp.where(head_first, delta_second, delta_first)
    lse_spare = spare(split_three(-lse_ref[...]), 1.0)
    delta_spare = spare(split_three(-delta), 0.0)
    qt_ref[0] = jnp.where(head_first, query, lse_spare).T.astype(bf16)
    qt_ref[1] = jnp.where(head_first, lse_spare, query).T.astype(bf16)
    gt_ref[0] = jnp.where(head_first, grad, delta_spare).T.astype(bf16)
    gt_ref[1] = jnp.where(head_first, delta_spare, grad).T.astype(bf16)
    dqt_ref[...] = jnp.zeros_like(dqt_ref)

    key_lanes = lanes_of((step, PAIR))
    key_first = key_lanes < HEAD_DIM
    key_spare = key_lanes & (HEAD_DIM - 1)
    key_row = lax.broadcasted_iota(jnp.int32, (step, PAIR), 0)
    ones = jnp.where(key_spare < 3, 1.0, 0.0)
    per_block = rows // step
    tiles = [slice(t, min(t + TILE, query_rows)) for t in range(0, query_rows, TILE)]

    def operands(unit):
        chunk, head = divmod(unit, 2)
        place = slice(chunk * step, (chunk + 1) * step)
        block = chunk // per_block
        limit = limits[item, block] - (chunk - block * per_block) * step
        bias = jnp.where(key_row >= limit, NEGATIVE, 0.0)
        key = k_ref[place, :].astype(f32)
        value = v_ref[place, :].astype(f32)
        mine = key_first if head == 0 else jnp.logical_not(key_first)
        key_head = jnp.where(mine, key, jnp.where(key_spare == 3, bias, ones)).astype(bf16)
        value_head = jnp.where(mine, value, ones).astype(bf16)
        half = key.T[head * HEAD_DIM:(head + 1) * HEAD_DIM].astype(bf16)
        return key_head, value_head, half

    units = 2 * blocks * per_block
    dks, dvs, half = [], [], None
    for unit in range(-1, units):
        more = unit + 1 < units
        if more:
            key_head, value_head, next_half = operands(unit + 1)
            which = (unit + 1) % 2
        dk, dv = None, None
        for tile in tiles:
            if more:
                probs = jnp.exp(dot_rows(key_head, qt_ref[which, :, tile]))
                grad_probs = dot_rows(value_head, gt_ref[which, :, tile])
                prob_refs[which][:, tile] = probs.astype(bf16)
                score_refs[which][:, tile] = (probs * grad_probs).astype(bf16)
            if unit >= 0:
                grad_scores = score_refs[unit % 2][:, tile]
                dv_part = dot_rows(prob_refs[unit % 2][:, tile], g_ref[tile, :])
                dk_part = dot_rows(grad_scores, q_ref[tile, :])
                dv = dv_part if dv is None else dv + dv_part
                dk = dk_part if dk is None else dk + dk_part
                own = slice(unit % 2 * HEAD_DIM, (unit % 2 + 1) * HEAD_DIM)
                dqt_ref[own, tile] += dot_rows(half, grad_scores)
        half = next_half if more else None
        if unit >= 0:
            dks.append(dk)
            dvs.append(dv)
        if unit >= 0 and unit % 2 == 1:
            place = slice(unit // 2 * step, (unit // 2 + 1) * step)
            cat_ref[place, :PAIR] = jnp.where(key_first, dks[-2], dks[-1]).astype(bf16)
            cat_ref[place, PAIR:2 * PAIR] = jnp.where(key_first, dvs[-2], dvs[-1]).astype(bf16)

    result = dqt_ref[...].T
    if last:
        cat_ref[:, 2 * PAIR:] = ((result + before_ref[...]) * SCALE).astype(bf16)
    else:
        dq_ref[...] = result
    added = dot_left(hat_ref[...], cat_ref[...])
    sums = column_sums(cat_ref[...].astype(f32))
    items = pl.num_programs(1)
    here = pl.ds(pair, 1)

    @pl.when((item == 0) & (pair == 0))
    def _():
        sums_acc[...] = jnp.zeros_like(sums_acc)

    @pl.when(item == 0)
    def _():
        dw_acc[...] = added
        if last:
            dw_acc[:, :2 * PAIR] += dw_in[0]
            sums_acc[here, :2 * PAIR] = sums_in[0, :1, :]

    @pl.when(item > 0)
    def _():
        dw_acc[...] += added

    sums_acc[here, :] += sums

    @pl.when(item == items - 1)
    def _():
        if last:
            half = dw_acc.shape[0] // 2
            place = pl.ds(pl.multiple_of(pair * half, half), half)
            keep_ref[place, :], send_ref[place, :] = halves(core[0], dw_acc[...])
        else:
            dw_ref[0] = dw_acc[...]
            sums_ref[0] = jnp.broadcast_to(sums_acc[here, :], sums_ref.shape[1:])

    if last:

        @pl.when((item == items - 1) & (pair == pl.num_programs(0) - 1))
        def _():
            end = slice(keep_ref.shape[0] - sums_acc.shape[0] // 2, None)
            keep_ref[end, :], send_ref[end, :] = halves(core[0], sums_acc[...])


def attend_back(
    limits, core, queries, keys, values, grads, outs, lse, hat, rows, blocks, first, count, before,
    spare, tokens,
):
    total, width = queries.shape
    items = total // rows
    key_count = rows * blocks
    step = chunk_of(rows, 208)
    last = before is not None
    cat = (3 if last else 2) * PAIR
    query_block = pl.BlockSpec((rows, PAIR), lambda p, i, *_: (i, first + p))
    key_block = pl.BlockSpec((key_count, PAIR), lambda p, i, *_: (i, first + p))
    hat_block = pl.BlockSpec((key_count, width), lambda p, i, *_: (i, 0))
    cat_block = pl.BlockSpec((key_count, cat), lambda p, i, *_: (i, p))
    shape = jax.ShapeDtypeStruct
    cat_shape = shape((total * blocks, cat * count), bf16)
    if last:
        (part, _, dw_part, sums_part), skip = before
        extra = [part, dw_part, sums_part]
        extra_specs = [
            pl.BlockSpec((rows, PAIR), lambda p, i, *_: (i, skip + p)),
            pl.BlockSpec((1, width, 2 * PAIR), lambda p, i, *_: (skip + p, 0, 0)),
            pl.BlockSpec((1, 8, 2 * PAIR), lambda p, i, *_: (skip + p, 0, 0)),
        ]
        half = (count * width // 2 + spare, cat)
        out_shape = [cat_shape] + [shape(half, bf16)] * 2
        out_specs = [cat_block] + [whole(half)] * 2
    else:
        extra, extra_specs = [], []
        out_shape = [
            shape((total, PAIR * count), f32),
            cat_shape,
            shape((count, width, cat), f32),
            shape((count, 8, cat), f32),
        ]
        out_specs = [
            pl.BlockSpec((rows, PAIR), lambda p, i, *_: (i, p)),
            cat_block,
            pl.BlockSpec((1, width, cat), lambda p, i, *_: (p, 0, 0)),
            pl.BlockSpec((1, 8, cat), lambda p, i, *_: (p, 0, 0)),
        ]
    return pl.pallas_call(
        functools.partial(backward_kernel, last, len(tokens), rows, blocks, step),
        grid_spec=pltpu.PrefetchScalarGridSpec(
            num_scalar_prefetch=2,
            grid=(count, items),
            in_specs=[query_block, key_block, key_block]
            + [query_block] * 3
            + [hat_block]
            + extra_specs
            + [ANYWHERE] * len(tokens),
            out_specs=out_specs,
            scratch_shapes=[
                pltpu.VMEM((width, cat), f32),
                pltpu.VMEM((2 * spare, cat), f32),
                pltpu.VMEM((2, PAIR, rows), bf16),
                pltpu.VMEM((2, PAIR, rows), bf16),
                pltpu.VMEM((PAIR, rows), f32),
            ]
            + [pltpu.VMEM((step, rows), bf16)] * 4,
        ),
        out_shape=out_shape,
        compiler_params=params(2),
        cost_estimate=cost(
            40 * total * key_count * PAIR * count,
            16 * total * PAIR * count,
            2 * total * key_count * count,
        ),
        name="attend_back",
    )(limits, core, queries, keys, values, grads, outs, lse, hat, *extra, *tokens)


TAIL = (
    0.11766257643469796, 0.04569441499095793, 0.3247791815669602,
    -0.3176994983341737, 0.44333179065269035, -0.11376846615922903,
)


def normal(value):
    bell = jnp.exp(value * value * -0.5)
    part = 1.0 / (1.0 + (0.39 * math.sqrt(0.5)) * jnp.abs(value))
    total = TAIL[-1]
    for factor in TAIL[-2::-1]:
        total = total * part + factor
    tail = total * part * bell
    return jnp.where(value > 0.0, 1.0 - tail, tail), bell * (1.0 / math.sqrt(2.0 * math.pi))


def feed_kernel(
    core, x_ref, mix_ref, dy_ref, w_output, w_expand, w_reduce, b_output, b_expand, b_reduce, gain, shift,
    y_ref, dmid_ref, dmix_ref, keep_ref, send_ref,
    middle_ref, normed_ref, y_acc, grad_acc, line_ref,
):
    part = pl.program_id(0)

    half = w_output.shape[0] // 2

    def put(index, block):
        place = pl.ds(pl.multiple_of(index * half, half), half)
        keep_ref[place, :], send_ref[place, :] = halves(core[0], block)

    @pl.when(part == 0)
    def _():
        mixed = mix_ref[...].astype(bf16)
        middle = x_ref[...].astype(f32) + dot_rows(mixed, w_output[...]) + b_output[...]
        middle_ref[...] = middle
        hat, _ = hat_rows(middle)
        normed_ref[...] = (hat * gain[...] + shift[...]).astype(bf16)
        y_acc[...] = middle + b_reduce[...]
        grad_acc[...] = jnp.zeros_like(grad_acc)
        line_ref[...] = jnp.zeros_like(line_ref)
        line_ref[1:2, :] = column_sums(dy_ref[...].astype(f32))

    normed = normed_ref[...]
    upper = dot_rows(normed, w_expand[...]) + b_expand[...]
    cumulative, density = normal(upper)
    active = (upper * cumulative).astype(bf16)
    slope = cumulative + upper * density
    y_acc[...] += dot_rows(active, w_reduce[...])
    put(1 + 2 * part, dot_left(active, dy_ref[...]))
    grad_upper = (dot_right(dy_ref[...], w_reduce[...]) * slope).astype(bf16)
    line_ref[pl.ds(4 + part, 1), :] = column_sums(grad_upper.astype(f32))
    put(2 + 2 * part, dot_left(normed, grad_upper))
    grad_acc[...] += dot_right(grad_upper, w_expand[...])

    @pl.when(part == pl.num_programs(0) - 1)
    def _():
        y_ref[...] = y_acc[...].astype(bf16)
        grad = grad_acc[...]
        hat, inverse = hat_rows(middle_ref[...])
        line_ref[2:3, :] = column_sums(grad * hat)
        line_ref[3:4, :] = column_sums(grad)
        dmid = hat_back(grad * gain[...], hat, inverse) + dy_ref[...].astype(f32)
        dmid_ref[...] = dmid
        branch = dmid.astype(bf16)
        line_ref[0:1, :] = column_sums(branch.astype(f32))
        put(0, dot_left(mix_ref[...].astype(bf16), branch))
        end = slice(keep_ref.shape[0] - line_ref.shape[0] // 2, None)
        keep_ref[end, :], send_ref[end, :] = halves(core[0], line_ref[...])
        dmix_ref[...] = dot_right(branch, w_output[...]).astype(bf16)


def feed(core, spare, x, mixed, dy, w_output, w_expand, w_reduce, b_output, b_expand, b_reduce, gain, shift):
    rows, width = x.shape
    hidden = w_expand.shape[1]
    parts = hidden // width
    row = whole((rows, width))
    line = whole((1, width))
    expand = pl.BlockSpec((width, width), lambda i, *_: (0, i))
    reduce = pl.BlockSpec((width, width), lambda i, *_: (i, 0))
    hidden_line = pl.BlockSpec((1, width), lambda i, *_: (0, i))
    weights = ((1 + 2 * parts) * width // 2 + spare, width)
    shape = jax.ShapeDtypeStruct
    return pl.pallas_call(
        feed_kernel,
        grid_spec=pltpu.PrefetchScalarGridSpec(
            num_scalar_prefetch=1,
            grid=(parts,),
            in_specs=[row, row, row, whole((width, width)), expand, reduce, line, hidden_line, line, line, line],
            out_specs=[row, row, row, whole(weights), whole(weights)],
            scratch_shapes=[
                pltpu.VMEM((rows, width), f32),
                pltpu.VMEM((rows, width), bf16),
                pltpu.VMEM((rows, width), f32),
                pltpu.VMEM((rows, width), f32),
                pltpu.VMEM((2 * spare, width), f32),
            ],
        ),
        out_shape=[
            shape((rows, width), bf16),
            shape((rows, width), f32),
            shape((rows, width), bf16),
            shape(weights, bf16),
            shape(weights, bf16),
        ],
        compiler_params=params(1),
        cost_estimate=cost(12 * rows * width * hidden + 6 * rows * width * width, 20 * rows * width, 2 * rows * hidden),
        name="feed",
    )(core, x, mixed, dy, w_output, w_expand, w_reduce, b_output, b_expand, b_reduce, gain, shift)


def gather_parts(refs, part, parts):
    blocks = []
    for ref in refs:
        pairs = ref.shape[1] // (parts * PAIR)
        for pair in range(pairs):
            start = (pair * parts + part) * PAIR
            blocks.append(ref[:, start:start + PAIR])
    return jnp.concatenate(blocks, axis=1)


def other_kernel(cats, w_key, w_value, *rest):
    cat_refs, send_ref = rest[:cats], rest[-1]
    dk = gather_parts(cat_refs, 0, 2)
    dv = gather_parts(cat_refs, 1, 2)
    send_ref[...] = (dot_right(dk, w_key[...]) + dot_right(dv, w_value[...])).astype(bf16)


def other_grads(cats, w_key, w_value, rows, after):
    total, width = cats[0].shape[0], w_key.shape[0]
    step = chunk_of(rows, 272)
    return pl.pallas_call(
        functools.partial(other_kernel, len(cats)),
        grid=(total // step,),
        in_specs=[whole((width, width))] * 2
        + [pl.BlockSpec((step, c.shape[1]), lambda i: (i, 0)) for c in cats]
        + [ANYWHERE] * len(after),
        out_specs=pl.BlockSpec((step, width), lambda i: (i, 0)),
        out_shape=jax.ShapeDtypeStruct((total, width), bf16),
        compiler_params=params(1),
        cost_estimate=cost(4 * total * width * width, 8 * total * width),
        name="other_grads",
    )(w_key, w_value, *cats, *after)


def own_kernel(cats, x_ref, recv_ref, dmid_ref, w_query, w_key, w_value, gain, *rest):
    cat_refs, dx_ref = rest[:cats], rest[-1]
    dk = gather_parts(cat_refs, 0, 3)
    dv = gather_parts(cat_refs, 1, 3)
    dq = gather_parts(cat_refs, 2, 3)
    grad = dot_right(dq, w_query[...]) + dot_right(dk, w_key[...]) + dot_right(dv, w_value[...])
    for index in range(recv_ref.shape[0]):
        grad = grad + recv_ref[index].astype(f32)
    hat, inverse = hat_rows(x_ref[...].astype(f32))
    dx_ref[...] = hat_back(grad * gain[...], hat, inverse) + dmid_ref[...]


def own_grads(x, cats, recv, dmid, w_query, w_key, w_value, gain):
    rows, width = x.shape
    step = chunk_of(rows, 272)
    row = pl.BlockSpec((step, width), lambda i: (i, 0))
    return pl.pallas_call(
        functools.partial(own_kernel, len(cats)),
        grid=(rows // step,),
        in_specs=[row, pl.BlockSpec((recv.shape[0], step, width), lambda i: (0, i, 0)), row]
        + [whole((width, width))] * 3
        + [whole((1, width))]
        + [pl.BlockSpec((step, c.shape[1]), lambda i: (i, 0)) for c in cats],
        out_specs=row,
        out_shape=jax.ShapeDtypeStruct((rows, width), f32),
        compiler_params=params(1),
        cost_estimate=cost(rows * width, rows * width),
        name="own_grads",
    )(x, recv, dmid, w_query, w_key, w_value, gain, *cats)


class Slice:
    def __init__(self):
        group, rest = lax.axis_size("grp"), lax.axis_size("rest")
        batch = rest * lax.axis_size("core")
        side = 2 if rest % 2 == 0 else 1
        rest //= side
        high = 2 if rest % 2 == 0 else 1
        self.sizes = {"core": 2, "side": side, "member": group, "high": high, "low": rest // high}
        self.count = group * batch
        self.here = self.coords(lax.axis_index(ALL))

    def coords(self, linear):
        out = {}
        for name in ("member", "core", "side", "low", "high"):
            out[name] = linear % self.sizes[name]
            linear = linear // self.sizes[name]
        return out

    def linear(self, coords):
        total = 0
        for name in ("high", "low", "side", "core", "member"):
            total = total * self.sizes[name] + coords[name]
        return total

    def size(self, stage):
        return math.prod(self.sizes[name] for name in stage)

    def place(self, stage, coords=None):
        coords = self.here if coords is None else coords
        total = 0
        for name in stage:
            total = total * self.sizes[name] + coords[name]
        return total

    def send(self, array, stage, shift):
        pairs = []
        for source in range(self.count):
            coords = self.coords(source)
            place = (self.place(stage, coords) + shift) % self.size(stage)
            for name in reversed(stage):
                coords[name] = place % self.sizes[name]
                place //= self.sizes[name]
            pairs.append((source, self.linear(coords)))
        return lax.ppermute(array, ALL, pairs)

    def spread(self, parts, stage):
        return [parts[0]] + [self.send(part, stage, s) for s, part in enumerate(parts) if s > 0]

    def share(self, array, stage):
        return self.spread([array] * self.size(stage), stage)

    def origins(self, stage):
        size = self.size(stage)
        return ((self.place(stage) - jnp.arange(size)) % size).astype(jnp.int32)

    def in_order(self, parts, stage):
        if len(parts) <= 2:
            return parts
        stack = jnp.stack(parts)
        order = self.origins(stage)
        return [lax.dynamic_index_in_dim(stack, order[i], 0, False) for i in range(len(parts))]


def behind(array, *others):
    return lax.optimization_barrier((array, *others))[0]


def cut_kernel(size, groups, pipelined, place, *refs):
    ins, outs = refs[:2 * groups], refs[len(refs) - size:]

    def put(shift, out):
        start = 0
        for index in range(groups):
            keep, came = ins[2 * index], ins[2 * index + 1]
            rows = keep.shape[0] if pipelined else keep.shape[0] // size
            at = 0 if pipelined else pl.multiple_of((place[0] + shift) % size * rows, 16)
            span = pl.ds(at, rows)
            total = keep[span, :].astype(f32) + came[span, :].astype(f32)
            out[start:start + rows, :] = total.astype(bf16)
            start += rows

    for shift, out in enumerate(outs):
        if pipelined:
            pl.when(pl.program_id(0) == shift)(functools.partial(put, shift, out))
        else:
            put(shift, out)


def cut(pairs, place, size, after=(), pipelined=False):
    arrays = [array for pair in pairs for array in pair]
    width = arrays[0].shape[1]
    part = (sum(keep.shape[0] for keep, _ in pairs) // size, width)
    if pipelined:
        in_specs = [
            pl.BlockSpec((a.shape[0] // size, width), lambda s, place: ((place[0] + s) % size, 0))
            for a in arrays
        ]
    else:
        in_specs = [whole(a.shape) for a in arrays]
    return pl.pallas_call(
        functools.partial(cut_kernel, size, len(pairs), pipelined),
        grid_spec=pltpu.PrefetchScalarGridSpec(
            num_scalar_prefetch=1,
            grid=(size if pipelined else 1,),
            in_specs=in_specs + [ANYWHERE] * len(after),
            out_specs=[whole(part)] * size,
        ),
        out_shape=[jax.ShapeDtypeStruct(part, bf16)] * size,
        compiler_params=params(1),
        cost_estimate=cost(size * part[0] * width, 6 * size * part[0] * width),
        name="cut",
    )(jnp.reshape(place, (1,)).astype(jnp.int32), *arrays, *after)


def add_up(parts):
    total = parts[0].astype(f32)
    for part in parts[1:]:
        total = total + part.astype(f32)
    return total.astype(bf16)


def place_pieces(places, core, pieces, flats):
    size = len(pieces) // 2
    for which in range(2):
        target = core[0] if which == 0 else 1 - core[0]
        for index in range(size):
            piece, at = pieces[which * size + index], 0
            for flat in flats:
                rows = flat.shape[1] // size
                span = pl.ds(pl.multiple_of(places[index] * rows, 16), rows)
                flat[target, span, :] = piece[at:at + rows, :]
                at += rows


def feed_weights_kernel(places, core, *refs):
    pieces, (dwo_ref, dwe_ref, dwr_ref, *line_refs, dbe_ref, flat) = refs[:-10], refs[-9:]
    place_pieces(places, core, pieces, [flat])
    width = dwo_ref.shape[0]
    half = width // 2
    parts = dwr_ref.shape[0] // width
    for side in range(2):
        rows = slice(side * half, (side + 1) * half)
        dwo_ref[rows, :] = flat[side, :half, :].astype(f32)
        for part in range(parts):
            start = (1 + 2 * part) * half
            down = slice(part * width + side * half, part * width + (side + 1) * half)
            across = slice(part * width, (part + 1) * width)
            dwr_ref[down, :] = flat[side, start:start + half, :].astype(f32)
            dwe_ref[rows, across] = flat[side, start + half:start + width, :].astype(f32)
    start = (1 + 2 * parts) * half
    lines = flat[0, start:start + 16, :].astype(f32)
    for index, ref in enumerate(line_refs):
        ref[...] = lines[index:index + 1]
    for part in range(parts):
        dbe_ref[:, part * width:(part + 1) * width] = lines[4 + part:5 + part]


def feed_weights(places, core, own, came, hidden, after):
    rows, width = own[0].shape
    shapes = [(width, width), (width, hidden), (hidden, width)] + [(1, width)] * 4 + [(1, hidden)]
    return pl.pallas_call(
        feed_weights_kernel,
        grid_spec=pltpu.PrefetchScalarGridSpec(
            num_scalar_prefetch=2,
            grid=(1,),
            in_specs=[whole((rows, width))] * (2 * len(own)) + [ANYWHERE] * len(after),
            out_specs=[whole(s) for s in shapes],
            scratch_shapes=[pltpu.VMEM((2, len(own) * rows, width), bf16)],
        ),
        out_shape=[jax.ShapeDtypeStruct(s, f32) for s in shapes],
        compiler_params=params(1),
        cost_estimate=cost(0, 12 * len(own) * rows * width),
        name="feed_weights",
    )(places, core, *own, *came, *after)


def project_weights_kernel(calls, places, core, *refs):
    flats, refs = refs[len(refs) - len(calls):], refs[:len(refs) - len(calls)]
    pieces, refs = refs[:-16], refs[-16:]
    weights, (gain, shift), refs = refs[:3], refs[3:5], refs[5:]
    outs, (dgain_ref, dshift_ref, dbq_ref, dbv_ref), refs = refs[:3], refs[3:7], refs[7:]
    gains, shifts, cross_acc, plain_acc = refs
    pair = pl.program_id(0)
    width = gains.shape[0]
    half = width // 2

    @pl.when(pair == 0)
    def _():
        place_pieces(places, core, pieces, flats)
        gains[...] = jnp.broadcast_to(gain[...], (PAIR, width)).T
        shifts[...] = jnp.broadcast_to(shift[...], (PAIR, width)).T
        cross_acc[...] = jnp.zeros_like(cross_acc)
        plain_acc[...] = jnp.zeros_like(plain_acc)

    def put(flat, pairs, index):
        sums = flat[0, pairs * half:pairs * half + 16, :].astype(f32)[index:index + 1]
        dbv_ref[...] = sums[:, PAIR:2 * PAIR]
        dbq_ref[...] = sums[:, 2 * PAIR:]
        for side in range(2):
            down = slice(side * half, (side + 1) * half)
            block = flat[side, index * half:(index + 1) * half, :].astype(f32)
            for which, (out, weight) in enumerate(zip(outs, weights)):
                lanes = slice(which * PAIR, (which + 1) * PAIR)
                part, line = block[:, lanes], sums[:, lanes]
                out[down, :] = gains[down, :] * part + shifts[down, :] * line
                own = weight[down, :].astype(f32)
                cross_acc[down, :] += own * part
                plain_acc[down, :] += own * line

    first = 0
    for flat, pairs in zip(flats, calls):
        for index in range(pairs):
            pl.when(pair == first + index)(functools.partial(put, flat, pairs, index))
        first += pairs

    @pl.when(pair == PAIRS - 1)
    def _():
        for acc, out in ((cross_acc, dgain_ref), (plain_acc, dshift_ref)):
            column = jnp.broadcast_to(jnp.sum(acc[...], axis=1, keepdims=True), (width, PAIR))
            out[...] = column.T[:1]


def project_weights(places, core, own, came, w_key, w_value, w_query, gain, shift, calls, spare):
    width = w_query.shape[0]
    rows, cat = own[0].shape
    line = whole((1, width))
    column_block = pl.BlockSpec((width, PAIR), lambda p, *_: (0, p))
    line_block = pl.BlockSpec((1, PAIR), lambda p, *_: (0, p))
    return pl.pallas_call(
        functools.partial(project_weights_kernel, calls),
        grid_spec=pltpu.PrefetchScalarGridSpec(
            num_scalar_prefetch=2,
            grid=(PAIRS,),
            in_specs=[whole((rows, cat))] * (2 * len(own)) + [column_block] * 3 + [line] * 2,
            out_specs=[column_block] * 3 + [line] * 2 + [line_block] * 2,
            scratch_shapes=[pltpu.VMEM((width, PAIR), f32)] * 4
            + [pltpu.VMEM((2, count * width // 2 + spare, cat), bf16) for count in calls],
        ),
        out_shape=[jax.ShapeDtypeStruct((width, width), f32)] * 3
        + [jax.ShapeDtypeStruct((1, width), f32)] * 4,
        compiler_params=params(1),
        cost_estimate=cost(0, 20 * width * width),
        name="project_weights",
    )(places, core, *own, *came, w_key, w_value, w_query, gain, shift)


def body(
    layer_input,
    lang_counts,
    w_query,
    w_key,
    w_value,
    w_output,
    w_expand,
    w_reduce,
    b_query,
    b_value,
    b_output,
    b_expand,
    b_reduce,
    gain_attn,
    shift_attn,
    gain_mlp,
    shift_mlp,
    cotangent,
):
    items, own_rows, width = layer_input.shape
    group = lax.axis_size("grp")
    me = lax.axis_index("grp")
    rows = -(-own_rows // 16) * 16
    total = items * rows
    patch_rows = VIEWS * PATCH
    shifts = range(1, group)

    def padded(array):
        if rows != own_rows:
            array = jnp.pad(array, ((0, 0), (0, rows - own_rows), (0, 0)))
        return array.reshape(total, width)

    def unpadded(array):
        return array.reshape(items, rows, width)[:, :own_rows]

    def limit_of(owner):
        return jnp.clip(patch_rows + lang_counts - owner * own_rows, 0, own_rows)

    def line(vector):
        return vector.reshape(1, -1)

    def group_shift(array, shift):
        return lax.ppermute(array, "grp", [(i, (i + shift) % group) for i in range(group)])

    def joined(parts):
        if len(parts) == 1:
            return parts[0]
        return jnp.stack([p.reshape(items, rows, width) for p in parts], 1).reshape(-1, width)

    x = padded(layer_input)
    dy = padded(cotangent)
    others = [group_shift(x, -shift) for shift in shifts]
    own_limits = limit_of(me).reshape(items, 1)
    other_limits = jnp.stack([limit_of((me + shift) % group) for shift in shifts], 1)

    weights = (w_query, w_key, w_value, line(b_query), line(b_value))
    norms = (line(gain_attn), line(shift_attn))
    hat, keys, values, queries = project(x, *norms, *weights, with_query=True)
    first = attend(own_limits, queries, keys, values, rows, 1, None)
    x_other = joined(others)
    hat_other, keys_other, values_other = project(x_other, *norms, *weights, with_query=False)
    mixed, lse = attend(other_limits, queries, keys_other, values_other, rows, group - 1, first)

    devices = Slice()
    plane = ("side", "member")
    core = jnp.reshape(devices.here["core"], (1,)).astype(jnp.int32)
    plane_place, plane_size = devices.place(plane), devices.size(plane)
    spare = 16 * plane_size
    output, dmid, dmix, keep, give = feed(
        core, spare, x, mixed, dy, w_output, w_expand, w_reduce, line(b_output), line(b_expand),
        line(b_reduce), line(gain_mlp), line(shift_mlp),
    )

    def summed(value, stage):
        return add_up(devices.in_order(devices.share(value, (stage,)), (stage,)))

    def back_other(first, count, tokens):
        return attend_back(
            other_limits, core, queries, keys_other, values_other, dmix, mixed, lse, hat_other,
            rows, group - 1, first, count, None, spare, tokens,
        )

    def back_own(first, count, before, tokens):
        return attend_back(
            own_limits, core, queries, keys, values, dmix, mixed, lse, hat,
            rows, 1, first, count, before, spare, tokens,
        )

    feed_pair = devices.spread([keep, give], ("core",))
    other_first = back_other(0, 1, [])
    parts = cut([feed_pair], plane_place, plane_size, other_first[1:2], True)
    other_rest = back_other(1, PAIRS - 1, parts[:1])
    feed_sum = behind(add_up(devices.spread(parts, plane)), other_rest[1])
    cat_first, *pair_first = back_own(0, 1, (other_first, 0), [feed_sum])
    feed_sum = behind(summed(feed_sum, "low"), cat_first)
    send = other_grads([other_first[1], other_rest[1]], w_key, w_value, rows, [feed_sum])
    cat_middle, *pair_middle = back_own(1, PAIRS - 2, (other_rest, 0), [feed_sum, send])
    send = send.reshape(items, group - 1, rows, width)
    received = jnp.stack(
        [group_shift(send[:, shift - 1].reshape(total, width), shift) for shift in shifts]
    )
    pair_first = devices.spread(pair_first, ("core",))
    feed_sum = behind(summed(feed_sum, "high"), cat_middle, pair_first[1])
    cat_last, *pair_last = back_own(PAIRS - 1, 1, (other_rest, PAIRS - 2), [feed_sum, received])
    feed_own = devices.share(feed_sum, plane)
    dx = own_grads(
        x, [cat_first, cat_middle, cat_last], received, dmid, w_query, w_key, w_value, line(gain_attn)
    )
    pairs = [pair_first] + [devices.spread(pair, ("core",)) for pair in (pair_middle, pair_last)]
    parts = devices.spread(cut(pairs, plane_place, plane_size, [dx, *feed_own]), plane)
    feed_came = [devices.send(piece, ("core",), 1) for piece in feed_own]
    places = devices.origins(plane)
    dwo, dwe, dwr, dbo, dbr, dgain_mlp, dshift_mlp, dbe = feed_weights(
        places, core, feed_own, feed_came, w_expand.shape[1], parts[:1]
    )
    value = behind(add_up(parts), dwo)
    value = summed(summed(value, "low"), "high")
    project_own = devices.share(value, plane)
    project_came = [devices.send(piece, ("core",), 1) for piece in project_own]
    dwk, dwv, dwq, dgain, dshift, dbq, dbv = project_weights(
        places, core, project_own, project_came, w_key, w_value, w_query, *norms, (1, PAIRS - 2, 1), spare
    )
    small = (dbq, dbv, dbo, dbe, dbr, dgain, dshift, dgain_mlp, dshift_mlp)
    return (
        unpadded(output),
        unpadded(dx),
        dwq, dwk, dwv, dwo, dwe, dwr,
        *(vector.reshape(-1) for vector in small),
    )


def solution(mesh):
    batch, group = mesh.shape["dp"], mesh.shape["grp"]
    mesh = jax.sharding.Mesh(mesh.devices.reshape(batch // 2, 2, group), ALL)
    items = ("rest", "core")
    rows = P(items, "grp", None)
    in_specs = (rows, P(items)) + (P(),) * 15 + (rows,)
    out_specs = (rows, rows) + (P(),) * 15
    return jax.shard_map(body, mesh=mesh, in_specs=in_specs, out_specs=out_specs, check_vma=False)
```

```python
import functools
import math

import jax
import jax.numpy as jnp
from jax import lax
from jax.experimental import pallas as pl
from jax.experimental.pallas import tpu as pltpu
from jax.sharding import PartitionSpec as P

HEADS = 8
HEAD_DIM = 64
VIEWS = 5
PATCH = 400
PAIR = 2 * HEAD_DIM
PAIRS = HEADS // 2
TILE = 256

EPSILON = 1e-05
NEGATIVE = -1e30
SCALE = 1.0 / math.sqrt(HEAD_DIM)

bf16 = jnp.bfloat16
f32 = jnp.float32


def dot_rows(left, right):
    return lax.dot_general(
        left, right, (((1,), (0,)), ((), ())), preferred_element_type=f32
    )


def dot_left(left, right):
    return lax.dot_general(
        left, right, (((0,), (0,)), ((), ())), preferred_element_type=f32
    )


def dot_right(left, right):
    return lax.dot_general(
        left, right, (((1,), (1,)), ((), ())), preferred_element_type=f32
    )


def chunk_of(rows, limit):
    best = 16
    for size in range(16, limit + 1, 16):
        if rows % size == 0:
            best = size
    return best


def hat_rows(matrix):
    center = matrix - jnp.mean(matrix, axis=-1, keepdims=True)
    spread = jnp.mean(center * center, axis=-1, keepdims=True)
    inverse = lax.rsqrt(spread + EPSILON)
    return center * inverse, inverse


def hat_back(grad_hat, hat, inverse):
    mean_grad = jnp.mean(grad_hat, axis=-1, keepdims=True)
    mean_cross = jnp.mean(grad_hat * hat, axis=-1, keepdims=True)
    return inverse * (grad_hat - mean_grad - hat * mean_cross)


def column_sums(matrix):
    return jnp.sum(matrix, axis=0, keepdims=True)


ALL = ("rest", "core", "grp")
VMEM_MIB = 60
ANYWHERE = pl.BlockSpec(memory_space=pl.ANY)


def params(axes):
    return pltpu.CompilerParams(
        dimension_semantics=("arbitrary",) * axes, vmem_limit_bytes=VMEM_MIB << 20
    )


def cost(flops, bytes_accessed, transcendentals=0):
    return pl.CostEstimate(
        flops=int(flops), bytes_accessed=int(bytes_accessed), transcendentals=int(transcendentals)
    )


def whole(shape):
    return pl.BlockSpec(shape, lambda *_: (0,) * len(shape))


def project_kernel(with_query, x_ref, gain, shift, w_query, w_key, w_value, b_query, b_value, *outs):
    hat, _ = hat_rows(x_ref[...].astype(f32))
    normed = (hat * gain[...] + shift[...]).astype(bf16)
    if with_query:
        hat_ref, key_ref, value_ref, query_ref = outs
        query = (dot_rows(normed, w_query[...]) + b_query[...]).astype(bf16)
        query_ref[...] = (query.astype(f32) * SCALE).astype(bf16)
    else:
        hat_ref, key_ref, value_ref = outs
    hat_ref[...] = hat.astype(bf16)
    key_ref[...] = dot_rows(normed, w_key[...]).astype(bf16)
    value_ref[...] = (dot_rows(normed, w_value[...]) + b_value[...]).astype(bf16)


def project(x, gain, shift, w_query, w_key, w_value, b_query, b_value, with_query):
    rows, width = x.shape
    step = chunk_of(rows, 272)
    count = 4 if with_query else 3
    row_block = pl.BlockSpec((step, width), lambda i: (i, 0))
    return pl.pallas_call(
        functools.partial(project_kernel, with_query),
        grid=(rows // step,),
        in_specs=[row_block, whole((1, width)), whole((1, width))]
        + [whole((width, width))] * 3
        + [whole((1, width))] * 2,
        out_specs=[row_block] * count,
        out_shape=[jax.ShapeDtypeStruct((rows, width), bf16)] * count,
        compiler_params=params(1),
        cost_estimate=cost(2 * rows * width * width * (count - 1), 2 * rows * width * (count + 1)),
        name="project",
    )(x, gain, shift, w_query, w_key, w_value, b_query, b_value)


def lanes_of(shape):
    return lax.broadcasted_iota(jnp.int32, shape, 1)


def forward_kernel(
    final, rows, blocks, step, limits, q_ref, k_ref, v_ref, *rest
):
    if final:
        acc_in, top_in, sum_in, out_ref, lse_ref, kt_ref, va_ref, *score_refs = rest
    else:
        acc_out, top_out, sum_out, kt_ref, va_ref, *score_refs = rest
    item = pl.program_id(0)
    key_count = rows * blocks
    query_rows = q_ref.shape[0]
    keys = k_ref[...].astype(f32)
    values = v_ref[...].astype(f32)
    first = lanes_of((key_count, PAIR)) < HEAD_DIM
    flipped = keys.T.astype(bf16)
    key_id = lax.broadcasted_iota(jnp.int32, (8, key_count), 1)
    bias = jnp.zeros((8, key_count), f32)
    for block in range(blocks):
        here = (key_id >= block * rows + limits[item, block]) & (key_id < (block + 1) * rows)
        bias = jnp.where(here, NEGATIVE, bias)
    bias = jnp.where(lax.broadcasted_iota(jnp.int32, (8, key_count), 0) == 0, bias, 0.0)
    spare = jnp.concatenate([bias, jnp.zeros((HEAD_DIM - 8, key_count), f32)], 0).astype(bf16)
    kt_ref[0, :HEAD_DIM, :] = flipped[:HEAD_DIM]
    kt_ref[0, HEAD_DIM:, :] = spare
    kt_ref[1, :HEAD_DIM, :] = spare
    kt_ref[1, HEAD_DIM:, :] = flipped[HEAD_DIM:]
    va_ref[0] = jnp.where(first, values, 1.0).astype(bf16)
    va_ref[1] = jnp.where(first, 1.0, values).astype(bf16)
    lanes = lanes_of((step, PAIR))
    head_first = lanes < HEAD_DIM
    one = jnp.where((lanes & (HEAD_DIM - 1)) == 0, 1.0, 0.0)
    tiles = [slice(t, min(t + TILE, key_count)) for t in range(0, key_count, TILE)]

    def query_of(unit):
        chunk, head = divmod(unit, 2)
        query = q_ref[chunk * step:(chunk + 1) * step, :].astype(f32)
        mine = head_first if head == 0 else jnp.logical_not(head_first)
        return jnp.where(mine, query, one).astype(bf16)

    units = 2 * (query_rows // step)
    outs, tops = [], []
    for unit in range(-1, units):
        query = query_of(unit + 1) if unit + 1 < units else None
        out, best = None, None
        for tile in tiles:
            if query is not None:
                scores = dot_rows(query, kt_ref[(unit + 1) % 2, :, tile])
                score_refs[(unit + 1) % 2][:, tile] = scores
                high = jnp.max(scores, axis=1, keepdims=True)
                best = high if best is None else jnp.maximum(best, high)
            if unit >= 0:
                weights = jnp.exp(score_refs[unit % 2][:, tile] - tops[unit]).astype(bf16)
                added = dot_rows(weights, va_ref[unit % 2, tile, :])
                out = added if out is None else out + added
        if best is not None:
            tops.append(best)
        if out is not None:
            outs.append(out)
        if unit % 2 == 0 or unit < 0:
            continue
        chunk = unit // 2
        place = slice(chunk * step, (chunk + 1) * step)
        acc = jnp.where(head_first, outs[unit - 1], outs[unit])
        total = pltpu.roll(jnp.where(head_first, outs[unit], outs[unit - 1]), HEAD_DIM, 1)
        top = jnp.where(head_first, tops[unit - 1], tops[unit])
        if final:
            other_top = top_in[place, :]
            new_top = jnp.maximum(top, other_top)
            scale_here = jnp.exp(top - new_top)
            scale_there = jnp.exp(other_top - new_top)
            total = total * scale_here + sum_in[place, :] * scale_there
            acc = acc * scale_here + acc_in[place, :] * scale_there
            out_ref[place, :] = acc / total
            lse_ref[place, :] = pltpu.roll(new_top + jnp.log(total), HEAD_DIM, 1)
        else:
            acc_out[place, :] = acc
            top_out[place, :] = top
            sum_out[place, :] = total


def attend(limits, queries, keys, values, rows, blocks, before):
    total, width = queries.shape
    items = total // rows
    key_count = rows * blocks
    step = chunk_of(rows, 208)
    query_block = pl.BlockSpec((rows, PAIR), lambda i, p, *_: (i, p))
    key_block = pl.BlockSpec((key_count, PAIR), lambda i, p, *_: (i, p))
    final = before is not None
    extra = list(before) if final else []
    outs = 2 if final else 3
    return pl.pallas_call(
        functools.partial(forward_kernel, final, rows, blocks, step),
        grid_spec=pltpu.PrefetchScalarGridSpec(
            num_scalar_prefetch=1,
            grid=(items, PAIRS),
            in_specs=[query_block, key_block, key_block] + [query_block] * len(extra),
            out_specs=[query_block] * outs,
            scratch_shapes=[
                pltpu.VMEM((2, PAIR, key_count), bf16),
                pltpu.VMEM((2, key_count, PAIR), bf16),
                pltpu.VMEM((step, key_count), f32),
                pltpu.VMEM((step, key_count), f32),
            ],
        ),
        out_shape=[jax.ShapeDtypeStruct((total, width), f32)] * outs,
        compiler_params=params(2),
        cost_estimate=cost(
            16 * total * key_count * width, 12 * total * width, total * key_count * HEADS
        ),
        name="attend",
    )(limits, queries, keys, values, *extra)


def split_three(value):
    high = value.astype(bf16).astype(f32)
    rest = value - high
    middle = rest.astype(bf16).astype(f32)
    return high, middle, rest - middle


def halves(core, block):
    half = block.shape[0] // 2
    upper, lower = block[:half], block[half:]
    mine = jnp.where(core == 0, upper, lower)
    theirs = jnp.where(core == 0, lower, upper)
    return mine.astype(bf16), theirs.astype(bf16)


def backward_kernel(
    last, tokens, rows, blocks, step, limits, core,
    q_ref, k_ref, v_ref, g_ref, out_ref, lse_ref, hat_ref, *rest,
):
    if last:
        before_ref, dw_in, sums_in, *rest = rest
        cat_ref, keep_ref, send_ref, dw_acc, sums_acc, qt_ref, gt_ref, dqt_ref, *wide = rest[tokens:]
    else:
        dq_ref, cat_ref, dw_ref, sums_ref, dw_acc, sums_acc, qt_ref, gt_ref, dqt_ref, *wide = rest[tokens:]
    prob_refs, score_refs = wide[:2], wide[2:]
    pair = pl.program_id(0)
    item = pl.program_id(1)
    query_rows = q_ref.shape[0]
    lanes = lanes_of((query_rows, PAIR))
    head_first = lanes < HEAD_DIM
    spare_lane = lanes & (HEAD_DIM - 1)

    def spare(parts, mask_one):
        high, middle, low = parts
        value = jnp.where(spare_lane == 0, high, 0.0)
        value = jnp.where(spare_lane == 1, middle, value)
        value = jnp.where(spare_lane == 2, low, value)
        return jnp.where(spare_lane == 3, mask_one, value)

    query = q_ref[...].astype(f32)
    grad = g_ref[...].astype(f32)
    product = grad * out_ref[...]
    delta_first = jnp.sum(jnp.where(head_first, product, 0.0), axis=1, keepdims=True)
    delta_second = jnp.sum(jnp.where(head_first, 0.0, product), axis=1, keepdims=True)
    delta = jnp.where(head_first, delta_second, delta_first)
    lse_spare = spare(split_three(-lse_ref[...]), 1.0)
    delta_spare = spare(split_three(-delta), 0.0)
    qt_ref[0] = jnp.where(head_first, query, lse_spare).T.astype(bf16)
    qt_ref[1] = jnp.where(head_first, lse_spare, query).T.astype(bf16)
    gt_ref[0] = jnp.where(head_first, grad, delta_spare).T.astype(bf16)
    gt_ref[1] = jnp.where(head_first, delta_spare, grad).T.astype(bf16)
    dqt_ref[...] = jnp.zeros_like(dqt_ref)

    key_lanes = lanes_of((step, PAIR))
    key_first = key_lanes < HEAD_DIM
    key_spare = key_lanes & (HEAD_DIM - 1)
    key_row = lax.broadcasted_iota(jnp.int32, (step, PAIR), 0)
    ones = jnp.where(key_spare < 3, 1.0, 0.0)
    per_block = rows // step
    tiles = [slice(t, min(t + TILE, query_rows)) for t in range(0, query_rows, TILE)]

    def operands(unit):
        chunk, head = divmod(unit, 2)
        place = slice(chunk * step, (chunk + 1) * step)
        block = chunk // per_block
        limit = limits[item, block] - (chunk - block * per_block) * step
        bias = jnp.where(key_row >= limit, NEGATIVE, 0.0)
        key = k_ref[place, :].astype(f32)
        value = v_ref[place, :].astype(f32)
        mine = key_first if head == 0 else jnp.logical_not(key_first)
        key_head = jnp.where(mine, key, jnp.where(key_spare == 3, bias, ones)).astype(bf16)
        value_head = jnp.where(mine, value, ones).astype(bf16)
        half = key.T[head * HEAD_DIM:(head + 1) * HEAD_DIM].astype(bf16)
        return key_head, value_head, half

    units = 2 * blocks * per_block
    dks, dvs, half = [], [], None
    for unit in range(-1, units):
        more = unit + 1 < units
        if more:
            key_head, value_head, next_half = operands(unit + 1)
            which = (unit + 1) % 2
        dk, dv = None, None
        for tile in tiles:
            if more:
                probs = jnp.exp(dot_rows(key_head, qt_ref[which, :, tile]))
                grad_probs = dot_rows(value_head, gt_ref[which, :, tile])
                prob_refs[which][:, tile] = probs.astype(bf16)
                score_refs[which][:, tile] = (probs * grad_probs).astype(bf16)
            if unit >= 0:
                grad_scores = score_refs[unit % 2][:, tile]
                dv_part = dot_rows(prob_refs[unit % 2][:, tile], g_ref[tile, :])
                dk_part = dot_rows(grad_scores, q_ref[tile, :])
                dv = dv_part if dv is None else dv + dv_part
                dk = dk_part if dk is None else dk + dk_part
                own = slice(unit % 2 * HEAD_DIM, (unit % 2 + 1) * HEAD_DIM)
                dqt_ref[own, tile] += dot_rows(half, grad_scores)
        half = next_half if more else None
        if unit >= 0:
            dks.append(dk)
            dvs.append(dv)
        if unit >= 0 and unit % 2 == 1:
            place = slice(unit // 2 * step, (unit // 2 + 1) * step)
            cat_ref[place, :PAIR] = jnp.where(key_first, dks[-2], dks[-1]).astype(bf16)
            cat_ref[place, PAIR:2 * PAIR] = jnp.where(key_first, dvs[-2], dvs[-1]).astype(bf16)

    result = dqt_ref[...].T
    if last:
        cat_ref[:, 2 * PAIR:] = ((result + before_ref[...]) * SCALE).astype(bf16)
    else:
        dq_ref[...] = result
    added = dot_left(hat_ref[...], cat_ref[...])
    sums = column_sums(cat_ref[...].astype(f32))
    items = pl.num_programs(1)
    here = pl.ds(pair, 1)

    @pl.when((item == 0) & (pair == 0))
    def _():
        sums_acc[...] = jnp.zeros_like(sums_acc)

    @pl.when(item == 0)
    def _():
        dw_acc[...] = added
        if last:
            dw_acc[:, :2 * PAIR] += dw_in[0]
            sums_acc[here, :2 * PAIR] = sums_in[0, :1, :]

    @pl.when(item > 0)
    def _():
        dw_acc[...] += added

    sums_acc[here, :] += sums

    @pl.when(item == items - 1)
    def _():
        if last:
            half = dw_acc.shape[0] // 2
            place = pl.ds(pl.multiple_of(pair * half, half), half)
            keep_ref[place, :], send_ref[place, :] = halves(core[0], dw_acc[...])
        else:
            dw_ref[0] = dw_acc[...]
            sums_ref[0] = jnp.broadcast_to(sums_acc[here, :], sums_ref.shape[1:])

    if last:

        @pl.when((item == items - 1) & (pair == pl.num_programs(0) - 1))
        def _():
            end = slice(keep_ref.shape[0] - sums_acc.shape[0] // 2, None)
            keep_ref[end, :], send_ref[end, :] = halves(core[0], sums_acc[...])


def attend_back(
    limits, core, queries, keys, values, grads, outs, lse, hat, rows, blocks, first, count, before,
    spare, tokens,
):
    total, width = queries.shape
    items = total // rows
    key_count = rows * blocks
    step = chunk_of(rows, 208)
    last = before is not None
    cat = (3 if last else 2) * PAIR
    query_block = pl.BlockSpec((rows, PAIR), lambda p, i, *_: (i, first + p))
    key_block = pl.BlockSpec((key_count, PAIR), lambda p, i, *_: (i, first + p))
    hat_block = pl.BlockSpec((key_count, width), lambda p, i, *_: (i, 0))
    cat_block = pl.BlockSpec((key_count, cat), lambda p, i, *_: (i, p))
    shape = jax.ShapeDtypeStruct
    cat_shape = shape((total * blocks, cat * count), bf16)
    if last:
        (part, _, dw_part, sums_part), skip = before
        extra = [part, dw_part, sums_part]
        extra_specs = [
            pl.BlockSpec((rows, PAIR), lambda p, i, *_: (i, skip + p)),
            pl.BlockSpec((1, width, 2 * PAIR), lambda p, i, *_: (skip + p, 0, 0)),
            pl.BlockSpec((1, 8, 2 * PAIR), lambda p, i, *_: (skip + p, 0, 0)),
        ]
        half = (count * width // 2 + spare, cat)
        out_shape = [cat_shape] + [shape(half, bf16)] * 2
        out_specs = [cat_block] + [whole(half)] * 2
    else:
        extra, extra_specs = [], []
        out_shape = [
            shape((total, PAIR * count), f32),
            cat_shape,
            shape((count, width, cat), f32),
            shape((count, 8, cat), f32),
        ]
        out_specs = [
            pl.BlockSpec((rows, PAIR), lambda p, i, *_: (i, p)),
            cat_block,
            pl.BlockSpec((1, width, cat), lambda p, i, *_: (p, 0, 0)),
            pl.BlockSpec((1, 8, cat), lambda p, i, *_: (p, 0, 0)),
        ]
    return pl.pallas_call(
        functools.partial(backward_kernel, last, len(tokens), rows, blocks, step),
        grid_spec=pltpu.PrefetchScalarGridSpec(
            num_scalar_prefetch=2,
            grid=(count, items),
            in_specs=[query_block, key_block, key_block]
            + [query_block] * 3
            + [hat_block]
            + extra_specs
            + [ANYWHERE] * len(tokens),
            out_specs=out_specs,
            scratch_shapes=[
                pltpu.VMEM((width, cat), f32),
                pltpu.VMEM((2 * spare, cat), f32),
                pltpu.VMEM((2, PAIR, rows), bf16),
                pltpu.VMEM((2, PAIR, rows), bf16),
                pltpu.VMEM((PAIR, rows), f32),
            ]
            + [pltpu.VMEM((step, rows), bf16)] * 4,
        ),
        out_shape=out_shape,
        compiler_params=params(2),
        cost_estimate=cost(
            40 * total * key_count * PAIR * count,
            16 * total * PAIR * count,
            2 * total * key_count * count,
        ),
        name="attend_back",
    )(limits, core, queries, keys, values, grads, outs, lse, hat, *extra, *tokens)


def feed_kernel(
    core, x_ref, mix_ref, dy_ref, w_output, w_expand, w_reduce, b_output, b_expand, b_reduce, gain, shift,
    y_ref, dmid_ref, dmix_ref, keep_ref, send_ref,
    middle_ref, normed_ref, y_acc, grad_acc, line_ref,
):
    part = pl.program_id(0)

    half = w_output.shape[0] // 2

    def put(index, block):
        place = pl.ds(pl.multiple_of(index * half, half), half)
        keep_ref[place, :], send_ref[place, :] = halves(core[0], block)

    @pl.when(part == 0)
    def _():
        mixed = mix_ref[...].astype(bf16)
        middle = x_ref[...].astype(f32) + dot_rows(mixed, w_output[...]) + b_output[...]
        middle_ref[...] = middle
        hat, _ = hat_rows(middle)
        normed_ref[...] = (hat * gain[...] + shift[...]).astype(bf16)
        y_acc[...] = middle + b_reduce[...]
        grad_acc[...] = jnp.zeros_like(grad_acc)
        line_ref[...] = jnp.zeros_like(line_ref)
        line_ref[1:2, :] = column_sums(dy_ref[...].astype(f32))

    normed = normed_ref[...]
    upper = dot_rows(normed, w_expand[...]) + b_expand[...]
    cumulative = 0.5 * lax.erf(upper * math.sqrt(0.5)) + 0.5
    density = jnp.exp(upper * upper * -0.5) * (1.0 / math.sqrt(2.0 * math.pi))
    active = (upper * cumulative).astype(bf16)
    slope = cumulative + upper * density
    y_acc[...] += dot_rows(active, w_reduce[...])
    put(1 + 2 * part, dot_left(active, dy_ref[...]))
    grad_upper = (dot_right(dy_ref[...], w_reduce[...]) * slope).astype(bf16)
    line_ref[pl.ds(4 + part, 1), :] = column_sums(grad_upper.astype(f32))
    put(2 + 2 * part, dot_left(normed, grad_upper))
    grad_acc[...] += dot_right(grad_upper, w_expand[...])

    @pl.when(part == pl.num_programs(0) - 1)
    def _():
        y_ref[...] = y_acc[...].astype(bf16)
        grad = grad_acc[...]
        hat, inverse = hat_rows(middle_ref[...])
        line_ref[2:3, :] = column_sums(grad * hat)
        line_ref[3:4, :] = column_sums(grad)
        dmid = hat_back(grad * gain[...], hat, inverse) + dy_ref[...].astype(f32)
        dmid_ref[...] = dmid
        branch = dmid.astype(bf16)
        line_ref[0:1, :] = column_sums(branch.astype(f32))
        put(0, dot_left(mix_ref[...].astype(bf16), branch))
        end = slice(keep_ref.shape[0] - line_ref.shape[0] // 2, None)
        keep_ref[end, :], send_ref[end, :] = halves(core[0], line_ref[...])
        dmix_ref[...] = dot_right(branch, w_output[...]).astype(bf16)


def feed(core, spare, x, mixed, dy, w_output, w_expand, w_reduce, b_output, b_expand, b_reduce, gain, shift):
    rows, width = x.shape
    hidden = w_expand.shape[1]
    parts = hidden // width
    row = whole((rows, width))
    line = whole((1, width))
    expand = pl.BlockSpec((width, width), lambda i, *_: (0, i))
    reduce = pl.BlockSpec((width, width), lambda i, *_: (i, 0))
    hidden_line = pl.BlockSpec((1, width), lambda i, *_: (0, i))
    weights = ((1 + 2 * parts) * width // 2 + spare, width)
    shape = jax.ShapeDtypeStruct
    return pl.pallas_call(
        feed_kernel,
        grid_spec=pltpu.PrefetchScalarGridSpec(
            num_scalar_prefetch=1,
            grid=(parts,),
            in_specs=[row, row, row, whole((width, width)), expand, reduce, line, hidden_line, line, line, line],
            out_specs=[row, row, row, whole(weights), whole(weights)],
            scratch_shapes=[
                pltpu.VMEM((rows, width), f32),
                pltpu.VMEM((rows, width), bf16),
                pltpu.VMEM((rows, width), f32),
                pltpu.VMEM((rows, width), f32),
                pltpu.VMEM((2 * spare, width), f32),
            ],
        ),
        out_shape=[
            shape((rows, width), bf16),
            shape((rows, width), f32),
            shape((rows, width), bf16),
            shape(weights, bf16),
            shape(weights, bf16),
        ],
        compiler_params=params(1),
        cost_estimate=cost(12 * rows * width * hidden + 6 * rows * width * width, 20 * rows * width, 2 * rows * hidden),
        name="feed",
    )(core, x, mixed, dy, w_output, w_expand, w_reduce, b_output, b_expand, b_reduce, gain, shift)


def gather_parts(refs, part, parts):
    blocks = []
    for ref in refs:
        pairs = ref.shape[1] // (parts * PAIR)
        for pair in range(pairs):
            start = (pair * parts + part) * PAIR
            blocks.append(ref[:, start:start + PAIR])
    return jnp.concatenate(blocks, axis=1)


def other_kernel(cats, w_key, w_value, *rest):
    cat_refs, send_ref = rest[:cats], rest[-1]
    dk = gather_parts(cat_refs, 0, 2)
    dv = gather_parts(cat_refs, 1, 2)
    send_ref[...] = (dot_right(dk, w_key[...]) + dot_right(dv, w_value[...])).astype(bf16)


def other_grads(cats, w_key, w_value, rows, after):
    total, width = cats[0].shape[0], w_key.shape[0]
    step = chunk_of(rows, 272)
    return pl.pallas_call(
        functools.partial(other_kernel, len(cats)),
        grid=(total // step,),
        in_specs=[whole((width, width))] * 2
        + [pl.BlockSpec((step, c.shape[1]), lambda i: (i, 0)) for c in cats]
        + [ANYWHERE] * len(after),
        out_specs=pl.BlockSpec((step, width), lambda i: (i, 0)),
        out_shape=jax.ShapeDtypeStruct((total, width), bf16),
        compiler_params=params(1),
        cost_estimate=cost(4 * total * width * width, 8 * total * width),
        name="other_grads",
    )(w_key, w_value, *cats, *after)


def own_kernel(cats, x_ref, recv_ref, dmid_ref, w_query, w_key, w_value, gain, *rest):
    cat_refs, dx_ref = rest[:cats], rest[-1]
    dk = gather_parts(cat_refs, 0, 3)
    dv = gather_parts(cat_refs, 1, 3)
    dq = gather_parts(cat_refs, 2, 3)
    grad = dot_right(dq, w_query[...]) + dot_right(dk, w_key[...]) + dot_right(dv, w_value[...])
    for index in range(recv_ref.shape[0]):
        grad = grad + recv_ref[index].astype(f32)
    hat, inverse = hat_rows(x_ref[...].astype(f32))
    dx_ref[...] = hat_back(grad * gain[...], hat, inverse) + dmid_ref[...]


def own_grads(x, cats, recv, dmid, w_query, w_key, w_value, gain, after):
    rows, width = x.shape
    step = chunk_of(rows, 272)
    row = pl.BlockSpec((step, width), lambda i: (i, 0))
    return pl.pallas_call(
        functools.partial(own_kernel, len(cats)),
        grid=(rows // step,),
        in_specs=[row, pl.BlockSpec((recv.shape[0], step, width), lambda i: (0, i, 0)), row]
        + [whole((width, width))] * 3
        + [whole((1, width))]
        + [pl.BlockSpec((step, c.shape[1]), lambda i: (i, 0)) for c in cats]
        + [ANYWHERE] * len(after),
        out_specs=row,
        out_shape=jax.ShapeDtypeStruct((rows, width), f32),
        compiler_params=params(1),
        cost_estimate=cost(6 * rows * width * width, 16 * rows * width),
        name="own_grads",
    )(x, recv, dmid, w_query, w_key, w_value, gain, *cats, *after)


class Slice:
    def __init__(self):
        group, rest = lax.axis_size("grp"), lax.axis_size("rest")
        batch = rest * lax.axis_size("core")
        side = 2 if rest % 2 == 0 else 1
        rest //= side
        high = 2 if rest % 2 == 0 else 1
        self.sizes = {"core": 2, "side": side, "member": group, "high": high, "low": rest // high}
        self.count = group * batch
        self.here = self.coords(lax.axis_index(ALL))

    def coords(self, linear):
        out = {}
        for name in ("member", "core", "side", "low", "high"):
            out[name] = linear % self.sizes[name]
            linear = linear // self.sizes[name]
        return out

    def linear(self, coords):
        total = 0
        for name in ("high", "low", "side", "core", "member"):
            total = total * self.sizes[name] + coords[name]
        return total

    def size(self, stage):
        return math.prod(self.sizes[name] for name in stage)

    def place(self, stage, coords=None):
        coords = self.here if coords is None else coords
        total = 0
        for name in stage:
            total = total * self.sizes[name] + coords[name]
        return total

    def send(self, array, stage, shift):
        pairs = []
        for source in range(self.count):
            coords = self.coords(source)
            place = (self.place(stage, coords) + shift) % self.size(stage)
            for name in reversed(stage):
                coords[name] = place % self.sizes[name]
                place //= self.sizes[name]
            pairs.append((source, self.linear(coords)))
        return lax.ppermute(array, ALL, pairs)

    def spread(self, parts, stage):
        return [parts[0]] + [self.send(part, stage, s) for s, part in enumerate(parts) if s > 0]

    def share(self, array, stage):
        return self.spread([array] * self.size(stage), stage)

    def origins(self, stage):
        size = self.size(stage)
        return ((self.place(stage) - jnp.arange(size)) % size).astype(jnp.int32)

    def in_order(self, parts, stage):
        if len(parts) <= 2:
            return parts
        stack = jnp.stack(parts)
        order = self.origins(stage)
        return [lax.dynamic_index_in_dim(stack, order[i], 0, False) for i in range(len(parts))]


def behind(array, *others):
    return lax.optimization_barrier((array, *others))[0]


def cut_kernel(size, groups, pipelined, place, *refs):
    ins, outs = refs[:2 * groups], refs[len(refs) - size:]

    def put(shift, out):
        start = 0
        for index in range(groups):
            keep, came = ins[2 * index], ins[2 * index + 1]
            rows = keep.shape[0] if pipelined else keep.shape[0] // size
            at = 0 if pipelined else pl.multiple_of((place[0] + shift) % size * rows, 16)
            span = pl.ds(at, rows)
            total = keep[span, :].astype(f32) + came[span, :].astype(f32)
            out[start:start + rows, :] = total.astype(bf16)
            start += rows

    for shift, out in enumerate(outs):
        if pipelined:
            pl.when(pl.program_id(0) == shift)(functools.partial(put, shift, out))
        else:
            put(shift, out)


def cut(pairs, place, size, after=(), pipelined=False):
    arrays = [array for pair in pairs for array in pair]
    width = arrays[0].shape[1]
    part = (sum(keep.shape[0] for keep, _ in pairs) // size, width)
    if pipelined:
        in_specs = [
            pl.BlockSpec((a.shape[0] // size, width), lambda s, place: ((place[0] + s) % size, 0))
            for a in arrays
        ]
    else:
        in_specs = [whole(a.shape) for a in arrays]
    return pl.pallas_call(
        functools.partial(cut_kernel, size, len(pairs), pipelined),
        grid_spec=pltpu.PrefetchScalarGridSpec(
            num_scalar_prefetch=1,
            grid=(size if pipelined else 1,),
            in_specs=in_specs + [ANYWHERE] * len(after),
            out_specs=[whole(part)] * size,
        ),
        out_shape=[jax.ShapeDtypeStruct(part, bf16)] * size,
        compiler_params=params(1),
        cost_estimate=cost(size * part[0] * width, 6 * size * part[0] * width),
        name="cut",
    )(jnp.reshape(place, (1,)).astype(jnp.int32), *arrays, *after)


def add_up(parts):
    total = parts[0].astype(f32)
    for part in parts[1:]:
        total = total + part.astype(f32)
    return total.astype(bf16)


def place_pieces(places, core, pieces, flats):
    size = len(pieces) // 2
    for which in range(2):
        target = core[0] if which == 0 else 1 - core[0]
        for index in range(size):
            piece, at = pieces[which * size + index], 0
            for flat in flats:
                rows = flat.shape[1] // size
                span = pl.ds(pl.multiple_of(places[index] * rows, 16), rows)
                flat[target, span, :] = piece[at:at + rows, :]
                at += rows


def feed_weights_kernel(size, places, core, *refs):
    pieces, (dwo_ref, dwe_ref, dwr_ref, *line_refs, dbe_ref, flat) = refs[:2 * size], refs[-9:]
    width = dwo_ref.shape[0]
    half = width // 2
    step = pl.program_id(0)
    parts = pl.num_programs(0) - 1

    @pl.when(step == 0)
    def _():
        place_pieces(places, core, pieces, [flat])

    @pl.when(step < parts)
    def _():
        start = pl.multiple_of((1 + 2 * step) * half, half)
        for side in range(2):
            rows = slice(side * half, (side + 1) * half)
            dwr_ref[rows, :] = flat[side, pl.ds(start, half), :].astype(f32)
            dwe_ref[rows, :] = flat[side, pl.ds(start + half, half), :].astype(f32)

    @pl.when(step == parts)
    def _():
        for side in range(2):
            dwo_ref[side * half:(side + 1) * half, :] = flat[side, :half, :].astype(f32)
        count = dbe_ref.shape[1] // width
        start = (1 + 2 * count) * half
        lines = flat[0, start:start + 16, :].astype(f32)
        for index, ref in enumerate(line_refs):
            ref[...] = lines[index:index + 1]
        for part in range(count):
            dbe_ref[:, part * width:(part + 1) * width] = lines[4 + part:5 + part]


def feed_weights(places, core, own, came, hidden, after):
    rows, width = own[0].shape
    parts = hidden // width
    shapes = [(width, width), (width, hidden), (hidden, width)] + [(1, width)] * 4 + [(1, hidden)]
    out_specs = [whole(s) for s in shapes]
    out_specs[1] = pl.BlockSpec((width, width), lambda p, *_: (0, jnp.minimum(p, parts - 1)))
    out_specs[2] = pl.BlockSpec((width, width), lambda p, *_: (jnp.minimum(p, parts - 1), 0))
    return pl.pallas_call(
        functools.partial(feed_weights_kernel, len(own)),
        grid_spec=pltpu.PrefetchScalarGridSpec(
            num_scalar_prefetch=2,
            grid=(parts + 1,),
            in_specs=[whole((rows, width))] * (2 * len(own)) + [ANYWHERE] * len(after),
            out_specs=out_specs,
            scratch_shapes=[pltpu.VMEM((2, len(own) * rows, width), bf16)],
        ),
        out_shape=[jax.ShapeDtypeStruct(s, f32) for s in shapes],
        compiler_params=params(1),
        cost_estimate=cost(0, 12 * len(own) * rows * width),
        name="feed_weights",
    )(places, core, *own, *came, *after)


def project_weights_kernel(calls, places, core, *refs):
    flats, refs = refs[len(refs) - len(calls):], refs[:len(refs) - len(calls)]
    pieces, refs = refs[:-16], refs[-16:]
    weights, (gain, shift), refs = refs[:3], refs[3:5], refs[5:]
    outs, (dgain_ref, dshift_ref, dbq_ref, dbv_ref), refs = refs[:3], refs[3:7], refs[7:]
    gains, shifts, cross_acc, plain_acc = refs
    pair = pl.program_id(0)
    width = gains.shape[0]
    half = width // 2

    @pl.when(pair == 0)
    def _():
        place_pieces(places, core, pieces, flats)
        gains[...] = jnp.broadcast_to(gain[...], (PAIR, width)).T
        shifts[...] = jnp.broadcast_to(shift[...], (PAIR, width)).T
        cross_acc[...] = jnp.zeros_like(cross_acc)
        plain_acc[...] = jnp.zeros_like(plain_acc)

    def put(flat, pairs, index):
        sums = flat[0, pairs * half:pairs * half + 16, :].astype(f32)[index:index + 1]
        dbv_ref[...] = sums[:, PAIR:2 * PAIR]
        dbq_ref[...] = sums[:, 2 * PAIR:]
        for side in range(2):
            down = slice(side * half, (side + 1) * half)
            block = flat[side, index * half:(index + 1) * half, :].astype(f32)
            for which, (out, weight) in enumerate(zip(outs, weights)):
                lanes = slice(which * PAIR, (which + 1) * PAIR)
                part, line = block[:, lanes], sums[:, lanes]
                out[down, :] = gains[down, :] * part + shifts[down, :] * line
                own = weight[down, :].astype(f32)
                cross_acc[down, :] += own * part
                plain_acc[down, :] += own * line

    first = 0
    for flat, pairs in zip(flats, calls):
        for index in range(pairs):
            pl.when(pair == first + index)(functools.partial(put, flat, pairs, index))
        first += pairs

    @pl.when(pair == PAIRS - 1)
    def _():
        for acc, out in ((cross_acc, dgain_ref), (plain_acc, dshift_ref)):
            column = jnp.broadcast_to(jnp.sum(acc[...], axis=1, keepdims=True), (width, PAIR))
            out[...] = column.T[:1]


def project_weights(places, core, own, came, w_key, w_value, w_query, gain, shift, calls, spare):
    width = w_query.shape[0]
    rows, cat = own[0].shape
    line = whole((1, width))
    column_block = pl.BlockSpec((width, PAIR), lambda p, *_: (0, p))
    line_block = pl.BlockSpec((1, PAIR), lambda p, *_: (0, p))
    return pl.pallas_call(
        functools.partial(project_weights_kernel, calls),
        grid_spec=pltpu.PrefetchScalarGridSpec(
            num_scalar_prefetch=2,
            grid=(PAIRS,),
            in_specs=[whole((rows, cat))] * (2 * len(own)) + [column_block] * 3 + [line] * 2,
            out_specs=[column_block] * 3 + [line] * 2 + [line_block] * 2,
            scratch_shapes=[pltpu.VMEM((width, PAIR), f32)] * 4
            + [pltpu.VMEM((2, count * width // 2 + spare, cat), bf16) for count in calls],
        ),
        out_shape=[jax.ShapeDtypeStruct((width, width), f32)] * 3
        + [jax.ShapeDtypeStruct((1, width), f32)] * 4,
        compiler_params=params(1),
        cost_estimate=cost(0, 20 * width * width),
        name="project_weights",
    )(places, core, *own, *came, w_key, w_value, w_query, gain, shift)


def body(
    layer_input,
    lang_counts,
    w_query,
    w_key,
    w_value,
    w_output,
    w_expand,
    w_reduce,
    b_query,
    b_value,
    b_output,
    b_expand,
    b_reduce,
    gain_attn,
    shift_attn,
    gain_mlp,
    shift_mlp,
    cotangent,
):
    items, own_rows, width = layer_input.shape
    group = lax.axis_size("grp")
    me = lax.axis_index("grp")
    rows = -(-own_rows // 16) * 16
    total = items * rows
    patch_rows = VIEWS * PATCH
    shifts = range(1, group)

    def padded(array):
        if rows != own_rows:
            array = jnp.pad(array, ((0, 0), (0, rows - own_rows), (0, 0)))
        return array.reshape(total, width)

    def unpadded(array):
        return array.reshape(items, rows, width)[:, :own_rows]

    def limit_of(owner):
        return jnp.clip(patch_rows + lang_counts - owner * own_rows, 0, own_rows)

    def line(vector):
        return vector.reshape(1, -1)

    def group_shift(array, shift):
        return lax.ppermute(array, "grp", [(i, (i + shift) % group) for i in range(group)])

    def joined(parts):
        if len(parts) == 1:
            return parts[0]
        return jnp.stack([p.reshape(items, rows, width) for p in parts], 1).reshape(-1, width)

    x = padded(layer_input)
    dy = padded(cotangent)
    others = [group_shift(x, -shift) for shift in shifts]
    own_limits = limit_of(me).reshape(items, 1)
    other_limits = jnp.stack([limit_of((me + shift) % group) for shift in shifts], 1)

    weights = (w_query, w_key, w_value, line(b_query), line(b_value))
    norms = (line(gain_attn), line(shift_attn))
    hat, keys, values, queries = project(x, *norms, *weights, with_query=True)
    first = attend(own_limits, queries, keys, values, rows, 1, None)
    x_other = joined(others)
    hat_other, keys_other, values_other = project(x_other, *norms, *weights, with_query=False)
    mixed, lse = attend(other_limits, queries, keys_other, values_other, rows, group - 1, first)

    devices = Slice()
    plane = ("side", "member")
    core = jnp.reshape(devices.here["core"], (1,)).astype(jnp.int32)
    plane_place, plane_size = devices.place(plane), devices.size(plane)
    spare = 16 * plane_size
    output, dmid, dmix, keep, give = feed(
        core, spare, x, mixed, dy, w_output, w_expand, w_reduce, line(b_output), line(b_expand),
        line(b_reduce), line(gain_mlp), line(shift_mlp),
    )

    def summed(value, stage):
        return add_up(devices.in_order(devices.share(value, (stage,)), (stage,)))

    def back_other(first, count, tokens):
        return attend_back(
            other_limits, core, queries, keys_other, values_other, dmix, mixed, lse, hat_other,
            rows, group - 1, first, count, None, spare, tokens,
        )

    def back_own(first, count, before, tokens):
        return attend_back(
            own_limits, core, queries, keys, values, dmix, mixed, lse, hat,
            rows, 1, first, count, before, spare, tokens,
        )

    feed_pair = devices.spread([keep, give], ("core",))
    other_first = back_other(0, 1, [])
    parts = cut([feed_pair], plane_place, plane_size, other_first[1:2], True)
    other_rest = back_other(1, PAIRS - 1, parts[:1])
    feed_sum = behind(add_up(devices.spread(parts, plane)), other_rest[1])
    cat_first, *pair_first = back_own(0, 1, (other_first, 0), [feed_sum])
    feed_sum = behind(summed(feed_sum, "low"), cat_first)
    send = other_grads([other_first[1], other_rest[1]], w_key, w_value, rows, [feed_sum])
    cat_middle, *pair_middle = back_own(1, PAIRS - 2, (other_rest, 0), [feed_sum, send])
    send = send.reshape(items, group - 1, rows, width)
    received = jnp.stack(
        [group_shift(send[:, shift - 1].reshape(total, width), shift) for shift in shifts]
    )
    pair_first = devices.spread(pair_first, ("core",))
    feed_sum = behind(summed(feed_sum, "high"), cat_middle, pair_first[1])
    cat_last, *pair_last = back_own(PAIRS - 1, 1, (other_rest, PAIRS - 2), [feed_sum, received])
    feed_own = devices.share(feed_sum, plane)
    pairs = [pair_first] + [devices.spread(pair, ("core",)) for pair in (pair_middle, pair_last)]
    parts = devices.spread(cut(pairs, plane_place, plane_size), plane)
    dx = own_grads(
        x, [cat_first, cat_middle, cat_last], received, dmid, w_query, w_key, w_value, line(gain_attn),
        parts[:1],
    )
    value = behind(add_up(parts), dx)
    value = summed(summed(value, "low"), "high")
    project_own = devices.share(value, plane)
    feed_came = [devices.send(behind(piece, value), ("core",), 1) for piece in feed_own]
    places = devices.origins(plane)
    dwo, dwe, dwr, dbo, dbr, dgain_mlp, dshift_mlp, dbe = feed_weights(
        places, core, feed_own, feed_came, w_expand.shape[1], project_own[1:]
    )
    project_came = [devices.send(piece, ("core",), 1) for piece in project_own]
    dwk, dwv, dwq, dgain, dshift, dbq, dbv = project_weights(
        places, core, project_own, project_came, w_key, w_value, w_query, *norms, (1, PAIRS - 2, 1), spare
    )
    small = (dbq, dbv, dbo, dbe, dbr, dgain, dshift, dgain_mlp, dshift_mlp)
    return (
        unpadded(output),
        unpadded(dx),
        dwq, dwk, dwv, dwo, dwe, dwr,
        *(vector.reshape(-1) for vector in small),
    )


def solution(mesh):
    batch, group = mesh.shape["dp"], mesh.shape["grp"]
    mesh = jax.sharding.Mesh(mesh.devices.reshape(batch // 2, 2, group), ALL)
    items = ("rest", "core")
    rows = P(items, "grp", None)
    in_specs = (rows, P(items)) + (P(),) * 15 + (rows,)
    out_specs = (rows, rows) + (P(),) * 15
    return jax.shard_map(body, mesh=mesh, in_specs=in_specs, out_specs=out_specs, check_vma=False)
```

```python
import functools
import math

import jax
import jax.numpy as jnp
from jax import lax
from jax.experimental import pallas as pl
from jax.experimental.pallas import tpu as pltpu
from jax.sharding import PartitionSpec as P

HEADS = 8
HEAD_DIM = 64
VIEWS = 5
PATCH = 400
PAIR = 2 * HEAD_DIM
PAIRS = HEADS // 2
TILE = 256

EPSILON = 1e-05
NEGATIVE = -1e30
SCALE = 1.0 / math.sqrt(HEAD_DIM)

bf16 = jnp.bfloat16
f32 = jnp.float32


def dot_rows(left, right):
    return lax.dot_general(
        left, right, (((1,), (0,)), ((), ())), preferred_element_type=f32
    )


def dot_left(left, right):
    return lax.dot_general(
        left, right, (((0,), (0,)), ((), ())), preferred_element_type=f32
    )


def dot_right(left, right):
    return lax.dot_general(
        left, right, (((1,), (1,)), ((), ())), preferred_element_type=f32
    )


def chunk_of(rows, limit):
    best = 16
    for size in range(16, limit + 1, 16):
        if rows % size == 0:
            best = size
    return best


def hat_rows(matrix):
    center = matrix - jnp.mean(matrix, axis=-1, keepdims=True)
    spread = jnp.mean(center * center, axis=-1, keepdims=True)
    inverse = lax.rsqrt(spread + EPSILON)
    return center * inverse, inverse


def hat_back(grad_hat, hat, inverse):
    mean_grad = jnp.mean(grad_hat, axis=-1, keepdims=True)
    mean_cross = jnp.mean(grad_hat * hat, axis=-1, keepdims=True)
    return inverse * (grad_hat - mean_grad - hat * mean_cross)


def column_sums(matrix):
    return jnp.sum(matrix, axis=0, keepdims=True)


ALL = ("rest", "core", "grp")
VMEM_MIB = 60
ANYWHERE = pl.BlockSpec(memory_space=pl.ANY)


def params(axes):
    return pltpu.CompilerParams(
        dimension_semantics=("arbitrary",) * axes, vmem_limit_bytes=VMEM_MIB << 20
    )


def cost(flops, bytes_accessed, transcendentals=0):
    return pl.CostEstimate(
        flops=int(flops), bytes_accessed=int(bytes_accessed), transcendentals=int(transcendentals)
    )


def whole(shape):
    return pl.BlockSpec(shape, lambda *_: (0,) * len(shape))


def lanes_of(shape):
    return lax.broadcasted_iota(jnp.int32, shape, 1)


def forward_kernel(final, rows, blocks, step, limits, x_ref, gain, shift, w_key, w_value, b_value, *rest):
    if final:
        q_ref, acc_in, top_in, sum_in, *rest = rest
        hat_ref, k_ref, v_ref, out_ref, lse_ref, *rest = rest
    else:
        w_query, b_query, *rest = rest
        hat_ref, k_ref, v_ref, q_ref, acc_out, top_out, sum_out, *rest = rest
    normed, kt_ref, va_ref, *score_refs = rest
    item = pl.program_id(0)
    key_count = rows * blocks
    query_rows = q_ref.shape[0]

    @pl.when(pl.program_id(1) == 0)
    def _():
        hat, _ = hat_rows(x_ref[...].astype(f32))
        hat_ref[...] = hat.astype(bf16)
        normed[...] = (hat * gain[...] + shift[...]).astype(bf16)

    weights = [w_key[...], w_value[...]] if final else [w_key[...], w_value[...], w_query[...]]
    projected = dot_rows(normed[...], jnp.concatenate(weights, axis=1))
    k_ref[...] = projected[:, :PAIR].astype(bf16)
    v_ref[...] = (projected[:, PAIR:2 * PAIR] + b_value[...]).astype(bf16)
    if not final:
        query = (projected[:, 2 * PAIR:] + b_query[...]).astype(bf16)
        q_ref[...] = (query.astype(f32) * SCALE).astype(bf16)
    keys = k_ref[...].astype(f32)
    values = v_ref[...].astype(f32)
    first = lanes_of((key_count, PAIR)) < HEAD_DIM
    flipped = keys.T.astype(bf16)
    key_id = lax.broadcasted_iota(jnp.int32, (8, key_count), 1)
    bias = jnp.zeros((8, key_count), f32)
    for block in range(blocks):
        here = (key_id >= block * rows + limits[item, block]) & (key_id < (block + 1) * rows)
        bias = jnp.where(here, NEGATIVE, bias)
    bias = jnp.where(lax.broadcasted_iota(jnp.int32, (8, key_count), 0) == 0, bias, 0.0)
    spare = jnp.concatenate([bias, jnp.zeros((HEAD_DIM - 8, key_count), f32)], 0).astype(bf16)
    kt_ref[0, :HEAD_DIM, :] = flipped[:HEAD_DIM]
    kt_ref[0, HEAD_DIM:, :] = spare
    kt_ref[1, :HEAD_DIM, :] = spare
    kt_ref[1, HEAD_DIM:, :] = flipped[HEAD_DIM:]
    va_ref[0] = jnp.where(first, values, 1.0).astype(bf16)
    va_ref[1] = jnp.where(first, 1.0, values).astype(bf16)
    lanes = lanes_of((step, PAIR))
    head_first = lanes < HEAD_DIM
    one = jnp.where((lanes & (HEAD_DIM - 1)) == 0, 1.0, 0.0)
    tiles = [slice(t, min(t + TILE, key_count)) for t in range(0, key_count, TILE)]

    def query_of(unit):
        chunk, head = divmod(unit, 2)
        query = q_ref[chunk * step:(chunk + 1) * step, :].astype(f32)
        mine = head_first if head == 0 else jnp.logical_not(head_first)
        return jnp.where(mine, query, one).astype(bf16)

    units = 2 * (query_rows // step)
    outs, tops = [], []
    for unit in range(-1, units):
        query = query_of(unit + 1) if unit + 1 < units else None
        out, best = None, None
        for tile in tiles:
            if query is not None:
                scores = dot_rows(query, kt_ref[(unit + 1) % 2, :, tile])
                score_refs[(unit + 1) % 2][:, tile] = scores
                high = jnp.max(scores, axis=1, keepdims=True)
                best = high if best is None else jnp.maximum(best, high)
            if unit >= 0:
                weights = jnp.exp(score_refs[unit % 2][:, tile] - tops[unit]).astype(bf16)
                added = dot_rows(weights, va_ref[unit % 2, tile, :])
                out = added if out is None else out + added
        if best is not None:
            tops.append(best)
        if out is not None:
            outs.append(out)
        if unit % 2 == 0 or unit < 0:
            continue
        chunk = unit // 2
        place = slice(chunk * step, (chunk + 1) * step)
        acc = jnp.where(head_first, outs[unit - 1], outs[unit])
        total = pltpu.roll(jnp.where(head_first, outs[unit], outs[unit - 1]), HEAD_DIM, 1)
        top = jnp.where(head_first, tops[unit - 1], tops[unit])
        if final:
            other_top = top_in[place, :]
            new_top = jnp.maximum(top, other_top)
            scale_here = jnp.exp(top - new_top)
            scale_there = jnp.exp(other_top - new_top)
            total = total * scale_here + sum_in[place, :] * scale_there
            acc = acc * scale_here + acc_in[place, :] * scale_there
            out_ref[place, :] = acc / total
            lse_ref[place, :] = pltpu.roll(new_top + jnp.log(total), HEAD_DIM, 1)
        else:
            acc_out[place, :] = acc
            top_out[place, :] = top
            sum_out[place, :] = total


def attend(limits, x, norms, w_key, w_value, b_value, query, rows, blocks, before):
    width = x.shape[1]
    key_count = rows * blocks
    items = x.shape[0] // key_count
    total = items * rows
    step = chunk_of(rows, 208)
    query_block = pl.BlockSpec((rows, PAIR), lambda i, p, *_: (i, p))
    key_block = pl.BlockSpec((key_count, PAIR), lambda i, p, *_: (i, p))
    row_block = pl.BlockSpec((key_count, width), lambda i, p, *_: (i, 0))
    weight_block = pl.BlockSpec((width, PAIR), lambda i, p, *_: (0, p))
    line_block = pl.BlockSpec((1, PAIR), lambda i, p, *_: (0, p))
    final = before is not None
    shape = jax.ShapeDtypeStruct
    out_specs = [row_block, key_block, key_block]
    out_shape = [shape(x.shape, bf16)] * 3
    if final:
        extra, extra_specs = [query, *before], [query_block] * (1 + len(before))
        out_specs += [query_block] * 2
        out_shape += [shape((total, width), f32)] * 2
    else:
        extra, extra_specs = list(query), [weight_block, line_block]
        out_specs += [query_block] * 4
        out_shape += [shape((total, width), bf16)] + [shape((total, width), f32)] * 3
    return pl.pallas_call(
        functools.partial(forward_kernel, final, rows, blocks, step),
        grid_spec=pltpu.PrefetchScalarGridSpec(
            num_scalar_prefetch=1,
            grid=(items, PAIRS),
            in_specs=[row_block, whole((1, width)), whole((1, width))]
            + [weight_block] * 2
            + [line_block]
            + extra_specs,
            out_specs=out_specs,
            scratch_shapes=[
                pltpu.VMEM((key_count, width), bf16),
                pltpu.VMEM((2, PAIR, key_count), bf16),
                pltpu.VMEM((2, key_count, PAIR), bf16),
                pltpu.VMEM((step, key_count), f32),
                pltpu.VMEM((step, key_count), f32),
            ],
        ),
        out_shape=out_shape,
        compiler_params=params(2),
        cost_estimate=cost(
            16 * total * key_count * width, 12 * total * width, total * key_count * HEADS
        ),
        name="attend",
    )(limits, x, *norms, w_key, w_value, b_value, *extra)


def split_three(value):
    high = value.astype(bf16).astype(f32)
    rest = value - high
    middle = rest.astype(bf16).astype(f32)
    return high, middle, rest - middle


def halves(core, block):
    half = block.shape[0] // 2
    upper, lower = block[:half], block[half:]
    mine = jnp.where(core == 0, upper, lower)
    theirs = jnp.where(core == 0, lower, upper)
    return mine.astype(bf16), theirs.astype(bf16)


def backward_kernel(
    last, tokens, rows, blocks, step, limits, core,
    q_ref, k_ref, v_ref, g_ref, out_ref, lse_ref, hat_ref, *rest,
):
    if last:
        before_ref, dw_in, sums_in, *rest = rest
        cat_ref, keep_ref, send_ref, dw_acc, sums_acc, qt_ref, gt_ref, dqt_ref, *wide = rest[tokens:]
    else:
        dq_ref, cat_ref, dw_ref, sums_ref, dw_acc, sums_acc, qt_ref, gt_ref, dqt_ref, *wide = rest[tokens:]
    prob_refs, score_refs = wide[:2], wide[2:]
    pair = pl.program_id(0)
    item = pl.program_id(1)
    query_rows = q_ref.shape[0]
    lanes = lanes_of((query_rows, PAIR))
    head_first = lanes < HEAD_DIM
    spare_lane = lanes & (HEAD_DIM - 1)

    def spare(parts, mask_one):
        high, middle, low = parts
        value = jnp.where(spare_lane == 0, high, 0.0)
        value = jnp.where(spare_lane == 1, middle, value)
        value = jnp.where(spare_lane == 2, low, value)
        return jnp.where(spare_lane == 3, mask_one, value)

    query = q_ref[...].astype(f32)
    grad = g_ref[...].astype(f32)
    product = grad * out_ref[...]
    delta_first = jnp.sum(jnp.where(head_first, product, 0.0), axis=1, keepdims=True)
    delta_second = jnp.sum(jnp.where(head_first, 0.0, product), axis=1, keepdims=True)
    delta = jnp.where(head_first, delta_second, delta_first)
    lse_spare = spare(split_three(-lse_ref[...]), 1.0)
    delta_spare = spare(split_three(-delta), 0.0)
    qt_ref[0] = jnp.where(head_first, query, lse_spare).T.astype(bf16)
    qt_ref[1] = jnp.where(head_first, lse_spare, query).T.astype(bf16)
    gt_ref[0] = jnp.where(head_first, grad, delta_spare).T.astype(bf16)
    gt_ref[1] = jnp.where(head_first, delta_spare, grad).T.astype(bf16)
    dqt_ref[...] = jnp.zeros_like(dqt_ref)

    key_lanes = lanes_of((step, PAIR))
    key_first = key_lanes < HEAD_DIM
    key_spare = key_lanes & (HEAD_DIM - 1)
    key_row = lax.broadcasted_iota(jnp.int32, (step, PAIR), 0)
    ones = jnp.where(key_spare < 3, 1.0, 0.0)
    per_block = rows // step
    tiles = [slice(t, min(t + TILE, query_rows)) for t in range(0, query_rows, TILE)]

    def operands(unit):
        chunk, head = divmod(unit, 2)
        place = slice(chunk * step, (chunk + 1) * step)
        block = chunk // per_block
        limit = limits[item, block] - (chunk - block * per_block) * step
        bias = jnp.where(key_row >= limit, NEGATIVE, 0.0)
        key = k_ref[place, :].astype(f32)
        value = v_ref[place, :].astype(f32)
        mine = key_first if head == 0 else jnp.logical_not(key_first)
        key_head = jnp.where(mine, key, jnp.where(key_spare == 3, bias, ones)).astype(bf16)
        value_head = jnp.where(mine, value, ones).astype(bf16)
        half = key.T[head * HEAD_DIM:(head + 1) * HEAD_DIM].astype(bf16)
        return key_head, value_head, half

    units = 2 * blocks * per_block
    dks, dvs, half = [], [], None
    for unit in range(-1, units):
        more = unit + 1 < units
        if more:
            key_head, value_head, next_half = operands(unit + 1)
            which = (unit + 1) % 2
        dk, dv = None, None
        for tile in tiles:
            if more:
                probs = jnp.exp(dot_rows(key_head, qt_ref[which, :, tile]))
                grad_probs = dot_rows(value_head, gt_ref[which, :, tile])
                prob_refs[which][:, tile] = probs.astype(bf16)
                score_refs[which][:, tile] = (probs * grad_probs).astype(bf16)
            if unit >= 0:
                grad_scores = score_refs[unit % 2][:, tile]
                dv_part = dot_rows(prob_refs[unit % 2][:, tile], g_ref[tile, :])
                dk_part = dot_rows(grad_scores, q_ref[tile, :])
                dv = dv_part if dv is None else dv + dv_part
                dk = dk_part if dk is None else dk + dk_part
                own = slice(unit % 2 * HEAD_DIM, (unit % 2 + 1) * HEAD_DIM)
                dqt_ref[own, tile] += dot_rows(half, grad_scores)
        half = next_half if more else None
        if unit >= 0:
            dks.append(dk)
            dvs.append(dv)
        if unit >= 0 and unit % 2 == 1:
            place = slice(unit // 2 * step, (unit // 2 + 1) * step)
            cat_ref[place, :PAIR] = jnp.where(key_first, dks[-2], dks[-1]).astype(bf16)
            cat_ref[place, PAIR:2 * PAIR] = jnp.where(key_first, dvs[-2], dvs[-1]).astype(bf16)

    result = dqt_ref[...].T
    if last:
        cat_ref[:, 2 * PAIR:] = ((result + before_ref[...]) * SCALE).astype(bf16)
    else:
        dq_ref[...] = result
    added = dot_left(hat_ref[...], cat_ref[...])
    sums = column_sums(cat_ref[...].astype(f32))
    items = pl.num_programs(1)
    here = pl.ds(pair, 1)

    @pl.when((item == 0) & (pair == 0))
    def _():
        sums_acc[...] = jnp.zeros_like(sums_acc)

    @pl.when(item == 0)
    def _():
        dw_acc[...] = added
        if last:
            dw_acc[:, :2 * PAIR] += dw_in[0]
            sums_acc[here, :2 * PAIR] = sums_in[0, :1, :]

    @pl.when(item > 0)
    def _():
        dw_acc[...] += added

    sums_acc[here, :] += sums

    @pl.when(item == items - 1)
    def _():
        if last:
            half = dw_acc.shape[0] // 2
            place = pl.ds(pl.multiple_of(pair * half, half), half)
            keep_ref[place, :], send_ref[place, :] = halves(core[0], dw_acc[...])
        else:
            dw_ref[0] = dw_acc[...]
            sums_ref[0] = jnp.broadcast_to(sums_acc[here, :], sums_ref.shape[1:])

    if last:

        @pl.when((item == items - 1) & (pair == pl.num_programs(0) - 1))
        def _():
            end = slice(keep_ref.shape[0] - sums_acc.shape[0] // 2, None)
            keep_ref[end, :], send_ref[end, :] = halves(core[0], sums_acc[...])


def attend_back(
    limits, core, queries, keys, values, grads, outs, lse, hat, rows, blocks, first, count, before,
    spare, tokens,
):
    total, width = queries.shape
    items = total // rows
    key_count = rows * blocks
    step = chunk_of(rows, 208)
    last = before is not None
    cat = (3 if last else 2) * PAIR
    query_block = pl.BlockSpec((rows, PAIR), lambda p, i, *_: (i, first + p))
    key_block = pl.BlockSpec((key_count, PAIR), lambda p, i, *_: (i, first + p))
    hat_block = pl.BlockSpec((key_count, width), lambda p, i, *_: (i, 0))
    cat_block = pl.BlockSpec((key_count, cat), lambda p, i, *_: (i, p))
    shape = jax.ShapeDtypeStruct
    cat_shape = shape((total * blocks, cat * count), bf16)
    if last:
        (part, _, dw_part, sums_part), skip = before
        extra = [part, dw_part, sums_part]
        extra_specs = [
            pl.BlockSpec((rows, PAIR), lambda p, i, *_: (i, skip + p)),
            pl.BlockSpec((1, width, 2 * PAIR), lambda p, i, *_: (skip + p, 0, 0)),
            pl.BlockSpec((1, 8, 2 * PAIR), lambda p, i, *_: (skip + p, 0, 0)),
        ]
        half = (count * width // 2 + spare, cat)
        out_shape = [cat_shape] + [shape(half, bf16)] * 2
        out_specs = [cat_block] + [whole(half)] * 2
    else:
        extra, extra_specs = [], []
        out_shape = [
            shape((total, PAIR * count), f32),
            cat_shape,
            shape((count, width, cat), f32),
            shape((count, 8, cat), f32),
        ]
        out_specs = [
            pl.BlockSpec((rows, PAIR), lambda p, i, *_: (i, p)),
            cat_block,
            pl.BlockSpec((1, width, cat), lambda p, i, *_: (p, 0, 0)),
            pl.BlockSpec((1, 8, cat), lambda p, i, *_: (p, 0, 0)),
        ]
    return pl.pallas_call(
        functools.partial(backward_kernel, last, len(tokens), rows, blocks, step),
        grid_spec=pltpu.PrefetchScalarGridSpec(
            num_scalar_prefetch=2,
            grid=(count, items),
            in_specs=[query_block, key_block, key_block]
            + [query_block] * 3
            + [hat_block]
            + extra_specs
            + [ANYWHERE] * len(tokens),
            out_specs=out_specs,
            scratch_shapes=[
                pltpu.VMEM((width, cat), f32),
                pltpu.VMEM((2 * spare, cat), f32),
                pltpu.VMEM((2, PAIR, rows), bf16),
                pltpu.VMEM((2, PAIR, rows), bf16),
                pltpu.VMEM((PAIR, rows), f32),
            ]
            + [pltpu.VMEM((step, rows), bf16)] * 4,
        ),
        out_shape=out_shape,
        compiler_params=params(2),
        cost_estimate=cost(
            40 * total * key_count * PAIR * count,
            16 * total * PAIR * count,
            2 * total * key_count * count,
        ),
        name="attend_back",
    )(limits, core, queries, keys, values, grads, outs, lse, hat, *extra, *tokens)


def feed_kernel(
    core, x_ref, mix_ref, dy_ref, w_output, w_expand, w_reduce, b_output, b_expand, b_reduce, gain, shift,
    y_ref, dmid_ref, dmix_ref, keep_ref, send_ref,
    middle_ref, normed_ref, y_acc, grad_acc, line_ref,
):
    part = pl.program_id(0)

    half = w_output.shape[0] // 2

    def put(index, block):
        place = pl.ds(pl.multiple_of(index * half, half), half)
        keep_ref[place, :], send_ref[place, :] = halves(core[0], block)

    @pl.when(part == 0)
    def _():
        mixed = mix_ref[...].astype(bf16)
        middle = x_ref[...].astype(f32) + dot_rows(mixed, w_output[...]) + b_output[...]
        middle_ref[...] = middle
        hat, _ = hat_rows(middle)
        normed_ref[...] = (hat * gain[...] + shift[...]).astype(bf16)
        y_acc[...] = middle + b_reduce[...]
        grad_acc[...] = jnp.zeros_like(grad_acc)
        line_ref[...] = jnp.zeros_like(line_ref)
        line_ref[1:2, :] = column_sums(dy_ref[...].astype(f32))

    normed = normed_ref[...]
    upper = dot_rows(normed, w_expand[...]) + b_expand[...]
    cumulative = 0.5 * lax.erf(upper * math.sqrt(0.5)) + 0.5
    density = jnp.exp(upper * upper * -0.5) * (1.0 / math.sqrt(2.0 * math.pi))
    active = (upper * cumulative).astype(bf16)
    slope = cumulative + upper * density
    y_acc[...] += dot_rows(active, w_reduce[...])
    put(1 + 2 * part, dot_left(active, dy_ref[...]))
    grad_upper = (dot_right(dy_ref[...], w_reduce[...]) * slope).astype(bf16)
    line_ref[pl.ds(4 + part, 1), :] = column_sums(grad_upper.astype(f32))
    put(2 + 2 * part, dot_left(normed, grad_upper))
    grad_acc[...] += dot_right(grad_upper, w_expand[...])

    @pl.when(part == pl.num_programs(0) - 1)
    def _():
        y_ref[...] = y_acc[...].astype(bf16)
        grad = grad_acc[...]
        hat, inverse = hat_rows(middle_ref[...])
        line_ref[2:3, :] = column_sums(grad * hat)
        line_ref[3:4, :] = column_sums(grad)
        dmid = hat_back(grad * gain[...], hat, inverse) + dy_ref[...].astype(f32)
        dmid_ref[...] = dmid
        branch = dmid.astype(bf16)
        line_ref[0:1, :] = column_sums(branch.astype(f32))
        put(0, dot_left(mix_ref[...].astype(bf16), branch))
        end = slice(keep_ref.shape[0] - line_ref.shape[0] // 2, None)
        keep_ref[end, :], send_ref[end, :] = halves(core[0], line_ref[...])
        dmix_ref[...] = dot_right(branch, w_output[...]).astype(bf16)


def feed(core, spare, x, mixed, dy, w_output, w_expand, w_reduce, b_output, b_expand, b_reduce, gain, shift):
    rows, width = x.shape
    hidden = w_expand.shape[1]
    parts = hidden // width
    row = whole((rows, width))
    line = whole((1, width))
    expand = pl.BlockSpec((width, width), lambda i, *_: (0, i))
    reduce = pl.BlockSpec((width, width), lambda i, *_: (i, 0))
    hidden_line = pl.BlockSpec((1, width), lambda i, *_: (0, i))
    weights = ((1 + 2 * parts) * width // 2 + spare, width)
    shape = jax.ShapeDtypeStruct
    return pl.pallas_call(
        feed_kernel,
        grid_spec=pltpu.PrefetchScalarGridSpec(
            num_scalar_prefetch=1,
            grid=(parts,),
            in_specs=[row, row, row, whole((width, width)), expand, reduce, line, hidden_line, line, line, line],
            out_specs=[row, row, row, whole(weights), whole(weights)],
            scratch_shapes=[
                pltpu.VMEM((rows, width), f32),
                pltpu.VMEM((rows, width), bf16),
                pltpu.VMEM((rows, width), f32),
                pltpu.VMEM((rows, width), f32),
                pltpu.VMEM((2 * spare, width), f32),
            ],
        ),
        out_shape=[
            shape((rows, width), bf16),
            shape((rows, width), f32),
            shape((rows, width), bf16),
            shape(weights, bf16),
            shape(weights, bf16),
        ],
        compiler_params=params(1),
        cost_estimate=cost(12 * rows * width * hidden + 6 * rows * width * width, 20 * rows * width, 2 * rows * hidden),
        name="feed",
    )(core, x, mixed, dy, w_output, w_expand, w_reduce, b_output, b_expand, b_reduce, gain, shift)


def gather_parts(refs, part, parts):
    blocks = []
    for ref in refs:
        pairs = ref.shape[1] // (parts * PAIR)
        for pair in range(pairs):
            start = (pair * parts + part) * PAIR
            blocks.append(ref[:, start:start + PAIR])
    return jnp.concatenate(blocks, axis=1)


def other_kernel(cats, w_key, w_value, *rest):
    cat_refs, send_ref = rest[:cats], rest[-1]
    dk = gather_parts(cat_refs, 0, 2)
    dv = gather_parts(cat_refs, 1, 2)
    send_ref[...] = (dot_right(dk, w_key[...]) + dot_right(dv, w_value[...])).astype(bf16)


def other_grads(cats, w_key, w_value, rows, after):
    total, width = cats[0].shape[0], w_key.shape[0]
    step = chunk_of(rows, 272)
    return pl.pallas_call(
        functools.partial(other_kernel, len(cats)),
        grid=(total // step,),
        in_specs=[whole((width, width))] * 2
        + [pl.BlockSpec((step, c.shape[1]), lambda i: (i, 0)) for c in cats]
        + [ANYWHERE] * len(after),
        out_specs=pl.BlockSpec((step, width), lambda i: (i, 0)),
        out_shape=jax.ShapeDtypeStruct((total, width), bf16),
        compiler_params=params(1),
        cost_estimate=cost(4 * total * width * width, 8 * total * width),
        name="other_grads",
    )(w_key, w_value, *cats, *after)


def own_kernel(cats, x_ref, recv_ref, dmid_ref, w_query, w_key, w_value, gain, *rest):
    cat_refs, dx_ref = rest[:cats], rest[-1]
    dk = gather_parts(cat_refs, 0, 3)
    dv = gather_parts(cat_refs, 1, 3)
    dq = gather_parts(cat_refs, 2, 3)
    grad = dot_right(dq, w_query[...]) + dot_right(dk, w_key[...]) + dot_right(dv, w_value[...])
    for index in range(recv_ref.shape[0]):
        grad = grad + recv_ref[index].astype(f32)
    hat, inverse = hat_rows(x_ref[...].astype(f32))
    dx_ref[...] = hat_back(grad * gain[...], hat, inverse) + dmid_ref[...]


def own_grads(x, cats, recv, dmid, w_query, w_key, w_value, gain, after):
    rows, width = x.shape
    step = chunk_of(rows, 272)
    row = pl.BlockSpec((step, width), lambda i: (i, 0))
    return pl.pallas_call(
        functools.partial(own_kernel, len(cats)),
        grid=(rows // step,),
        in_specs=[row, pl.BlockSpec((recv.shape[0], step, width), lambda i: (0, i, 0)), row]
        + [whole((width, width))] * 3
        + [whole((1, width))]
        + [pl.BlockSpec((step, c.shape[1]), lambda i: (i, 0)) for c in cats]
        + [ANYWHERE] * len(after),
        out_specs=row,
        out_shape=jax.ShapeDtypeStruct((rows, width), f32),
        compiler_params=params(1),
        cost_estimate=cost(6 * rows * width * width, 16 * rows * width),
        name="own_grads",
    )(x, recv, dmid, w_query, w_key, w_value, gain, *cats, *after)


class Slice:
    def __init__(self):
        group, rest = lax.axis_size("grp"), lax.axis_size("rest")
        batch = rest * lax.axis_size("core")
        side = 2 if rest % 2 == 0 else 1
        rest //= side
        high = 2 if rest % 2 == 0 else 1
        self.sizes = {"core": 2, "side": side, "member": group, "high": high, "low": rest // high}
        self.count = group * batch
        self.here = self.coords(lax.axis_index(ALL))

    def coords(self, linear):
        out = {}
        for name in ("member", "core", "side", "low", "high"):
            out[name] = linear % self.sizes[name]
            linear = linear // self.sizes[name]
        return out

    def linear(self, coords):
        total = 0
        for name in ("high", "low", "side", "core", "member"):
            total = total * self.sizes[name] + coords[name]
        return total

    def size(self, stage):
        return math.prod(self.sizes[name] for name in stage)

    def place(self, stage, coords=None):
        coords = self.here if coords is None else coords
        total = 0
        for name in stage:
            total = total * self.sizes[name] + coords[name]
        return total

    def send(self, array, stage, shift):
        pairs = []
        for source in range(self.count):
            coords = self.coords(source)
            place = (self.place(stage, coords) + shift) % self.size(stage)
            for name in reversed(stage):
                coords[name] = place % self.sizes[name]
                place //= self.sizes[name]
            pairs.append((source, self.linear(coords)))
        return lax.ppermute(array, ALL, pairs)

    def spread(self, parts, stage):
        return [parts[0]] + [self.send(part, stage, s) for s, part in enumerate(parts) if s > 0]

    def share(self, array, stage):
        return self.spread([array] * self.size(stage), stage)

    def origins(self, stage):
        size = self.size(stage)
        return ((self.place(stage) - jnp.arange(size)) % size).astype(jnp.int32)

    def in_order(self, parts, stage):
        if len(parts) <= 2:
            return parts
        stack = jnp.stack(parts)
        order = self.origins(stage)
        return [lax.dynamic_index_in_dim(stack, order[i], 0, False) for i in range(len(parts))]


def behind(array, *others):
    return lax.optimization_barrier((array, *others))[0]


def cut_kernel(size, groups, pipelined, place, *refs):
    ins, outs = refs[:2 * groups], refs[len(refs) - size:]

    def put(shift, out):
        start = 0
        for index in range(groups):
            keep, came = ins[2 * index], ins[2 * index + 1]
            rows = keep.shape[0] if pipelined else keep.shape[0] // size
            at = 0 if pipelined else pl.multiple_of((place[0] + shift) % size * rows, 16)
            span = pl.ds(at, rows)
            total = keep[span, :].astype(f32) + came[span, :].astype(f32)
            out[start:start + rows, :] = total.astype(bf16)
            start += rows

    for shift, out in enumerate(outs):
        if pipelined:
            pl.when(pl.program_id(0) == shift)(functools.partial(put, shift, out))
        else:
            put(shift, out)


def cut(pairs, place, size, after=(), pipelined=False):
    arrays = [array for pair in pairs for array in pair]
    width = arrays[0].shape[1]
    part = (sum(keep.shape[0] for keep, _ in pairs) // size, width)
    if pipelined:
        in_specs = [
            pl.BlockSpec((a.shape[0] // size, width), lambda s, place: ((place[0] + s) % size, 0))
            for a in arrays
        ]
    else:
        in_specs = [whole(a.shape) for a in arrays]
    return pl.pallas_call(
        functools.partial(cut_kernel, size, len(pairs), pipelined),
        grid_spec=pltpu.PrefetchScalarGridSpec(
            num_scalar_prefetch=1,
            grid=(size if pipelined else 1,),
            in_specs=in_specs + [ANYWHERE] * len(after),
            out_specs=[whole(part)] * size,
        ),
        out_shape=[jax.ShapeDtypeStruct(part, bf16)] * size,
        compiler_params=params(1),
        cost_estimate=cost(size * part[0] * width, 6 * size * part[0] * width),
        name="cut",
    )(jnp.reshape(place, (1,)).astype(jnp.int32), *arrays, *after)


def add_up(parts):
    total = parts[0].astype(f32)
    for part in parts[1:]:
        total = total + part.astype(f32)
    return total.astype(bf16)


def place_pieces(places, core, pieces, flats):
    size = len(pieces) // 2
    for which in range(2):
        target = core[0] if which == 0 else 1 - core[0]
        for index in range(size):
            piece, at = pieces[which * size + index], 0
            for flat in flats:
                rows = flat.shape[1] // size
                span = pl.ds(pl.multiple_of(places[index] * rows, 16), rows)
                flat[target, span, :] = piece[at:at + rows, :]
                at += rows


def feed_weights_kernel(size, places, core, *refs):
    pieces, (dwo_ref, dwe_ref, dwr_ref, *line_refs, dbe_ref, flat) = refs[:2 * size], refs[-9:]
    width = dwo_ref.shape[0]
    half = width // 2
    step = pl.program_id(0)
    parts = pl.num_programs(0) - 1

    @pl.when(step == 0)
    def _():
        place_pieces(places, core, pieces, [flat])

    @pl.when(step < parts)
    def _():
        start = pl.multiple_of((1 + 2 * step) * half, half)
        for side in range(2):
            rows = slice(side * half, (side + 1) * half)
            dwr_ref[rows, :] = flat[side, pl.ds(start, half), :].astype(f32)
            dwe_ref[rows, :] = flat[side, pl.ds(start + half, half), :].astype(f32)

    @pl.when(step == parts)
    def _():
        for side in range(2):
            dwo_ref[side * half:(side + 1) * half, :] = flat[side, :half, :].astype(f32)
        count = dbe_ref.shape[1] // width
        start = (1 + 2 * count) * half
        lines = flat[0, start:start + 16, :].astype(f32)
        for index, ref in enumerate(line_refs):
            ref[...] = lines[index:index + 1]
        for part in range(count):
            dbe_ref[:, part * width:(part + 1) * width] = lines[4 + part:5 + part]


def feed_weights(places, core, own, came, hidden, after):
    rows, width = own[0].shape
    parts = hidden // width
    shapes = [(width, width), (width, hidden), (hidden, width)] + [(1, width)] * 4 + [(1, hidden)]
    out_specs = [whole(s) for s in shapes]
    out_specs[1] = pl.BlockSpec((width, width), lambda p, *_: (0, jnp.minimum(p, parts - 1)))
    out_specs[2] = pl.BlockSpec((width, width), lambda p, *_: (jnp.minimum(p, parts - 1), 0))
    return pl.pallas_call(
        functools.partial(feed_weights_kernel, len(own)),
        grid_spec=pltpu.PrefetchScalarGridSpec(
            num_scalar_prefetch=2,
            grid=(parts + 1,),
            in_specs=[whole((rows, width))] * (2 * len(own)) + [ANYWHERE] * len(after),
            out_specs=out_specs,
            scratch_shapes=[pltpu.VMEM((2, len(own) * rows, width), bf16)],
        ),
        out_shape=[jax.ShapeDtypeStruct(s, f32) for s in shapes],
        compiler_params=params(1),
        cost_estimate=cost(0, 12 * len(own) * rows * width),
        name="feed_weights",
    )(places, core, *own, *came, *after)


def project_weights_kernel(calls, places, core, *refs):
    flats, refs = refs[len(refs) - len(calls):], refs[:len(refs) - len(calls)]
    pieces, refs = refs[:-16], refs[-16:]
    weights, (gain, shift), refs = refs[:3], refs[3:5], refs[5:]
    outs, (dgain_ref, dshift_ref, dbq_ref, dbv_ref), refs = refs[:3], refs[3:7], refs[7:]
    gains, shifts, cross_acc, plain_acc = refs
    pair = pl.program_id(0)
    width = gains.shape[0]
    half = width // 2

    @pl.when(pair == 0)
    def _():
        place_pieces(places, core, pieces, flats)
        gains[...] = jnp.broadcast_to(gain[...], (PAIR, width)).T
        shifts[...] = jnp.broadcast_to(shift[...], (PAIR, width)).T
        cross_acc[...] = jnp.zeros_like(cross_acc)
        plain_acc[...] = jnp.zeros_like(plain_acc)

    def put(flat, pairs, index):
        sums = flat[0, pairs * half:pairs * half + 16, :].astype(f32)[index:index + 1]
        dbv_ref[...] = sums[:, PAIR:2 * PAIR]
        dbq_ref[...] = sums[:, 2 * PAIR:]
        for side in range(2):
            down = slice(side * half, (side + 1) * half)
            block = flat[side, index * half:(index + 1) * half, :].astype(f32)
            for which, (out, weight) in enumerate(zip(outs, weights)):
                lanes = slice(which * PAIR, (which + 1) * PAIR)
                part, line = block[:, lanes], sums[:, lanes]
                out[down, :] = gains[down, :] * part + shifts[down, :] * line
                own = weight[down, :].astype(f32)
                cross_acc[down, :] += own * part
                plain_acc[down, :] += own * line

    first = 0
    for flat, pairs in zip(flats, calls):
        for index in range(pairs):
            pl.when(pair == first + index)(functools.partial(put, flat, pairs, index))
        first += pairs

    @pl.when(pair == PAIRS - 1)
    def _():
        for acc, out in ((cross_acc, dgain_ref), (plain_acc, dshift_ref)):
            column = jnp.broadcast_to(jnp.sum(acc[...], axis=1, keepdims=True), (width, PAIR))
            out[...] = column.T[:1]


def project_weights(places, core, own, came, w_key, w_value, w_query, gain, shift, calls, spare):
    width = w_query.shape[0]
    rows, cat = own[0].shape
    line = whole((1, width))
    column_block = pl.BlockSpec((width, PAIR), lambda p, *_: (0, p))
    line_block = pl.BlockSpec((1, PAIR), lambda p, *_: (0, p))
    return pl.pallas_call(
        functools.partial(project_weights_kernel, calls),
        grid_spec=pltpu.PrefetchScalarGridSpec(
            num_scalar_prefetch=2,
            grid=(PAIRS,),
            in_specs=[whole((rows, cat))] * (2 * len(own)) + [column_block] * 3 + [line] * 2,
            out_specs=[column_block] * 3 + [line] * 2 + [line_block] * 2,
            scratch_shapes=[pltpu.VMEM((width, PAIR), f32)] * 4
            + [pltpu.VMEM((2, count * width // 2 + spare, cat), bf16) for count in calls],
        ),
        out_shape=[jax.ShapeDtypeStruct((width, width), f32)] * 3
        + [jax.ShapeDtypeStruct((1, width), f32)] * 4,
        compiler_params=params(1),
        cost_estimate=cost(0, 20 * width * width),
        name="project_weights",
    )(places, core, *own, *came, w_key, w_value, w_query, gain, shift)


def body(
    layer_input,
    lang_counts,
    w_query,
    w_key,
    w_value,
    w_output,
    w_expand,
    w_reduce,
    b_query,
    b_value,
    b_output,
    b_expand,
    b_reduce,
    gain_attn,
    shift_attn,
    gain_mlp,
    shift_mlp,
    cotangent,
):
    items, own_rows, width = layer_input.shape
    group = lax.axis_size("grp")
    me = lax.axis_index("grp")
    rows = -(-own_rows // 16) * 16
    total = items * rows
    patch_rows = VIEWS * PATCH
    shifts = range(1, group)

    def padded(array):
        if rows != own_rows:
            array = jnp.pad(array, ((0, 0), (0, rows - own_rows), (0, 0)))
        return array.reshape(total, width)

    def unpadded(array):
        return array.reshape(items, rows, width)[:, :own_rows]

    def limit_of(owner):
        return jnp.clip(patch_rows + lang_counts - owner * own_rows, 0, own_rows)

    def line(vector):
        return vector.reshape(1, -1)

    def group_shift(array, shift):
        return lax.ppermute(array, "grp", [(i, (i + shift) % group) for i in range(group)])

    def joined(parts):
        if len(parts) == 1:
            return parts[0]
        return jnp.stack([p.reshape(items, rows, width) for p in parts], 1).reshape(-1, width)

    x = padded(layer_input)
    dy = padded(cotangent)
    others = [group_shift(x, -shift) for shift in shifts]
    own_limits = limit_of(me).reshape(items, 1)
    other_limits = jnp.stack([limit_of((me + shift) % group) for shift in shifts], 1)

    norms = (line(gain_attn), line(shift_attn))
    hat, keys, values, queries, *first = attend(
        own_limits, x, norms, w_key, w_value, line(b_value), (w_query, line(b_query)), rows, 1, None
    )
    hat_other, keys_other, values_other, mixed, lse = attend(
        other_limits, joined(others), norms, w_key, w_value, line(b_value), queries, rows, group - 1, first
    )

    devices = Slice()
    plane = ("side", "member")
    core = jnp.reshape(devices.here["core"], (1,)).astype(jnp.int32)
    plane_place, plane_size = devices.place(plane), devices.size(plane)
    spare = 16 * plane_size
    output, dmid, dmix, keep, give = feed(
        core, spare, x, mixed, dy, w_output, w_expand, w_reduce, line(b_output), line(b_expand),
        line(b_reduce), line(gain_mlp), line(shift_mlp),
    )

    def summed(value, stage):
        return add_up(devices.in_order(devices.share(value, (stage,)), (stage,)))

    def back_other(first, count, tokens):
        return attend_back(
            other_limits, core, queries, keys_other, values_other, dmix, mixed, lse, hat_other,
            rows, group - 1, first, count, None, spare, tokens,
        )

    def back_own(first, count, before, tokens):
        return attend_back(
            own_limits, core, queries, keys, values, dmix, mixed, lse, hat,
            rows, 1, first, count, before, spare, tokens,
        )

    feed_pair = devices.spread([keep, give], ("core",))
    other_first = back_other(0, 1, [])
    parts = cut([feed_pair], plane_place, plane_size, other_first[1:2], True)
    other_rest = back_other(1, PAIRS - 1, parts[:1])
    feed_sum = behind(add_up(devices.spread(parts, plane)), other_rest[1])
    cat_first, *pair_first = back_own(0, 1, (other_first, 0), [feed_sum])
    feed_sum = behind(summed(feed_sum, "low"), cat_first)
    send = other_grads([other_first[1], other_rest[1]], w_key, w_value, rows, [feed_sum])
    cat_middle, *pair_middle = back_own(1, PAIRS - 2, (other_rest, 0), [feed_sum, send])
    send = send.reshape(items, group - 1, rows, width)
    received = jnp.stack(
        [group_shift(send[:, shift - 1].reshape(total, width), shift) for shift in shifts]
    )
    pair_first = devices.spread(pair_first, ("core",))
    feed_sum = behind(summed(feed_sum, "high"), cat_middle, pair_first[1])
    feed_own = devices.share(feed_sum, plane)
    pairs = [pair_first, devices.spread(pair_middle, ("core",))]
    parts = cut(pairs, plane_place, plane_size, [feed_sum])
    cat_last, *pair_last = back_own(PAIRS - 1, 1, (other_rest, PAIRS - 2), [feed_sum, received, parts[0]])
    parts = devices.spread(parts, plane)
    dx = own_grads(
        x, [cat_first, cat_middle, cat_last], received, dmid, w_query, w_key, w_value, line(gain_attn), []
    )
    last = cut(
        [devices.spread(pair_last, ("core",))], plane_place, plane_size, [dx, *feed_own, *parts[1:]]
    )
    last = devices.spread(last, plane)
    value = jnp.concatenate([add_up(parts), add_up(last)], 0)
    value = summed(value, "low")
    feed_came = [devices.send(behind(piece, value), ("core",), 1) for piece in feed_own]
    places = devices.origins(plane)
    dwo, dwe, dwr, dbo, dbr, dgain_mlp, dshift_mlp, dbe = feed_weights(
        places, core, feed_own, feed_came, w_expand.shape[1], []
    )
    first, *came = devices.in_order(devices.share(value, ("high",)), ("high",))
    value = add_up([behind(first, dwo), *came])
    project_own = devices.share(value, plane)
    project_came = [devices.send(piece, ("core",), 1) for piece in project_own]
    dwk, dwv, dwq, dgain, dshift, dbq, dbv = project_weights(
        places, core, project_own, project_came, w_key, w_value, w_query, *norms, (1, PAIRS - 2, 1), spare
    )
    small = (dbq, dbv, dbo, dbe, dbr, dgain, dshift, dgain_mlp, dshift_mlp)
    return (
        unpadded(output),
        unpadded(dx),
        dwq, dwk, dwv, dwo, dwe, dwr,
        *(vector.reshape(-1) for vector in small),
    )


def solution(mesh):
    batch, group = mesh.shape["dp"], mesh.shape["grp"]
    mesh = jax.sharding.Mesh(mesh.devices.reshape(batch // 2, 2, group), ALL)
    items = ("rest", "core")
    rows = P(items, "grp", None)
    in_specs = (rows, P(items)) + (P(),) * 15 + (rows,)
    out_specs = (rows, rows) + (P(),) * 15
    return jax.shard_map(body, mesh=mesh, in_specs=in_specs, out_specs=out_specs, check_vma=False)
```

```python
import functools
import math

import jax
import jax.numpy as jnp
from jax import lax
from jax.experimental import pallas as pl
from jax.experimental.pallas import tpu as pltpu
from jax.sharding import PartitionSpec as P

HEADS = 8
HEAD_DIM = 64
VIEWS = 5
PATCH = 400
PAIR = 2 * HEAD_DIM
PAIRS = HEADS // 2
TILE = 256

EPSILON = 1e-05
NEGATIVE = -1e30
SCALE = 1.0 / math.sqrt(HEAD_DIM)

bf16 = jnp.bfloat16
f32 = jnp.float32


def dot_rows(left, right):
    return lax.dot_general(
        left, right, (((1,), (0,)), ((), ())), preferred_element_type=f32
    )


def dot_left(left, right):
    return lax.dot_general(
        left, right, (((0,), (0,)), ((), ())), preferred_element_type=f32
    )


def dot_right(left, right):
    return lax.dot_general(
        left, right, (((1,), (1,)), ((), ())), preferred_element_type=f32
    )


def chunk_of(rows, limit):
    best = 16
    for size in range(16, limit + 1, 16):
        if rows % size == 0:
            best = size
    return best


def hat_rows(matrix):
    center = matrix - jnp.mean(matrix, axis=-1, keepdims=True)
    spread = jnp.mean(center * center, axis=-1, keepdims=True)
    inverse = lax.rsqrt(spread + EPSILON)
    return center * inverse, inverse


def hat_back(grad_hat, hat, inverse):
    mean_grad = jnp.mean(grad_hat, axis=-1, keepdims=True)
    mean_cross = jnp.mean(grad_hat * hat, axis=-1, keepdims=True)
    return inverse * (grad_hat - mean_grad - hat * mean_cross)


def column_sums(matrix):
    return jnp.sum(matrix, axis=0, keepdims=True)


ALL = ("rest", "core", "grp")
VMEM_MIB = 60
ANYWHERE = pl.BlockSpec(memory_space=pl.ANY)


def params(axes):
    return pltpu.CompilerParams(
        dimension_semantics=("arbitrary",) * axes, vmem_limit_bytes=VMEM_MIB << 20
    )


def cost(flops, bytes_accessed, transcendentals=0):
    return pl.CostEstimate(
        flops=int(flops), bytes_accessed=int(bytes_accessed), transcendentals=int(transcendentals)
    )


def whole(shape):
    return pl.BlockSpec(shape, lambda *_: (0,) * len(shape))


def lanes_of(shape):
    return lax.broadcasted_iota(jnp.int32, shape, 1)


def forward_kernel(final, rows, blocks, step, limits, x_ref, gain, shift, w_key, w_value, b_value, *rest):
    if final:
        q_ref, acc_in, top_in, sum_in, *rest = rest
        hat_ref, k_ref, v_ref, out_ref, lse_ref, *rest = rest
    else:
        w_query, b_query, *rest = rest
        hat_ref, k_ref, v_ref, q_ref, acc_out, top_out, sum_out, *rest = rest
    normed, kt_ref, va_ref, *score_refs = rest
    item = pl.program_id(0)
    key_count = rows * blocks
    query_rows = q_ref.shape[0]

    @pl.when(pl.program_id(1) == 0)
    def _():
        hat, _ = hat_rows(x_ref[...].astype(f32))
        hat_ref[...] = hat.astype(bf16)
        normed[...] = (hat * gain[...] + shift[...]).astype(bf16)

    weights = [w_key[...], w_value[...]] if final else [w_key[...], w_value[...], w_query[...]]
    projected = dot_rows(normed[...], jnp.concatenate(weights, axis=1))
    k_ref[...] = projected[:, :PAIR].astype(bf16)
    v_ref[...] = (projected[:, PAIR:2 * PAIR] + b_value[...]).astype(bf16)
    if not final:
        query = (projected[:, 2 * PAIR:] + b_query[...]).astype(bf16)
        q_ref[...] = (query.astype(f32) * SCALE).astype(bf16)
    keys = k_ref[...].astype(f32)
    values = v_ref[...].astype(f32)
    first = lanes_of((key_count, PAIR)) < HEAD_DIM
    flipped = keys.T.astype(bf16)
    key_id = lax.broadcasted_iota(jnp.int32, (8, key_count), 1)
    bias = jnp.zeros((8, key_count), f32)
    for block in range(blocks):
        here = (key_id >= block * rows + limits[item, block]) & (key_id < (block + 1) * rows)
        bias = jnp.where(here, NEGATIVE, bias)
    bias = jnp.where(lax.broadcasted_iota(jnp.int32, (8, key_count), 0) == 0, bias, 0.0)
    spare = jnp.concatenate([bias, jnp.zeros((HEAD_DIM - 8, key_count), f32)], 0).astype(bf16)
    kt_ref[0, :HEAD_DIM, :] = flipped[:HEAD_DIM]
    kt_ref[0, HEAD_DIM:, :] = spare
    kt_ref[1, :HEAD_DIM, :] = spare
    kt_ref[1, HEAD_DIM:, :] = flipped[HEAD_DIM:]
    va_ref[0] = jnp.where(first, values, 1.0).astype(bf16)
    va_ref[1] = jnp.where(first, 1.0, values).astype(bf16)
    lanes = lanes_of((step, PAIR))
    head_first = lanes < HEAD_DIM
    one = jnp.where((lanes & (HEAD_DIM - 1)) == 0, 1.0, 0.0)
    tiles = [slice(t, min(t + TILE, key_count)) for t in range(0, key_count, TILE)]

    def query_of(unit):
        chunk, head = divmod(unit, 2)
        query = q_ref[chunk * step:(chunk + 1) * step, :].astype(f32)
        mine = head_first if head == 0 else jnp.logical_not(head_first)
        return jnp.where(mine, query, one).astype(bf16)

    units = 2 * (query_rows // step)
    outs, tops = [], []
    for unit in range(-1, units):
        query = query_of(unit + 1) if unit + 1 < units else None
        out, best = None, None
        for tile in tiles:
            if query is not None:
                scores = dot_rows(query, kt_ref[(unit + 1) % 2, :, tile])
                score_refs[(unit + 1) % 2][:, tile] = scores
                high = jnp.max(scores, axis=1, keepdims=True)
                best = high if best is None else jnp.maximum(best, high)
            if unit >= 0:
                weights = jnp.exp(score_refs[unit % 2][:, tile] - tops[unit]).astype(bf16)
                added = dot_rows(weights, va_ref[unit % 2, tile, :])
                out = added if out is None else out + added
        if best is not None:
            tops.append(best)
        if out is not None:
            outs.append(out)
        if unit % 2 == 0 or unit < 0:
            continue
        chunk = unit // 2
        place = slice(chunk * step, (chunk + 1) * step)
        acc = jnp.where(head_first, outs[unit - 1], outs[unit])
        total = pltpu.roll(jnp.where(head_first, outs[unit], outs[unit - 1]), HEAD_DIM, 1)
        top = jnp.where(head_first, tops[unit - 1], tops[unit])
        if final:
            other_top = top_in[place, :]
            new_top = jnp.maximum(top, other_top)
            scale_here = jnp.exp(top - new_top)
            scale_there = jnp.exp(other_top - new_top)
            total = total * scale_here + sum_in[place, :] * scale_there
            acc = acc * scale_here + acc_in[place, :] * scale_there
            out_ref[place, :] = acc / total
            lse_ref[place, :] = pltpu.roll(new_top + jnp.log(total), HEAD_DIM, 1)
        else:
            acc_out[place, :] = acc
            top_out[place, :] = top
            sum_out[place, :] = total


def attend(limits, x, norms, w_key, w_value, b_value, query, rows, blocks, before):
    width = x.shape[1]
    key_count = rows * blocks
    items = x.shape[0] // key_count
    total = items * rows
    step = chunk_of(rows, 208)
    query_block = pl.BlockSpec((rows, PAIR), lambda i, p, *_: (i, p))
    key_block = pl.BlockSpec((key_count, PAIR), lambda i, p, *_: (i, p))
    row_block = pl.BlockSpec((key_count, width), lambda i, p, *_: (i, 0))
    weight_block = pl.BlockSpec((width, PAIR), lambda i, p, *_: (0, p))
    line_block = pl.BlockSpec((1, PAIR), lambda i, p, *_: (0, p))
    final = before is not None
    shape = jax.ShapeDtypeStruct
    out_specs = [row_block, key_block, key_block]
    out_shape = [shape(x.shape, bf16)] * 3
    if final:
        extra, extra_specs = [query, *before], [query_block] * (1 + len(before))
        out_specs += [query_block] * 2
        out_shape += [shape((total, width), f32)] * 2
    else:
        extra, extra_specs = list(query), [weight_block, line_block]
        out_specs += [query_block] * 4
        out_shape += [shape((total, width), bf16)] + [shape((total, width), f32)] * 3
    return pl.pallas_call(
        functools.partial(forward_kernel, final, rows, blocks, step),
        grid_spec=pltpu.PrefetchScalarGridSpec(
            num_scalar_prefetch=1,
            grid=(items, PAIRS),
            in_specs=[row_block, whole((1, width)), whole((1, width))]
            + [weight_block] * 2
            + [line_block]
            + extra_specs,
            out_specs=out_specs,
            scratch_shapes=[
                pltpu.VMEM((key_count, width), bf16),
                pltpu.VMEM((2, PAIR, key_count), bf16),
                pltpu.VMEM((2, key_count, PAIR), bf16),
                pltpu.VMEM((step, key_count), f32),
                pltpu.VMEM((step, key_count), f32),
            ],
        ),
        out_shape=out_shape,
        compiler_params=params(2),
        cost_estimate=cost(
            16 * total * key_count * width, 12 * total * width, total * key_count * HEADS
        ),
        name="attend",
    )(limits, x, *norms, w_key, w_value, b_value, *extra)


def split_three(value):
    high = value.astype(bf16).astype(f32)
    rest = value - high
    middle = rest.astype(bf16).astype(f32)
    return high, middle, rest - middle


def halves(core, block):
    half = block.shape[0] // 2
    upper, lower = block[:half], block[half:]
    mine = jnp.where(core == 0, upper, lower)
    theirs = jnp.where(core == 0, lower, upper)
    return mine.astype(bf16), theirs.astype(bf16)


def backward_kernel(
    last, tokens, rows, blocks, step, limits, core,
    q_ref, k_ref, v_ref, g_ref, out_ref, lse_ref, hat_ref, *rest,
):
    if last:
        before_ref, dw_in, sums_in, *rest = rest
        cat_ref, keep_ref, send_ref, dw_acc, sums_acc, qt_ref, gt_ref, dqt_ref, *wide = rest[tokens:]
    else:
        dq_ref, cat_ref, dw_ref, sums_ref, dw_acc, sums_acc, qt_ref, gt_ref, dqt_ref, *wide = rest[tokens:]
    prob_refs, score_refs = wide[:2], wide[2:]
    pair = pl.program_id(0)
    item = pl.program_id(1)
    query_rows = q_ref.shape[0]
    lanes = lanes_of((query_rows, PAIR))
    head_first = lanes < HEAD_DIM
    spare_lane = lanes & (HEAD_DIM - 1)

    def spare(parts, mask_one):
        high, middle, low = parts
        value = jnp.where(spare_lane == 0, high, 0.0)
        value = jnp.where(spare_lane == 1, middle, value)
        value = jnp.where(spare_lane == 2, low, value)
        return jnp.where(spare_lane == 3, mask_one, value)

    query = q_ref[...].astype(f32)
    grad = g_ref[...].astype(f32)
    product = grad * out_ref[...]
    delta_first = jnp.sum(jnp.where(head_first, product, 0.0), axis=1, keepdims=True)
    delta_second = jnp.sum(jnp.where(head_first, 0.0, product), axis=1, keepdims=True)
    delta = jnp.where(head_first, delta_second, delta_first)
    lse_spare = spare(split_three(-lse_ref[...]), 1.0)
    delta_spare = spare(split_three(-delta), 0.0)
    qt_ref[0] = jnp.where(head_first, query, lse_spare).T.astype(bf16)
    qt_ref[1] = jnp.where(head_first, lse_spare, query).T.astype(bf16)
    gt_ref[0] = jnp.where(head_first, grad, delta_spare).T.astype(bf16)
    gt_ref[1] = jnp.where(head_first, delta_spare, grad).T.astype(bf16)
    dqt_ref[...] = jnp.zeros_like(dqt_ref)

    key_lanes = lanes_of((step, PAIR))
    key_first = key_lanes < HEAD_DIM
    key_spare = key_lanes & (HEAD_DIM - 1)
    key_row = lax.broadcasted_iota(jnp.int32, (step, PAIR), 0)
    ones = jnp.where(key_spare < 3, 1.0, 0.0)
    per_block = rows // step
    tiles = [slice(t, min(t + TILE, query_rows)) for t in range(0, query_rows, TILE)]

    def operands(unit):
        chunk, head = divmod(unit, 2)
        place = slice(chunk * step, (chunk + 1) * step)
        block = chunk // per_block
        limit = limits[item, block] - (chunk - block * per_block) * step
        bias = jnp.where(key_row >= limit, NEGATIVE, 0.0)
        key = k_ref[place, :].astype(f32)
        value = v_ref[place, :].astype(f32)
        mine = key_first if head == 0 else jnp.logical_not(key_first)
        key_head = jnp.where(mine, key, jnp.where(key_spare == 3, bias, ones)).astype(bf16)
        value_head = jnp.where(mine, value, ones).astype(bf16)
        half = key.T[head * HEAD_DIM:(head + 1) * HEAD_DIM].astype(bf16)
        return key_head, value_head, half

    units = 2 * blocks * per_block
    dks, dvs, half = [], [], None
    for unit in range(-1, units):
        more = unit + 1 < units
        if more:
            key_head, value_head, next_half = operands(unit + 1)
            which = (unit + 1) % 2
        dk, dv = None, None
        for tile in tiles:
            if more:
                probs = jnp.exp(dot_rows(key_head, qt_ref[which, :, tile]))
                grad_probs = dot_rows(value_head, gt_ref[which, :, tile])
                prob_refs[which][:, tile] = probs.astype(bf16)
                score_refs[which][:, tile] = (probs * grad_probs).astype(bf16)
            if unit >= 0:
                grad_scores = score_refs[unit % 2][:, tile]
                dv_part = dot_rows(prob_refs[unit % 2][:, tile], g_ref[tile, :])
                dk_part = dot_rows(grad_scores, q_ref[tile, :])
                dv = dv_part if dv is None else dv + dv_part
                dk = dk_part if dk is None else dk + dk_part
                own = slice(unit % 2 * HEAD_DIM, (unit % 2 + 1) * HEAD_DIM)
                dqt_ref[own, tile] += dot_rows(half, grad_scores)
        half = next_half if more else None
        if unit >= 0:
            dks.append(dk)
            dvs.append(dv)
        if unit >= 0 and unit % 2 == 1:
            place = slice(unit // 2 * step, (unit // 2 + 1) * step)
            cat_ref[place, :PAIR] = jnp.where(key_first, dks[-2], dks[-1]).astype(bf16)
            cat_ref[place, PAIR:2 * PAIR] = jnp.where(key_first, dvs[-2], dvs[-1]).astype(bf16)

    result = dqt_ref[...].T
    if last:
        cat_ref[:, 2 * PAIR:] = ((result + before_ref[...]) * SCALE).astype(bf16)
    else:
        dq_ref[...] = result
    added = dot_left(hat_ref[...], cat_ref[...])
    sums = column_sums(cat_ref[...].astype(f32))
    items = pl.num_programs(1)
    here = pl.ds(pair, 1)

    @pl.when((item == 0) & (pair == 0))
    def _():
        sums_acc[...] = jnp.zeros_like(sums_acc)

    @pl.when(item == 0)
    def _():
        dw_acc[...] = added
        if last:
            dw_acc[:, :2 * PAIR] += dw_in[0]
            sums_acc[here, :2 * PAIR] = sums_in[0, :1, :]

    @pl.when(item > 0)
    def _():
        dw_acc[...] += added

    sums_acc[here, :] += sums

    @pl.when(item == items - 1)
    def _():
        if last:
            half = dw_acc.shape[0] // 2
            place = pl.ds(pl.multiple_of(pair * half, half), half)
            keep_ref[place, :], send_ref[place, :] = halves(core[0], dw_acc[...])
        else:
            dw_ref[0] = dw_acc[...]
            sums_ref[0] = jnp.broadcast_to(sums_acc[here, :], sums_ref.shape[1:])

    if last:

        @pl.when((item == items - 1) & (pair == pl.num_programs(0) - 1))
        def _():
            end = slice(keep_ref.shape[0] - sums_acc.shape[0] // 2, None)
            keep_ref[end, :], send_ref[end, :] = halves(core[0], sums_acc[...])


def attend_back(
    limits, core, queries, keys, values, grads, outs, lse, hat, rows, blocks, first, count, before,
    spare, tokens,
):
    total, width = queries.shape
    items = total // rows
    key_count = rows * blocks
    step = chunk_of(rows, 208)
    last = before is not None
    cat = (3 if last else 2) * PAIR
    query_block = pl.BlockSpec((rows, PAIR), lambda p, i, *_: (i, first + p))
    key_block = pl.BlockSpec((key_count, PAIR), lambda p, i, *_: (i, first + p))
    hat_block = pl.BlockSpec((key_count, width), lambda p, i, *_: (i, 0))
    cat_block = pl.BlockSpec((key_count, cat), lambda p, i, *_: (i, p))
    shape = jax.ShapeDtypeStruct
    cat_shape = shape((total * blocks, cat * count), bf16)
    if last:
        (part, _, dw_part, sums_part), skip = before
        extra = [part, dw_part, sums_part]
        extra_specs = [
            pl.BlockSpec((rows, PAIR), lambda p, i, *_: (i, skip + p)),
            pl.BlockSpec((1, width, 2 * PAIR), lambda p, i, *_: (skip + p, 0, 0)),
            pl.BlockSpec((1, 8, 2 * PAIR), lambda p, i, *_: (skip + p, 0, 0)),
        ]
        half = (count * width // 2 + spare, cat)
        out_shape = [cat_shape] + [shape(half, bf16)] * 2
        out_specs = [cat_block] + [whole(half)] * 2
    else:
        extra, extra_specs = [], []
        out_shape = [
            shape((total, PAIR * count), f32),
            cat_shape,
            shape((count, width, cat), f32),
            shape((count, 8, cat), f32),
        ]
        out_specs = [
            pl.BlockSpec((rows, PAIR), lambda p, i, *_: (i, p)),
            cat_block,
            pl.BlockSpec((1, width, cat), lambda p, i, *_: (p, 0, 0)),
            pl.BlockSpec((1, 8, cat), lambda p, i, *_: (p, 0, 0)),
        ]
    return pl.pallas_call(
        functools.partial(backward_kernel, last, len(tokens), rows, blocks, step),
        grid_spec=pltpu.PrefetchScalarGridSpec(
            num_scalar_prefetch=2,
            grid=(count, items),
            in_specs=[query_block, key_block, key_block]
            + [query_block] * 3
            + [hat_block]
            + extra_specs
            + [ANYWHERE] * len(tokens),
            out_specs=out_specs,
            scratch_shapes=[
                pltpu.VMEM((width, cat), f32),
                pltpu.VMEM((2 * spare, cat), f32),
                pltpu.VMEM((2, PAIR, rows), bf16),
                pltpu.VMEM((2, PAIR, rows), bf16),
                pltpu.VMEM((PAIR, rows), f32),
            ]
            + [pltpu.VMEM((step, rows), bf16)] * 4,
        ),
        out_shape=out_shape,
        compiler_params=params(2),
        cost_estimate=cost(
            40 * total * key_count * PAIR * count,
            16 * total * PAIR * count,
            2 * total * key_count * count,
        ),
        name="attend_back",
    )(limits, core, queries, keys, values, grads, outs, lse, hat, *extra, *tokens)


def feed_kernel(
    core, x_ref, mix_ref, dy_ref, w_output, w_expand, w_reduce, b_output, b_expand, b_reduce, gain, shift,
    y_ref, dmid_ref, dmix_ref, keep_ref, send_ref,
    middle_ref, normed_ref, y_acc, grad_acc, line_ref,
):
    part = pl.program_id(0)

    half = w_output.shape[0] // 2

    def put(index, block):
        place = pl.ds(pl.multiple_of(index * half, half), half)
        keep_ref[place, :], send_ref[place, :] = halves(core[0], block)

    @pl.when(part == 0)
    def _():
        mixed = mix_ref[...].astype(bf16)
        middle = x_ref[...].astype(f32) + dot_rows(mixed, w_output[...]) + b_output[...]
        middle_ref[...] = middle
        hat, _ = hat_rows(middle)
        normed_ref[...] = (hat * gain[...] + shift[...]).astype(bf16)
        y_acc[...] = middle + b_reduce[...]
        grad_acc[...] = jnp.zeros_like(grad_acc)
        line_ref[...] = jnp.zeros_like(line_ref)
        line_ref[1:2, :] = column_sums(dy_ref[...].astype(f32))

    normed = normed_ref[...]
    upper = dot_rows(normed, w_expand[...]) + b_expand[...]
    cumulative = 0.5 * lax.erf(upper * math.sqrt(0.5)) + 0.5
    density = jnp.exp(upper * upper * -0.5) * (1.0 / math.sqrt(2.0 * math.pi))
    active = (upper * cumulative).astype(bf16)
    slope = cumulative + upper * density
    y_acc[...] += dot_rows(active, w_reduce[...])
    put(1 + 2 * part, dot_left(active, dy_ref[...]))
    grad_upper = (dot_right(dy_ref[...], w_reduce[...]) * slope).astype(bf16)
    line_ref[pl.ds(4 + part, 1), :] = column_sums(grad_upper.astype(f32))
    put(2 + 2 * part, dot_left(normed, grad_upper))
    grad_acc[...] += dot_right(grad_upper, w_expand[...])

    @pl.when(part == pl.num_programs(0) - 1)
    def _():
        y_ref[...] = y_acc[...].astype(bf16)
        grad = grad_acc[...]
        hat, inverse = hat_rows(middle_ref[...])
        line_ref[2:3, :] = column_sums(grad * hat)
        line_ref[3:4, :] = column_sums(grad)
        dmid = hat_back(grad * gain[...], hat, inverse) + dy_ref[...].astype(f32)
        dmid_ref[...] = dmid
        branch = dmid.astype(bf16)
        line_ref[0:1, :] = column_sums(branch.astype(f32))
        put(0, dot_left(mix_ref[...].astype(bf16), branch))
        end = slice(keep_ref.shape[0] - line_ref.shape[0] // 2, None)
        keep_ref[end, :], send_ref[end, :] = halves(core[0], line_ref[...])
        dmix_ref[...] = dot_right(branch, w_output[...]).astype(bf16)


def feed(core, spare, x, mixed, dy, w_output, w_expand, w_reduce, b_output, b_expand, b_reduce, gain, shift):
    rows, width = x.shape
    hidden = w_expand.shape[1]
    parts = hidden // width
    row = whole((rows, width))
    line = whole((1, width))
    expand = pl.BlockSpec((width, width), lambda i, *_: (0, i))
    reduce = pl.BlockSpec((width, width), lambda i, *_: (i, 0))
    hidden_line = pl.BlockSpec((1, width), lambda i, *_: (0, i))
    weights = ((1 + 2 * parts) * width // 2 + spare, width)
    shape = jax.ShapeDtypeStruct
    return pl.pallas_call(
        feed_kernel,
        grid_spec=pltpu.PrefetchScalarGridSpec(
            num_scalar_prefetch=1,
            grid=(parts,),
            in_specs=[row, row, row, whole((width, width)), expand, reduce, line, hidden_line, line, line, line],
            out_specs=[row, row, row, whole(weights), whole(weights)],
            scratch_shapes=[
                pltpu.VMEM((rows, width), f32),
                pltpu.VMEM((rows, width), bf16),
                pltpu.VMEM((rows, width), f32),
                pltpu.VMEM((rows, width), f32),
                pltpu.VMEM((2 * spare, width), f32),
            ],
        ),
        out_shape=[
            shape((rows, width), bf16),
            shape((rows, width), f32),
            shape((rows, width), bf16),
            shape(weights, bf16),
            shape(weights, bf16),
        ],
        compiler_params=params(1),
        cost_estimate=cost(12 * rows * width * hidden + 6 * rows * width * width, 20 * rows * width, 2 * rows * hidden),
        name="feed",
    )(core, x, mixed, dy, w_output, w_expand, w_reduce, b_output, b_expand, b_reduce, gain, shift)


def gather_parts(refs, part, parts):
    blocks = []
    for ref in refs:
        pairs = ref.shape[1] // (parts * PAIR)
        for pair in range(pairs):
            start = (pair * parts + part) * PAIR
            blocks.append(ref[:, start:start + PAIR])
    return jnp.concatenate(blocks, axis=1)


def other_kernel(cats, w_key, w_value, *rest):
    cat_refs, send_ref = rest[:cats], rest[-1]
    dk = gather_parts(cat_refs, 0, 2)
    dv = gather_parts(cat_refs, 1, 2)
    send_ref[...] = (dot_right(dk, w_key[...]) + dot_right(dv, w_value[...])).astype(bf16)


def other_grads(cats, w_key, w_value, rows, after):
    total, width = cats[0].shape[0], w_key.shape[0]
    step = chunk_of(rows, 272)
    return pl.pallas_call(
        functools.partial(other_kernel, len(cats)),
        grid=(total // step,),
        in_specs=[whole((width, width))] * 2
        + [pl.BlockSpec((step, c.shape[1]), lambda i: (i, 0)) for c in cats]
        + [ANYWHERE] * len(after),
        out_specs=pl.BlockSpec((step, width), lambda i: (i, 0)),
        out_shape=jax.ShapeDtypeStruct((total, width), bf16),
        compiler_params=params(1),
        cost_estimate=cost(4 * total * width * width, 8 * total * width),
        name="other_grads",
    )(w_key, w_value, *cats, *after)


def own_kernel(cats, x_ref, recv_ref, dmid_ref, w_query, w_key, w_value, gain, *rest):
    cat_refs, dx_ref = rest[:cats], rest[-1]
    dk = gather_parts(cat_refs, 0, 3)
    dv = gather_parts(cat_refs, 1, 3)
    dq = gather_parts(cat_refs, 2, 3)
    grad = dot_right(dq, w_query[...]) + dot_right(dk, w_key[...]) + dot_right(dv, w_value[...])
    for index in range(recv_ref.shape[0]):
        grad = grad + recv_ref[index].astype(f32)
    hat, inverse = hat_rows(x_ref[...].astype(f32))
    dx_ref[...] = hat_back(grad * gain[...], hat, inverse) + dmid_ref[...]


def own_grads(x, cats, recv, dmid, w_query, w_key, w_value, gain, after):
    rows, width = x.shape
    step = chunk_of(rows, 272)
    row = pl.BlockSpec((step, width), lambda i: (i, 0))
    return pl.pallas_call(
        functools.partial(own_kernel, len(cats)),
        grid=(rows // step,),
        in_specs=[row, pl.BlockSpec((recv.shape[0], step, width), lambda i: (0, i, 0)), row]
        + [whole((width, width))] * 3
        + [whole((1, width))]
        + [pl.BlockSpec((step, c.shape[1]), lambda i: (i, 0)) for c in cats]
        + [ANYWHERE] * len(after),
        out_specs=row,
        out_shape=jax.ShapeDtypeStruct((rows, width), f32),
        compiler_params=params(1),
        cost_estimate=cost(6 * rows * width * width, 16 * rows * width),
        name="own_grads",
    )(x, recv, dmid, w_query, w_key, w_value, gain, *cats, *after)


class Slice:
    def __init__(self):
        group, rest = lax.axis_size("grp"), lax.axis_size("rest")
        batch = rest * lax.axis_size("core")
        side = 2 if rest % 2 == 0 else 1
        rest //= side
        high = 2 if rest % 2 == 0 else 1
        self.sizes = {"core": 2, "side": side, "member": group, "high": high, "low": rest // high}
        self.count = group * batch
        self.here = self.coords(lax.axis_index(ALL))

    def coords(self, linear):
        out = {}
        for name in ("member", "core", "side", "low", "high"):
            out[name] = linear % self.sizes[name]
            linear = linear // self.sizes[name]
        return out

    def linear(self, coords):
        total = 0
        for name in ("high", "low", "side", "core", "member"):
            total = total * self.sizes[name] + coords[name]
        return total

    def size(self, stage):
        return math.prod(self.sizes[name] for name in stage)

    def place(self, stage, coords=None):
        coords = self.here if coords is None else coords
        total = 0
        for name in stage:
            total = total * self.sizes[name] + coords[name]
        return total

    def send(self, array, stage, shift):
        pairs = []
        for source in range(self.count):
            coords = self.coords(source)
            place = (self.place(stage, coords) + shift) % self.size(stage)
            for name in reversed(stage):
                coords[name] = place % self.sizes[name]
                place //= self.sizes[name]
            pairs.append((source, self.linear(coords)))
        return lax.ppermute(array, ALL, pairs)

    def spread(self, parts, stage):
        return [parts[0]] + [self.send(part, stage, s) for s, part in enumerate(parts) if s > 0]

    def share(self, array, stage):
        return self.spread([array] * self.size(stage), stage)

    def origins(self, stage):
        size = self.size(stage)
        return ((self.place(stage) - jnp.arange(size)) % size).astype(jnp.int32)

    def in_order(self, parts, stage):
        if len(parts) <= 2:
            return parts
        stack = jnp.stack(parts)
        order = self.origins(stage)
        return [lax.dynamic_index_in_dim(stack, order[i], 0, False) for i in range(len(parts))]


def behind(array, *others):
    return lax.optimization_barrier((array, *others))[0] if others else array


def cut_kernel(size, groups, place, *refs):
    ins, outs = refs[:2 * groups], refs[2 * groups:]
    for shift, out in enumerate(outs):
        start = 0
        for index in range(groups):
            keep, came = ins[2 * index], ins[2 * index + 1]
            rows = keep.shape[0] // size
            span = pl.ds(pl.multiple_of((place[0] + shift) % size * rows, 16), rows)
            total = keep[span, :].astype(f32) + came[span, :].astype(f32)
            out[start:start + rows, :] = total.astype(bf16)
            start += rows


def cut(pairs, place, size):
    arrays = [array for pair in pairs for array in pair]
    width = arrays[0].shape[1]
    part = (sum(keep.shape[0] for keep, _ in pairs) // size, width)
    return pl.pallas_call(
        functools.partial(cut_kernel, size, len(pairs)),
        grid_spec=pltpu.PrefetchScalarGridSpec(
            num_scalar_prefetch=1,
            grid=(1,),
            in_specs=[whole(a.shape) for a in arrays],
            out_specs=[whole(part)] * size,
        ),
        out_shape=[jax.ShapeDtypeStruct(part, bf16)] * size,
        compiler_params=params(1),
        cost_estimate=cost(size * part[0] * width, 6 * size * part[0] * width),
        name="cut",
    )(jnp.reshape(place, (1,)).astype(jnp.int32), *arrays)


def add_up(parts):
    total = parts[0].astype(f32)
    for part in parts[1:]:
        total = total + part.astype(f32)
    return total.astype(bf16)


def place_pieces(places, core, pieces, flats):
    size = len(pieces) // 2
    for which in range(2):
        target = core[0] if which == 0 else 1 - core[0]
        for index in range(size):
            piece, at = pieces[which * size + index], 0
            for flat in flats:
                rows = flat.shape[1] // size
                span = pl.ds(pl.multiple_of(places[index] * rows, 16), rows)
                flat[target, span, :] = piece[at:at + rows, :]
                at += rows


def feed_weights_kernel(size, places, core, *refs):
    pieces, (dwo_ref, dwe_ref, dwr_ref, *line_refs, dbe_ref, flat) = refs[:2 * size], refs[-9:]
    width = dwo_ref.shape[0]
    half = width // 2
    step = pl.program_id(0)
    parts = pl.num_programs(0) - 1

    @pl.when(step == 0)
    def _():
        place_pieces(places, core, pieces, [flat])

    @pl.when(step < parts)
    def _():
        start = pl.multiple_of((1 + 2 * step) * half, half)
        for side in range(2):
            rows = slice(side * half, (side + 1) * half)
            dwr_ref[rows, :] = flat[side, pl.ds(start, half), :].astype(f32)
            dwe_ref[rows, :] = flat[side, pl.ds(start + half, half), :].astype(f32)

    @pl.when(step == parts)
    def _():
        for side in range(2):
            dwo_ref[side * half:(side + 1) * half, :] = flat[side, :half, :].astype(f32)
        count = dbe_ref.shape[1] // width
        start = (1 + 2 * count) * half
        lines = flat[0, start:start + 16, :].astype(f32)
        for index, ref in enumerate(line_refs):
            ref[...] = lines[index:index + 1]
        for part in range(count):
            dbe_ref[:, part * width:(part + 1) * width] = lines[4 + part:5 + part]


def feed_weights(places, core, own, came, hidden, after):
    rows, width = own[0].shape
    parts = hidden // width
    shapes = [(width, width), (width, hidden), (hidden, width)] + [(1, width)] * 4 + [(1, hidden)]
    out_specs = [whole(s) for s in shapes]
    out_specs[1] = pl.BlockSpec((width, width), lambda p, *_: (0, jnp.minimum(p, parts - 1)))
    out_specs[2] = pl.BlockSpec((width, width), lambda p, *_: (jnp.minimum(p, parts - 1), 0))
    return pl.pallas_call(
        functools.partial(feed_weights_kernel, len(own)),
        grid_spec=pltpu.PrefetchScalarGridSpec(
            num_scalar_prefetch=2,
            grid=(parts + 1,),
            in_specs=[whole((rows, width))] * (2 * len(own)) + [ANYWHERE] * len(after),
            out_specs=out_specs,
            scratch_shapes=[pltpu.VMEM((2, len(own) * rows, width), bf16)],
        ),
        out_shape=[jax.ShapeDtypeStruct(s, f32) for s in shapes],
        compiler_params=params(1),
        cost_estimate=cost(0, 12 * len(own) * rows * width),
        name="feed_weights",
    )(places, core, *own, *came, *after)


def project_weights_kernel(calls, places, core, *refs):
    flats, refs = refs[len(refs) - len(calls):], refs[:len(refs) - len(calls)]
    pieces, refs = refs[:-16], refs[-16:]
    weights, (gain, shift), refs = refs[:3], refs[3:5], refs[5:]
    outs, (dgain_ref, dshift_ref, dbq_ref, dbv_ref), refs = refs[:3], refs[3:7], refs[7:]
    gains, shifts, cross_acc, plain_acc = refs
    pair = pl.program_id(0)
    width = gains.shape[0]
    half = width // 2

    @pl.when(pair == 0)
    def _():
        place_pieces(places, core, pieces, flats)
        gains[...] = jnp.broadcast_to(gain[...], (PAIR, width)).T
        shifts[...] = jnp.broadcast_to(shift[...], (PAIR, width)).T
        cross_acc[...] = jnp.zeros_like(cross_acc)
        plain_acc[...] = jnp.zeros_like(plain_acc)

    def put(flat, pairs, index):
        sums = flat[0, pairs * half:pairs * half + 16, :].astype(f32)[index:index + 1]
        dbv_ref[...] = sums[:, PAIR:2 * PAIR]
        dbq_ref[...] = sums[:, 2 * PAIR:]
        for side in range(2):
            down = slice(side * half, (side + 1) * half)
            block = flat[side, index * half:(index + 1) * half, :].astype(f32)
            for which, (out, weight) in enumerate(zip(outs, weights)):
                lanes = slice(which * PAIR, (which + 1) * PAIR)
                part, line = block[:, lanes], sums[:, lanes]
                out[down, :] = gains[down, :] * part + shifts[down, :] * line
                own = weight[down, :].astype(f32)
                cross_acc[down, :] += own * part
                plain_acc[down, :] += own * line

    first = 0
    for flat, pairs in zip(flats, calls):
        for index in range(pairs):
            pl.when(pair == first + index)(functools.partial(put, flat, pairs, index))
        first += pairs

    @pl.when(pair == PAIRS - 1)
    def _():
        for acc, out in ((cross_acc, dgain_ref), (plain_acc, dshift_ref)):
            column = jnp.broadcast_to(jnp.sum(acc[...], axis=1, keepdims=True), (width, PAIR))
            out[...] = column.T[:1]


def project_weights(places, core, own, came, w_key, w_value, w_query, gain, shift, calls, spare):
    width = w_query.shape[0]
    rows, cat = own[0].shape
    line = whole((1, width))
    column_block = pl.BlockSpec((width, PAIR), lambda p, *_: (0, p))
    line_block = pl.BlockSpec((1, PAIR), lambda p, *_: (0, p))
    return pl.pallas_call(
        functools.partial(project_weights_kernel, calls),
        grid_spec=pltpu.PrefetchScalarGridSpec(
            num_scalar_prefetch=2,
            grid=(PAIRS,),
            in_specs=[whole((rows, cat))] * (2 * len(own)) + [column_block] * 3 + [line] * 2,
            out_specs=[column_block] * 3 + [line] * 2 + [line_block] * 2,
            scratch_shapes=[pltpu.VMEM((width, PAIR), f32)] * 4
            + [pltpu.VMEM((2, count * width // 2 + spare, cat), bf16) for count in calls],
        ),
        out_shape=[jax.ShapeDtypeStruct((width, width), f32)] * 3
        + [jax.ShapeDtypeStruct((1, width), f32)] * 4,
        compiler_params=params(1),
        cost_estimate=cost(0, 20 * width * width),
        name="project_weights",
    )(places, core, *own, *came, w_key, w_value, w_query, gain, shift)


def body(
    layer_input,
    lang_counts,
    w_query,
    w_key,
    w_value,
    w_output,
    w_expand,
    w_reduce,
    b_query,
    b_value,
    b_output,
    b_expand,
    b_reduce,
    gain_attn,
    shift_attn,
    gain_mlp,
    shift_mlp,
    cotangent,
):
    items, own_rows, width = layer_input.shape
    group = lax.axis_size("grp")
    me = lax.axis_index("grp")
    rows = -(-own_rows // 16) * 16
    total = items * rows
    patch_rows = VIEWS * PATCH
    shifts = range(1, group)

    def padded(array):
        if rows != own_rows:
            array = jnp.pad(array, ((0, 0), (0, rows - own_rows), (0, 0)))
        return array.reshape(total, width)

    def unpadded(array):
        return array.reshape(items, rows, width)[:, :own_rows]

    def limit_of(owner):
        return jnp.clip(patch_rows + lang_counts - owner * own_rows, 0, own_rows)

    def line(vector):
        return vector.reshape(1, -1)

    def group_shift(array, shift):
        return lax.ppermute(array, "grp", [(i, (i + shift) % group) for i in range(group)])

    def joined(parts):
        if len(parts) == 1:
            return parts[0]
        return jnp.stack([p.reshape(items, rows, width) for p in parts], 1).reshape(-1, width)

    x = padded(layer_input)
    dy = padded(cotangent)
    others = [group_shift(x, -shift) for shift in shifts]
    own_limits = limit_of(me).reshape(items, 1)
    other_limits = jnp.stack([limit_of((me + shift) % group) for shift in shifts], 1)

    norms = (line(gain_attn), line(shift_attn))
    hat, keys, values, queries, *first = attend(
        own_limits, x, norms, w_key, w_value, line(b_value), (w_query, line(b_query)), rows, 1, None
    )
    hat_other, keys_other, values_other, mixed, lse = attend(
        other_limits, joined(others), norms, w_key, w_value, line(b_value), queries, rows, group - 1, first
    )

    devices = Slice()
    plane = ("side", "member")
    core = jnp.reshape(devices.here["core"], (1,)).astype(jnp.int32)
    plane_place, plane_size = devices.place(plane), devices.size(plane)
    spare = 16 * plane_size
    output, dmid, dmix, keep, give = feed(
        core, spare, x, mixed, dy, w_output, w_expand, w_reduce, line(b_output), line(b_expand),
        line(b_reduce), line(gain_mlp), line(shift_mlp),
    )

    def summed(value, stage, *after):
        own, *came = devices.share(value, (stage,))
        return add_up(devices.in_order([behind(own, *after), *came], (stage,)))

    def back_other(first, count, tokens):
        return attend_back(
            other_limits, core, queries, keys_other, values_other, dmix, mixed, lse, hat_other,
            rows, group - 1, first, count, None, spare, tokens,
        )

    def back_own(first, count, before, tokens):
        return attend_back(
            own_limits, core, queries, keys, values, dmix, mixed, lse, hat,
            rows, 1, first, count, before, spare, tokens,
        )

    feed_pair = devices.spread([keep, give], ("core",))
    other_first = back_other(0, 1, [])
    feed_pair = [behind(half, other_first[1]) for half in feed_pair]
    share_rows = feed_pair[0].shape[0] // plane_size
    parts = [
        add_up([
            lax.dynamic_slice_in_dim(half, (plane_place + s) % plane_size * share_rows, share_rows)
            for half in feed_pair
        ])
        for s in range(plane_size)
    ]
    other_rest = back_other(1, PAIRS - 1, parts[:1])
    own, *came = devices.spread(parts, plane)
    feed_sum = add_up([behind(own, other_rest[1]), *came])
    cat_first, *pair_first = back_own(0, 1, (other_first, 0), [feed_sum])
    feed_sum = summed(feed_sum, "low", cat_first)
    send = other_grads([other_first[1], other_rest[1]], w_key, w_value, rows, [feed_sum])
    cat_middle, *pair_middle = back_own(1, PAIRS - 2, (other_rest, 0), [feed_sum, send])
    send = send.reshape(items, group - 1, rows, width)
    received = jnp.stack(
        [group_shift(send[:, shift - 1].reshape(total, width), shift) for shift in shifts]
    )
    pair_first = devices.spread(pair_first, ("core",))
    feed_sum = summed(feed_sum, "high", cat_middle, pair_first[1])
    cat_last, *pair_last = back_own(PAIRS - 1, 1, (other_rest, PAIRS - 2), [feed_sum])
    feed_own = devices.share(feed_sum, plane)
    pairs = [pair_first] + [devices.spread(pair, ("core",)) for pair in (pair_middle, pair_last)]
    parts = devices.spread(cut(pairs, plane_place, plane_size), plane)
    dx = own_grads(
        x, [cat_first, cat_middle, cat_last], received, dmid, w_query, w_key, w_value, line(gain_attn),
        parts[:1],
    )
    own, *came = parts
    value = add_up([behind(own, dx), *came])
    value = summed(summed(value, "low"), "high")
    project_own = devices.share(value, plane)
    feed_came = [devices.send(behind(piece, value), ("core",), 1) for piece in feed_own]
    places = devices.origins(plane)
    dwo, dwe, dwr, dbo, dbr, dgain_mlp, dshift_mlp, dbe = feed_weights(
        places, core, feed_own, feed_came, w_expand.shape[1], []
    )
    project_own = [project_own[0]] + [behind(piece, dwo) for piece in project_own[1:]]
    project_came = [devices.send(piece, ("core",), 1) for piece in project_own]
    dwk, dwv, dwq, dgain, dshift, dbq, dbv = project_weights(
        places, core, project_own, project_came, w_key, w_value, w_query, *norms, (1, PAIRS - 2, 1), spare
    )
    small = (dbq, dbv, dbo, dbe, dbr, dgain, dshift, dgain_mlp, dshift_mlp)
    return (
        unpadded(output),
        unpadded(dx),
        dwq, dwk, dwv, dwo, dwe, dwr,
        *(vector.reshape(-1) for vector in small),
    )


def solution(mesh):
    batch, group = mesh.shape["dp"], mesh.shape["grp"]
    mesh = jax.sharding.Mesh(mesh.devices.reshape(batch // 2, 2, group), ALL)
    items = ("rest", "core")
    rows = P(items, "grp", None)
    in_specs = (rows, P(items)) + (P(),) * 15 + (rows,)
    out_specs = (rows, rows) + (P(),) * 15
    return jax.shard_map(body, mesh=mesh, in_specs=in_specs, out_specs=out_specs, check_vma=False)
```

```python
import functools
import math

import jax
import jax.numpy as jnp
from jax import lax
from jax.experimental import pallas as pl
from jax.experimental.pallas import tpu as pltpu
from jax.sharding import PartitionSpec as P

HEADS = 8
HEAD_DIM = 64
VIEWS = 5
PATCH = 400
PAIR = 2 * HEAD_DIM
PAIRS = HEADS // 2
TILE = 256

EPSILON = 1e-05
NEGATIVE = -1e30
SCALE = 1.0 / math.sqrt(HEAD_DIM)

bf16 = jnp.bfloat16
f32 = jnp.float32


def dot_rows(left, right):
    return lax.dot_general(
        left, right, (((1,), (0,)), ((), ())), preferred_element_type=f32
    )


def dot_left(left, right):
    return lax.dot_general(
        left, right, (((0,), (0,)), ((), ())), preferred_element_type=f32
    )


def dot_right(left, right):
    return lax.dot_general(
        left, right, (((1,), (1,)), ((), ())), preferred_element_type=f32
    )


def chunk_of(rows, limit):
    best = 16
    for size in range(16, limit + 1, 16):
        if rows % size == 0:
            best = size
    return best


def hat_rows(matrix):
    center = matrix - jnp.mean(matrix, axis=-1, keepdims=True)
    spread = jnp.mean(center * center, axis=-1, keepdims=True)
    inverse = lax.rsqrt(spread + EPSILON)
    return center * inverse, inverse


def hat_back(grad_hat, hat, inverse):
    mean_grad = jnp.mean(grad_hat, axis=-1, keepdims=True)
    mean_cross = jnp.mean(grad_hat * hat, axis=-1, keepdims=True)
    return inverse * (grad_hat - mean_grad - hat * mean_cross)


def column_sums(matrix):
    return jnp.sum(matrix, axis=0, keepdims=True)


ALL = ("rest", "core", "grp")
VMEM_MIB = 60
ANYWHERE = pl.BlockSpec(memory_space=pl.ANY)


def params(axes):
    return pltpu.CompilerParams(
        dimension_semantics=("arbitrary",) * axes, vmem_limit_bytes=VMEM_MIB << 20
    )


def cost(flops, bytes_accessed, transcendentals=0):
    return pl.CostEstimate(
        flops=int(flops), bytes_accessed=int(bytes_accessed), transcendentals=int(transcendentals)
    )


def whole(shape):
    return pl.BlockSpec(shape, lambda *_: (0,) * len(shape))


def lanes_of(shape):
    return lax.broadcasted_iota(jnp.int32, shape, 1)


def forward_kernel(final, rows, blocks, step, limits, x_ref, gain, shift, w_key, w_value, b_value, *rest):
    if final:
        q_ref, acc_in, top_in, sum_in, *rest = rest
        hat_ref, k_ref, v_ref, out_ref, lse_ref, *rest = rest
    else:
        w_query, b_query, *rest = rest
        hat_ref, k_ref, v_ref, q_ref, acc_out, top_out, sum_out, *rest = rest
    normed, kt_ref, va_ref, *score_refs = rest
    item = pl.program_id(0)
    key_count = rows * blocks
    query_rows = q_ref.shape[0]

    @pl.when(pl.program_id(1) == 0)
    def _():
        hat, _ = hat_rows(x_ref[...].astype(f32))
        hat_ref[...] = hat.astype(bf16)
        normed[...] = (hat * gain[...] + shift[...]).astype(bf16)

    weights = [w_key[...], w_value[...]] if final else [w_key[...], w_value[...], w_query[...]]
    projected = dot_rows(normed[...], jnp.concatenate(weights, axis=1))
    k_ref[...] = projected[:, :PAIR].astype(bf16)
    v_ref[...] = (projected[:, PAIR:2 * PAIR] + b_value[...]).astype(bf16)
    if not final:
        query = (projected[:, 2 * PAIR:] + b_query[...]).astype(bf16)
        q_ref[...] = (query.astype(f32) * SCALE).astype(bf16)
    keys = k_ref[...].astype(f32)
    values = v_ref[...].astype(f32)
    first = lanes_of((key_count, PAIR)) < HEAD_DIM
    flipped = keys.T.astype(bf16)
    key_id = lax.broadcasted_iota(jnp.int32, (8, key_count), 1)
    bias = jnp.zeros((8, key_count), f32)
    for block in range(blocks):
        here = (key_id >= block * rows + limits[item, block]) & (key_id < (block + 1) * rows)
        bias = jnp.where(here, NEGATIVE, bias)
    bias = jnp.where(lax.broadcasted_iota(jnp.int32, (8, key_count), 0) == 0, bias, 0.0)
    spare = jnp.concatenate([bias, jnp.zeros((HEAD_DIM - 8, key_count), f32)], 0).astype(bf16)
    kt_ref[0, :HEAD_DIM, :] = flipped[:HEAD_DIM]
    kt_ref[0, HEAD_DIM:, :] = spare
    kt_ref[1, :HEAD_DIM, :] = spare
    kt_ref[1, HEAD_DIM:, :] = flipped[HEAD_DIM:]
    va_ref[0] = jnp.where(first, values, 1.0).astype(bf16)
    va_ref[1] = jnp.where(first, 1.0, values).astype(bf16)
    lanes = lanes_of((step, PAIR))
    head_first = lanes < HEAD_DIM
    one = jnp.where((lanes & (HEAD_DIM - 1)) == 0, 1.0, 0.0)
    tiles = [slice(t, min(t + TILE, key_count)) for t in range(0, key_count, TILE)]

    def query_of(unit):
        chunk, head = divmod(unit, 2)
        query = q_ref[chunk * step:(chunk + 1) * step, :].astype(f32)
        mine = head_first if head == 0 else jnp.logical_not(head_first)
        return jnp.where(mine, query, one).astype(bf16)

    units = 2 * (query_rows // step)
    outs, tops = [], []
    for unit in range(-1, units):
        query = query_of(unit + 1) if unit + 1 < units else None
        out, best = None, None
        for tile in tiles:
            if query is not None:
                scores = dot_rows(query, kt_ref[(unit + 1) % 2, :, tile])
                score_refs[(unit + 1) % 2][:, tile] = scores
                high = jnp.max(scores, axis=1, keepdims=True)
                best = high if best is None else jnp.maximum(best, high)
            if unit >= 0:
                weights = jnp.exp(score_refs[unit % 2][:, tile] - tops[unit]).astype(bf16)
                added = dot_rows(weights, va_ref[unit % 2, tile, :])
                out = added if out is None else out + added
        if best is not None:
            tops.append(best)
        if out is not None:
            outs.append(out)
        if unit % 2 == 0 or unit < 0:
            continue
        chunk = unit // 2
        place = slice(chunk * step, (chunk + 1) * step)
        acc = jnp.where(head_first, outs[unit - 1], outs[unit])
        total = pltpu.roll(jnp.where(head_first, outs[unit], outs[unit - 1]), HEAD_DIM, 1)
        top = jnp.where(head_first, tops[unit - 1], tops[unit])
        if final:
            other_top = top_in[place, :]
            new_top = jnp.maximum(top, other_top)
            scale_here = jnp.exp(top - new_top)
            scale_there = jnp.exp(other_top - new_top)
            total = total * scale_here + sum_in[place, :] * scale_there
            acc = acc * scale_here + acc_in[place, :] * scale_there
            out_ref[place, :] = acc / total
            lse_ref[place, :] = pltpu.roll(new_top + jnp.log(total), HEAD_DIM, 1)
        else:
            acc_out[place, :] = acc
            top_out[place, :] = top
            sum_out[place, :] = total


def attend(limits, x, norms, w_key, w_value, b_value, query, rows, blocks, before):
    width = x.shape[1]
    key_count = rows * blocks
    items = x.shape[0] // key_count
    total = items * rows
    step = chunk_of(rows, 208)
    query_block = pl.BlockSpec((rows, PAIR), lambda i, p, *_: (i, p))
    key_block = pl.BlockSpec((key_count, PAIR), lambda i, p, *_: (i, p))
    row_block = pl.BlockSpec((key_count, width), lambda i, p, *_: (i, 0))
    weight_block = pl.BlockSpec((width, PAIR), lambda i, p, *_: (0, p))
    line_block = pl.BlockSpec((1, PAIR), lambda i, p, *_: (0, p))
    final = before is not None
    shape = jax.ShapeDtypeStruct
    out_specs = [row_block, key_block, key_block]
    out_shape = [shape(x.shape, bf16)] * 3
    if final:
        extra, extra_specs = [query, *before], [query_block] * (1 + len(before))
        out_specs += [query_block] * 2
        out_shape += [shape((total, width), f32)] * 2
    else:
        extra, extra_specs = list(query), [weight_block, line_block]
        out_specs += [query_block] * 4
        out_shape += [shape((total, width), bf16)] + [shape((total, width), f32)] * 3
    return pl.pallas_call(
        functools.partial(forward_kernel, final, rows, blocks, step),
        grid_spec=pltpu.PrefetchScalarGridSpec(
            num_scalar_prefetch=1,
            grid=(items, PAIRS),
            in_specs=[row_block, whole((1, width)), whole((1, width))]
            + [weight_block] * 2
            + [line_block]
            + extra_specs,
            out_specs=out_specs,
            scratch_shapes=[
                pltpu.VMEM((key_count, width), bf16),
                pltpu.VMEM((2, PAIR, key_count), bf16),
                pltpu.VMEM((2, key_count, PAIR), bf16),
                pltpu.VMEM((step, key_count), f32),
                pltpu.VMEM((step, key_count), f32),
            ],
        ),
        out_shape=out_shape,
        compiler_params=params(2),
        cost_estimate=cost(
            16 * total * key_count * width, 12 * total * width, total * key_count * HEADS
        ),
        name="attend",
    )(limits, x, *norms, w_key, w_value, b_value, *extra)


def split_three(value):
    high = value.astype(bf16).astype(f32)
    rest = value - high
    middle = rest.astype(bf16).astype(f32)
    return high, middle, rest - middle


def halves(core, block):
    half = block.shape[0] // 2
    upper, lower = block[:half], block[half:]
    mine = jnp.where(core == 0, upper, lower)
    theirs = jnp.where(core == 0, lower, upper)
    return mine.astype(bf16), theirs.astype(bf16)


def backward_kernel(
    last, tokens, rows, blocks, step, limits, core,
    q_ref, k_ref, v_ref, g_ref, out_ref, lse_ref, hat_ref, *rest,
):
    if last:
        before_ref, dw_in, sums_in, *rest = rest
        cat_ref, keep_ref, send_ref, dw_acc, sums_acc, qt_ref, gt_ref, dqt_ref, *wide = rest[tokens:]
    else:
        dq_ref, cat_ref, dw_ref, sums_ref, dw_acc, sums_acc, qt_ref, gt_ref, dqt_ref, *wide = rest[tokens:]
    prob_refs, score_refs = wide[:2], wide[2:]
    pair = pl.program_id(0)
    item = pl.program_id(1)
    query_rows = q_ref.shape[0]
    lanes = lanes_of((query_rows, PAIR))
    head_first = lanes < HEAD_DIM
    spare_lane = lanes & (HEAD_DIM - 1)

    def spare(parts, mask_one):
        high, middle, low = parts
        value = jnp.where(spare_lane == 0, high, 0.0)
        value = jnp.where(spare_lane == 1, middle, value)
        value = jnp.where(spare_lane == 2, low, value)
        return jnp.where(spare_lane == 3, mask_one, value)

    query = q_ref[...].astype(f32)
    grad = g_ref[...].astype(f32)
    product = grad * out_ref[...]
    delta_first = jnp.sum(jnp.where(head_first, product, 0.0), axis=1, keepdims=True)
    delta_second = jnp.sum(jnp.where(head_first, 0.0, product), axis=1, keepdims=True)
    delta = jnp.where(head_first, delta_second, delta_first)
    lse_spare = spare(split_three(-lse_ref[...]), 1.0)
    delta_spare = spare(split_three(-delta), 0.0)
    qt_ref[0] = jnp.where(head_first, query, lse_spare).T.astype(bf16)
    qt_ref[1] = jnp.where(head_first, lse_spare, query).T.astype(bf16)
    gt_ref[0] = jnp.where(head_first, grad, delta_spare).T.astype(bf16)
    gt_ref[1] = jnp.where(head_first, delta_spare, grad).T.astype(bf16)
    dqt_ref[...] = jnp.zeros_like(dqt_ref)

    key_lanes = lanes_of((step, PAIR))
    key_first = key_lanes < HEAD_DIM
    key_spare = key_lanes & (HEAD_DIM - 1)
    key_row = lax.broadcasted_iota(jnp.int32, (step, PAIR), 0)
    ones = jnp.where(key_spare < 3, 1.0, 0.0)
    per_block = rows // step
    tiles = [slice(t, min(t + TILE, query_rows)) for t in range(0, query_rows, TILE)]

    def operands(unit):
        chunk, head = divmod(unit, 2)
        place = slice(chunk * step, (chunk + 1) * step)
        block = chunk // per_block
        limit = limits[item, block] - (chunk - block * per_block) * step
        bias = jnp.where(key_row >= limit, NEGATIVE, 0.0)
        key = k_ref[place, :].astype(f32)
        value = v_ref[place, :].astype(f32)
        mine = key_first if head == 0 else jnp.logical_not(key_first)
        key_head = jnp.where(mine, key, jnp.where(key_spare == 3, bias, ones)).astype(bf16)
        value_head = jnp.where(mine, value, ones).astype(bf16)
        half = key.T[head * HEAD_DIM:(head + 1) * HEAD_DIM].astype(bf16)
        return key_head, value_head, half

    units = 2 * blocks * per_block
    dks, dvs, half = [], [], None
    for unit in range(-1, units):
        more = unit + 1 < units
        if more:
            key_head, value_head, next_half = operands(unit + 1)
            which = (unit + 1) % 2
        dk, dv = None, None
        for tile in tiles:
            if more:
                probs = jnp.exp(dot_rows(key_head, qt_ref[which, :, tile]))
                grad_probs = dot_rows(value_head, gt_ref[which, :, tile])
                prob_refs[which][:, tile] = probs.astype(bf16)
                score_refs[which][:, tile] = (probs * grad_probs).astype(bf16)
            if unit >= 0:
                grad_scores = score_refs[unit % 2][:, tile]
                dv_part = dot_rows(prob_refs[unit % 2][:, tile], g_ref[tile, :])
                dk_part = dot_rows(grad_scores, q_ref[tile, :])
                dv = dv_part if dv is None else dv + dv_part
                dk = dk_part if dk is None else dk + dk_part
                own = slice(unit % 2 * HEAD_DIM, (unit % 2 + 1) * HEAD_DIM)
                dqt_ref[own, tile] += dot_rows(half, grad_scores)
        half = next_half if more else None
        if unit >= 0:
            dks.append(dk)
            dvs.append(dv)
        if unit >= 0 and unit % 2 == 1:
            place = slice(unit // 2 * step, (unit // 2 + 1) * step)
            cat_ref[place, :PAIR] = jnp.where(key_first, dks[-2], dks[-1]).astype(bf16)
            cat_ref[place, PAIR:2 * PAIR] = jnp.where(key_first, dvs[-2], dvs[-1]).astype(bf16)

    result = dqt_ref[...].T
    if last:
        cat_ref[:, 2 * PAIR:] = ((result + before_ref[...]) * SCALE).astype(bf16)
    else:
        dq_ref[...] = result
    added = dot_left(hat_ref[...], cat_ref[...])
    sums = column_sums(cat_ref[...].astype(f32))
    items = pl.num_programs(1)
    here = pl.ds(pair, 1)

    @pl.when((item == 0) & (pair == 0))
    def _():
        sums_acc[...] = jnp.zeros_like(sums_acc)

    @pl.when(item == 0)
    def _():
        dw_acc[...] = added
        if last:
            dw_acc[:, :2 * PAIR] += dw_in[0]
            sums_acc[here, :2 * PAIR] = sums_in[0, :1, :]

    @pl.when(item > 0)
    def _():
        dw_acc[...] += added

    sums_acc[here, :] += sums

    @pl.when(item == items - 1)
    def _():
        if last:
            half = dw_acc.shape[0] // 2
            place = pl.ds(pl.multiple_of(pair * half, half), half)
            keep_ref[place, :], send_ref[place, :] = halves(core[0], dw_acc[...])
        else:
            dw_ref[0] = dw_acc[...]
            sums_ref[0] = jnp.broadcast_to(sums_acc[here, :], sums_ref.shape[1:])

    if last:

        @pl.when((item == items - 1) & (pair == pl.num_programs(0) - 1))
        def _():
            end = slice(keep_ref.shape[0] - sums_acc.shape[0] // 2, None)
            keep_ref[end, :], send_ref[end, :] = halves(core[0], sums_acc[...])


def attend_back(
    limits, core, queries, keys, values, grads, outs, lse, hat, rows, blocks, first, count, before,
    spare, tokens,
):
    total, width = queries.shape
    items = total // rows
    key_count = rows * blocks
    step = chunk_of(rows, 208)
    last = before is not None
    cat = (3 if last else 2) * PAIR
    query_block = pl.BlockSpec((rows, PAIR), lambda p, i, *_: (i, first + p))
    key_block = pl.BlockSpec((key_count, PAIR), lambda p, i, *_: (i, first + p))
    hat_block = pl.BlockSpec((key_count, width), lambda p, i, *_: (i, 0))
    cat_block = pl.BlockSpec((key_count, cat), lambda p, i, *_: (i, p))
    shape = jax.ShapeDtypeStruct
    cat_shape = shape((total * blocks, cat * count), bf16)
    if last:
        (part, _, dw_part, sums_part), skip = before
        extra = [part, dw_part, sums_part]
        extra_specs = [
            pl.BlockSpec((rows, PAIR), lambda p, i, *_: (i, skip + p)),
            pl.BlockSpec((1, width, 2 * PAIR), lambda p, i, *_: (skip + p, 0, 0)),
            pl.BlockSpec((1, 8, 2 * PAIR), lambda p, i, *_: (skip + p, 0, 0)),
        ]
        half = (count * width // 2 + spare, cat)
        out_shape = [cat_shape] + [shape(half, bf16)] * 2
        out_specs = [cat_block] + [whole(half)] * 2
    else:
        extra, extra_specs = [], []
        out_shape = [
            shape((total, PAIR * count), f32),
            cat_shape,
            shape((count, width, cat), f32),
            shape((count, 8, cat), f32),
        ]
        out_specs = [
            pl.BlockSpec((rows, PAIR), lambda p, i, *_: (i, p)),
            cat_block,
            pl.BlockSpec((1, width, cat), lambda p, i, *_: (p, 0, 0)),
            pl.BlockSpec((1, 8, cat), lambda p, i, *_: (p, 0, 0)),
        ]
    return pl.pallas_call(
        functools.partial(backward_kernel, last, len(tokens), rows, blocks, step),
        grid_spec=pltpu.PrefetchScalarGridSpec(
            num_scalar_prefetch=2,
            grid=(count, items),
            in_specs=[query_block, key_block, key_block]
            + [query_block] * 3
            + [hat_block]
            + extra_specs
            + [ANYWHERE] * len(tokens),
            out_specs=out_specs,
            scratch_shapes=[
                pltpu.VMEM((width, cat), f32),
                pltpu.VMEM((2 * spare, cat), f32),
                pltpu.VMEM((2, PAIR, rows), bf16),
                pltpu.VMEM((2, PAIR, rows), bf16),
                pltpu.VMEM((PAIR, rows), f32),
            ]
            + [pltpu.VMEM((step, rows), bf16)] * 4,
        ),
        out_shape=out_shape,
        compiler_params=params(2),
        cost_estimate=cost(
            total * PAIR * count,
            total * PAIR * count,
        ),
        name="attend_back",
    )(limits, core, queries, keys, values, grads, outs, lse, hat, *extra, *tokens)


def feed_kernel(
    core, x_ref, mix_ref, dy_ref, w_output, w_expand, w_reduce, b_output, b_expand, b_reduce, gain, shift,
    y_ref, dmid_ref, dmix_ref, keep_ref, send_ref,
    middle_ref, normed_ref, y_acc, grad_acc, line_ref,
):
    part = pl.program_id(0)

    half = w_output.shape[0] // 2

    def put(index, block):
        place = pl.ds(pl.multiple_of(index * half, half), half)
        keep_ref[place, :], send_ref[place, :] = halves(core[0], block)

    @pl.when(part == 0)
    def _():
        mixed = mix_ref[...].astype(bf16)
        middle = x_ref[...].astype(f32) + dot_rows(mixed, w_output[...]) + b_output[...]
        middle_ref[...] = middle
        hat, _ = hat_rows(middle)
        normed_ref[...] = (hat * gain[...] + shift[...]).astype(bf16)
        y_acc[...] = middle + b_reduce[...]
        grad_acc[...] = jnp.zeros_like(grad_acc)
        line_ref[...] = jnp.zeros_like(line_ref)
        line_ref[1:2, :] = column_sums(dy_ref[...].astype(f32))

    normed = normed_ref[...]
    upper = dot_rows(normed, w_expand[...]) + b_expand[...]
    cumulative = 0.5 * lax.erf(upper * math.sqrt(0.5)) + 0.5
    density = jnp.exp(upper * upper * -0.5) * (1.0 / math.sqrt(2.0 * math.pi))
    active = (upper * cumulative).astype(bf16)
    slope = cumulative + upper * density
    y_acc[...] += dot_rows(active, w_reduce[...])
    put(1 + 2 * part, dot_left(active, dy_ref[...]))
    grad_upper = (dot_right(dy_ref[...], w_reduce[...]) * slope).astype(bf16)
    line_ref[pl.ds(4 + part, 1), :] = column_sums(grad_upper.astype(f32))
    put(2 + 2 * part, dot_left(normed, grad_upper))
    grad_acc[...] += dot_right(grad_upper, w_expand[...])

    @pl.when(part == pl.num_programs(0) - 1)
    def _():
        y_ref[...] = y_acc[...].astype(bf16)
        grad = grad_acc[...]
        hat, inverse = hat_rows(middle_ref[...])
        line_ref[2:3, :] = column_sums(grad * hat)
        line_ref[3:4, :] = column_sums(grad)
        dmid = hat_back(grad * gain[...], hat, inverse) + dy_ref[...].astype(f32)
        dmid_ref[...] = dmid
        branch = dmid.astype(bf16)
        line_ref[0:1, :] = column_sums(branch.astype(f32))
        put(0, dot_left(mix_ref[...].astype(bf16), branch))
        end = slice(keep_ref.shape[0] - line_ref.shape[0] // 2, None)
        keep_ref[end, :], send_ref[end, :] = halves(core[0], line_ref[...])
        dmix_ref[...] = dot_right(branch, w_output[...]).astype(bf16)


def feed(core, spare, x, mixed, dy, w_output, w_expand, w_reduce, b_output, b_expand, b_reduce, gain, shift):
    rows, width = x.shape
    hidden = w_expand.shape[1]
    parts = hidden // width
    row = whole((rows, width))
    line = whole((1, width))
    expand = pl.BlockSpec((width, width), lambda i, *_: (0, i))
    reduce = pl.BlockSpec((width, width), lambda i, *_: (i, 0))
    hidden_line = pl.BlockSpec((1, width), lambda i, *_: (0, i))
    weights = ((1 + 2 * parts) * width // 2 + spare, width)
    shape = jax.ShapeDtypeStruct
    return pl.pallas_call(
        feed_kernel,
        grid_spec=pltpu.PrefetchScalarGridSpec(
            num_scalar_prefetch=1,
            grid=(parts,),
            in_specs=[row, row, row, whole((width, width)), expand, reduce, line, hidden_line, line, line, line],
            out_specs=[row, row, row, whole(weights), whole(weights)],
            scratch_shapes=[
                pltpu.VMEM((rows, width), f32),
                pltpu.VMEM((rows, width), bf16),
                pltpu.VMEM((rows, width), f32),
                pltpu.VMEM((rows, width), f32),
                pltpu.VMEM((2 * spare, width), f32),
            ],
        ),
        out_shape=[
            shape((rows, width), bf16),
            shape((rows, width), f32),
            shape((rows, width), bf16),
            shape(weights, bf16),
            shape(weights, bf16),
        ],
        compiler_params=params(1),
        cost_estimate=cost(12 * rows * width * hidden + 6 * rows * width * width, 20 * rows * width, 2 * rows * hidden),
        name="feed",
    )(core, x, mixed, dy, w_output, w_expand, w_reduce, b_output, b_expand, b_reduce, gain, shift)


def gather_parts(refs, part, parts):
    blocks = []
    for ref in refs:
        pairs = ref.shape[1] // (parts * PAIR)
        for pair in range(pairs):
            start = (pair * parts + part) * PAIR
            blocks.append(ref[:, start:start + PAIR])
    return jnp.concatenate(blocks, axis=1)


def other_kernel(cats, w_key, w_value, *rest):
    cat_refs, send_ref = rest[:cats], rest[-1]
    dk = gather_parts(cat_refs, 0, 2)
    dv = gather_parts(cat_refs, 1, 2)
    send_ref[...] = (dot_right(dk, w_key[...]) + dot_right(dv, w_value[...])).astype(bf16)


def other_grads(cats, w_key, w_value, rows, after):
    total, width = cats[0].shape[0], w_key.shape[0]
    step = chunk_of(rows, 272)
    return pl.pallas_call(
        functools.partial(other_kernel, len(cats)),
        grid=(total // step,),
        in_specs=[whole((width, width))] * 2
        + [pl.BlockSpec((step, c.shape[1]), lambda i: (i, 0)) for c in cats]
        + [ANYWHERE] * len(after),
        out_specs=pl.BlockSpec((step, width), lambda i: (i, 0)),
        out_shape=jax.ShapeDtypeStruct((total, width), bf16),
        compiler_params=params(1),
        cost_estimate=cost(total * width, total * width),
        name="other_grads",
    )(w_key, w_value, *cats, *after)


def own_kernel(cats, x_ref, recv_ref, dmid_ref, w_query, w_key, w_value, gain, *rest):
    cat_refs, dx_ref = rest[:cats], rest[-1]
    dk = gather_parts(cat_refs, 0, 3)
    dv = gather_parts(cat_refs, 1, 3)
    dq = gather_parts(cat_refs, 2, 3)
    grad = dot_right(dq, w_query[...]) + dot_right(dk, w_key[...]) + dot_right(dv, w_value[...])
    for index in range(recv_ref.shape[0]):
        grad = grad + recv_ref[index].astype(f32)
    hat, inverse = hat_rows(x_ref[...].astype(f32))
    dx_ref[...] = hat_back(grad * gain[...], hat, inverse) + dmid_ref[...]


def own_grads(x, cats, recv, dmid, w_query, w_key, w_value, gain, after):
    rows, width = x.shape
    step = chunk_of(rows, 272)
    row = pl.BlockSpec((step, width), lambda i: (i, 0))
    return pl.pallas_call(
        functools.partial(own_kernel, len(cats)),
        grid=(rows // step,),
        in_specs=[row, pl.BlockSpec((recv.shape[0], step, width), lambda i: (0, i, 0)), row]
        + [whole((width, width))] * 3
        + [whole((1, width))]
        + [pl.BlockSpec((step, c.shape[1]), lambda i: (i, 0)) for c in cats]
        + [ANYWHERE] * len(after),
        out_specs=row,
        out_shape=jax.ShapeDtypeStruct((rows, width), f32),
        compiler_params=params(1),
        cost_estimate=cost(rows * width, rows * width),
        name="own_grads",
    )(x, recv, dmid, w_query, w_key, w_value, gain, *cats, *after)


class Slice:
    def __init__(self):
        group, rest = lax.axis_size("grp"), lax.axis_size("rest")
        batch = rest * lax.axis_size("core")
        side = 2 if rest % 2 == 0 else 1
        rest //= side
        high = 2 if rest % 2 == 0 else 1
        self.sizes = {"core": 2, "side": side, "member": group, "high": high, "low": rest // high}
        self.count = group * batch
        self.here = self.coords(lax.axis_index(ALL))

    def coords(self, linear):
        out = {}
        for name in ("member", "core", "side", "low", "high"):
            out[name] = linear % self.sizes[name]
            linear = linear // self.sizes[name]
        return out

    def linear(self, coords):
        total = 0
        for name in ("high", "low", "side", "core", "member"):
            total = total * self.sizes[name] + coords[name]
        return total

    def size(self, stage):
        return math.prod(self.sizes[name] for name in stage)

    def place(self, stage, coords=None):
        coords = self.here if coords is None else coords
        total = 0
        for name in stage:
            total = total * self.sizes[name] + coords[name]
        return total

    def send(self, array, stage, shift):
        pairs = []
        for source in range(self.count):
            coords = self.coords(source)
            place = (self.place(stage, coords) + shift) % self.size(stage)
            for name in reversed(stage):
                coords[name] = place % self.sizes[name]
                place //= self.sizes[name]
            pairs.append((source, self.linear(coords)))
        return lax.ppermute(array, ALL, pairs)

    def spread(self, parts, stage):
        return [parts[0]] + [self.send(part, stage, s) for s, part in enumerate(parts) if s > 0]

    def share(self, array, stage):
        return self.spread([array] * self.size(stage), stage)

    def origins(self, stage):
        size = self.size(stage)
        return ((self.place(stage) - jnp.arange(size)) % size).astype(jnp.int32)

    def in_order(self, parts, stage):
        if len(parts) <= 2:
            return parts
        stack = jnp.stack(parts)
        order = self.origins(stage)
        return [lax.dynamic_index_in_dim(stack, order[i], 0, False) for i in range(len(parts))]


def behind(array, *others):
    return lax.optimization_barrier((array, *others))[0] if others else array


def cut_kernel(size, groups, place, *refs):
    ins, outs = refs[:2 * groups], refs[2 * groups:]
    for shift, out in enumerate(outs):
        start = 0
        for index in range(groups):
            keep, came = ins[2 * index], ins[2 * index + 1]
            rows = keep.shape[0] // size
            span = pl.ds(pl.multiple_of((place[0] + shift) % size * rows, 16), rows)
            total = keep[span, :].astype(f32) + came[span, :].astype(f32)
            out[start:start + rows, :] = total.astype(bf16)
            start += rows


def cut(pairs, place, size):
    arrays = [array for pair in pairs for array in pair]
    width = arrays[0].shape[1]
    part = (sum(keep.shape[0] for keep, _ in pairs) // size, width)
    return pl.pallas_call(
        functools.partial(cut_kernel, size, len(pairs)),
        grid_spec=pltpu.PrefetchScalarGridSpec(
            num_scalar_prefetch=1,
            grid=(1,),
            in_specs=[whole(a.shape) for a in arrays],
            out_specs=[whole(part)] * size,
        ),
        out_shape=[jax.ShapeDtypeStruct(part, bf16)] * size,
        compiler_params=params(1),
        cost_estimate=cost(size * part[0] * width, 6 * size * part[0] * width),
        name="cut",
    )(jnp.reshape(place, (1,)).astype(jnp.int32), *arrays)


def add_up(parts):
    total = parts[0].astype(f32)
    for part in parts[1:]:
        total = total + part.astype(f32)
    return total.astype(bf16)


def place_pieces(places, core, pieces, flats):
    size = len(pieces) // 2
    for which in range(2):
        target = core[0] if which == 0 else 1 - core[0]
        for index in range(size):
            piece, at = pieces[which * size + index], 0
            for flat in flats:
                rows = flat.shape[1] // size
                span = pl.ds(pl.multiple_of(places[index] * rows, 16), rows)
                flat[target, span, :] = piece[at:at + rows, :]
                at += rows


def feed_weights_kernel(size, places, core, *refs):
    pieces, (dwo_ref, dwe_ref, dwr_ref, *line_refs, dbe_ref, flat) = refs[:2 * size], refs[-9:]
    width = dwo_ref.shape[0]
    half = width // 2
    step = pl.program_id(0)
    parts = pl.num_programs(0) - 1

    @pl.when(step == 0)
    def _():
        place_pieces(places, core, pieces, [flat])

    @pl.when(step < parts)
    def _():
        start = pl.multiple_of((1 + 2 * step) * half, half)
        for side in range(2):
            rows = slice(side * half, (side + 1) * half)
            dwr_ref[rows, :] = flat[side, pl.ds(start, half), :].astype(f32)
            dwe_ref[rows, :] = flat[side, pl.ds(start + half, half), :].astype(f32)

    @pl.when(step == parts)
    def _():
        for side in range(2):
            dwo_ref[side * half:(side + 1) * half, :] = flat[side, :half, :].astype(f32)
        count = dbe_ref.shape[1] // width
        start = (1 + 2 * count) * half
        lines = flat[0, start:start + 16, :].astype(f32)
        for index, ref in enumerate(line_refs):
            ref[...] = lines[index:index + 1]
        for part in range(count):
            dbe_ref[:, part * width:(part + 1) * width] = lines[4 + part:5 + part]


def feed_weights(places, core, own, came, hidden, after):
    rows, width = own[0].shape
    parts = hidden // width
    shapes = [(width, width), (width, hidden), (hidden, width)] + [(1, width)] * 4 + [(1, hidden)]
    out_specs = [whole(s) for s in shapes]
    out_specs[1] = pl.BlockSpec((width, width), lambda p, *_: (0, jnp.minimum(p, parts - 1)))
    out_specs[2] = pl.BlockSpec((width, width), lambda p, *_: (jnp.minimum(p, parts - 1), 0))
    return pl.pallas_call(
        functools.partial(feed_weights_kernel, len(own)),
        grid_spec=pltpu.PrefetchScalarGridSpec(
            num_scalar_prefetch=2,
            grid=(parts + 1,),
            in_specs=[whole((rows, width))] * (2 * len(own)) + [ANYWHERE] * len(after),
            out_specs=out_specs,
            scratch_shapes=[pltpu.VMEM((2, len(own) * rows, width), bf16)],
        ),
        out_shape=[jax.ShapeDtypeStruct(s, f32) for s in shapes],
        compiler_params=params(1),
        cost_estimate=cost(0, rows * width),
        name="feed_weights",
    )(places, core, *own, *came, *after)


def project_weights_kernel(calls, places, core, *refs):
    flats, refs = refs[len(refs) - len(calls):], refs[:len(refs) - len(calls)]
    pieces, refs = refs[:-16], refs[-16:]
    weights, (gain, shift), refs = refs[:3], refs[3:5], refs[5:]
    outs, (dgain_ref, dshift_ref, dbq_ref, dbv_ref), refs = refs[:3], refs[3:7], refs[7:]
    gains, shifts, cross_acc, plain_acc = refs
    pair = pl.program_id(0)
    width = gains.shape[0]
    half = width // 2

    @pl.when(pair == 0)
    def _():
        place_pieces(places, core, pieces, flats)
        gains[...] = jnp.broadcast_to(gain[...], (PAIR, width)).T
        shifts[...] = jnp.broadcast_to(shift[...], (PAIR, width)).T
        cross_acc[...] = jnp.zeros_like(cross_acc)
        plain_acc[...] = jnp.zeros_like(plain_acc)

    def put(flat, pairs, index):
        sums = flat[0, pairs * half:pairs * half + 16, :].astype(f32)[index:index + 1]
        dbv_ref[...] = sums[:, PAIR:2 * PAIR]
        dbq_ref[...] = sums[:, 2 * PAIR:]
        for side in range(2):
            down = slice(side * half, (side + 1) * half)
            block = flat[side, index * half:(index + 1) * half, :].astype(f32)
            for which, (out, weight) in enumerate(zip(outs, weights)):
                lanes = slice(which * PAIR, (which + 1) * PAIR)
                part, line = block[:, lanes], sums[:, lanes]
                out[down, :] = gains[down, :] * part + shifts[down, :] * line
                own = weight[down, :].astype(f32)
                cross_acc[down, :] += own * part
                plain_acc[down, :] += own * line

    first = 0
    for flat, pairs in zip(flats, calls):
        for index in range(pairs):
            pl.when(pair == first + index)(functools.partial(put, flat, pairs, index))
        first += pairs

    @pl.when(pair == PAIRS - 1)
    def _():
        for acc, out in ((cross_acc, dgain_ref), (plain_acc, dshift_ref)):
            column = jnp.broadcast_to(jnp.sum(acc[...], axis=1, keepdims=True), (width, PAIR))
            out[...] = column.T[:1]


def project_weights(places, core, own, came, w_key, w_value, w_query, gain, shift, calls, spare):
    width = w_query.shape[0]
    rows, cat = own[0].shape
    line = whole((1, width))
    column_block = pl.BlockSpec((width, PAIR), lambda p, *_: (0, p))
    line_block = pl.BlockSpec((1, PAIR), lambda p, *_: (0, p))
    return pl.pallas_call(
        functools.partial(project_weights_kernel, calls),
        grid_spec=pltpu.PrefetchScalarGridSpec(
            num_scalar_prefetch=2,
            grid=(PAIRS,),
            in_specs=[whole((rows, cat))] * (2 * len(own)) + [column_block] * 3 + [line] * 2,
            out_specs=[column_block] * 3 + [line] * 2 + [line_block] * 2,
            scratch_shapes=[pltpu.VMEM((width, PAIR), f32)] * 4
            + [pltpu.VMEM((2, count * width // 2 + spare, cat), bf16) for count in calls],
        ),
        out_shape=[jax.ShapeDtypeStruct((width, width), f32)] * 3
        + [jax.ShapeDtypeStruct((1, width), f32)] * 4,
        compiler_params=params(1),
        cost_estimate=cost(0, 20 * width * width),
        name="project_weights",
    )(places, core, *own, *came, w_key, w_value, w_query, gain, shift)


def body(
    layer_input,
    lang_counts,
    w_query,
    w_key,
    w_value,
    w_output,
    w_expand,
    w_reduce,
    b_query,
    b_value,
    b_output,
    b_expand,
    b_reduce,
    gain_attn,
    shift_attn,
    gain_mlp,
    shift_mlp,
    cotangent,
):
    items, own_rows, width = layer_input.shape
    group = lax.axis_size("grp")
    me = lax.axis_index("grp")
    rows = -(-own_rows // 16) * 16
    total = items * rows
    patch_rows = VIEWS * PATCH
    shifts = range(1, group)

    def padded(array):
        if rows != own_rows:
            array = jnp.pad(array, ((0, 0), (0, rows - own_rows), (0, 0)))
        return array.reshape(total, width)

    def unpadded(array):
        return array.reshape(items, rows, width)[:, :own_rows]

    def limit_of(owner):
        return jnp.clip(patch_rows + lang_counts - owner * own_rows, 0, own_rows)

    def line(vector):
        return vector.reshape(1, -1)

    def group_shift(array, shift):
        return lax.ppermute(array, "grp", [(i, (i + shift) % group) for i in range(group)])

    def joined(parts):
        if len(parts) == 1:
            return parts[0]
        return jnp.stack([p.reshape(items, rows, width) for p in parts], 1).reshape(-1, width)

    x = padded(layer_input)
    dy = padded(cotangent)
    others = [group_shift(x, -shift) for shift in shifts]
    own_limits = limit_of(me).reshape(items, 1)
    other_limits = jnp.stack([limit_of((me + shift) % group) for shift in shifts], 1)

    norms = (line(gain_attn), line(shift_attn))
    hat, keys, values, queries, *first = attend(
        own_limits, x, norms, w_key, w_value, line(b_value), (w_query, line(b_query)), rows, 1, None
    )
    hat_other, keys_other, values_other, mixed, lse = attend(
        other_limits, joined(others), norms, w_key, w_value, line(b_value), queries, rows, group - 1, first
    )

    devices = Slice()
    plane = ("side", "member")
    core = jnp.reshape(devices.here["core"], (1,)).astype(jnp.int32)
    plane_place, plane_size = devices.place(plane), devices.size(plane)
    spare = 16 * plane_size
    output, dmid, dmix, keep, give = feed(
        core, spare, x, mixed, dy, w_output, w_expand, w_reduce, line(b_output), line(b_expand),
        line(b_reduce), line(gain_mlp), line(shift_mlp),
    )

    def summed(value, stage, *after):
        own, *came = devices.share(value, (stage,))
        return add_up(devices.in_order([behind(own, *after), *came], (stage,)))

    def back_other(first, count, tokens):
        return attend_back(
            other_limits, core, queries, keys_other, values_other, dmix, mixed, lse, hat_other,
            rows, group - 1, first, count, None, spare, tokens,
        )

    def back_own(first, count, before, tokens):
        return attend_back(
            own_limits, core, queries, keys, values, dmix, mixed, lse, hat,
            rows, 1, first, count, before, spare, tokens,
        )

    feed_pair = devices.spread([keep, give], ("core",))
    other_first = back_other(0, 1, [])
    feed_pair = [behind(half, other_first[1]) for half in feed_pair]
    share_rows = feed_pair[0].shape[0] // plane_size
    parts = [
        add_up([
            lax.dynamic_slice_in_dim(half, (plane_place + s) % plane_size * share_rows, share_rows)
            for half in feed_pair
        ])
        for s in range(plane_size)
    ]
    other_rest = back_other(1, PAIRS - 1, parts[:1])
    own, *came = devices.spread(parts, plane)
    feed_sum = add_up([behind(own, other_rest[1]), *came])
    cat_first, *pair_first = back_own(0, 1, (other_first, 0), [feed_sum])
    feed_sum = summed(feed_sum, "low", cat_first)
    send = other_grads([other_first[1], other_rest[1]], w_key, w_value, rows, [feed_sum])
    cat_middle, *pair_middle = back_own(1, PAIRS - 2, (other_rest, 0), [feed_sum, send])
    send = send.reshape(items, group - 1, rows, width)
    received = jnp.stack(
        [group_shift(send[:, shift - 1].reshape(total, width), shift) for shift in shifts]
    )
    pair_first = devices.spread(pair_first, ("core",))
    feed_sum = summed(feed_sum, "high", cat_middle, pair_first[1])
    cat_last, *pair_last = back_own(PAIRS - 1, 1, (other_rest, PAIRS - 2), [feed_sum])
    feed_own = devices.share(feed_sum, plane)
    pairs = [pair_first] + [devices.spread(pair, ("core",)) for pair in (pair_middle, pair_last)]
    parts = devices.spread(cut(pairs, plane_place, plane_size), plane)
    dx = own_grads(
        x, [cat_first, cat_middle, cat_last], received, dmid, w_query, w_key, w_value, line(gain_attn),
        parts[:1],
    )
    own, *came = parts
    value = add_up([behind(own, dx), *came])
    value = summed(value, "low")
    feed_came = [devices.send(behind(piece, value), ("core",), 1) for piece in feed_own]
    value = summed(value, "high")
    project_own = devices.share(value, plane)
    places = devices.origins(plane)
    dwo, dwe, dwr, dbo, dbr, dgain_mlp, dshift_mlp, dbe = feed_weights(
        places, core, feed_own, feed_came, w_expand.shape[1], []
    )
    project_own = [project_own[0]] + [behind(piece, dwo) for piece in project_own[1:]]
    project_came = [devices.send(piece, ("core",), 1) for piece in project_own]
    dwk, dwv, dwq, dgain, dshift, dbq, dbv = project_weights(
        places, core, project_own, project_came, w_key, w_value, w_query, *norms, (1, PAIRS - 2, 1), spare
    )
    small = (dbq, dbv, dbo, dbe, dbr, dgain, dshift, dgain_mlp, dshift_mlp)
    return (
        unpadded(output),
        unpadded(dx),
        dwq, dwk, dwv, dwo, dwe, dwr,
        *(vector.reshape(-1) for vector in small),
    )


def solution(mesh):
    batch, group = mesh.shape["dp"], mesh.shape["grp"]
    mesh = jax.sharding.Mesh(mesh.devices.reshape(batch // 2, 2, group), ALL)
    items = ("rest", "core")
    rows = P(items, "grp", None)
    in_specs = (rows, P(items)) + (P(),) * 15 + (rows,)
    out_specs = (rows, rows) + (P(),) * 15
    return jax.shard_map(body, mesh=mesh, in_specs=in_specs, out_specs=out_specs, check_vma=False)
```

```python
import functools
import math

import jax
import jax.numpy as jnp
from jax import lax
from jax.experimental import pallas as pl
from jax.experimental.pallas import tpu as pltpu
from jax.sharding import PartitionSpec as P

HEADS = 8
HEAD_DIM = 64
VIEWS = 5
PATCH = 400
PAIR = 2 * HEAD_DIM
PAIRS = HEADS // 2
TILE = 256

EPSILON = 1e-05
NEGATIVE = -1e30
SCALE = 1.0 / math.sqrt(HEAD_DIM)

bf16 = jnp.bfloat16
f32 = jnp.float32


def dot_rows(left, right):
    return lax.dot_general(
        left, right, (((1,), (0,)), ((), ())), preferred_element_type=f32
    )


def dot_left(left, right):
    return lax.dot_general(
        left, right, (((0,), (0,)), ((), ())), preferred_element_type=f32
    )


def dot_right(left, right):
    return lax.dot_general(
        left, right, (((1,), (1,)), ((), ())), preferred_element_type=f32
    )


def chunk_of(rows, limit):
    best = 16
    for size in range(16, limit + 1, 16):
        if rows % size == 0:
            best = size
    return best


def hat_rows(matrix):
    center = matrix - jnp.mean(matrix, axis=-1, keepdims=True)
    spread = jnp.mean(center * center, axis=-1, keepdims=True)
    inverse = lax.rsqrt(spread + EPSILON)
    return center * inverse, inverse


def hat_back(grad_hat, hat, inverse):
    mean_grad = jnp.mean(grad_hat, axis=-1, keepdims=True)
    mean_cross = jnp.mean(grad_hat * hat, axis=-1, keepdims=True)
    return inverse * (grad_hat - mean_grad - hat * mean_cross)


def column_sums(matrix):
    return jnp.sum(matrix, axis=0, keepdims=True)


ALL = ("rest", "core", "grp")
VMEM_MIB = 60
ANYWHERE = pl.BlockSpec(memory_space=pl.ANY)


def params(axes):
    return pltpu.CompilerParams(
        dimension_semantics=("arbitrary",) * axes, vmem_limit_bytes=VMEM_MIB << 20
    )


def cost(flops, bytes_accessed, transcendentals=0):
    return pl.CostEstimate(
        flops=int(flops), bytes_accessed=int(bytes_accessed), transcendentals=int(transcendentals)
    )


def whole(shape):
    return pl.BlockSpec(shape, lambda *_: (0,) * len(shape))


def lanes_of(shape):
    return lax.broadcasted_iota(jnp.int32, shape, 1)


def forward_kernel(final, rows, blocks, step, limits, x_ref, gain, shift, w_key, w_value, b_value, *rest):
    if final:
        q_ref, acc_in, top_in, sum_in, *rest = rest
        hat_ref, k_ref, v_ref, out_ref, lse_ref, *rest = rest
    else:
        w_query, b_query, *rest = rest
        hat_ref, k_ref, v_ref, q_ref, acc_out, top_out, sum_out, *rest = rest
    normed, kt_ref, va_ref, *score_refs = rest
    item = pl.program_id(0)
    key_count = rows * blocks
    query_rows = q_ref.shape[0]

    @pl.when(pl.program_id(1) == 0)
    def _():
        hat, _ = hat_rows(x_ref[...].astype(f32))
        hat_ref[...] = hat.astype(bf16)
        normed[...] = (hat * gain[...] + shift[...]).astype(bf16)

    weights = [w_key[...], w_value[...]] if final else [w_key[...], w_value[...], w_query[...]]
    projected = dot_rows(normed[...], jnp.concatenate(weights, axis=1))
    k_ref[...] = projected[:, :PAIR].astype(bf16)
    v_ref[...] = (projected[:, PAIR:2 * PAIR] + b_value[...]).astype(bf16)
    if not final:
        query = (projected[:, 2 * PAIR:] + b_query[...]).astype(bf16)
        q_ref[...] = (query.astype(f32) * SCALE).astype(bf16)
    keys = k_ref[...].astype(f32)
    values = v_ref[...].astype(f32)
    first = lanes_of((key_count, PAIR)) < HEAD_DIM
    flipped = keys.T.astype(bf16)
    key_id = lax.broadcasted_iota(jnp.int32, (8, key_count), 1)
    bias = jnp.zeros((8, key_count), f32)
    for block in range(blocks):
        here = (key_id >= block * rows + limits[item, block]) & (key_id < (block + 1) * rows)
        bias = jnp.where(here, NEGATIVE, bias)
    bias = jnp.where(lax.broadcasted_iota(jnp.int32, (8, key_count), 0) == 0, bias, 0.0)
    spare = jnp.concatenate([bias, jnp.zeros((HEAD_DIM - 8, key_count), f32)], 0).astype(bf16)
    kt_ref[0, :HEAD_DIM, :] = flipped[:HEAD_DIM]
    kt_ref[0, HEAD_DIM:, :] = spare
    kt_ref[1, :HEAD_DIM, :] = spare
    kt_ref[1, HEAD_DIM:, :] = flipped[HEAD_DIM:]
    va_ref[0] = jnp.where(first, values, 1.0).astype(bf16)
    va_ref[1] = jnp.where(first, 1.0, values).astype(bf16)
    lanes = lanes_of((step, PAIR))
    head_first = lanes < HEAD_DIM
    one = jnp.where((lanes & (HEAD_DIM - 1)) == 0, 1.0, 0.0)
    tiles = [slice(t, min(t + TILE, key_count)) for t in range(0, key_count, TILE)]

    def query_of(unit):
        chunk, head = divmod(unit, 2)
        query = q_ref[chunk * step:(chunk + 1) * step, :].astype(f32)
        mine = head_first if head == 0 else jnp.logical_not(head_first)
        return jnp.where(mine, query, one).astype(bf16)

    units = 2 * (query_rows // step)
    outs, tops = [], []
    for unit in range(-1, units):
        query = query_of(unit + 1) if unit + 1 < units else None
        out, best = None, None
        for tile in tiles:
            if query is not None:
                scores = dot_rows(query, kt_ref[(unit + 1) % 2, :, tile])
                score_refs[(unit + 1) % 2][:, tile] = scores
                high = jnp.max(scores, axis=1, keepdims=True)
                best = high if best is None else jnp.maximum(best, high)
            if unit >= 0:
                weights = jnp.exp(score_refs[unit % 2][:, tile] - tops[unit]).astype(bf16)
                added = dot_rows(weights, va_ref[unit % 2, tile, :])
                out = added if out is None else out + added
        if best is not None:
            tops.append(best)
        if out is not None:
            outs.append(out)
        if unit % 2 == 0 or unit < 0:
            continue
        chunk = unit // 2
        place = slice(chunk * step, (chunk + 1) * step)
        acc = jnp.where(head_first, outs[unit - 1], outs[unit])
        total = pltpu.roll(jnp.where(head_first, outs[unit], outs[unit - 1]), HEAD_DIM, 1)
        top = jnp.where(head_first, tops[unit - 1], tops[unit])
        if final:
            other_top = top_in[place, :]
            new_top = jnp.maximum(top, other_top)
            scale_here = jnp.exp(top - new_top)
            scale_there = jnp.exp(other_top - new_top)
            total = total * scale_here + sum_in[place, :] * scale_there
            acc = acc * scale_here + acc_in[place, :] * scale_there
            out_ref[place, :] = acc / total
            lse_ref[place, :] = pltpu.roll(new_top + jnp.log(total), HEAD_DIM, 1)
        else:
            acc_out[place, :] = acc
            top_out[place, :] = top
            sum_out[place, :] = total


def attend(limits, x, norms, w_key, w_value, b_value, query, rows, blocks, before):
    width = x.shape[1]
    key_count = rows * blocks
    items = x.shape[0] // key_count
    total = items * rows
    step = chunk_of(rows, 208)
    query_block = pl.BlockSpec((rows, PAIR), lambda i, p, *_: (i, p))
    key_block = pl.BlockSpec((key_count, PAIR), lambda i, p, *_: (i, p))
    row_block = pl.BlockSpec((key_count, width), lambda i, p, *_: (i, 0))
    weight_block = pl.BlockSpec((width, PAIR), lambda i, p, *_: (0, p))
    line_block = pl.BlockSpec((1, PAIR), lambda i, p, *_: (0, p))
    final = before is not None
    shape = jax.ShapeDtypeStruct
    out_specs = [row_block, key_block, key_block]
    out_shape = [shape(x.shape, bf16)] * 3
    if final:
        extra, extra_specs = [query, *before], [query_block] * (1 + len(before))
        out_specs += [query_block] * 2
        out_shape += [shape((total, width), f32)] * 2
    else:
        extra, extra_specs = list(query), [weight_block, line_block]
        out_specs += [query_block] * 4
        out_shape += [shape((total, width), bf16)] + [shape((total, width), f32)] * 3
    return pl.pallas_call(
        functools.partial(forward_kernel, final, rows, blocks, step),
        grid_spec=pltpu.PrefetchScalarGridSpec(
            num_scalar_prefetch=1,
            grid=(items, PAIRS),
            in_specs=[row_block, whole((1, width)), whole((1, width))]
            + [weight_block] * 2
            + [line_block]
            + extra_specs,
            out_specs=out_specs,
            scratch_shapes=[
                pltpu.VMEM((key_count, width), bf16),
                pltpu.VMEM((2, PAIR, key_count), bf16),
                pltpu.VMEM((2, key_count, PAIR), bf16),
                pltpu.VMEM((step, key_count), f32),
                pltpu.VMEM((step, key_count), f32),
            ],
        ),
        out_shape=out_shape,
        compiler_params=params(2),
        cost_estimate=cost(
            16 * total * key_count * width, 12 * total * width, total * key_count * HEADS
        ),
        name="attend",
    )(limits, x, *norms, w_key, w_value, b_value, *extra)


def split_three(value):
    high = value.astype(bf16).astype(f32)
    rest = value - high
    middle = rest.astype(bf16).astype(f32)
    return high, middle, rest - middle


def halves(core, block):
    half = block.shape[0] // 2
    upper, lower = block[:half], block[half:]
    mine = jnp.where(core == 0, upper, lower)
    theirs = jnp.where(core == 0, lower, upper)
    return mine.astype(bf16), theirs.astype(bf16)


def backward_kernel(
    last, tokens, rows, blocks, step, limits, core,
    q_ref, k_ref, v_ref, g_ref, out_ref, lse_ref, hat_ref, *rest,
):
    if last:
        before_ref, dw_in, sums_in, *rest = rest
        cat_ref, keep_ref, send_ref, dw_acc, sums_acc, qt_ref, gt_ref, dqt_ref, *wide = rest[tokens:]
    else:
        dq_ref, cat_ref, dw_ref, sums_ref, dw_acc, sums_acc, qt_ref, gt_ref, dqt_ref, *wide = rest[tokens:]
    prob_refs, score_refs = wide[:2], wide[2:]
    pair = pl.program_id(0)
    item = pl.program_id(1)
    query_rows = q_ref.shape[0]
    lanes = lanes_of((query_rows, PAIR))
    head_first = lanes < HEAD_DIM
    spare_lane = lanes & (HEAD_DIM - 1)

    def spare(parts, mask_one):
        high, middle, low = parts
        value = jnp.where(spare_lane == 0, high, 0.0)
        value = jnp.where(spare_lane == 1, middle, value)
        value = jnp.where(spare_lane == 2, low, value)
        return jnp.where(spare_lane == 3, mask_one, value)

    query = q_ref[...].astype(f32)
    grad = g_ref[...].astype(f32)
    product = grad * out_ref[...]
    delta_first = jnp.sum(jnp.where(head_first, product, 0.0), axis=1, keepdims=True)
    delta_second = jnp.sum(jnp.where(head_first, 0.0, product), axis=1, keepdims=True)
    delta = jnp.where(head_first, delta_second, delta_first)
    lse_spare = spare(split_three(-lse_ref[...]), 1.0)
    delta_spare = spare(split_three(-delta), 0.0)
    qt_ref[0] = jnp.where(head_first, query, lse_spare).T.astype(bf16)
    qt_ref[1] = jnp.where(head_first, lse_spare, query).T.astype(bf16)
    gt_ref[0] = jnp.where(head_first, grad, delta_spare).T.astype(bf16)
    gt_ref[1] = jnp.where(head_first, delta_spare, grad).T.astype(bf16)
    dqt_ref[...] = jnp.zeros_like(dqt_ref)

    key_lanes = lanes_of((step, PAIR))
    key_first = key_lanes < HEAD_DIM
    key_spare = key_lanes & (HEAD_DIM - 1)
    key_row = lax.broadcasted_iota(jnp.int32, (step, PAIR), 0)
    ones = jnp.where(key_spare < 3, 1.0, 0.0)
    per_block = rows // step
    tiles = [slice(t, min(t + TILE, query_rows)) for t in range(0, query_rows, TILE)]

    def operands(unit):
        chunk, head = divmod(unit, 2)
        place = slice(chunk * step, (chunk + 1) * step)
        block = chunk // per_block
        limit = limits[item, block] - (chunk - block * per_block) * step
        bias = jnp.where(key_row >= limit, NEGATIVE, 0.0)
        key = k_ref[place, :].astype(f32)
        value = v_ref[place, :].astype(f32)
        mine = key_first if head == 0 else jnp.logical_not(key_first)
        key_head = jnp.where(mine, key, jnp.where(key_spare == 3, bias, ones)).astype(bf16)
        value_head = jnp.where(mine, value, ones).astype(bf16)
        half = key.T[head * HEAD_DIM:(head + 1) * HEAD_DIM].astype(bf16)
        return key_head, value_head, half

    units = 2 * blocks * per_block
    dks, dvs, half = [], [], None
    for unit in range(-1, units):
        more = unit + 1 < units
        if more:
            key_head, value_head, next_half = operands(unit + 1)
            which = (unit + 1) % 2
        dk, dv = None, None
        for tile in tiles:
            if more:
                probs = jnp.exp(dot_rows(key_head, qt_ref[which, :, tile]))
                grad_probs = dot_rows(value_head, gt_ref[which, :, tile])
                prob_refs[which][:, tile] = probs.astype(bf16)
                score_refs[which][:, tile] = (probs * grad_probs).astype(bf16)
            if unit >= 0:
                grad_scores = score_refs[unit % 2][:, tile]
                dv_part = dot_rows(prob_refs[unit % 2][:, tile], g_ref[tile, :])
                dk_part = dot_rows(grad_scores, q_ref[tile, :])
                dv = dv_part if dv is None else dv + dv_part
                dk = dk_part if dk is None else dk + dk_part
                own = slice(unit % 2 * HEAD_DIM, (unit % 2 + 1) * HEAD_DIM)
                dqt_ref[own, tile] += dot_rows(half, grad_scores)
        half = next_half if more else None
        if unit >= 0:
            dks.append(dk)
            dvs.append(dv)
        if unit >= 0 and unit % 2 == 1:
            place = slice(unit // 2 * step, (unit // 2 + 1) * step)
            cat_ref[place, :PAIR] = jnp.where(key_first, dks[-2], dks[-1]).astype(bf16)
            cat_ref[place, PAIR:2 * PAIR] = jnp.where(key_first, dvs[-2], dvs[-1]).astype(bf16)

    result = dqt_ref[...].T
    if last:
        cat_ref[:, 2 * PAIR:] = ((result + before_ref[...]) * SCALE).astype(bf16)
    else:
        dq_ref[...] = result
    added = dot_left(hat_ref[...], cat_ref[...])
    sums = column_sums(cat_ref[...].astype(f32))
    items = pl.num_programs(1)
    here = pl.ds(pair, 1)

    @pl.when((item == 0) & (pair == 0))
    def _():
        sums_acc[...] = jnp.zeros_like(sums_acc)

    @pl.when(item == 0)
    def _():
        dw_acc[...] = added
        if last:
            dw_acc[:, :2 * PAIR] += dw_in[0]
            sums_acc[here, :2 * PAIR] = sums_in[0, :1, :]

    @pl.when(item > 0)
    def _():
        dw_acc[...] += added

    sums_acc[here, :] += sums

    @pl.when(item == items - 1)
    def _():
        if last:
            half = dw_acc.shape[0] // 2
            place = pl.ds(pl.multiple_of(pair * half, half), half)
            keep_ref[place, :], send_ref[place, :] = halves(core[0], dw_acc[...])
        else:
            dw_ref[0] = dw_acc[...]
            sums_ref[0] = jnp.broadcast_to(sums_acc[here, :], sums_ref.shape[1:])

    if last:

        @pl.when((item == items - 1) & (pair == pl.num_programs(0) - 1))
        def _():
            end = slice(keep_ref.shape[0] - sums_acc.shape[0] // 2, None)
            keep_ref[end, :], send_ref[end, :] = halves(core[0], sums_acc[...])


def attend_back(
    limits, core, queries, keys, values, grads, outs, lse, hat, rows, blocks, first, count, before,
    spare, tokens,
):
    total, width = queries.shape
    items = total // rows
    key_count = rows * blocks
    step = chunk_of(rows, 208)
    last = before is not None
    cat = (3 if last else 2) * PAIR
    query_block = pl.BlockSpec((rows, PAIR), lambda p, i, *_: (i, first + p))
    key_block = pl.BlockSpec((key_count, PAIR), lambda p, i, *_: (i, first + p))
    hat_block = pl.BlockSpec((key_count, width), lambda p, i, *_: (i, 0))
    cat_block = pl.BlockSpec((key_count, cat), lambda p, i, *_: (i, p))
    shape = jax.ShapeDtypeStruct
    cat_shape = shape((total * blocks, cat * count), bf16)
    if last:
        (part, _, dw_part, sums_part), skip = before
        extra = [part, dw_part, sums_part]
        extra_specs = [
            pl.BlockSpec((rows, PAIR), lambda p, i, *_: (i, skip + p)),
            pl.BlockSpec((1, width, 2 * PAIR), lambda p, i, *_: (skip + p, 0, 0)),
            pl.BlockSpec((1, 8, 2 * PAIR), lambda p, i, *_: (skip + p, 0, 0)),
        ]
        half = (count * width // 2 + spare, cat)
        out_shape = [cat_shape] + [shape(half, bf16)] * 2
        out_specs = [cat_block] + [whole(half)] * 2
    else:
        extra, extra_specs = [], []
        out_shape = [
            shape((total, PAIR * count), f32),
            cat_shape,
            shape((count, width, cat), f32),
            shape((count, 8, cat), f32),
        ]
        out_specs = [
            pl.BlockSpec((rows, PAIR), lambda p, i, *_: (i, p)),
            cat_block,
            pl.BlockSpec((1, width, cat), lambda p, i, *_: (p, 0, 0)),
            pl.BlockSpec((1, 8, cat), lambda p, i, *_: (p, 0, 0)),
        ]
    return pl.pallas_call(
        functools.partial(backward_kernel, last, len(tokens), rows, blocks, step),
        grid_spec=pltpu.PrefetchScalarGridSpec(
            num_scalar_prefetch=2,
            grid=(count, items),
            in_specs=[query_block, key_block, key_block]
            + [query_block] * 3
            + [hat_block]
            + extra_specs
            + [ANYWHERE] * len(tokens),
            out_specs=out_specs,
            scratch_shapes=[
                pltpu.VMEM((width, cat), f32),
                pltpu.VMEM((2 * spare, cat), f32),
                pltpu.VMEM((2, PAIR, rows), bf16),
                pltpu.VMEM((2, PAIR, rows), bf16),
                pltpu.VMEM((PAIR, rows), f32),
            ]
            + [pltpu.VMEM((step, rows), bf16)] * 4,
        ),
        out_shape=out_shape,
        compiler_params=params(2),
        cost_estimate=cost(
            total * PAIR * count,
            total * PAIR * count,
        ),
        name="attend_back",
    )(limits, core, queries, keys, values, grads, outs, lse, hat, *extra, *tokens)


def feed_kernel(
    core, x_ref, mix_ref, dy_ref, w_output, w_expand, w_reduce, b_output, b_expand, b_reduce, gain, shift,
    y_ref, dmid_ref, dmix_ref, keep_ref, send_ref,
    middle_ref, normed_ref, y_acc, grad_acc, line_ref,
):
    part = pl.program_id(0)

    half = w_output.shape[0] // 2

    def put(index, block):
        place = pl.ds(pl.multiple_of(index * half, half), half)
        keep_ref[place, :], send_ref[place, :] = halves(core[0], block)

    @pl.when(part == 0)
    def _():
        mixed = mix_ref[...].astype(bf16)
        middle = x_ref[...].astype(f32) + dot_rows(mixed, w_output[...]) + b_output[...]
        middle_ref[...] = middle
        hat, _ = hat_rows(middle)
        normed_ref[...] = (hat * gain[...] + shift[...]).astype(bf16)
        y_acc[...] = middle + b_reduce[...]
        grad_acc[...] = jnp.zeros_like(grad_acc)
        line_ref[...] = jnp.zeros_like(line_ref)
        line_ref[1:2, :] = column_sums(dy_ref[...].astype(f32))

    normed = normed_ref[...]
    upper = dot_rows(normed, w_expand[...]) + b_expand[...]
    cumulative = 0.5 * lax.erf(upper * math.sqrt(0.5)) + 0.5
    density = jnp.exp(upper * upper * -0.5) * (1.0 / math.sqrt(2.0 * math.pi))
    active = (upper * cumulative).astype(bf16)
    slope = cumulative + upper * density
    y_acc[...] += dot_rows(active, w_reduce[...])
    put(1 + 2 * part, dot_left(active, dy_ref[...]))
    grad_upper = (dot_right(dy_ref[...], w_reduce[...]) * slope).astype(bf16)
    line_ref[pl.ds(4 + part, 1), :] = column_sums(grad_upper.astype(f32))
    put(2 + 2 * part, dot_left(normed, grad_upper))
    grad_acc[...] += dot_right(grad_upper, w_expand[...])

    @pl.when(part == pl.num_programs(0) - 1)
    def _():
        y_ref[...] = y_acc[...].astype(bf16)
        grad = grad_acc[...]
        hat, inverse = hat_rows(middle_ref[...])
        line_ref[2:3, :] = column_sums(grad * hat)
        line_ref[3:4, :] = column_sums(grad)
        dmid = hat_back(grad * gain[...], hat, inverse) + dy_ref[...].astype(f32)
        dmid_ref[...] = dmid
        branch = dmid.astype(bf16)
        line_ref[0:1, :] = column_sums(branch.astype(f32))
        put(0, dot_left(mix_ref[...].astype(bf16), branch))
        end = slice(keep_ref.shape[0] - line_ref.shape[0] // 2, None)
        keep_ref[end, :], send_ref[end, :] = halves(core[0], line_ref[...])
        dmix_ref[...] = dot_right(branch, w_output[...]).astype(bf16)


def feed(core, spare, x, mixed, dy, w_output, w_expand, w_reduce, b_output, b_expand, b_reduce, gain, shift):
    rows, width = x.shape
    hidden = w_expand.shape[1]
    parts = hidden // width
    row = whole((rows, width))
    line = whole((1, width))
    expand = pl.BlockSpec((width, width), lambda i, *_: (0, i))
    reduce = pl.BlockSpec((width, width), lambda i, *_: (i, 0))
    hidden_line = pl.BlockSpec((1, width), lambda i, *_: (0, i))
    weights = ((1 + 2 * parts) * width // 2 + spare, width)
    shape = jax.ShapeDtypeStruct
    return pl.pallas_call(
        feed_kernel,
        grid_spec=pltpu.PrefetchScalarGridSpec(
            num_scalar_prefetch=1,
            grid=(parts,),
            in_specs=[row, row, row, whole((width, width)), expand, reduce, line, hidden_line, line, line, line],
            out_specs=[row, row, row, whole(weights), whole(weights)],
            scratch_shapes=[
                pltpu.VMEM((rows, width), f32),
                pltpu.VMEM((rows, width), bf16),
                pltpu.VMEM((rows, width), f32),
                pltpu.VMEM((rows, width), f32),
                pltpu.VMEM((2 * spare, width), f32),
            ],
        ),
        out_shape=[
            shape((rows, width), bf16),
            shape((rows, width), f32),
            shape((rows, width), bf16),
            shape(weights, bf16),
            shape(weights, bf16),
        ],
        compiler_params=params(1),
        cost_estimate=cost(12 * rows * width * hidden + 6 * rows * width * width, 20 * rows * width, 2 * rows * hidden),
        name="feed",
    )(core, x, mixed, dy, w_output, w_expand, w_reduce, b_output, b_expand, b_reduce, gain, shift)


def gather_parts(refs, part, parts):
    blocks = []
    for ref in refs:
        pairs = ref.shape[1] // (parts * PAIR)
        for pair in range(pairs):
            start = (pair * parts + part) * PAIR
            blocks.append(ref[:, start:start + PAIR])
    return jnp.concatenate(blocks, axis=1)


def other_kernel(cats, w_key, w_value, *rest):
    cat_refs, send_ref = rest[:cats], rest[-1]
    dk = gather_parts(cat_refs, 0, 2)
    dv = gather_parts(cat_refs, 1, 2)
    send_ref[...] = (dot_right(dk, w_key[...]) + dot_right(dv, w_value[...])).astype(bf16)


def other_grads(cats, w_key, w_value, rows, after):
    total, width = cats[0].shape[0], w_key.shape[0]
    step = chunk_of(rows, 272)
    return pl.pallas_call(
        functools.partial(other_kernel, len(cats)),
        grid=(total // step,),
        in_specs=[whole((width, width))] * 2
        + [pl.BlockSpec((step, c.shape[1]), lambda i: (i, 0)) for c in cats]
        + [ANYWHERE] * len(after),
        out_specs=pl.BlockSpec((step, width), lambda i: (i, 0)),
        out_shape=jax.ShapeDtypeStruct((total, width), bf16),
        compiler_params=params(1),
        cost_estimate=cost(total * width, total * width),
        name="other_grads",
    )(w_key, w_value, *cats, *after)


def own_kernel(cats, x_ref, recv_ref, dmid_ref, w_query, w_key, w_value, gain, *rest):
    cat_refs, dx_ref = rest[:cats], rest[-1]
    dk = gather_parts(cat_refs, 0, 3)
    dv = gather_parts(cat_refs, 1, 3)
    dq = gather_parts(cat_refs, 2, 3)
    grad = dot_right(dq, w_query[...]) + dot_right(dk, w_key[...]) + dot_right(dv, w_value[...])
    for index in range(recv_ref.shape[0]):
        grad = grad + recv_ref[index].astype(f32)
    hat, inverse = hat_rows(x_ref[...].astype(f32))
    dx_ref[...] = hat_back(grad * gain[...], hat, inverse) + dmid_ref[...]


def own_grads(x, cats, recv, dmid, w_query, w_key, w_value, gain, after):
    rows, width = x.shape
    step = chunk_of(rows, 272)
    row = pl.BlockSpec((step, width), lambda i: (i, 0))
    return pl.pallas_call(
        functools.partial(own_kernel, len(cats)),
        grid=(rows // step,),
        in_specs=[row, pl.BlockSpec((recv.shape[0], step, width), lambda i: (0, i, 0)), row]
        + [whole((width, width))] * 3
        + [whole((1, width))]
        + [pl.BlockSpec((step, c.shape[1]), lambda i: (i, 0)) for c in cats]
        + [ANYWHERE] * len(after),
        out_specs=row,
        out_shape=jax.ShapeDtypeStruct((rows, width), f32),
        compiler_params=params(1),
        cost_estimate=cost(6 * rows * width * width, 16 * rows * width),
        name="own_grads",
    )(x, recv, dmid, w_query, w_key, w_value, gain, *cats, *after)


class Slice:
    def __init__(self):
        group, rest = lax.axis_size("grp"), lax.axis_size("rest")
        batch = rest * lax.axis_size("core")
        side = 2 if rest % 2 == 0 else 1
        rest //= side
        high = 2 if rest % 2 == 0 else 1
        self.sizes = {"core": 2, "side": side, "member": group, "high": high, "low": rest // high}
        self.count = group * batch
        self.here = self.coords(lax.axis_index(ALL))

    def coords(self, linear):
        out = {}
        for name in ("member", "core", "side", "low", "high"):
            out[name] = linear % self.sizes[name]
            linear = linear // self.sizes[name]
        return out

    def linear(self, coords):
        total = 0
        for name in ("high", "low", "side", "core", "member"):
            total = total * self.sizes[name] + coords[name]
        return total

    def size(self, stage):
        return math.prod(self.sizes[name] for name in stage)

    def place(self, stage, coords=None):
        coords = self.here if coords is None else coords
        total = 0
        for name in stage:
            total = total * self.sizes[name] + coords[name]
        return total

    def send(self, array, stage, shift):
        pairs = []
        for source in range(self.count):
            coords = self.coords(source)
            place = (self.place(stage, coords) + shift) % self.size(stage)
            for name in reversed(stage):
                coords[name] = place % self.sizes[name]
                place //= self.sizes[name]
            pairs.append((source, self.linear(coords)))
        return lax.ppermute(array, ALL, pairs)

    def spread(self, parts, stage):
        return [parts[0]] + [self.send(part, stage, s) for s, part in enumerate(parts) if s > 0]

    def share(self, array, stage):
        return self.spread([array] * self.size(stage), stage)

    def origins(self, stage):
        size = self.size(stage)
        return ((self.place(stage) - jnp.arange(size)) % size).astype(jnp.int32)

    def in_order(self, parts, stage):
        if len(parts) <= 2:
            return parts
        stack = jnp.stack(parts)
        order = self.origins(stage)
        return [lax.dynamic_index_in_dim(stack, order[i], 0, False) for i in range(len(parts))]


def behind(array, *others):
    return lax.optimization_barrier((array, *others))[0] if others else array


def cut_kernel(size, groups, place, *refs):
    ins, outs = refs[:2 * groups], refs[2 * groups:]
    for shift, out in enumerate(outs):
        start = 0
        for index in range(groups):
            keep, came = ins[2 * index], ins[2 * index + 1]
            rows = keep.shape[0] // size
            span = pl.ds(pl.multiple_of((place[0] + shift) % size * rows, 16), rows)
            total = keep[span, :].astype(f32) + came[span, :].astype(f32)
            out[start:start + rows, :] = total.astype(bf16)
            start += rows


def cut(pairs, place, size):
    arrays = [array for pair in pairs for array in pair]
    width = arrays[0].shape[1]
    part = (sum(keep.shape[0] for keep, _ in pairs) // size, width)
    return pl.pallas_call(
        functools.partial(cut_kernel, size, len(pairs)),
        grid_spec=pltpu.PrefetchScalarGridSpec(
            num_scalar_prefetch=1,
            grid=(1,),
            in_specs=[whole(a.shape) for a in arrays],
            out_specs=[whole(part)] * size,
        ),
        out_shape=[jax.ShapeDtypeStruct(part, bf16)] * size,
        compiler_params=params(1),
        cost_estimate=cost(size * part[0] * width, 6 * size * part[0] * width),
        name="cut",
    )(jnp.reshape(place, (1,)).astype(jnp.int32), *arrays)


def add_up(parts):
    total = parts[0].astype(f32)
    for part in parts[1:]:
        total = total + part.astype(f32)
    return total.astype(bf16)


def join_kernel(places, *refs):
    out = refs[-1]
    for index, ref in enumerate(refs[:-1]):
        rows = ref.shape[0]
        out[pl.ds(pl.multiple_of(places[index] * rows, 16), rows), :] = ref[...]


def join(places, parts):
    rows, width = parts[0].shape
    shape = (len(parts) * rows, width)
    return pl.pallas_call(
        join_kernel,
        grid_spec=pltpu.PrefetchScalarGridSpec(
            num_scalar_prefetch=1,
            grid=(1,),
            in_specs=[whole(part.shape) for part in parts],
            out_specs=whole(shape),
        ),
        out_shape=jax.ShapeDtypeStruct(shape, bf16),
        compiler_params=params(1),
        cost_estimate=cost(0, rows * width),
        name="join",
    )(places, *parts)


def place_pieces(places, core, pieces, flats):
    size = len(pieces) // 2
    for which in range(2):
        target = core[0] if which == 0 else 1 - core[0]
        for index in range(size):
            piece, at = pieces[which * size + index], 0
            for flat in flats:
                rows = flat.shape[1] // size
                span = pl.ds(pl.multiple_of(places[index] * rows, 16), rows)
                flat[target, span, :] = piece[at:at + rows, :]
                at += rows


def feed_weights_kernel(size, places, core, *refs):
    pieces, (dwo_ref, dwe_ref, dwr_ref, *line_refs, dbe_ref, flat) = refs[:2 * size], refs[-9:]
    width = dwo_ref.shape[0]
    half = width // 2
    step = pl.program_id(0)
    parts = pl.num_programs(0) - 1

    @pl.when(step == 0)
    def _():
        place_pieces(places, core, pieces, [flat])

    @pl.when(step < parts)
    def _():
        start = pl.multiple_of((1 + 2 * step) * half, half)
        for side in range(2):
            rows = slice(side * half, (side + 1) * half)
            dwr_ref[rows, :] = flat[side, pl.ds(start, half), :].astype(f32)
            dwe_ref[rows, :] = flat[side, pl.ds(start + half, half), :].astype(f32)

    @pl.when(step == parts)
    def _():
        for side in range(2):
            dwo_ref[side * half:(side + 1) * half, :] = flat[side, :half, :].astype(f32)
        count = dbe_ref.shape[1] // width
        start = (1 + 2 * count) * half
        lines = flat[0, start:start + 16, :].astype(f32)
        for index, ref in enumerate(line_refs):
            ref[...] = lines[index:index + 1]
        for part in range(count):
            dbe_ref[:, part * width:(part + 1) * width] = lines[4 + part:5 + part]


def feed_weights(places, core, own, came, hidden, after):
    rows, width = own[0].shape
    parts = hidden // width
    shapes = [(width, width), (width, hidden), (hidden, width)] + [(1, width)] * 4 + [(1, hidden)]
    out_specs = [whole(s) for s in shapes]
    out_specs[1] = pl.BlockSpec((width, width), lambda p, *_: (0, jnp.minimum(p, parts - 1)))
    out_specs[2] = pl.BlockSpec((width, width), lambda p, *_: (jnp.minimum(p, parts - 1), 0))
    return pl.pallas_call(
        functools.partial(feed_weights_kernel, len(own)),
        grid_spec=pltpu.PrefetchScalarGridSpec(
            num_scalar_prefetch=2,
            grid=(parts + 1,),
            in_specs=[whole((rows, width))] * (2 * len(own)) + [ANYWHERE] * len(after),
            out_specs=out_specs,
            scratch_shapes=[pltpu.VMEM((2, len(own) * rows, width), bf16)],
        ),
        out_shape=[jax.ShapeDtypeStruct(s, f32) for s in shapes],
        compiler_params=params(1),
        cost_estimate=cost(0, 12 * len(own) * rows * width),
        name="feed_weights",
    )(places, core, *own, *came, *after)


def project_weights_kernel(calls, places, core, *refs):
    flats, refs = refs[len(refs) - len(calls):], refs[:len(refs) - len(calls)]
    pieces, refs = refs[:-16], refs[-16:]
    weights, (gain, shift), refs = refs[:3], refs[3:5], refs[5:]
    outs, (dgain_ref, dshift_ref, dbq_ref, dbv_ref), refs = refs[:3], refs[3:7], refs[7:]
    gains, shifts, cross_acc, plain_acc = refs
    pair = pl.program_id(0)
    width = gains.shape[0]
    half = width // 2

    @pl.when(pair == 0)
    def _():
        place_pieces(places, core, pieces, flats)
        gains[...] = jnp.broadcast_to(gain[...], (PAIR, width)).T
        shifts[...] = jnp.broadcast_to(shift[...], (PAIR, width)).T
        cross_acc[...] = jnp.zeros_like(cross_acc)
        plain_acc[...] = jnp.zeros_like(plain_acc)

    def put(flat, pairs, index):
        sums = flat[0, pairs * half:pairs * half + 16, :].astype(f32)[index:index + 1]
        dbv_ref[...] = sums[:, PAIR:2 * PAIR]
        dbq_ref[...] = sums[:, 2 * PAIR:]
        for side in range(2):
            down = slice(side * half, (side + 1) * half)
            block = flat[side, index * half:(index + 1) * half, :].astype(f32)
            for which, (out, weight) in enumerate(zip(outs, weights)):
                lanes = slice(which * PAIR, (which + 1) * PAIR)
                part, line = block[:, lanes], sums[:, lanes]
                out[down, :] = gains[down, :] * part + shifts[down, :] * line
                own = weight[down, :].astype(f32)
                cross_acc[down, :] += own * part
                plain_acc[down, :] += own * line

    first = 0
    for flat, pairs in zip(flats, calls):
        for index in range(pairs):
            pl.when(pair == first + index)(functools.partial(put, flat, pairs, index))
        first += pairs

    @pl.when(pair == PAIRS - 1)
    def _():
        for acc, out in ((cross_acc, dgain_ref), (plain_acc, dshift_ref)):
            column = jnp.broadcast_to(jnp.sum(acc[...], axis=1, keepdims=True), (width, PAIR))
            out[...] = column.T[:1]


def project_weights(places, core, own, came, w_key, w_value, w_query, gain, shift, calls, spare):
    width = w_query.shape[0]
    rows, cat = own[0].shape
    line = whole((1, width))
    column_block = pl.BlockSpec((width, PAIR), lambda p, *_: (0, p))
    line_block = pl.BlockSpec((1, PAIR), lambda p, *_: (0, p))
    return pl.pallas_call(
        functools.partial(project_weights_kernel, calls),
        grid_spec=pltpu.PrefetchScalarGridSpec(
            num_scalar_prefetch=2,
            grid=(PAIRS,),
            in_specs=[whole((rows, cat))] * (2 * len(own)) + [column_block] * 3 + [line] * 2,
            out_specs=[column_block] * 3 + [line] * 2 + [line_block] * 2,
            scratch_shapes=[pltpu.VMEM((width, PAIR), f32)] * 4
            + [pltpu.VMEM((2, count * width // 2 + spare, cat), bf16) for count in calls],
        ),
        out_shape=[jax.ShapeDtypeStruct((width, width), f32)] * 3
        + [jax.ShapeDtypeStruct((1, width), f32)] * 4,
        compiler_params=params(1),
        cost_estimate=cost(0, 20 * width * width),
        name="project_weights",
    )(places, core, *own, *came, w_key, w_value, w_query, gain, shift)


def body(
    layer_input,
    lang_counts,
    w_query,
    w_key,
    w_value,
    w_output,
    w_expand,
    w_reduce,
    b_query,
    b_value,
    b_output,
    b_expand,
    b_reduce,
    gain_attn,
    shift_attn,
    gain_mlp,
    shift_mlp,
    cotangent,
):
    items, own_rows, width = layer_input.shape
    group = lax.axis_size("grp")
    me = lax.axis_index("grp")
    rows = -(-own_rows // 16) * 16
    total = items * rows
    patch_rows = VIEWS * PATCH
    shifts = range(1, group)

    def padded(array):
        if rows != own_rows:
            array = jnp.pad(array, ((0, 0), (0, rows - own_rows), (0, 0)))
        return array.reshape(total, width)

    def unpadded(array):
        return array.reshape(items, rows, width)[:, :own_rows]

    def limit_of(owner):
        return jnp.clip(patch_rows + lang_counts - owner * own_rows, 0, own_rows)

    def line(vector):
        return vector.reshape(1, -1)

    def group_shift(array, shift):
        return lax.ppermute(array, "grp", [(i, (i + shift) % group) for i in range(group)])

    def joined(parts):
        if len(parts) == 1:
            return parts[0]
        return jnp.stack([p.reshape(items, rows, width) for p in parts], 1).reshape(-1, width)

    x = padded(layer_input)
    dy = padded(cotangent)
    others = [group_shift(x, -shift) for shift in shifts]
    own_limits = limit_of(me).reshape(items, 1)
    other_limits = jnp.stack([limit_of((me + shift) % group) for shift in shifts], 1)

    norms = (line(gain_attn), line(shift_attn))
    hat, keys, values, queries, *first = attend(
        own_limits, x, norms, w_key, w_value, line(b_value), (w_query, line(b_query)), rows, 1, None
    )
    hat_other, keys_other, values_other, mixed, lse = attend(
        other_limits, joined(others), norms, w_key, w_value, line(b_value), queries, rows, group - 1, first
    )

    devices = Slice()
    plane = ("side", "member")
    core = jnp.reshape(devices.here["core"], (1,)).astype(jnp.int32)
    plane_place, plane_size = devices.place(plane), devices.size(plane)
    spare = 16 * plane_size
    line_stage = ("high", "low") if devices.size(("high", "low")) <= 4 else ("high",)
    line_size = devices.size(line_stage)
    output, dmid, dmix, keep, give = feed(
        core, spare * line_size, x, mixed, dy, w_output, w_expand, w_reduce, line(b_output), line(b_expand),
        line(b_reduce), line(gain_mlp), line(shift_mlp),
    )

    def summed(value, stage, *after):
        own, *came = devices.share(value, (stage,))
        return add_up(devices.in_order([behind(own, *after), *came], (stage,)))

    def back_other(first, count, tokens):
        return attend_back(
            other_limits, core, queries, keys_other, values_other, dmix, mixed, lse, hat_other,
            rows, group - 1, first, count, None, spare, tokens,
        )

    def back_own(first, count, before, tokens):
        return attend_back(
            own_limits, core, queries, keys, values, dmix, mixed, lse, hat,
            rows, 1, first, count, before, spare, tokens,
        )

    feed_pair = devices.spread([keep, give], ("core",))
    other_first = back_other(0, 1, [])
    feed_pair = [behind(half, other_first[1]) for half in feed_pair]

    def cut_plain(arrays, stage):
        size, place = devices.size(stage), devices.place(stage)
        rows = arrays[0].shape[0] // size
        return [
            add_up([lax.dynamic_slice_in_dim(a, (place + s) % size * rows, rows) for a in arrays])
            for s in range(size)
        ]

    parts = cut_plain(feed_pair, plane)
    other_rest = back_other(1, PAIRS - 1, parts[:1])
    own, *came = devices.spread(parts, plane)
    parts = cut_plain([behind(own, other_rest[1]), *came], line_stage)
    send = other_grads([other_first[1], other_rest[1]], w_key, w_value, rows, parts[:1])
    send = send.reshape(items, group - 1, rows, width)
    received = jnp.stack(
        [group_shift(send[:, shift - 1].reshape(total, width), shift) for shift in shifts]
    )
    cat_first, *pair_first = back_own(0, 1, (other_first, 0), [parts[0], send])
    own, *came = devices.spread(parts, line_stage)
    feed_sum = add_up([behind(own, cat_first), *came])
    if "low" not in line_stage:
        feed_sum = summed(feed_sum, "low")
    cat_second, *pair_second = back_own(1, 1, (other_rest, 0), [feed_sum])
    own, *came = devices.share(feed_sum, line_stage)
    feed_sum = join(devices.origins(line_stage), [behind(own, cat_second), *came])
    pair_first = devices.spread(pair_first, ("core",))
    cat_last, *pair_last = back_own(2, PAIRS - 2, (other_rest, 1), [feed_sum, received, pair_first[1]])
    feed_own = devices.share(feed_sum, plane)
    keep, came = devices.spread(pair_last, ("core",))
    pairs = [pair_first, devices.spread(pair_second, ("core",)), [behind(keep, *feed_own), came]]
    parts = devices.spread(cut(pairs, plane_place, plane_size), plane)
    dx = own_grads(
        x, [cat_first, cat_second, cat_last], received, dmid, w_query, w_key, w_value, line(gain_attn),
        parts[:1],
    )
    own, *came = parts
    value = summed(add_up([behind(own, dx), *came]), "low")
    feed_came = [devices.send(behind(piece, value), ("core",), 1) for piece in feed_own]
    places = devices.origins(plane)
    dwo, dwe, dwr, dbo, dbr, dgain_mlp, dshift_mlp, dbe = feed_weights(
        places, core, feed_own, feed_came, w_expand.shape[1], []
    )
    value = summed(value, "high", dwo)
    project_own = devices.share(value, plane)
    project_came = [devices.send(piece, ("core",), 1) for piece in project_own]
    dwk, dwv, dwq, dgain, dshift, dbq, dbv = project_weights(
        places, core, project_own, project_came, w_key, w_value, w_query, *norms, (1, 1, PAIRS - 2), spare
    )
    small = (dbq, dbv, dbo, dbe, dbr, dgain, dshift, dgain_mlp, dshift_mlp)
    return (
        unpadded(output),
        unpadded(dx),
        dwq, dwk, dwv, dwo, dwe, dwr,
        *(vector.reshape(-1) for vector in small),
    )


def solution(mesh):
    batch, group = mesh.shape["dp"], mesh.shape["grp"]
    mesh = jax.sharding.Mesh(mesh.devices.reshape(batch // 2, 2, group), ALL)
    items = ("rest", "core")
    rows = P(items, "grp", None)
    in_specs = (rows, P(items)) + (P(),) * 15 + (rows,)
    out_specs = (rows, rows) + (P(),) * 15
    return jax.shard_map(body, mesh=mesh, in_specs=in_specs, out_specs=out_specs, check_vma=False)
```

```python
import functools
import math

import jax
import jax.numpy as jnp
from jax import lax
from jax.experimental import pallas as pl
from jax.experimental.pallas import tpu as pltpu
from jax.sharding import PartitionSpec as P

HEADS = 8
HEAD_DIM = 64
VIEWS = 5
PATCH = 400
PAIR = 2 * HEAD_DIM
PAIRS = HEADS // 2
TILE = 256

EPSILON = 1e-05
NEGATIVE = -1e30
SCALE = 1.0 / math.sqrt(HEAD_DIM)

bf16 = jnp.bfloat16
f32 = jnp.float32


def dot_rows(left, right):
    return lax.dot_general(
        left, right, (((1,), (0,)), ((), ())), preferred_element_type=f32
    )


def dot_left(left, right):
    return lax.dot_general(
        left, right, (((0,), (0,)), ((), ())), preferred_element_type=f32
    )


def dot_right(left, right):
    return lax.dot_general(
        left, right, (((1,), (1,)), ((), ())), preferred_element_type=f32
    )


def chunk_of(rows, limit):
    best = 16
    for size in range(16, limit + 1, 16):
        if rows % size == 0:
            best = size
    return best


def hat_rows(matrix):
    center = matrix - jnp.mean(matrix, axis=-1, keepdims=True)
    spread = jnp.mean(center * center, axis=-1, keepdims=True)
    inverse = lax.rsqrt(spread + EPSILON)
    return center * inverse, inverse


def hat_back(grad_hat, hat, inverse):
    mean_grad = jnp.mean(grad_hat, axis=-1, keepdims=True)
    mean_cross = jnp.mean(grad_hat * hat, axis=-1, keepdims=True)
    return inverse * (grad_hat - mean_grad - hat * mean_cross)


def column_sums(matrix):
    return jnp.sum(matrix, axis=0, keepdims=True)


ALL = ("rest", "core", "grp")
VMEM_MIB = 60
ANYWHERE = pl.BlockSpec(memory_space=pl.ANY)


def params(axes):
    return pltpu.CompilerParams(
        dimension_semantics=("arbitrary",) * axes, vmem_limit_bytes=VMEM_MIB << 20
    )


def cost(flops, bytes_accessed, transcendentals=0):
    return pl.CostEstimate(
        flops=int(flops), bytes_accessed=int(bytes_accessed), transcendentals=int(transcendentals)
    )


def whole(shape):
    return pl.BlockSpec(shape, lambda *_: (0,) * len(shape))


def lanes_of(shape):
    return lax.broadcasted_iota(jnp.int32, shape, 1)


def forward_kernel(final, rows, blocks, step, limits, x_ref, gain, shift, w_key, w_value, b_value, *rest):
    if final:
        q_ref, acc_in, top_in, sum_in, *rest = rest
        hat_ref, k_ref, v_ref, out_ref, lse_ref, *rest = rest
    else:
        w_query, b_query, *rest = rest
        hat_ref, k_ref, v_ref, q_ref, acc_out, top_out, sum_out, *rest = rest
    normed, kt_ref, va_ref, *score_refs = rest
    item = pl.program_id(0)
    key_count = rows * blocks
    query_rows = q_ref.shape[0]

    @pl.when(pl.program_id(1) == 0)
    def _():
        hat, _ = hat_rows(x_ref[...].astype(f32))
        hat_ref[...] = hat.astype(bf16)
        normed[...] = (hat * gain[...] + shift[...]).astype(bf16)

    weights = [w_key[...], w_value[...]] if final else [w_key[...], w_value[...], w_query[...]]
    projected = dot_rows(normed[...], jnp.concatenate(weights, axis=1))
    k_ref[...] = projected[:, :PAIR].astype(bf16)
    v_ref[...] = (projected[:, PAIR:2 * PAIR] + b_value[...]).astype(bf16)
    if not final:
        query = (projected[:, 2 * PAIR:] + b_query[...]).astype(bf16)
        q_ref[...] = (query.astype(f32) * SCALE).astype(bf16)
    keys = k_ref[...].astype(f32)
    values = v_ref[...].astype(f32)
    first = lanes_of((key_count, PAIR)) < HEAD_DIM
    flipped = keys.T.astype(bf16)
    key_id = lax.broadcasted_iota(jnp.int32, (8, key_count), 1)
    bias = jnp.zeros((8, key_count), f32)
    for block in range(blocks):
        here = (key_id >= block * rows + limits[item, block]) & (key_id < (block + 1) * rows)
        bias = jnp.where(here, NEGATIVE, bias)
    bias = jnp.where(lax.broadcasted_iota(jnp.int32, (8, key_count), 0) == 0, bias, 0.0)
    spare = jnp.concatenate([bias, jnp.zeros((HEAD_DIM - 8, key_count), f32)], 0).astype(bf16)
    kt_ref[0, :HEAD_DIM, :] = flipped[:HEAD_DIM]
    kt_ref[0, HEAD_DIM:, :] = spare
    kt_ref[1, :HEAD_DIM, :] = spare
    kt_ref[1, HEAD_DIM:, :] = flipped[HEAD_DIM:]
    va_ref[0] = jnp.where(first, values, 1.0).astype(bf16)
    va_ref[1] = jnp.where(first, 1.0, values).astype(bf16)
    lanes = lanes_of((step, PAIR))
    head_first = lanes < HEAD_DIM
    one = jnp.where((lanes & (HEAD_DIM - 1)) == 0, 1.0, 0.0)
    tiles = [slice(t, min(t + TILE, key_count)) for t in range(0, key_count, TILE)]

    def query_of(unit):
        chunk, head = divmod(unit, 2)
        query = q_ref[chunk * step:(chunk + 1) * step, :].astype(f32)
        mine = head_first if head == 0 else jnp.logical_not(head_first)
        return jnp.where(mine, query, one).astype(bf16)

    units = 2 * (query_rows // step)
    outs, tops = [], []
    for unit in range(-1, units):
        query = query_of(unit + 1) if unit + 1 < units else None
        out, best = None, None
        for tile in tiles:
            if query is not None:
                scores = dot_rows(query, kt_ref[(unit + 1) % 2, :, tile])
                score_refs[(unit + 1) % 2][:, tile] = scores
                high = jnp.max(scores, axis=1, keepdims=True)
                best = high if best is None else jnp.maximum(best, high)
            if unit >= 0:
                weights = jnp.exp(score_refs[unit % 2][:, tile] - tops[unit]).astype(bf16)
                added = dot_rows(weights, va_ref[unit % 2, tile, :])
                out = added if out is None else out + added
        if best is not None:
            tops.append(best)
        if out is not None:
            outs.append(out)
        if unit % 2 == 0 or unit < 0:
            continue
        chunk = unit // 2
        place = slice(chunk * step, (chunk + 1) * step)
        acc = jnp.where(head_first, outs[unit - 1], outs[unit])
        total = pltpu.roll(jnp.where(head_first, outs[unit], outs[unit - 1]), HEAD_DIM, 1)
        top = jnp.where(head_first, tops[unit - 1], tops[unit])
        if final:
            other_top = top_in[place, :]
            new_top = jnp.maximum(top, other_top)
            scale_here = jnp.exp(top - new_top)
            scale_there = jnp.exp(other_top - new_top)
            total = total * scale_here + sum_in[place, :] * scale_there
            acc = acc * scale_here + acc_in[place, :] * scale_there
            out_ref[place, :] = acc / total
            lse_ref[place, :] = pltpu.roll(new_top + jnp.log(total), HEAD_DIM, 1)
        else:
            acc_out[place, :] = acc
            top_out[place, :] = top
            sum_out[place, :] = total


def attend(limits, x, norms, w_key, w_value, b_value, query, rows, blocks, before):
    width = x.shape[1]
    key_count = rows * blocks
    items = x.shape[0] // key_count
    total = items * rows
    step = chunk_of(rows, 208)
    query_block = pl.BlockSpec((rows, PAIR), lambda i, p, *_: (i, p))
    key_block = pl.BlockSpec((key_count, PAIR), lambda i, p, *_: (i, p))
    row_block = pl.BlockSpec((key_count, width), lambda i, p, *_: (i, 0))
    weight_block = pl.BlockSpec((width, PAIR), lambda i, p, *_: (0, p))
    line_block = pl.BlockSpec((1, PAIR), lambda i, p, *_: (0, p))
    final = before is not None
    shape = jax.ShapeDtypeStruct
    out_specs = [row_block, key_block, key_block]
    out_shape = [shape(x.shape, bf16)] * 3
    if final:
        extra, extra_specs = [query, *before], [query_block] * (1 + len(before))
        out_specs += [query_block] * 2
        out_shape += [shape((total, width), f32)] * 2
    else:
        extra, extra_specs = list(query), [weight_block, line_block]
        out_specs += [query_block] * 4
        out_shape += [shape((total, width), bf16)] + [shape((total, width), f32)] * 3
    return pl.pallas_call(
        functools.partial(forward_kernel, final, rows, blocks, step),
        grid_spec=pltpu.PrefetchScalarGridSpec(
            num_scalar_prefetch=1,
            grid=(items, PAIRS),
            in_specs=[row_block, whole((1, width)), whole((1, width))]
            + [weight_block] * 2
            + [line_block]
            + extra_specs,
            out_specs=out_specs,
            scratch_shapes=[
                pltpu.VMEM((key_count, width), bf16),
                pltpu.VMEM((2, PAIR, key_count), bf16),
                pltpu.VMEM((2, key_count, PAIR), bf16),
                pltpu.VMEM((step, key_count), f32),
                pltpu.VMEM((step, key_count), f32),
            ],
        ),
        out_shape=out_shape,
        compiler_params=params(2),
        cost_estimate=cost(
            16 * total * key_count * width, 12 * total * width, total * key_count * HEADS
        ),
        name="attend",
    )(limits, x, *norms, w_key, w_value, b_value, *extra)


def split_three(value):
    high = value.astype(bf16).astype(f32)
    rest = value - high
    middle = rest.astype(bf16).astype(f32)
    return high, middle, rest - middle


def halves(core, block):
    half = block.shape[0] // 2
    upper, lower = block[:half], block[half:]
    mine = jnp.where(core == 0, upper, lower)
    theirs = jnp.where(core == 0, lower, upper)
    return mine.astype(bf16), theirs.astype(bf16)


def backward_kernel(
    last, tokens, rows, blocks, step, limits, core,
    q_ref, k_ref, v_ref, g_ref, out_ref, lse_ref, hat_ref, *rest,
):
    if last:
        before_ref, dw_in, sums_in, *rest = rest
        cat_ref, keep_ref, send_ref, dw_acc, sums_acc, qt_ref, gt_ref, dqt_ref, *wide = rest[tokens:]
    else:
        dq_ref, cat_ref, dw_ref, sums_ref, dw_acc, sums_acc, qt_ref, gt_ref, dqt_ref, *wide = rest[tokens:]
    prob_refs, score_refs = wide[:2], wide[2:]
    pair = pl.program_id(0)
    item = pl.program_id(1)
    query_rows = q_ref.shape[0]
    lanes = lanes_of((query_rows, PAIR))
    head_first = lanes < HEAD_DIM
    spare_lane = lanes & (HEAD_DIM - 1)

    def spare(parts, mask_one):
        high, middle, low = parts
        value = jnp.where(spare_lane == 0, high, 0.0)
        value = jnp.where(spare_lane == 1, middle, value)
        value = jnp.where(spare_lane == 2, low, value)
        return jnp.where(spare_lane == 3, mask_one, value)

    query = q_ref[...].astype(f32)
    grad = g_ref[...].astype(f32)
    product = grad * out_ref[...]
    delta_first = jnp.sum(jnp.where(head_first, product, 0.0), axis=1, keepdims=True)
    delta_second = jnp.sum(jnp.where(head_first, 0.0, product), axis=1, keepdims=True)
    delta = jnp.where(head_first, delta_second, delta_first)
    lse_spare = spare(split_three(-lse_ref[...]), 1.0)
    delta_spare = spare(split_three(-delta), 0.0)
    qt_ref[0] = jnp.where(head_first, query, lse_spare).T.astype(bf16)
    qt_ref[1] = jnp.where(head_first, lse_spare, query).T.astype(bf16)
    gt_ref[0] = jnp.where(head_first, grad, delta_spare).T.astype(bf16)
    gt_ref[1] = jnp.where(head_first, delta_spare, grad).T.astype(bf16)
    dqt_ref[...] = jnp.zeros_like(dqt_ref)

    key_lanes = lanes_of((step, PAIR))
    key_first = key_lanes < HEAD_DIM
    key_spare = key_lanes & (HEAD_DIM - 1)
    key_row = lax.broadcasted_iota(jnp.int32, (step, PAIR), 0)
    ones = jnp.where(key_spare < 3, 1.0, 0.0)
    per_block = rows // step
    tiles = [slice(t, min(t + TILE, query_rows)) for t in range(0, query_rows, TILE)]

    def operands(unit):
        chunk, head = divmod(unit, 2)
        place = slice(chunk * step, (chunk + 1) * step)
        block = chunk // per_block
        limit = limits[item, block] - (chunk - block * per_block) * step
        bias = jnp.where(key_row >= limit, NEGATIVE, 0.0)
        key = k_ref[place, :].astype(f32)
        value = v_ref[place, :].astype(f32)
        mine = key_first if head == 0 else jnp.logical_not(key_first)
        key_head = jnp.where(mine, key, jnp.where(key_spare == 3, bias, ones)).astype(bf16)
        value_head = jnp.where(mine, value, ones).astype(bf16)
        half = key.T[head * HEAD_DIM:(head + 1) * HEAD_DIM].astype(bf16)
        return key_head, value_head, half

    units = 2 * blocks * per_block
    dks, dvs, half = [], [], None
    for unit in range(-1, units):
        more = unit + 1 < units
        if more:
            key_head, value_head, next_half = operands(unit + 1)
            which = (unit + 1) % 2
        dk, dv = None, None
        for tile in tiles:
            if more:
                probs = jnp.exp(dot_rows(key_head, qt_ref[which, :, tile]))
                grad_probs = dot_rows(value_head, gt_ref[which, :, tile])
                prob_refs[which][:, tile] = probs.astype(bf16)
                score_refs[which][:, tile] = (probs * grad_probs).astype(bf16)
            if unit >= 0:
                grad_scores = score_refs[unit % 2][:, tile]
                dv_part = dot_rows(prob_refs[unit % 2][:, tile], g_ref[tile, :])
                dk_part = dot_rows(grad_scores, q_ref[tile, :])
                dv = dv_part if dv is None else dv + dv_part
                dk = dk_part if dk is None else dk + dk_part
                own = slice(unit % 2 * HEAD_DIM, (unit % 2 + 1) * HEAD_DIM)
                dqt_ref[own, tile] += dot_rows(half, grad_scores)
        half = next_half if more else None
        if unit >= 0:
            dks.append(dk)
            dvs.append(dv)
        if unit >= 0 and unit % 2 == 1:
            place = slice(unit // 2 * step, (unit // 2 + 1) * step)
            cat_ref[place, :PAIR] = jnp.where(key_first, dks[-2], dks[-1]).astype(bf16)
            cat_ref[place, PAIR:2 * PAIR] = jnp.where(key_first, dvs[-2], dvs[-1]).astype(bf16)

    result = dqt_ref[...].T
    if last:
        cat_ref[:, 2 * PAIR:] = ((result + before_ref[...]) * SCALE).astype(bf16)
    else:
        dq_ref[...] = result
    added = dot_left(hat_ref[...], cat_ref[...])
    sums = column_sums(cat_ref[...].astype(f32))
    items = pl.num_programs(1)
    here = pl.ds(pair, 1)

    @pl.when((item == 0) & (pair == 0))
    def _():
        sums_acc[...] = jnp.zeros_like(sums_acc)

    @pl.when(item == 0)
    def _():
        dw_acc[...] = added
        if last:
            dw_acc[:, :2 * PAIR] += dw_in[0]
            sums_acc[here, :2 * PAIR] = sums_in[0, :1, :]

    @pl.when(item > 0)
    def _():
        dw_acc[...] += added

    sums_acc[here, :] += sums

    @pl.when(item == items - 1)
    def _():
        if last:
            half = dw_acc.shape[0] // 2
            place = pl.ds(pl.multiple_of(pair * half, half), half)
            keep_ref[place, :], send_ref[place, :] = halves(core[0], dw_acc[...])
        else:
            dw_ref[0] = dw_acc[...]
            sums_ref[0] = jnp.broadcast_to(sums_acc[here, :], sums_ref.shape[1:])

    if last:

        @pl.when((item == items - 1) & (pair == pl.num_programs(0) - 1))
        def _():
            end = slice(keep_ref.shape[0] - sums_acc.shape[0] // 2, None)
            keep_ref[end, :], send_ref[end, :] = halves(core[0], sums_acc[...])


def attend_back(
    limits, core, queries, keys, values, grads, outs, lse, hat, rows, blocks, first, count, before,
    spare, tokens,
):
    total, width = queries.shape
    items = total // rows
    key_count = rows * blocks
    step = chunk_of(rows, 208)
    last = before is not None
    cat = (3 if last else 2) * PAIR
    query_block = pl.BlockSpec((rows, PAIR), lambda p, i, *_: (i, first + p))
    key_block = pl.BlockSpec((key_count, PAIR), lambda p, i, *_: (i, first + p))
    hat_block = pl.BlockSpec((key_count, width), lambda p, i, *_: (i, 0))
    cat_block = pl.BlockSpec((key_count, cat), lambda p, i, *_: (i, p))
    shape = jax.ShapeDtypeStruct
    cat_shape = shape((total * blocks, cat * count), bf16)
    if last:
        (part, _, dw_part, sums_part), skip = before
        extra = [part, dw_part, sums_part]
        extra_specs = [
            pl.BlockSpec((rows, PAIR), lambda p, i, *_: (i, skip + p)),
            pl.BlockSpec((1, width, 2 * PAIR), lambda p, i, *_: (skip + p, 0, 0)),
            pl.BlockSpec((1, 8, 2 * PAIR), lambda p, i, *_: (skip + p, 0, 0)),
        ]
        half = (count * width // 2 + spare, cat)
        out_shape = [cat_shape] + [shape(half, bf16)] * 2
        out_specs = [cat_block] + [whole(half)] * 2
    else:
        extra, extra_specs = [], []
        out_shape = [
            shape((total, PAIR * count), f32),
            cat_shape,
            shape((count, width, cat), f32),
            shape((count, 8, cat), f32),
        ]
        out_specs = [
            pl.BlockSpec((rows, PAIR), lambda p, i, *_: (i, p)),
            cat_block,
            pl.BlockSpec((1, width, cat), lambda p, i, *_: (p, 0, 0)),
            pl.BlockSpec((1, 8, cat), lambda p, i, *_: (p, 0, 0)),
        ]
    return pl.pallas_call(
        functools.partial(backward_kernel, last, len(tokens), rows, blocks, step),
        grid_spec=pltpu.PrefetchScalarGridSpec(
            num_scalar_prefetch=2,
            grid=(count, items),
            in_specs=[query_block, key_block, key_block]
            + [query_block] * 3
            + [hat_block]
            + extra_specs
            + [ANYWHERE] * len(tokens),
            out_specs=out_specs,
            scratch_shapes=[
                pltpu.VMEM((width, cat), f32),
                pltpu.VMEM((2 * spare, cat), f32),
                pltpu.VMEM((2, PAIR, rows), bf16),
                pltpu.VMEM((2, PAIR, rows), bf16),
                pltpu.VMEM((PAIR, rows), f32),
            ]
            + [pltpu.VMEM((step, rows), bf16)] * 4,
        ),
        out_shape=out_shape,
        compiler_params=params(2),
        cost_estimate=cost(
            total * PAIR * count,
            total * PAIR * count,
        ),
        name="attend_back",
    )(limits, core, queries, keys, values, grads, outs, lse, hat, *extra, *tokens)


def feed_kernel(
    core, x_ref, mix_ref, dy_ref, w_output, w_expand, w_reduce, b_output, b_expand, b_reduce, gain, shift,
    y_ref, dmid_ref, dmix_ref, keep_ref, send_ref,
    middle_ref, normed_ref, y_acc, grad_acc, line_ref, active_ref, grad_ref,
):
    part = pl.program_id(0)

    half = w_output.shape[0] // 2

    def put(index, block):
        place = pl.ds(pl.multiple_of(index * half, half), half)
        keep_ref[place, :], send_ref[place, :] = halves(core[0], block)

    @pl.when(part == 0)
    def _():
        mixed = mix_ref[...].astype(bf16)
        middle = x_ref[...].astype(f32) + dot_rows(mixed, w_output[...]) + b_output[...]
        middle_ref[...] = middle
        hat, _ = hat_rows(middle)
        normed_ref[...] = (hat * gain[...] + shift[...]).astype(bf16)
        y_acc[...] = middle + b_reduce[...]
        grad_acc[...] = jnp.zeros_like(grad_acc)
        line_ref[...] = jnp.zeros_like(line_ref)
        line_ref[1:2, :] = column_sums(dy_ref[...].astype(f32))

    rows = x_ref.shape[0]
    step = chunk_of(rows, 272)
    spans = [slice(start, start + step) for start in range(0, rows, step)]

    def into(span):
        upper = dot_rows(normed_ref[span, :], w_expand[...]) + b_expand[...]
        return upper, dot_right(dy_ref[span, :], w_reduce[...])

    def out_of(span, active, grad_upper):
        y_acc[span, :] += dot_rows(active, w_reduce[...])
        grad_acc[span, :] += dot_right(grad_upper, w_expand[...])

    ahead, behind_it, lines = into(spans[0]), None, None
    for index, span in enumerate(spans):
        upper, grad_active = ahead
        if index + 1 < len(spans):
            ahead = into(spans[index + 1])
        if behind_it is not None:
            out_of(*behind_it)
        cumulative = 0.5 * lax.erf(upper * math.sqrt(0.5)) + 0.5
        density = jnp.exp(upper * upper * -0.5) * (1.0 / math.sqrt(2.0 * math.pi))
        active = (upper * cumulative).astype(bf16)
        grad_upper = (grad_active * (cumulative + upper * density)).astype(bf16)
        active_ref[span, :] = active
        grad_ref[span, :] = grad_upper
        line = column_sums(grad_upper.astype(f32))
        lines = line if lines is None else lines + line
        behind_it = span, active, grad_upper
    out_of(*behind_it)
    put(1 + 2 * part, dot_left(active_ref[...], dy_ref[...]))
    put(2 + 2 * part, dot_left(normed_ref[...], grad_ref[...]))
    line_ref[pl.ds(4 + part, 1), :] = lines

    @pl.when(part == pl.num_programs(0) - 1)
    def _():
        y_ref[...] = y_acc[...].astype(bf16)
        grad = grad_acc[...]
        hat, inverse = hat_rows(middle_ref[...])
        line_ref[2:3, :] = column_sums(grad * hat)
        line_ref[3:4, :] = column_sums(grad)
        dmid = hat_back(grad * gain[...], hat, inverse) + dy_ref[...].astype(f32)
        dmid_ref[...] = dmid
        branch = dmid.astype(bf16)
        line_ref[0:1, :] = column_sums(branch.astype(f32))
        put(0, dot_left(mix_ref[...].astype(bf16), branch))
        end = slice(keep_ref.shape[0] - line_ref.shape[0] // 2, None)
        keep_ref[end, :], send_ref[end, :] = halves(core[0], line_ref[...])
        dmix_ref[...] = dot_right(branch, w_output[...]).astype(bf16)


def feed(core, spare, x, mixed, dy, w_output, w_expand, w_reduce, b_output, b_expand, b_reduce, gain, shift):
    rows, width = x.shape
    hidden = w_expand.shape[1]
    parts = hidden // width
    row = whole((rows, width))
    line = whole((1, width))
    expand = pl.BlockSpec((width, width), lambda i, *_: (0, i))
    reduce = pl.BlockSpec((width, width), lambda i, *_: (i, 0))
    hidden_line = pl.BlockSpec((1, width), lambda i, *_: (0, i))
    weights = ((1 + 2 * parts) * width // 2 + spare, width)
    shape = jax.ShapeDtypeStruct
    return pl.pallas_call(
        feed_kernel,
        grid_spec=pltpu.PrefetchScalarGridSpec(
            num_scalar_prefetch=1,
            grid=(parts,),
            in_specs=[row, row, row, whole((width, width)), expand, reduce, line, hidden_line, line, line, line],
            out_specs=[row, row, row, whole(weights), whole(weights)],
            scratch_shapes=[
                pltpu.VMEM((rows, width), f32),
                pltpu.VMEM((rows, width), bf16),
                pltpu.VMEM((rows, width), f32),
                pltpu.VMEM((rows, width), f32),
                pltpu.VMEM((2 * spare, width), f32),
                pltpu.VMEM((rows, width), bf16),
                pltpu.VMEM((rows, width), bf16),
            ],
        ),
        out_shape=[
            shape((rows, width), bf16),
            shape((rows, width), f32),
            shape((rows, width), bf16),
            shape(weights, bf16),
            shape(weights, bf16),
        ],
        compiler_params=params(1),
        cost_estimate=cost(12 * rows * width * hidden + 6 * rows * width * width, 20 * rows * width, 2 * rows * hidden),
        name="feed",
    )(core, x, mixed, dy, w_output, w_expand, w_reduce, b_output, b_expand, b_reduce, gain, shift)


def gather_parts(refs, part, parts):
    blocks = []
    for ref in refs:
        pairs = ref.shape[1] // (parts * PAIR)
        for pair in range(pairs):
            start = (pair * parts + part) * PAIR
            blocks.append(ref[:, start:start + PAIR])
    return jnp.concatenate(blocks, axis=1)


def other_kernel(cats, w_key, w_value, *rest):
    cat_refs, send_ref = rest[:cats], rest[-1]
    dk = gather_parts(cat_refs, 0, 2)
    dv = gather_parts(cat_refs, 1, 2)
    send_ref[...] = (dot_right(dk, w_key[...]) + dot_right(dv, w_value[...])).astype(bf16)


def other_grads(cats, w_key, w_value, rows, after):
    total, width = cats[0].shape[0], w_key.shape[0]
    step = chunk_of(rows, 272)
    return pl.pallas_call(
        functools.partial(other_kernel, len(cats)),
        grid=(total // step,),
        in_specs=[whole((width, width))] * 2
        + [pl.BlockSpec((step, c.shape[1]), lambda i: (i, 0)) for c in cats]
        + [ANYWHERE] * len(after),
        out_specs=pl.BlockSpec((step, width), lambda i: (i, 0)),
        out_shape=jax.ShapeDtypeStruct((total, width), bf16),
        compiler_params=params(1),
        cost_estimate=cost(4 * total * width * width, 8 * total * width),
        name="other_grads",
    )(w_key, w_value, *cats, *after)


def own_kernel(cats, x_ref, recv_ref, dmid_ref, w_query, w_key, w_value, gain, *rest):
    cat_refs, dx_ref = rest[:cats], rest[-1]
    dk = gather_parts(cat_refs, 0, 3)
    dv = gather_parts(cat_refs, 1, 3)
    dq = gather_parts(cat_refs, 2, 3)
    grad = dot_right(dq, w_query[...]) + dot_right(dk, w_key[...]) + dot_right(dv, w_value[...])
    for index in range(recv_ref.shape[0]):
        grad = grad + recv_ref[index].astype(f32)
    hat, inverse = hat_rows(x_ref[...].astype(f32))
    dx_ref[...] = hat_back(grad * gain[...], hat, inverse) + dmid_ref[...]


def own_grads(x, cats, recv, dmid, w_query, w_key, w_value, gain, after):
    rows, width = x.shape
    step = chunk_of(rows, 272)
    row = pl.BlockSpec((step, width), lambda i: (i, 0))
    return pl.pallas_call(
        functools.partial(own_kernel, len(cats)),
        grid=(rows // step,),
        in_specs=[row, pl.BlockSpec((recv.shape[0], step, width), lambda i: (0, i, 0)), row]
        + [whole((width, width))] * 3
        + [whole((1, width))]
        + [pl.BlockSpec((step, c.shape[1]), lambda i: (i, 0)) for c in cats]
        + [ANYWHERE] * len(after),
        out_specs=row,
        out_shape=jax.ShapeDtypeStruct((rows, width), f32),
        compiler_params=params(1),
        cost_estimate=cost(6 * rows * width * width, 16 * rows * width),
        name="own_grads",
    )(x, recv, dmid, w_query, w_key, w_value, gain, *cats, *after)


class Slice:
    def __init__(self):
        group, rest = lax.axis_size("grp"), lax.axis_size("rest")
        batch = rest * lax.axis_size("core")
        side = 2 if rest % 2 == 0 else 1
        rest //= side
        high = 2 if rest % 2 == 0 else 1
        self.sizes = {"core": 2, "side": side, "member": group, "high": high, "low": rest // high}
        self.count = group * batch
        self.here = self.coords(lax.axis_index(ALL))

    def coords(self, linear):
        out = {}
        for name in ("member", "core", "side", "low", "high"):
            out[name] = linear % self.sizes[name]
            linear = linear // self.sizes[name]
        return out

    def linear(self, coords):
        total = 0
        for name in ("high", "low", "side", "core", "member"):
            total = total * self.sizes[name] + coords[name]
        return total

    def size(self, stage):
        return math.prod(self.sizes[name] for name in stage)

    def place(self, stage, coords=None):
        coords = self.here if coords is None else coords
        total = 0
        for name in stage:
            total = total * self.sizes[name] + coords[name]
        return total

    def send(self, array, stage, shift):
        pairs = []
        for source in range(self.count):
            coords = self.coords(source)
            place = (self.place(stage, coords) + shift) % self.size(stage)
            for name in reversed(stage):
                coords[name] = place % self.sizes[name]
                place //= self.sizes[name]
            pairs.append((source, self.linear(coords)))
        return lax.ppermute(array, ALL, pairs)

    def spread(self, parts, stage):
        return [parts[0]] + [self.send(part, stage, s) for s, part in enumerate(parts) if s > 0]

    def share(self, array, stage):
        return self.spread([array] * self.size(stage), stage)

    def origins(self, stage):
        size = self.size(stage)
        return ((self.place(stage) - jnp.arange(size)) % size).astype(jnp.int32)

    def in_order(self, parts, stage):
        if len(parts) <= 2:
            return parts
        stack = jnp.stack(parts)
        order = self.origins(stage)
        return [lax.dynamic_index_in_dim(stack, order[i], 0, False) for i in range(len(parts))]


def behind(array, *others):
    return lax.optimization_barrier((array, *others))[0] if others else array


def cut_kernel(size, groups, place, *refs):
    ins, outs = refs[:2 * groups], refs[2 * groups:]
    for shift, out in enumerate(outs):
        start = 0
        for index in range(groups):
            keep, came = ins[2 * index], ins[2 * index + 1]
            rows = keep.shape[0] // size
            span = pl.ds(pl.multiple_of((place[0] + shift) % size * rows, 16), rows)
            total = keep[span, :].astype(f32) + came[span, :].astype(f32)
            out[start:start + rows, :] = total.astype(bf16)
            start += rows


def cut(pairs, place, size):
    arrays = [array for pair in pairs for array in pair]
    width = arrays[0].shape[1]
    part = (sum(keep.shape[0] for keep, _ in pairs) // size, width)
    return pl.pallas_call(
        functools.partial(cut_kernel, size, len(pairs)),
        grid_spec=pltpu.PrefetchScalarGridSpec(
            num_scalar_prefetch=1,
            grid=(1,),
            in_specs=[whole(a.shape) for a in arrays],
            out_specs=[whole(part)] * size,
        ),
        out_shape=[jax.ShapeDtypeStruct(part, bf16)] * size,
        compiler_params=params(1),
        cost_estimate=cost(size * part[0] * width, 6 * size * part[0] * width),
        name="cut",
    )(jnp.reshape(place, (1,)).astype(jnp.int32), *arrays)


def add_up(parts):
    total = parts[0].astype(f32)
    for part in parts[1:]:
        total = total + part.astype(f32)
    return total.astype(bf16)


def place_pieces(places, core, pieces, flats):
    size = len(pieces) // 2
    for which in range(2):
        target = core[0] if which == 0 else 1 - core[0]
        for index in range(size):
            piece, at = pieces[which * size + index], 0
            for flat in flats:
                rows = flat.shape[1] // size
                span = pl.ds(pl.multiple_of(places[index] * rows, 16), rows)
                flat[target, span, :] = piece[at:at + rows, :]
                at += rows


def feed_weights_kernel(size, places, core, *refs):
    pieces, (dwo_ref, dwe_ref, dwr_ref, *line_refs, dbe_ref, flat) = refs[:2 * size], refs[-9:]
    width = dwo_ref.shape[0]
    half = width // 2
    step = pl.program_id(0)
    parts = pl.num_programs(0) - 1

    @pl.when(step == 0)
    def _():
        place_pieces(places, core, pieces, [flat])

    @pl.when(step < parts)
    def _():
        start = pl.multiple_of((1 + 2 * step) * half, half)
        for side in range(2):
            rows = slice(side * half, (side + 1) * half)
            dwr_ref[rows, :] = flat[side, pl.ds(start, half), :].astype(f32)
            dwe_ref[rows, :] = flat[side, pl.ds(start + half, half), :].astype(f32)

    @pl.when(step == parts)
    def _():
        for side in range(2):
            dwo_ref[side * half:(side + 1) * half, :] = flat[side, :half, :].astype(f32)
        count = dbe_ref.shape[1] // width
        start = (1 + 2 * count) * half
        lines = flat[0, start:start + 16, :].astype(f32)
        for index, ref in enumerate(line_refs):
            ref[...] = lines[index:index + 1]
        for part in range(count):
            dbe_ref[:, part * width:(part + 1) * width] = lines[4 + part:5 + part]


def feed_weights(places, core, own, came, hidden, after):
    rows, width = own[0].shape
    parts = hidden // width
    shapes = [(width, width), (width, hidden), (hidden, width)] + [(1, width)] * 4 + [(1, hidden)]
    out_specs = [whole(s) for s in shapes]
    out_specs[1] = pl.BlockSpec((width, width), lambda p, *_: (0, jnp.minimum(p, parts - 1)))
    out_specs[2] = pl.BlockSpec((width, width), lambda p, *_: (jnp.minimum(p, parts - 1), 0))
    return pl.pallas_call(
        functools.partial(feed_weights_kernel, len(own)),
        grid_spec=pltpu.PrefetchScalarGridSpec(
            num_scalar_prefetch=2,
            grid=(parts + 1,),
            in_specs=[whole((rows, width))] * (2 * len(own)) + [ANYWHERE] * len(after),
            out_specs=out_specs,
            scratch_shapes=[pltpu.VMEM((2, len(own) * rows, width), bf16)],
        ),
        out_shape=[jax.ShapeDtypeStruct(s, f32) for s in shapes],
        compiler_params=params(1),
        cost_estimate=cost(0, 12 * len(own) * rows * width),
        name="feed_weights",
    )(places, core, *own, *came, *after)


def project_weights_kernel(calls, places, core, *refs):
    flats, refs = refs[len(refs) - len(calls):], refs[:len(refs) - len(calls)]
    pieces, refs = refs[:-16], refs[-16:]
    weights, (gain, shift), refs = refs[:3], refs[3:5], refs[5:]
    outs, (dgain_ref, dshift_ref, dbq_ref, dbv_ref), refs = refs[:3], refs[3:7], refs[7:]
    gains, shifts, cross_acc, plain_acc = refs
    pair = pl.program_id(0)
    width = gains.shape[0]
    half = width // 2

    @pl.when(pair == 0)
    def _():
        place_pieces(places, core, pieces, flats)
        gains[...] = jnp.broadcast_to(gain[...], (PAIR, width)).T
        shifts[...] = jnp.broadcast_to(shift[...], (PAIR, width)).T
        cross_acc[...] = jnp.zeros_like(cross_acc)
        plain_acc[...] = jnp.zeros_like(plain_acc)

    def put(flat, pairs, index):
        sums = flat[0, pairs * half:pairs * half + 16, :].astype(f32)[index:index + 1]
        dbv_ref[...] = sums[:, PAIR:2 * PAIR]
        dbq_ref[...] = sums[:, 2 * PAIR:]
        for side in range(2):
            down = slice(side * half, (side + 1) * half)
            block = flat[side, index * half:(index + 1) * half, :].astype(f32)
            for which, (out, weight) in enumerate(zip(outs, weights)):
                lanes = slice(which * PAIR, (which + 1) * PAIR)
                part, line = block[:, lanes], sums[:, lanes]
                out[down, :] = gains[down, :] * part + shifts[down, :] * line
                own = weight[down, :].astype(f32)
                cross_acc[down, :] += own * part
                plain_acc[down, :] += own * line

    first = 0
    for flat, pairs in zip(flats, calls):
        for index in range(pairs):
            pl.when(pair == first + index)(functools.partial(put, flat, pairs, index))
        first += pairs

    @pl.when(pair == PAIRS - 1)
    def _():
        for acc, out in ((cross_acc, dgain_ref), (plain_acc, dshift_ref)):
            column = jnp.broadcast_to(jnp.sum(acc[...], axis=1, keepdims=True), (width, PAIR))
            out[...] = column.T[:1]


def project_weights(places, core, own, came, w_key, w_value, w_query, gain, shift, calls, spare):
    width = w_query.shape[0]
    rows, cat = own[0].shape
    line = whole((1, width))
    column_block = pl.BlockSpec((width, PAIR), lambda p, *_: (0, p))
    line_block = pl.BlockSpec((1, PAIR), lambda p, *_: (0, p))
    return pl.pallas_call(
        functools.partial(project_weights_kernel, calls),
        grid_spec=pltpu.PrefetchScalarGridSpec(
            num_scalar_prefetch=2,
            grid=(PAIRS,),
            in_specs=[whole((rows, cat))] * (2 * len(own)) + [column_block] * 3 + [line] * 2,
            out_specs=[column_block] * 3 + [line] * 2 + [line_block] * 2,
            scratch_shapes=[pltpu.VMEM((width, PAIR), f32)] * 4
            + [pltpu.VMEM((2, count * width // 2 + spare, cat), bf16) for count in calls],
        ),
        out_shape=[jax.ShapeDtypeStruct((width, width), f32)] * 3
        + [jax.ShapeDtypeStruct((1, width), f32)] * 4,
        compiler_params=params(1),
        cost_estimate=cost(0, 20 * width * width),
        name="project_weights",
    )(places, core, *own, *came, w_key, w_value, w_query, gain, shift)


def body(
    layer_input,
    lang_counts,
    w_query,
    w_key,
    w_value,
    w_output,
    w_expand,
    w_reduce,
    b_query,
    b_value,
    b_output,
    b_expand,
    b_reduce,
    gain_attn,
    shift_attn,
    gain_mlp,
    shift_mlp,
    cotangent,
):
    items, own_rows, width = layer_input.shape
    group = lax.axis_size("grp")
    me = lax.axis_index("grp")
    rows = -(-own_rows // 16) * 16
    total = items * rows
    patch_rows = VIEWS * PATCH
    shifts = range(1, group)

    def padded(array):
        if rows != own_rows:
            array = jnp.pad(array, ((0, 0), (0, rows - own_rows), (0, 0)))
        return array.reshape(total, width)

    def unpadded(array):
        return array.reshape(items, rows, width)[:, :own_rows]

    def limit_of(owner):
        return jnp.clip(patch_rows + lang_counts - owner * own_rows, 0, own_rows)

    def line(vector):
        return vector.reshape(1, -1)

    def group_shift(array, shift):
        return lax.ppermute(array, "grp", [(i, (i + shift) % group) for i in range(group)])

    def joined(parts):
        if len(parts) == 1:
            return parts[0]
        return jnp.stack([p.reshape(items, rows, width) for p in parts], 1).reshape(-1, width)

    x = padded(layer_input)
    dy = padded(cotangent)
    others = [group_shift(x, -shift) for shift in shifts]
    own_limits = limit_of(me).reshape(items, 1)
    other_limits = jnp.stack([limit_of((me + shift) % group) for shift in shifts], 1)

    norms = (line(gain_attn), line(shift_attn))
    hat, keys, values, queries, *first = attend(
        own_limits, x, norms, w_key, w_value, line(b_value), (w_query, line(b_query)), rows, 1, None
    )
    hat_other, keys_other, values_other, mixed, lse = attend(
        other_limits, joined(others), norms, w_key, w_value, line(b_value), queries, rows, group - 1, first
    )

    devices = Slice()
    plane = ("side", "member")
    core = jnp.reshape(devices.here["core"], (1,)).astype(jnp.int32)
    plane_place, plane_size = devices.place(plane), devices.size(plane)
    spare = 16 * plane_size
    output, dmid, dmix, keep, give = feed(
        core, spare, x, mixed, dy, w_output, w_expand, w_reduce, line(b_output), line(b_expand),
        line(b_reduce), line(gain_mlp), line(shift_mlp),
    )

    def summed(value, stage, *after):
        own, *came = devices.share(value, (stage,))
        return add_up(devices.in_order([behind(own, *after), *came], (stage,)))

    def back_other(first, count, tokens):
        return attend_back(
            other_limits, core, queries, keys_other, values_other, dmix, mixed, lse, hat_other,
            rows, group - 1, first, count, None, spare, tokens,
        )

    def back_own(first, count, before, tokens):
        return attend_back(
            own_limits, core, queries, keys, values, dmix, mixed, lse, hat,
            rows, 1, first, count, before, spare, tokens,
        )

    feed_pair = devices.spread([keep, give], ("core",))
    other_first = back_other(0, 1, [])
    feed_pair = [behind(half, other_first[1]) for half in feed_pair]
    share_rows = feed_pair[0].shape[0] // plane_size
    parts = [
        add_up([
            lax.dynamic_slice_in_dim(half, (plane_place + s) % plane_size * share_rows, share_rows)
            for half in feed_pair
        ])
        for s in range(plane_size)
    ]
    other_rest = back_other(1, PAIRS - 1, parts[:1])
    own, *came = devices.spread(parts, plane)
    feed_sum = add_up([behind(own, other_rest[1]), *came])
    cat_first, *pair_first = back_own(0, 1, (other_first, 0), [feed_sum])
    feed_sum = summed(feed_sum, "low", cat_first)
    send = other_grads([other_first[1], other_rest[1]], w_key, w_value, rows, [feed_sum])
    cat_middle, *pair_middle = back_own(1, PAIRS - 2, (other_rest, 0), [feed_sum, send])
    send = send.reshape(items, group - 1, rows, width)
    received = jnp.stack(
        [group_shift(send[:, shift - 1].reshape(total, width), shift) for shift in shifts]
    )
    pair_first = devices.spread(pair_first, ("core",))
    feed_sum = summed(feed_sum, "high", cat_middle, pair_first[1])
    cat_last, *pair_last = back_own(PAIRS - 1, 1, (other_rest, PAIRS - 2), [feed_sum])
    feed_own = devices.share(feed_sum, plane)
    pairs = [pair_first] + [devices.spread(pair, ("core",)) for pair in (pair_middle, pair_last)]
    parts = devices.spread(cut(pairs, plane_place, plane_size), plane)
    dx = own_grads(
        x, [cat_first, cat_middle, cat_last], received, dmid, w_query, w_key, w_value, line(gain_attn),
        parts[:1],
    )
    own, *came = parts
    value = add_up([behind(own, dx), *came])
    value = summed(summed(value, "low"), "high")
    project_own = devices.share(value, plane)
    feed_came = [devices.send(behind(piece, value), ("core",), 1) for piece in feed_own]
    places = devices.origins(plane)
    dwo, dwe, dwr, dbo, dbr, dgain_mlp, dshift_mlp, dbe = feed_weights(
        places, core, feed_own, feed_came, w_expand.shape[1], []
    )
    project_own = [project_own[0]] + [behind(piece, dwo) for piece in project_own[1:]]
    project_came = [devices.send(piece, ("core",), 1) for piece in project_own]
    dwk, dwv, dwq, dgain, dshift, dbq, dbv = project_weights(
        places, core, project_own, project_came, w_key, w_value, w_query, *norms, (1, PAIRS - 2, 1), spare
    )
    small = (dbq, dbv, dbo, dbe, dbr, dgain, dshift, dgain_mlp, dshift_mlp)
    return (
        unpadded(output),
        unpadded(dx),
        dwq, dwk, dwv, dwo, dwe, dwr,
        *(vector.reshape(-1) for vector in small),
    )


def solution(mesh):
    batch, group = mesh.shape["dp"], mesh.shape["grp"]
    mesh = jax.sharding.Mesh(mesh.devices.reshape(batch // 2, 2, group), ALL)
    items = ("rest", "core")
    rows = P(items, "grp", None)
    in_specs = (rows, P(items)) + (P(),) * 15 + (rows,)
    out_specs = (rows, rows) + (P(),) * 15
    return jax.shard_map(body, mesh=mesh, in_specs=in_specs, out_specs=out_specs, check_vma=False)
```

```python
import functools
import math

import jax
import jax.numpy as jnp
from jax import lax
from jax.experimental import pallas as pl
from jax.experimental.pallas import tpu as pltpu
from jax.sharding import PartitionSpec as P

HEADS = 8
HEAD_DIM = 64
VIEWS = 5
PATCH = 400
PAIR = 2 * HEAD_DIM
PAIRS = HEADS // 2
TILE = 256

EPSILON = 1e-05
NEGATIVE = -1e30
SCALE = 1.0 / math.sqrt(HEAD_DIM)

bf16 = jnp.bfloat16
f32 = jnp.float32


def dot_rows(left, right):
    return lax.dot_general(
        left, right, (((1,), (0,)), ((), ())), preferred_element_type=f32
    )


def dot_left(left, right):
    return lax.dot_general(
        left, right, (((0,), (0,)), ((), ())), preferred_element_type=f32
    )


def dot_right(left, right):
    return lax.dot_general(
        left, right, (((1,), (1,)), ((), ())), preferred_element_type=f32
    )


def chunk_of(rows, limit):
    best = 16
    for size in range(16, limit + 1, 16):
        if rows % size == 0:
            best = size
    return best


def hat_rows(matrix):
    center = matrix - jnp.mean(matrix, axis=-1, keepdims=True)
    spread = jnp.mean(center * center, axis=-1, keepdims=True)
    inverse = lax.rsqrt(spread + EPSILON)
    return center * inverse, inverse


def hat_back(grad_hat, hat, inverse):
    mean_grad = jnp.mean(grad_hat, axis=-1, keepdims=True)
    mean_cross = jnp.mean(grad_hat * hat, axis=-1, keepdims=True)
    return inverse * (grad_hat - mean_grad - hat * mean_cross)


def column_sums(matrix):
    return jnp.sum(matrix, axis=0, keepdims=True)


ALL = ("rest", "core", "grp")
VMEM_MIB = 60
ANYWHERE = pl.BlockSpec(memory_space=pl.ANY)


def params(axes):
    return pltpu.CompilerParams(
        dimension_semantics=("arbitrary",) * axes, vmem_limit_bytes=VMEM_MIB << 20
    )


def cost(flops, bytes_accessed, transcendentals=0):
    return pl.CostEstimate(
        flops=int(flops), bytes_accessed=int(bytes_accessed), transcendentals=int(transcendentals)
    )


def whole(shape):
    return pl.BlockSpec(shape, lambda *_: (0,) * len(shape))


def lanes_of(shape):
    return lax.broadcasted_iota(jnp.int32, shape, 1)


def forward_kernel(final, rows, blocks, step, limits, x_ref, gain, shift, w_key, w_value, b_value, *rest):
    if final:
        q_ref, acc_in, top_in, sum_in, *rest = rest
        hat_ref, k_ref, v_ref, out_ref, lse_ref, *rest = rest
    else:
        w_query, b_query, *rest = rest
        hat_ref, k_ref, v_ref, q_ref, acc_out, top_out, sum_out, *rest = rest
    normed, kt_ref, va_ref, *score_refs = rest
    item = pl.program_id(0)
    key_count = rows * blocks
    query_rows = q_ref.shape[0]

    @pl.when(pl.program_id(1) == 0)
    def _():
        hat, _ = hat_rows(x_ref[...].astype(f32))
        hat_ref[...] = hat.astype(bf16)
        normed[...] = (hat * gain[...] + shift[...]).astype(bf16)

    weights = [w_key[...], w_value[...]] if final else [w_key[...], w_value[...], w_query[...]]
    projected = dot_rows(normed[...], jnp.concatenate(weights, axis=1))
    k_ref[...] = projected[:, :PAIR].astype(bf16)
    v_ref[...] = (projected[:, PAIR:2 * PAIR] + b_value[...]).astype(bf16)
    if not final:
        query = (projected[:, 2 * PAIR:] + b_query[...]).astype(bf16)
        q_ref[...] = (query.astype(f32) * SCALE).astype(bf16)
    keys = k_ref[...].astype(f32)
    values = v_ref[...].astype(f32)
    first = lanes_of((key_count, PAIR)) < HEAD_DIM
    flipped = keys.T.astype(bf16)
    key_id = lax.broadcasted_iota(jnp.int32, (8, key_count), 1)
    bias = jnp.zeros((8, key_count), f32)
    for block in range(blocks):
        here = (key_id >= block * rows + limits[item, block]) & (key_id < (block + 1) * rows)
        bias = jnp.where(here, NEGATIVE, bias)
    bias = jnp.where(lax.broadcasted_iota(jnp.int32, (8, key_count), 0) == 0, bias, 0.0)
    spare = jnp.concatenate([bias, jnp.zeros((HEAD_DIM - 8, key_count), f32)], 0).astype(bf16)
    kt_ref[0, :HEAD_DIM, :] = flipped[:HEAD_DIM]
    kt_ref[0, HEAD_DIM:, :] = spare
    kt_ref[1, :HEAD_DIM, :] = spare
    kt_ref[1, HEAD_DIM:, :] = flipped[HEAD_DIM:]
    va_ref[0] = jnp.where(first, values, 1.0).astype(bf16)
    va_ref[1] = jnp.where(first, 1.0, values).astype(bf16)
    lanes = lanes_of((step, PAIR))
    head_first = lanes < HEAD_DIM
    one = jnp.where((lanes & (HEAD_DIM - 1)) == 0, 1.0, 0.0)
    tiles = [slice(t, min(t + TILE, key_count)) for t in range(0, key_count, TILE)]

    def query_of(unit):
        chunk, head = divmod(unit, 2)
        query = q_ref[chunk * step:(chunk + 1) * step, :].astype(f32)
        mine = head_first if head == 0 else jnp.logical_not(head_first)
        return jnp.where(mine, query, one).astype(bf16)

    units = 2 * (query_rows // step)
    outs, tops = [], []
    for unit in range(-1, units):
        query = query_of(unit + 1) if unit + 1 < units else None
        out, best = None, None
        for tile in tiles:
            if query is not None:
                scores = dot_rows(query, kt_ref[(unit + 1) % 2, :, tile])
                score_refs[(unit + 1) % 2][:, tile] = scores
                high = jnp.max(scores, axis=1, keepdims=True)
                best = high if best is None else jnp.maximum(best, high)
            if unit >= 0:
                weights = jnp.exp(score_refs[unit % 2][:, tile] - tops[unit]).astype(bf16)
                added = dot_rows(weights, va_ref[unit % 2, tile, :])
                out = added if out is None else out + added
        if best is not None:
            tops.append(best)
        if out is not None:
            outs.append(out)
        if unit % 2 == 0 or unit < 0:
            continue
        chunk = unit // 2
        place = slice(chunk * step, (chunk + 1) * step)
        acc = jnp.where(head_first, outs[unit - 1], outs[unit])
        total = pltpu.roll(jnp.where(head_first, outs[unit], outs[unit - 1]), HEAD_DIM, 1)
        top = jnp.where(head_first, tops[unit - 1], tops[unit])
        if final:
            other_top = top_in[place, :]
            new_top = jnp.maximum(top, other_top)
            scale_here = jnp.exp(top - new_top)
            scale_there = jnp.exp(other_top - new_top)
            total = total * scale_here + sum_in[place, :] * scale_there
            acc = acc * scale_here + acc_in[place, :] * scale_there
            out_ref[place, :] = acc / total
            lse_ref[place, :] = pltpu.roll(new_top + jnp.log(total), HEAD_DIM, 1)
        else:
            acc_out[place, :] = acc
            top_out[place, :] = top
            sum_out[place, :] = total


def attend(limits, x, norms, w_key, w_value, b_value, query, rows, blocks, before):
    width = x.shape[1]
    key_count = rows * blocks
    items = x.shape[0] // key_count
    total = items * rows
    step = chunk_of(rows, 208)
    query_block = pl.BlockSpec((rows, PAIR), lambda i, p, *_: (i, p))
    key_block = pl.BlockSpec((key_count, PAIR), lambda i, p, *_: (i, p))
    row_block = pl.BlockSpec((key_count, width), lambda i, p, *_: (i, 0))
    weight_block = pl.BlockSpec((width, PAIR), lambda i, p, *_: (0, p))
    line_block = pl.BlockSpec((1, PAIR), lambda i, p, *_: (0, p))
    final = before is not None
    shape = jax.ShapeDtypeStruct
    out_specs = [row_block, key_block, key_block]
    out_shape = [shape(x.shape, bf16)] * 3
    if final:
        extra, extra_specs = [query, *before], [query_block] * (1 + len(before))
        out_specs += [query_block] * 2
        out_shape += [shape((total, width), f32)] * 2
    else:
        extra, extra_specs = list(query), [weight_block, line_block]
        out_specs += [query_block] * 4
        out_shape += [shape((total, width), bf16)] + [shape((total, width), f32)] * 3
    return pl.pallas_call(
        functools.partial(forward_kernel, final, rows, blocks, step),
        grid_spec=pltpu.PrefetchScalarGridSpec(
            num_scalar_prefetch=1,
            grid=(items, PAIRS),
            in_specs=[row_block, whole((1, width)), whole((1, width))]
            + [weight_block] * 2
            + [line_block]
            + extra_specs,
            out_specs=out_specs,
            scratch_shapes=[
                pltpu.VMEM((key_count, width), bf16),
                pltpu.VMEM((2, PAIR, key_count), bf16),
                pltpu.VMEM((2, key_count, PAIR), bf16),
                pltpu.VMEM((step, key_count), f32),
                pltpu.VMEM((step, key_count), f32),
            ],
        ),
        out_shape=out_shape,
        compiler_params=params(2),
        cost_estimate=cost(
            16 * total * key_count * width, 12 * total * width, total * key_count * HEADS
        ),
        name="attend",
    )(limits, x, *norms, w_key, w_value, b_value, *extra)


def split_three(value):
    high = value.astype(bf16).astype(f32)
    rest = value - high
    middle = rest.astype(bf16).astype(f32)
    return high, middle, rest - middle


def halves(core, block):
    half = block.shape[0] // 2
    upper, lower = block[:half], block[half:]
    mine = jnp.where(core == 0, upper, lower)
    theirs = jnp.where(core == 0, lower, upper)
    return mine.astype(bf16), theirs.astype(bf16)


def backward_kernel(
    last, tokens, rows, blocks, step, limits, core,
    q_ref, k_ref, v_ref, g_ref, out_ref, lse_ref, hat_ref, *rest,
):
    if last:
        before_ref, dw_in, sums_in, *rest = rest
        cat_ref, keep_ref, send_ref, dw_acc, sums_acc, qt_ref, gt_ref, dqt_ref, *wide = rest[tokens:]
    else:
        dq_ref, cat_ref, dw_ref, sums_ref, dw_acc, sums_acc, qt_ref, gt_ref, dqt_ref, *wide = rest[tokens:]
    prob_refs, score_refs, ends = wide[:2], wide[2:4], wide[4:]
    pair = pl.program_id(0)
    item = pl.program_id(1)
    query_rows = q_ref.shape[0]
    lanes = lanes_of((query_rows, PAIR))
    head_first = lanes < HEAD_DIM
    spare_lane = lanes & (HEAD_DIM - 1)

    def spare(parts, mask_one):
        high, middle, low = parts
        value = jnp.where(spare_lane == 0, high, 0.0)
        value = jnp.where(spare_lane == 1, middle, value)
        value = jnp.where(spare_lane == 2, low, value)
        return jnp.where(spare_lane == 3, mask_one, value)

    query = q_ref[...].astype(f32)
    grad = g_ref[...].astype(f32)
    product = grad * out_ref[...]
    delta_first = jnp.sum(jnp.where(head_first, product, 0.0), axis=1, keepdims=True)
    delta_second = jnp.sum(jnp.where(head_first, 0.0, product), axis=1, keepdims=True)
    delta = jnp.where(head_first, delta_second, delta_first)
    lse_spare = spare(split_three(-lse_ref[...]), 1.0)
    delta_spare = spare(split_three(-delta), 0.0)
    qt_ref[0] = jnp.where(head_first, query, lse_spare).T.astype(bf16)
    qt_ref[1] = jnp.where(head_first, lse_spare, query).T.astype(bf16)
    gt_ref[0] = jnp.where(head_first, grad, delta_spare).T.astype(bf16)
    gt_ref[1] = jnp.where(head_first, delta_spare, grad).T.astype(bf16)
    dqt_ref[...] = jnp.zeros_like(dqt_ref)
    main = query_rows // TILE * TILE
    short = query_rows - main
    if short:
        q_end, g_end, q_both, g_both, dq_end = ends
        end = slice(main, None)
        first_lanes = lanes_of((short, PAIR)) < HEAD_DIM
        for value, extra, end_ref, both_ref in (
            (query, lse_spare, q_end, q_both), (grad, delta_spare, g_end, g_both)
        ):
            value, extra = value[end], extra[end]
            both = jnp.concatenate(
                [jnp.where(first_lanes, value, 0.0), jnp.where(first_lanes, 0.0, value)], 0
            )
            extras = jnp.concatenate(
                [
                    jnp.where(first_lanes, pltpu.roll(extra, HEAD_DIM, 1), 0.0),
                    jnp.where(first_lanes, extra, 0.0),
                ],
                0,
            )
            both_ref[...] = both.astype(bf16)
            end_ref[:PAIR, :] = both.T.astype(bf16)
            end_ref[PAIR:, :] = extras.T.astype(bf16)
        dq_end[...] = jnp.zeros_like(dq_end)

    key_lanes = lanes_of((step, PAIR))
    key_first = key_lanes < HEAD_DIM
    key_spare = key_lanes & (HEAD_DIM - 1)
    key_row = lax.broadcasted_iota(jnp.int32, (step, PAIR), 0)
    ones = jnp.where(key_spare < 3, 1.0, 0.0)
    per_block = rows // step
    tiles = [slice(t, t + TILE) for t in range(0, main, TILE)]

    def bias_of(chunk):
        block = chunk // per_block
        limit = limits[item, block] - (chunk - block * per_block) * step
        return jnp.where(key_row >= limit, NEGATIVE, 0.0)

    def end_terms(chunk):
        place = slice(chunk * step, (chunk + 1) * step)
        key, value = k_ref[place, :], v_ref[place, :]
        one = jnp.where(key_lanes < 3, 1.0, 0.0)
        key_extra = jnp.where(key_lanes == 3, bias_of(chunk), one).astype(bf16)
        probs = jnp.exp(dot_rows(jnp.concatenate([key, key_extra], 1), q_end[...]))
        grad_probs = dot_rows(jnp.concatenate([value, one.astype(bf16)], 1), g_end[...])
        grad_scores = (probs * grad_probs).astype(bf16)
        dq_end[...] += dot_rows(key.astype(f32).T.astype(bf16), grad_scores)
        return dot_rows(grad_scores, q_both[...]), dot_rows(probs.astype(bf16), g_both[...])

    def operands(unit):
        chunk, head = divmod(unit, 2)
        place = slice(chunk * step, (chunk + 1) * step)
        bias = bias_of(chunk)
        key = k_ref[place, :].astype(f32)
        value = v_ref[place, :].astype(f32)
        mine = key_first if head == 0 else jnp.logical_not(key_first)
        key_head = jnp.where(mine, key, jnp.where(key_spare == 3, bias, ones)).astype(bf16)
        value_head = jnp.where(mine, value, ones).astype(bf16)
        half = key.T[head * HEAD_DIM:(head + 1) * HEAD_DIM].astype(bf16)
        return key_head, value_head, half

    units = 2 * blocks * per_block
    dks, dvs, half = [], [], None
    for unit in range(-1, units):
        more = unit + 1 < units
        if more:
            key_head, value_head, next_half = operands(unit + 1)
            which = (unit + 1) % 2
        dk, dv = None, None
        for tile in tiles:
            if more:
                probs = jnp.exp(dot_rows(key_head, qt_ref[which, :, tile]))
                grad_probs = dot_rows(value_head, gt_ref[which, :, tile])
                prob_refs[which][:, tile] = probs.astype(bf16)
                score_refs[which][:, tile] = (probs * grad_probs).astype(bf16)
            if unit >= 0:
                grad_scores = score_refs[unit % 2][:, tile]
                dv_part = dot_rows(prob_refs[unit % 2][:, tile], g_ref[tile, :])
                dk_part = dot_rows(grad_scores, q_ref[tile, :])
                dv = dv_part if dv is None else dv + dv_part
                dk = dk_part if dk is None else dk + dk_part
                own = slice(unit % 2 * HEAD_DIM, (unit % 2 + 1) * HEAD_DIM)
                dqt_ref[own, tile] += dot_rows(half, grad_scores)
        half = next_half if more else None
        if unit >= 0:
            dks.append(dk)
            dvs.append(dv)
        if unit >= 0 and unit % 2 == 1:
            place = slice(unit // 2 * step, (unit // 2 + 1) * step)
            dk_both = jnp.where(key_first, dks[-2], dks[-1])
            dv_both = jnp.where(key_first, dvs[-2], dvs[-1])
            if short:
                dk_end, dv_end = end_terms(unit // 2)
                dk_both, dv_both = dk_both + dk_end, dv_both + dv_end
            cat_ref[place, :PAIR] = dk_both.astype(bf16)
            cat_ref[place, PAIR:2 * PAIR] = dv_both.astype(bf16)

    results = [(slice(0, main), dqt_ref[...].T)]
    if short:
        both = dq_end[...].T
        results.append((slice(main, query_rows), jnp.where(first_lanes, both[:short], both[short:])))
    for place, result in results:
        if last:
            cat_ref[place, 2 * PAIR:] = ((result + before_ref[place, :]) * SCALE).astype(bf16)
        else:
            dq_ref[place, :] = result
    added = dot_left(hat_ref[...], cat_ref[...])
    sums = column_sums(cat_ref[...].astype(f32))
    items = pl.num_programs(1)
    here = pl.ds(pair, 1)

    @pl.when((item == 0) & (pair == 0))
    def _():
        sums_acc[...] = jnp.zeros_like(sums_acc)

    @pl.when(item == 0)
    def _():
        dw_acc[...] = added
        if last:
            dw_acc[:, :2 * PAIR] += dw_in[0]
            sums_acc[here, :2 * PAIR] = sums_in[0, :1, :]

    @pl.when(item > 0)
    def _():
        dw_acc[...] += added

    sums_acc[here, :] += sums

    @pl.when(item == items - 1)
    def _():
        if last:
            half = dw_acc.shape[0] // 2
            place = pl.ds(pl.multiple_of(pair * half, half), half)
            keep_ref[place, :], send_ref[place, :] = halves(core[0], dw_acc[...])
        else:
            dw_ref[0] = dw_acc[...]
            sums_ref[0] = jnp.broadcast_to(sums_acc[here, :], sums_ref.shape[1:])

    if last:

        @pl.when((item == items - 1) & (pair == pl.num_programs(0) - 1))
        def _():
            end = slice(keep_ref.shape[0] - sums_acc.shape[0] // 2, None)
            keep_ref[end, :], send_ref[end, :] = halves(core[0], sums_acc[...])


def attend_back(
    limits, core, queries, keys, values, grads, outs, lse, hat, rows, blocks, first, count, before,
    spare, tokens,
):
    total, width = queries.shape
    items = total // rows
    key_count = rows * blocks
    step = chunk_of(rows, 208)
    last = before is not None
    main = rows // TILE * TILE
    short = rows - main
    ends = [
        pltpu.VMEM((2 * PAIR, 2 * short), bf16),
        pltpu.VMEM((2 * PAIR, 2 * short), bf16),
        pltpu.VMEM((2 * short, PAIR), bf16),
        pltpu.VMEM((2 * short, PAIR), bf16),
        pltpu.VMEM((PAIR, 2 * short), f32),
    ] if short else []
    cat = (3 if last else 2) * PAIR
    query_block = pl.BlockSpec((rows, PAIR), lambda p, i, *_: (i, first + p))
    key_block = pl.BlockSpec((key_count, PAIR), lambda p, i, *_: (i, first + p))
    hat_block = pl.BlockSpec((key_count, width), lambda p, i, *_: (i, 0))
    cat_block = pl.BlockSpec((key_count, cat), lambda p, i, *_: (i, p))
    shape = jax.ShapeDtypeStruct
    cat_shape = shape((total * blocks, cat * count), bf16)
    if last:
        (part, _, dw_part, sums_part), skip = before
        extra = [part, dw_part, sums_part]
        extra_specs = [
            pl.BlockSpec((rows, PAIR), lambda p, i, *_: (i, skip + p)),
            pl.BlockSpec((1, width, 2 * PAIR), lambda p, i, *_: (skip + p, 0, 0)),
            pl.BlockSpec((1, 8, 2 * PAIR), lambda p, i, *_: (skip + p, 0, 0)),
        ]
        half = (count * width // 2 + spare, cat)
        out_shape = [cat_shape] + [shape(half, bf16)] * 2
        out_specs = [cat_block] + [whole(half)] * 2
    else:
        extra, extra_specs = [], []
        out_shape = [
            shape((total, PAIR * count), f32),
            cat_shape,
            shape((count, width, cat), f32),
            shape((count, 8, cat), f32),
        ]
        out_specs = [
            pl.BlockSpec((rows, PAIR), lambda p, i, *_: (i, p)),
            cat_block,
            pl.BlockSpec((1, width, cat), lambda p, i, *_: (p, 0, 0)),
            pl.BlockSpec((1, 8, cat), lambda p, i, *_: (p, 0, 0)),
        ]
    return pl.pallas_call(
        functools.partial(backward_kernel, last, len(tokens), rows, blocks, step),
        grid_spec=pltpu.PrefetchScalarGridSpec(
            num_scalar_prefetch=2,
            grid=(count, items),
            in_specs=[query_block, key_block, key_block]
            + [query_block] * 3
            + [hat_block]
            + extra_specs
            + [ANYWHERE] * len(tokens),
            out_specs=out_specs,
            scratch_shapes=[
                pltpu.VMEM((width, cat), f32),
                pltpu.VMEM((2 * spare, cat), f32),
                pltpu.VMEM((2, PAIR, rows), bf16),
                pltpu.VMEM((2, PAIR, rows), bf16),
                pltpu.VMEM((PAIR, main), f32),
            ]
            + [pltpu.VMEM((step, main), bf16)] * 4
            + ends,
        ),
        out_shape=out_shape,
        compiler_params=params(2),
        cost_estimate=cost(
            total * PAIR * count,
            total * PAIR * count,
        ),
        name="attend_back",
    )(limits, core, queries, keys, values, grads, outs, lse, hat, *extra, *tokens)


def feed_kernel(
    core, x_ref, mix_ref, dy_ref, w_output, w_expand, w_reduce, b_output, b_expand, b_reduce, gain, shift,
    y_ref, dmid_ref, dmix_ref, keep_ref, send_ref,
    middle_ref, normed_ref, y_acc, grad_acc, line_ref,
):
    part = pl.program_id(0)

    half = w_output.shape[0] // 2

    def put(index, block):
        place = pl.ds(pl.multiple_of(index * half, half), half)
        keep_ref[place, :], send_ref[place, :] = halves(core[0], block)

    @pl.when(part == 0)
    def _():
        mixed = mix_ref[...].astype(bf16)
        middle = x_ref[...].astype(f32) + dot_rows(mixed, w_output[...]) + b_output[...]
        middle_ref[...] = middle
        hat, _ = hat_rows(middle)
        normed_ref[...] = (hat * gain[...] + shift[...]).astype(bf16)
        y_acc[...] = middle + b_reduce[...]
        grad_acc[...] = jnp.zeros_like(grad_acc)
        line_ref[...] = jnp.zeros_like(line_ref)
        line_ref[1:2, :] = column_sums(dy_ref[...].astype(f32))

    normed = normed_ref[...]
    upper = dot_rows(normed, w_expand[...]) + b_expand[...]
    cumulative = 0.5 * lax.erf(upper * math.sqrt(0.5)) + 0.5
    density = jnp.exp(upper * upper * -0.5) * (1.0 / math.sqrt(2.0 * math.pi))
    active = (upper * cumulative).astype(bf16)
    slope = cumulative + upper * density
    y_acc[...] += dot_rows(active, w_reduce[...])
    put(1 + 2 * part, dot_left(active, dy_ref[...]))
    grad_upper = (dot_right(dy_ref[...], w_reduce[...]) * slope).astype(bf16)
    line_ref[pl.ds(4 + part, 1), :] = column_sums(grad_upper.astype(f32))
    put(2 + 2 * part, dot_left(normed, grad_upper))
    grad_acc[...] += dot_right(grad_upper, w_expand[...])

    @pl.when(part == pl.num_programs(0) - 1)
    def _():
        y_ref[...] = y_acc[...].astype(bf16)
        grad = grad_acc[...]
        hat, inverse = hat_rows(middle_ref[...])
        line_ref[2:3, :] = column_sums(grad * hat)
        line_ref[3:4, :] = column_sums(grad)
        dmid = hat_back(grad * gain[...], hat, inverse) + dy_ref[...].astype(f32)
        dmid_ref[...] = dmid
        branch = dmid.astype(bf16)
        line_ref[0:1, :] = column_sums(branch.astype(f32))
        put(0, dot_left(mix_ref[...].astype(bf16), branch))
        end = slice(keep_ref.shape[0] - line_ref.shape[0] // 2, None)
        keep_ref[end, :], send_ref[end, :] = halves(core[0], line_ref[...])
        dmix_ref[...] = dot_right(branch, w_output[...]).astype(bf16)


def feed(core, spare, x, mixed, dy, w_output, w_expand, w_reduce, b_output, b_expand, b_reduce, gain, shift):
    rows, width = x.shape
    hidden = w_expand.shape[1]
    parts = hidden // width
    row = whole((rows, width))
    line = whole((1, width))
    expand = pl.BlockSpec((width, width), lambda i, *_: (0, i))
    reduce = pl.BlockSpec((width, width), lambda i, *_: (i, 0))
    hidden_line = pl.BlockSpec((1, width), lambda i, *_: (0, i))
    weights = ((1 + 2 * parts) * width // 2 + spare, width)
    shape = jax.ShapeDtypeStruct
    return pl.pallas_call(
        feed_kernel,
        grid_spec=pltpu.PrefetchScalarGridSpec(
            num_scalar_prefetch=1,
            grid=(parts,),
            in_specs=[row, row, row, whole((width, width)), expand, reduce, line, hidden_line, line, line, line],
            out_specs=[row, row, row, whole(weights), whole(weights)],
            scratch_shapes=[
                pltpu.VMEM((rows, width), f32),
                pltpu.VMEM((rows, width), bf16),
                pltpu.VMEM((rows, width), f32),
                pltpu.VMEM((rows, width), f32),
                pltpu.VMEM((2 * spare, width), f32),
            ],
        ),
        out_shape=[
            shape((rows, width), bf16),
            shape((rows, width), f32),
            shape((rows, width), bf16),
            shape(weights, bf16),
            shape(weights, bf16),
        ],
        compiler_params=params(1),
        cost_estimate=cost(12 * rows * width * hidden + 6 * rows * width * width, 20 * rows * width, 2 * rows * hidden),
        name="feed",
    )(core, x, mixed, dy, w_output, w_expand, w_reduce, b_output, b_expand, b_reduce, gain, shift)


def gather_parts(refs, part, parts):
    blocks = []
    for ref in refs:
        pairs = ref.shape[1] // (parts * PAIR)
        for pair in range(pairs):
            start = (pair * parts + part) * PAIR
            blocks.append(ref[:, start:start + PAIR])
    return jnp.concatenate(blocks, axis=1)


def other_kernel(cats, w_key, w_value, *rest):
    cat_refs, send_ref = rest[:cats], rest[-1]
    dk = gather_parts(cat_refs, 0, 2)
    dv = gather_parts(cat_refs, 1, 2)
    send_ref[...] = (dot_right(dk, w_key[...]) + dot_right(dv, w_value[...])).astype(bf16)


def other_grads(cats, w_key, w_value, rows, after):
    total, width = cats[0].shape[0], w_key.shape[0]
    step = chunk_of(rows, 272)
    return pl.pallas_call(
        functools.partial(other_kernel, len(cats)),
        grid=(total // step,),
        in_specs=[whole((width, width))] * 2
        + [pl.BlockSpec((step, c.shape[1]), lambda i: (i, 0)) for c in cats]
        + [ANYWHERE] * len(after),
        out_specs=pl.BlockSpec((step, width), lambda i: (i, 0)),
        out_shape=jax.ShapeDtypeStruct((total, width), bf16),
        compiler_params=params(1),
        cost_estimate=cost(4 * total * width * width, 8 * total * width),
        name="other_grads",
    )(w_key, w_value, *cats, *after)


def own_kernel(cats, x_ref, recv_ref, dmid_ref, w_query, w_key, w_value, gain, *rest):
    cat_refs, dx_ref = rest[:cats], rest[-1]
    dk = gather_parts(cat_refs, 0, 3)
    dv = gather_parts(cat_refs, 1, 3)
    dq = gather_parts(cat_refs, 2, 3)
    grad = dot_right(dq, w_query[...]) + dot_right(dk, w_key[...]) + dot_right(dv, w_value[...])
    for index in range(recv_ref.shape[0]):
        grad = grad + recv_ref[index].astype(f32)
    hat, inverse = hat_rows(x_ref[...].astype(f32))
    dx_ref[...] = hat_back(grad * gain[...], hat, inverse) + dmid_ref[...]


def own_grads(x, cats, recv, dmid, w_query, w_key, w_value, gain, after):
    rows, width = x.shape
    step = chunk_of(rows, 272)
    row = pl.BlockSpec((step, width), lambda i: (i, 0))
    return pl.pallas_call(
        functools.partial(own_kernel, len(cats)),
        grid=(rows // step,),
        in_specs=[row, pl.BlockSpec((recv.shape[0], step, width), lambda i: (0, i, 0)), row]
        + [whole((width, width))] * 3
        + [whole((1, width))]
        + [pl.BlockSpec((step, c.shape[1]), lambda i: (i, 0)) for c in cats]
        + [ANYWHERE] * len(after),
        out_specs=row,
        out_shape=jax.ShapeDtypeStruct((rows, width), f32),
        compiler_params=params(1),
        cost_estimate=cost(6 * rows * width * width, 16 * rows * width),
        name="own_grads",
    )(x, recv, dmid, w_query, w_key, w_value, gain, *cats, *after)


class Slice:
    def __init__(self):
        group, rest = lax.axis_size("grp"), lax.axis_size("rest")
        batch = rest * lax.axis_size("core")
        side = 2 if rest % 2 == 0 else 1
        rest //= side
        high = 2 if rest % 2 == 0 else 1
        self.sizes = {"core": 2, "side": side, "member": group, "high": high, "low": rest // high}
        self.count = group * batch
        self.here = self.coords(lax.axis_index(ALL))

    def coords(self, linear):
        out = {}
        for name in ("member", "core", "side", "low", "high"):
            out[name] = linear % self.sizes[name]
            linear = linear // self.sizes[name]
        return out

    def linear(self, coords):
        total = 0
        for name in ("high", "low", "side", "core", "member"):
            total = total * self.sizes[name] + coords[name]
        return total

    def size(self, stage):
        return math.prod(self.sizes[name] for name in stage)

    def place(self, stage, coords=None):
        coords = self.here if coords is None else coords
        total = 0
        for name in stage:
            total = total * self.sizes[name] + coords[name]
        return total

    def send(self, array, stage, shift):
        pairs = []
        for source in range(self.count):
            coords = self.coords(source)
            place = (self.place(stage, coords) + shift) % self.size(stage)
            for name in reversed(stage):
                coords[name] = place % self.sizes[name]
                place //= self.sizes[name]
            pairs.append((source, self.linear(coords)))
        return lax.ppermute(array, ALL, pairs)

    def spread(self, parts, stage):
        return [parts[0]] + [self.send(part, stage, s) for s, part in enumerate(parts) if s > 0]

    def share(self, array, stage):
        return self.spread([array] * self.size(stage), stage)

    def origins(self, stage):
        size = self.size(stage)
        return ((self.place(stage) - jnp.arange(size)) % size).astype(jnp.int32)

    def in_order(self, parts, stage):
        if len(parts) <= 2:
            return parts
        stack = jnp.stack(parts)
        order = self.origins(stage)
        return [lax.dynamic_index_in_dim(stack, order[i], 0, False) for i in range(len(parts))]


def behind(array, *others):
    return lax.optimization_barrier((array, *others))[0] if others else array


def cut_kernel(size, groups, place, *refs):
    ins, outs = refs[:2 * groups], refs[2 * groups:]
    for shift, out in enumerate(outs):
        start = 0
        for index in range(groups):
            keep, came = ins[2 * index], ins[2 * index + 1]
            rows = keep.shape[0] // size
            span = pl.ds(pl.multiple_of((place[0] + shift) % size * rows, 16), rows)
            total = keep[span, :].astype(f32) + came[span, :].astype(f32)
            out[start:start + rows, :] = total.astype(bf16)
            start += rows


def cut(pairs, place, size):
    arrays = [array for pair in pairs for array in pair]
    width = arrays[0].shape[1]
    part = (sum(keep.shape[0] for keep, _ in pairs) // size, width)
    return pl.pallas_call(
        functools.partial(cut_kernel, size, len(pairs)),
        grid_spec=pltpu.PrefetchScalarGridSpec(
            num_scalar_prefetch=1,
            grid=(1,),
            in_specs=[whole(a.shape) for a in arrays],
            out_specs=[whole(part)] * size,
        ),
        out_shape=[jax.ShapeDtypeStruct(part, bf16)] * size,
        compiler_params=params(1),
        cost_estimate=cost(size * part[0] * width, 6 * size * part[0] * width),
        name="cut",
    )(jnp.reshape(place, (1,)).astype(jnp.int32), *arrays)


def add_up(parts):
    total = parts[0].astype(f32)
    for part in parts[1:]:
        total = total + part.astype(f32)
    return total.astype(bf16)


def place_pieces(places, core, pieces, flats):
    size = len(pieces) // 2
    for which in range(2):
        target = core[0] if which == 0 else 1 - core[0]
        for index in range(size):
            piece, at = pieces[which * size + index], 0
            for flat in flats:
                rows = flat.shape[1] // size
                span = pl.ds(pl.multiple_of(places[index] * rows, 16), rows)
                flat[target, span, :] = piece[at:at + rows, :]
                at += rows


def feed_weights_kernel(size, places, core, *refs):
    pieces, (dwo_ref, dwe_ref, dwr_ref, *line_refs, dbe_ref, flat) = refs[:2 * size], refs[-9:]
    width = dwo_ref.shape[0]
    half = width // 2
    step = pl.program_id(0)
    parts = pl.num_programs(0) - 1

    @pl.when(step == 0)
    def _():
        place_pieces(places, core, pieces, [flat])

    @pl.when(step < parts)
    def _():
        start = pl.multiple_of((1 + 2 * step) * half, half)
        for side in range(2):
            rows = slice(side * half, (side + 1) * half)
            dwr_ref[rows, :] = flat[side, pl.ds(start, half), :].astype(f32)
            dwe_ref[rows, :] = flat[side, pl.ds(start + half, half), :].astype(f32)

    @pl.when(step == parts)
    def _():
        for side in range(2):
            dwo_ref[side * half:(side + 1) * half, :] = flat[side, :half, :].astype(f32)
        count = dbe_ref.shape[1] // width
        start = (1 + 2 * count) * half
        lines = flat[0, start:start + 16, :].astype(f32)
        for index, ref in enumerate(line_refs):
            ref[...] = lines[index:index + 1]
        for part in range(count):
            dbe_ref[:, part * width:(part + 1) * width] = lines[4 + part:5 + part]


def feed_weights(places, core, own, came, hidden, after):
    rows, width = own[0].shape
    parts = hidden // width
    shapes = [(width, width), (width, hidden), (hidden, width)] + [(1, width)] * 4 + [(1, hidden)]
    out_specs = [whole(s) for s in shapes]
    out_specs[1] = pl.BlockSpec((width, width), lambda p, *_: (0, jnp.minimum(p, parts - 1)))
    out_specs[2] = pl.BlockSpec((width, width), lambda p, *_: (jnp.minimum(p, parts - 1), 0))
    return pl.pallas_call(
        functools.partial(feed_weights_kernel, len(own)),
        grid_spec=pltpu.PrefetchScalarGridSpec(
            num_scalar_prefetch=2,
            grid=(parts + 1,),
            in_specs=[whole((rows, width))] * (2 * len(own)) + [ANYWHERE] * len(after),
            out_specs=out_specs,
            scratch_shapes=[pltpu.VMEM((2, len(own) * rows, width), bf16)],
        ),
        out_shape=[jax.ShapeDtypeStruct(s, f32) for s in shapes],
        compiler_params=params(1),
        cost_estimate=cost(0, 12 * len(own) * rows * width),
        name="feed_weights",
    )(places, core, *own, *came, *after)


def project_weights_kernel(calls, places, core, *refs):
    flats, refs = refs[len(refs) - len(calls):], refs[:len(refs) - len(calls)]
    pieces, refs = refs[:-16], refs[-16:]
    weights, (gain, shift), refs = refs[:3], refs[3:5], refs[5:]
    outs, (dgain_ref, dshift_ref, dbq_ref, dbv_ref), refs = refs[:3], refs[3:7], refs[7:]
    gains, shifts, cross_acc, plain_acc = refs
    pair = pl.program_id(0)
    width = gains.shape[0]
    half = width // 2

    @pl.when(pair == 0)
    def _():
        place_pieces(places, core, pieces, flats)
        gains[...] = jnp.broadcast_to(gain[...], (PAIR, width)).T
        shifts[...] = jnp.broadcast_to(shift[...], (PAIR, width)).T
        cross_acc[...] = jnp.zeros_like(cross_acc)
        plain_acc[...] = jnp.zeros_like(plain_acc)

    def put(flat, pairs, index):
        sums = flat[0, pairs * half:pairs * half + 16, :].astype(f32)[index:index + 1]
        dbv_ref[...] = sums[:, PAIR:2 * PAIR]
        dbq_ref[...] = sums[:, 2 * PAIR:]
        for side in range(2):
            down = slice(side * half, (side + 1) * half)
            block = flat[side, index * half:(index + 1) * half, :].astype(f32)
            for which, (out, weight) in enumerate(zip(outs, weights)):
                lanes = slice(which * PAIR, (which + 1) * PAIR)
                part, line = block[:, lanes], sums[:, lanes]
                out[down, :] = gains[down, :] * part + shifts[down, :] * line
                own = weight[down, :].astype(f32)
                cross_acc[down, :] += own * part
                plain_acc[down, :] += own * line

    first = 0
    for flat, pairs in zip(flats, calls):
        for index in range(pairs):
            pl.when(pair == first + index)(functools.partial(put, flat, pairs, index))
        first += pairs

    @pl.when(pair == PAIRS - 1)
    def _():
        for acc, out in ((cross_acc, dgain_ref), (plain_acc, dshift_ref)):
            column = jnp.broadcast_to(jnp.sum(acc[...], axis=1, keepdims=True), (width, PAIR))
            out[...] = column.T[:1]


def project_weights(places, core, own, came, w_key, w_value, w_query, gain, shift, calls, spare):
    width = w_query.shape[0]
    rows, cat = own[0].shape
    line = whole((1, width))
    column_block = pl.BlockSpec((width, PAIR), lambda p, *_: (0, p))
    line_block = pl.BlockSpec((1, PAIR), lambda p, *_: (0, p))
    return pl.pallas_call(
        functools.partial(project_weights_kernel, calls),
        grid_spec=pltpu.PrefetchScalarGridSpec(
            num_scalar_prefetch=2,
            grid=(PAIRS,),
            in_specs=[whole((rows, cat))] * (2 * len(own)) + [column_block] * 3 + [line] * 2,
            out_specs=[column_block] * 3 + [line] * 2 + [line_block] * 2,
            scratch_shapes=[pltpu.VMEM((width, PAIR), f32)] * 4
            + [pltpu.VMEM((2, count * width // 2 + spare, cat), bf16) for count in calls],
        ),
        out_shape=[jax.ShapeDtypeStruct((width, width), f32)] * 3
        + [jax.ShapeDtypeStruct((1, width), f32)] * 4,
        compiler_params=params(1),
        cost_estimate=cost(0, 20 * width * width),
        name="project_weights",
    )(places, core, *own, *came, w_key, w_value, w_query, gain, shift)


def body(
    layer_input,
    lang_counts,
    w_query,
    w_key,
    w_value,
    w_output,
    w_expand,
    w_reduce,
    b_query,
    b_value,
    b_output,
    b_expand,
    b_reduce,
    gain_attn,
    shift_attn,
    gain_mlp,
    shift_mlp,
    cotangent,
):
    items, own_rows, width = layer_input.shape
    group = lax.axis_size("grp")
    me = lax.axis_index("grp")
    rows = -(-own_rows // 16) * 16
    total = items * rows
    patch_rows = VIEWS * PATCH
    shifts = range(1, group)

    def padded(array):
        if rows != own_rows:
            array = jnp.pad(array, ((0, 0), (0, rows - own_rows), (0, 0)))
        return array.reshape(total, width)

    def unpadded(array):
        return array.reshape(items, rows, width)[:, :own_rows]

    def limit_of(owner):
        return jnp.clip(patch_rows + lang_counts - owner * own_rows, 0, own_rows)

    def line(vector):
        return vector.reshape(1, -1)

    def group_shift(array, shift):
        return lax.ppermute(array, "grp", [(i, (i + shift) % group) for i in range(group)])

    def joined(parts):
        if len(parts) == 1:
            return parts[0]
        return jnp.stack([p.reshape(items, rows, width) for p in parts], 1).reshape(-1, width)

    x = padded(layer_input)
    dy = padded(cotangent)
    others = [group_shift(x, -shift) for shift in shifts]
    own_limits = limit_of(me).reshape(items, 1)
    other_limits = jnp.stack([limit_of((me + shift) % group) for shift in shifts], 1)

    norms = (line(gain_attn), line(shift_attn))
    hat, keys, values, queries, *first = attend(
        own_limits, x, norms, w_key, w_value, line(b_value), (w_query, line(b_query)), rows, 1, None
    )
    hat_other, keys_other, values_other, mixed, lse = attend(
        other_limits, joined(others), norms, w_key, w_value, line(b_value), queries, rows, group - 1, first
    )

    devices = Slice()
    plane = ("side", "member")
    core = jnp.reshape(devices.here["core"], (1,)).astype(jnp.int32)
    plane_place, plane_size = devices.place(plane), devices.size(plane)
    spare = 16 * plane_size
    output, dmid, dmix, keep, give = feed(
        core, spare, x, mixed, dy, w_output, w_expand, w_reduce, line(b_output), line(b_expand),
        line(b_reduce), line(gain_mlp), line(shift_mlp),
    )

    def summed(value, stage, *after):
        own, *came = devices.share(value, (stage,))
        return add_up(devices.in_order([behind(own, *after), *came], (stage,)))

    def back_other(first, count, tokens):
        return attend_back(
            other_limits, core, queries, keys_other, values_other, dmix, mixed, lse, hat_other,
            rows, group - 1, first, count, None, spare, tokens,
        )

    def back_own(first, count, before, tokens):
        return attend_back(
            own_limits, core, queries, keys, values, dmix, mixed, lse, hat,
            rows, 1, first, count, before, spare, tokens,
        )

    feed_pair = devices.spread([keep, give], ("core",))
    other_first = back_other(0, 1, [])
    feed_pair = [behind(half, other_first[1]) for half in feed_pair]
    share_rows = feed_pair[0].shape[0] // plane_size
    parts = [
        add_up([
            lax.dynamic_slice_in_dim(half, (plane_place + s) % plane_size * share_rows, share_rows)
            for half in feed_pair
        ])
        for s in range(plane_size)
    ]
    other_rest = back_other(1, PAIRS - 1, parts[:1])
    own, *came = devices.spread(parts, plane)
    feed_sum = add_up([behind(own, other_rest[1]), *came])
    cat_first, *pair_first = back_own(0, 1, (other_first, 0), [feed_sum])
    feed_sum = summed(feed_sum, "low", cat_first)
    send = other_grads([other_first[1], other_rest[1]], w_key, w_value, rows, [feed_sum])
    cat_middle, *pair_middle = back_own(1, PAIRS - 2, (other_rest, 0), [feed_sum, send])
    send = send.reshape(items, group - 1, rows, width)
    received = jnp.stack(
        [group_shift(send[:, shift - 1].reshape(total, width), shift) for shift in shifts]
    )
    pair_first = devices.spread(pair_first, ("core",))
    feed_sum = summed(feed_sum, "high", cat_middle, pair_first[1])
    cat_last, *pair_last = back_own(PAIRS - 1, 1, (other_rest, PAIRS - 2), [feed_sum])
    feed_own = devices.share(feed_sum, plane)
    pairs = [pair_first] + [devices.spread(pair, ("core",)) for pair in (pair_middle, pair_last)]
    parts = devices.spread(cut(pairs, plane_place, plane_size), plane)
    dx = own_grads(
        x, [cat_first, cat_middle, cat_last], received, dmid, w_query, w_key, w_value, line(gain_attn),
        parts[:1],
    )
    own, *came = parts
    value = add_up([behind(own, dx), *came])
    value = summed(summed(value, "low"), "high")
    project_own = devices.share(value, plane)
    feed_came = [devices.send(behind(piece, value), ("core",), 1) for piece in feed_own]
    places = devices.origins(plane)
    dwo, dwe, dwr, dbo, dbr, dgain_mlp, dshift_mlp, dbe = feed_weights(
        places, core, feed_own, feed_came, w_expand.shape[1], []
    )
    project_own = [project_own[0]] + [behind(piece, dwo) for piece in project_own[1:]]
    project_came = [devices.send(piece, ("core",), 1) for piece in project_own]
    dwk, dwv, dwq, dgain, dshift, dbq, dbv = project_weights(
        places, core, project_own, project_came, w_key, w_value, w_query, *norms, (1, PAIRS - 2, 1), spare
    )
    small = (dbq, dbv, dbo, dbe, dbr, dgain, dshift, dgain_mlp, dshift_mlp)
    return (
        unpadded(output),
        unpadded(dx),
        dwq, dwk, dwv, dwo, dwe, dwr,
        *(vector.reshape(-1) for vector in small),
    )


def solution(mesh):
    batch, group = mesh.shape["dp"], mesh.shape["grp"]
    mesh = jax.sharding.Mesh(mesh.devices.reshape(batch // 2, 2, group), ALL)
    items = ("rest", "core")
    rows = P(items, "grp", None)
    in_specs = (rows, P(items)) + (P(),) * 15 + (rows,)
    out_specs = (rows, rows) + (P(),) * 15
    return jax.shard_map(body, mesh=mesh, in_specs=in_specs, out_specs=out_specs, check_vma=False)
```

```python
import functools
import math

import jax
import jax.numpy as jnp
from jax import lax
from jax.experimental import pallas as pl
from jax.experimental.pallas import tpu as pltpu
from jax.sharding import PartitionSpec as P

HEADS = 8
HEAD_DIM = 64
VIEWS = 5
PATCH = 400
PAIR = 2 * HEAD_DIM
PAIRS = HEADS // 2
TILE = 256

EPSILON = 1e-05
NEGATIVE = -1e30
SCALE = 1.0 / math.sqrt(HEAD_DIM)

bf16 = jnp.bfloat16
f32 = jnp.float32


def dot_rows(left, right):
    return lax.dot_general(
        left, right, (((1,), (0,)), ((), ())), preferred_element_type=f32
    )


def dot_left(left, right):
    return lax.dot_general(
        left, right, (((0,), (0,)), ((), ())), preferred_element_type=f32
    )


def dot_right(left, right):
    return lax.dot_general(
        left, right, (((1,), (1,)), ((), ())), preferred_element_type=f32
    )


def chunk_of(rows, limit):
    best = 16
    for size in range(16, limit + 1, 16):
        if rows % size == 0:
            best = size
    return best


def hat_rows(matrix):
    center = matrix - jnp.mean(matrix, axis=-1, keepdims=True)
    spread = jnp.mean(center * center, axis=-1, keepdims=True)
    inverse = lax.rsqrt(spread + EPSILON)
    return center * inverse, inverse


def hat_back(grad_hat, hat, inverse):
    mean_grad = jnp.mean(grad_hat, axis=-1, keepdims=True)
    mean_cross = jnp.mean(grad_hat * hat, axis=-1, keepdims=True)
    return inverse * (grad_hat - mean_grad - hat * mean_cross)


def column_sums(matrix):
    return jnp.sum(matrix, axis=0, keepdims=True)


ALL = ("rest", "core", "grp")
VMEM_MIB = 60
ANYWHERE = pl.BlockSpec(memory_space=pl.ANY)


def params(axes, mib=VMEM_MIB):
    return pltpu.CompilerParams(
        dimension_semantics=("arbitrary",) * axes, vmem_limit_bytes=mib << 20
    )


def cost(flops, bytes_accessed, transcendentals=0):
    return pl.CostEstimate(
        flops=int(flops), bytes_accessed=int(bytes_accessed), transcendentals=int(transcendentals)
    )


def whole(shape):
    return pl.BlockSpec(shape, lambda *_: (0,) * len(shape))


def lanes_of(shape):
    return lax.broadcasted_iota(jnp.int32, shape, 1)


def forward_kernel(final, rows, blocks, step, limits, x_ref, gain, shift, w_key, w_value, b_value, *rest):
    if final:
        q_ref, acc_in, top_in, sum_in, *rest = rest
        hat_ref, k_ref, v_ref, out_ref, lse_ref, *rest = rest
    else:
        w_query, b_query, *rest = rest
        hat_ref, k_ref, v_ref, q_ref, acc_out, top_out, sum_out, *rest = rest
    normed, kt_ref, va_ref, *score_refs = rest
    item = pl.program_id(0)
    key_count = rows * blocks
    query_rows = q_ref.shape[0]

    @pl.when(pl.program_id(1) == 0)
    def _():
        hat, _ = hat_rows(x_ref[...].astype(f32))
        hat_ref[...] = hat.astype(bf16)
        normed[...] = (hat * gain[...] + shift[...]).astype(bf16)

    weights = [w_key[...], w_value[...]] if final else [w_key[...], w_value[...], w_query[...]]
    projected = dot_rows(normed[...], jnp.concatenate(weights, axis=1))
    k_ref[...] = projected[:, :PAIR].astype(bf16)
    v_ref[...] = (projected[:, PAIR:2 * PAIR] + b_value[...]).astype(bf16)
    if not final:
        query = (projected[:, 2 * PAIR:] + b_query[...]).astype(bf16)
        q_ref[...] = (query.astype(f32) * SCALE).astype(bf16)
    keys = k_ref[...].astype(f32)
    values = v_ref[...].astype(f32)
    first = lanes_of((key_count, PAIR)) < HEAD_DIM
    flipped = keys.T.astype(bf16)
    key_id = lax.broadcasted_iota(jnp.int32, (8, key_count), 1)
    bias = jnp.zeros((8, key_count), f32)
    for block in range(blocks):
        here = (key_id >= block * rows + limits[item, block]) & (key_id < (block + 1) * rows)
        bias = jnp.where(here, NEGATIVE, bias)
    bias = jnp.where(lax.broadcasted_iota(jnp.int32, (8, key_count), 0) == 0, bias, 0.0)
    spare = jnp.concatenate([bias, jnp.zeros((HEAD_DIM - 8, key_count), f32)], 0).astype(bf16)
    kt_ref[0, :HEAD_DIM, :] = flipped[:HEAD_DIM]
    kt_ref[0, HEAD_DIM:, :] = spare
    kt_ref[1, :HEAD_DIM, :] = spare
    kt_ref[1, HEAD_DIM:, :] = flipped[HEAD_DIM:]
    va_ref[0] = jnp.where(first, values, 1.0).astype(bf16)
    va_ref[1] = jnp.where(first, 1.0, values).astype(bf16)
    lanes = lanes_of((step, PAIR))
    head_first = lanes < HEAD_DIM
    one = jnp.where((lanes & (HEAD_DIM - 1)) == 0, 1.0, 0.0)
    tiles = [slice(t, min(t + TILE, key_count)) for t in range(0, key_count, TILE)]

    def query_of(unit):
        chunk, head = divmod(unit, 2)
        query = q_ref[chunk * step:(chunk + 1) * step, :].astype(f32)
        mine = head_first if head == 0 else jnp.logical_not(head_first)
        return jnp.where(mine, query, one).astype(bf16)

    units = 2 * (query_rows // step)
    outs, tops = [], []
    for unit in range(-1, units):
        query = query_of(unit + 1) if unit + 1 < units else None
        out, best = None, None
        for tile in tiles:
            if query is not None:
                scores = dot_rows(query, kt_ref[(unit + 1) % 2, :, tile])
                score_refs[(unit + 1) % 2][:, tile] = scores
                high = jnp.max(scores, axis=1, keepdims=True)
                best = high if best is None else jnp.maximum(best, high)
            if unit >= 0:
                weights = jnp.exp(score_refs[unit % 2][:, tile] - tops[unit]).astype(bf16)
                added = dot_rows(weights, va_ref[unit % 2, tile, :])
                out = added if out is None else out + added
        if best is not None:
            tops.append(best)
        if out is not None:
            outs.append(out)
        if unit % 2 == 0 or unit < 0:
            continue
        chunk = unit // 2
        place = slice(chunk * step, (chunk + 1) * step)
        acc = jnp.where(head_first, outs[unit - 1], outs[unit])
        total = pltpu.roll(jnp.where(head_first, outs[unit], outs[unit - 1]), HEAD_DIM, 1)
        top = jnp.where(head_first, tops[unit - 1], tops[unit])
        if final:
            other_top = top_in[place, :]
            new_top = jnp.maximum(top, other_top)
            scale_here = jnp.exp(top - new_top)
            scale_there = jnp.exp(other_top - new_top)
            total = total * scale_here + sum_in[place, :] * scale_there
            acc = acc * scale_here + acc_in[place, :] * scale_there
            out_ref[place, :] = acc / total
            lse_ref[place, :] = pltpu.roll(new_top + jnp.log(total), HEAD_DIM, 1)
        else:
            acc_out[place, :] = acc
            top_out[place, :] = top
            sum_out[place, :] = total


def attend(limits, x, norms, w_key, w_value, b_value, query, rows, blocks, before):
    width = x.shape[1]
    key_count = rows * blocks
    items = x.shape[0] // key_count
    total = items * rows
    step = chunk_of(rows, 208)
    query_block = pl.BlockSpec((rows, PAIR), lambda i, p, *_: (i, p))
    key_block = pl.BlockSpec((key_count, PAIR), lambda i, p, *_: (i, p))
    row_block = pl.BlockSpec((key_count, width), lambda i, p, *_: (i, 0))
    weight_block = pl.BlockSpec((width, PAIR), lambda i, p, *_: (0, p))
    line_block = pl.BlockSpec((1, PAIR), lambda i, p, *_: (0, p))
    final = before is not None
    shape = jax.ShapeDtypeStruct
    out_specs = [row_block, key_block, key_block]
    out_shape = [shape(x.shape, bf16)] * 3
    if final:
        extra, extra_specs = [query, *before], [query_block] * (1 + len(before))
        out_specs += [query_block] * 2
        out_shape += [shape((total, width), f32)] * 2
    else:
        extra, extra_specs = list(query), [weight_block, line_block]
        out_specs += [query_block] * 4
        out_shape += [shape((total, width), bf16)] + [shape((total, width), f32)] * 3
    return pl.pallas_call(
        functools.partial(forward_kernel, final, rows, blocks, step),
        grid_spec=pltpu.PrefetchScalarGridSpec(
            num_scalar_prefetch=1,
            grid=(items, PAIRS),
            in_specs=[row_block, whole((1, width)), whole((1, width))]
            + [weight_block] * 2
            + [line_block]
            + extra_specs,
            out_specs=out_specs,
            scratch_shapes=[
                pltpu.VMEM((key_count, width), bf16),
                pltpu.VMEM((2, PAIR, key_count), bf16),
                pltpu.VMEM((2, key_count, PAIR), bf16),
                pltpu.VMEM((step, key_count), f32),
                pltpu.VMEM((step, key_count), f32),
            ],
        ),
        out_shape=out_shape,
        compiler_params=params(2, 64),
        cost_estimate=cost(
            16 * total * key_count * width, 12 * total * width, total * key_count * HEADS
        ),
        name="attend",
    )(limits, x, *norms, w_key, w_value, b_value, *extra)


def split_three(value):
    high = value.astype(bf16).astype(f32)
    rest = value - high
    middle = rest.astype(bf16).astype(f32)
    return high, middle, rest - middle


def halves(core, block):
    half = block.shape[0] // 2
    upper, lower = block[:half], block[half:]
    mine = jnp.where(core == 0, upper, lower)
    theirs = jnp.where(core == 0, lower, upper)
    return mine.astype(bf16), theirs.astype(bf16)


def backward_kernel(
    last, tokens, rows, blocks, step, limits, core,
    q_ref, k_ref, v_ref, g_ref, out_ref, lse_ref, hat_ref, *rest,
):
    if last:
        before_ref, dw_in, sums_in, *rest = rest
        cat_ref, keep_ref, send_ref, dw_acc, sums_acc, qt_ref, gt_ref, dqt_ref, *wide = rest[tokens:]
    else:
        dq_ref, cat_ref, dw_ref, sums_ref, dw_acc, sums_acc, qt_ref, gt_ref, dqt_ref, *wide = rest[tokens:]
    prob_refs, score_refs, ends = wide[:2], wide[2:4], wide[4:]
    pair = pl.program_id(0)
    item = pl.program_id(1)
    query_rows = q_ref.shape[0]
    lanes = lanes_of((query_rows, PAIR))
    head_first = lanes < HEAD_DIM
    spare_lane = lanes & (HEAD_DIM - 1)

    def spare(parts, mask_one):
        high, middle, low = parts
        value = jnp.where(spare_lane == 0, high, 0.0)
        value = jnp.where(spare_lane == 1, middle, value)
        value = jnp.where(spare_lane == 2, low, value)
        return jnp.where(spare_lane == 3, mask_one, value)

    query = q_ref[...].astype(f32)
    grad = g_ref[...].astype(f32)
    product = grad * out_ref[...]
    delta_first = jnp.sum(jnp.where(head_first, product, 0.0), axis=1, keepdims=True)
    delta_second = jnp.sum(jnp.where(head_first, 0.0, product), axis=1, keepdims=True)
    delta = jnp.where(head_first, delta_second, delta_first)
    lse_spare = spare(split_three(-lse_ref[...]), 1.0)
    delta_spare = spare(split_three(-delta), 0.0)
    qt_ref[0] = jnp.where(head_first, query, lse_spare).T.astype(bf16)
    qt_ref[1] = jnp.where(head_first, lse_spare, query).T.astype(bf16)
    gt_ref[0] = jnp.where(head_first, grad, delta_spare).T.astype(bf16)
    gt_ref[1] = jnp.where(head_first, delta_spare, grad).T.astype(bf16)
    dqt_ref[...] = jnp.zeros_like(dqt_ref)
    main = query_rows // TILE * TILE
    short = query_rows - main
    if short:
        q_end, g_end, q_both, g_both, dq_end = ends
        end = slice(main, None)
        first_lanes = lanes_of((short, PAIR)) < HEAD_DIM
        for value, extra, end_ref, both_ref in (
            (query, lse_spare, q_end, q_both), (grad, delta_spare, g_end, g_both)
        ):
            value, extra = value[end], extra[end]
            both = jnp.concatenate(
                [jnp.where(first_lanes, value, 0.0), jnp.where(first_lanes, 0.0, value)], 0
            )
            extras = jnp.concatenate(
                [
                    jnp.where(first_lanes, pltpu.roll(extra, HEAD_DIM, 1), 0.0),
                    jnp.where(first_lanes, extra, 0.0),
                ],
                0,
            )
            both_ref[...] = both.astype(bf16)
            end_ref[:PAIR, :] = both.T.astype(bf16)
            end_ref[PAIR:, :] = extras.T.astype(bf16)
        dq_end[...] = jnp.zeros_like(dq_end)

    key_lanes = lanes_of((step, PAIR))
    key_first = key_lanes < HEAD_DIM
    key_spare = key_lanes & (HEAD_DIM - 1)
    key_row = lax.broadcasted_iota(jnp.int32, (step, PAIR), 0)
    ones = jnp.where(key_spare < 3, 1.0, 0.0)
    per_block = rows // step
    tiles = [slice(t, t + TILE) for t in range(0, main, TILE)]

    def bias_of(chunk):
        block = chunk // per_block
        limit = limits[item, block] - (chunk - block * per_block) * step
        return jnp.where(key_row >= limit, NEGATIVE, 0.0)

    def end_terms(chunk):
        place = slice(chunk * step, (chunk + 1) * step)
        key, value = k_ref[place, :], v_ref[place, :]
        one = jnp.where(key_lanes < 3, 1.0, 0.0)
        key_extra = jnp.where(key_lanes == 3, bias_of(chunk), one).astype(bf16)
        probs = jnp.exp(dot_rows(jnp.concatenate([key, key_extra], 1), q_end[...]))
        grad_probs = dot_rows(jnp.concatenate([value, one.astype(bf16)], 1), g_end[...])
        grad_scores = (probs * grad_probs).astype(bf16)
        dq_end[...] += dot_rows(key.astype(f32).T.astype(bf16), grad_scores)
        return dot_rows(grad_scores, q_both[...]), dot_rows(probs.astype(bf16), g_both[...])

    def operands(unit):
        chunk, head = divmod(unit, 2)
        place = slice(chunk * step, (chunk + 1) * step)
        bias = bias_of(chunk)
        key = k_ref[place, :].astype(f32)
        value = v_ref[place, :].astype(f32)
        mine = key_first if head == 0 else jnp.logical_not(key_first)
        key_head = jnp.where(mine, key, jnp.where(key_spare == 3, bias, ones)).astype(bf16)
        value_head = jnp.where(mine, value, ones).astype(bf16)
        half = key.T[head * HEAD_DIM:(head + 1) * HEAD_DIM].astype(bf16)
        return key_head, value_head, half

    units = 2 * blocks * per_block
    dks, dvs, half = [], [], None
    for unit in range(-1, units):
        more = unit + 1 < units
        if more:
            key_head, value_head, next_half = operands(unit + 1)
            which = (unit + 1) % 2
        dk, dv = None, None
        for tile in tiles:
            if more:
                probs = jnp.exp(dot_rows(key_head, qt_ref[which, :, tile]))
                grad_probs = dot_rows(value_head, gt_ref[which, :, tile])
                prob_refs[which][:, tile] = probs.astype(bf16)
                score_refs[which][:, tile] = (probs * grad_probs).astype(bf16)
            if unit >= 0:
                grad_scores = score_refs[unit % 2][:, tile]
                dv_part = dot_rows(prob_refs[unit % 2][:, tile], g_ref[tile, :])
                dk_part = dot_rows(grad_scores, q_ref[tile, :])
                dv = dv_part if dv is None else dv + dv_part
                dk = dk_part if dk is None else dk + dk_part
                own = slice(unit % 2 * HEAD_DIM, (unit % 2 + 1) * HEAD_DIM)
                dqt_ref[own, tile] += dot_rows(half, grad_scores)
        half = next_half if more else None
        if unit >= 0:
            dks.append(dk)
            dvs.append(dv)
        if unit >= 0 and unit % 2 == 1:
            place = slice(unit // 2 * step, (unit // 2 + 1) * step)
            dk_both = jnp.where(key_first, dks[-2], dks[-1])
            dv_both = jnp.where(key_first, dvs[-2], dvs[-1])
            if short:
                dk_end, dv_end = end_terms(unit // 2)
                dk_both, dv_both = dk_both + dk_end, dv_both + dv_end
            cat_ref[place, :PAIR] = dk_both.astype(bf16)
            cat_ref[place, PAIR:2 * PAIR] = dv_both.astype(bf16)

    results = [(slice(0, main), dqt_ref[...].T)]
    if short:
        both = dq_end[...].T
        results.append((slice(main, query_rows), jnp.where(first_lanes, both[:short], both[short:])))
    for place, result in results:
        if last:
            cat_ref[place, 2 * PAIR:] = ((result + before_ref[place, :]) * SCALE).astype(bf16)
        else:
            dq_ref[place, :] = result
    added = dot_left(hat_ref[...], cat_ref[...])
    sums = column_sums(cat_ref[...].astype(f32))
    items = pl.num_programs(1)
    here = pl.ds(pair, 1)

    @pl.when((item == 0) & (pair == 0))
    def _():
        sums_acc[...] = jnp.zeros_like(sums_acc)

    @pl.when(item == 0)
    def _():
        dw_acc[...] = added
        if last:
            dw_acc[:, :2 * PAIR] += dw_in[0]
            sums_acc[here, :2 * PAIR] = sums_in[0, :1, :]

    @pl.when(item > 0)
    def _():
        dw_acc[...] += added

    sums_acc[here, :] += sums

    @pl.when(item == items - 1)
    def _():
        if last:
            half = dw_acc.shape[0] // 2
            place = pl.ds(pl.multiple_of(pair * half, half), half)
            keep_ref[place, :], send_ref[place, :] = halves(core[0], dw_acc[...])
        else:
            dw_ref[0] = dw_acc[...]
            sums_ref[0] = jnp.broadcast_to(sums_acc[here, :], sums_ref.shape[1:])

    if last:

        @pl.when((item == items - 1) & (pair == pl.num_programs(0) - 1))
        def _():
            end = slice(keep_ref.shape[0] - sums_acc.shape[0] // 2, None)
            keep_ref[end, :], send_ref[end, :] = halves(core[0], sums_acc[...])


def attend_back(
    limits, core, queries, keys, values, grads, outs, lse, hat, rows, blocks, first, count, before,
    spare, tokens,
):
    total, width = queries.shape
    items = total // rows
    key_count = rows * blocks
    step = chunk_of(rows, 208)
    last = before is not None
    main = rows // TILE * TILE
    short = rows - main
    ends = [
        pltpu.VMEM((2 * PAIR, 2 * short), bf16),
        pltpu.VMEM((2 * PAIR, 2 * short), bf16),
        pltpu.VMEM((2 * short, PAIR), bf16),
        pltpu.VMEM((2 * short, PAIR), bf16),
        pltpu.VMEM((PAIR, 2 * short), f32),
    ] if short else []
    cat = (3 if last else 2) * PAIR
    query_block = pl.BlockSpec((rows, PAIR), lambda p, i, *_: (i, first + p))
    key_block = pl.BlockSpec((key_count, PAIR), lambda p, i, *_: (i, first + p))
    hat_block = pl.BlockSpec((key_count, width), lambda p, i, *_: (i, 0))
    cat_block = pl.BlockSpec((key_count, cat), lambda p, i, *_: (i, p))
    shape = jax.ShapeDtypeStruct
    cat_shape = shape((total * blocks, cat * count), bf16)
    if last:
        (part, _, dw_part, sums_part), skip = before
        extra = [part, dw_part, sums_part]
        extra_specs = [
            pl.BlockSpec((rows, PAIR), lambda p, i, *_: (i, skip + p)),
            pl.BlockSpec((1, width, 2 * PAIR), lambda p, i, *_: (skip + p, 0, 0)),
            pl.BlockSpec((1, 8, 2 * PAIR), lambda p, i, *_: (skip + p, 0, 0)),
        ]
        half = (count * width // 2 + spare, cat)
        out_shape = [cat_shape] + [shape(half, bf16)] * 2
        out_specs = [cat_block] + [whole(half)] * 2
    else:
        extra, extra_specs = [], []
        out_shape = [
            shape((total, PAIR * count), f32),
            cat_shape,
            shape((count, width, cat), f32),
            shape((count, 8, cat), f32),
        ]
        out_specs = [
            pl.BlockSpec((rows, PAIR), lambda p, i, *_: (i, p)),
            cat_block,
            pl.BlockSpec((1, width, cat), lambda p, i, *_: (p, 0, 0)),
            pl.BlockSpec((1, 8, cat), lambda p, i, *_: (p, 0, 0)),
        ]
    return pl.pallas_call(
        functools.partial(backward_kernel, last, len(tokens), rows, blocks, step),
        grid_spec=pltpu.PrefetchScalarGridSpec(
            num_scalar_prefetch=2,
            grid=(count, items),
            in_specs=[query_block, key_block, key_block]
            + [query_block] * 3
            + [hat_block]
            + extra_specs
            + [ANYWHERE] * len(tokens),
            out_specs=out_specs,
            scratch_shapes=[
                pltpu.VMEM((width, cat), f32),
                pltpu.VMEM((2 * spare, cat), f32),
                pltpu.VMEM((2, PAIR, rows), bf16),
                pltpu.VMEM((2, PAIR, rows), bf16),
                pltpu.VMEM((PAIR, main), f32),
            ]
            + [pltpu.VMEM((step, main), bf16)] * 4
            + ends,
        ),
        out_shape=out_shape,
        compiler_params=params(2),
        cost_estimate=cost(
            total * PAIR * count,
            total * PAIR * count,
        ),
        name="attend_back",
    )(limits, core, queries, keys, values, grads, outs, lse, hat, *extra, *tokens)


def feed_kernel(
    core, x_ref, mix_ref, dy_ref, w_output, w_expand, w_reduce, b_output, b_expand, b_reduce, gain, shift,
    y_ref, dmid_ref, dmix_ref, keep_ref, send_ref,
    middle_ref, normed_ref, y_acc, grad_acc, line_ref,
):
    part = pl.program_id(0)

    half = w_output.shape[0] // 2

    def put(index, block):
        place = pl.ds(pl.multiple_of(index * half, half), half)
        keep_ref[place, :], send_ref[place, :] = halves(core[0], block)

    @pl.when(part == 0)
    def _():
        mixed = mix_ref[...].astype(bf16)
        middle = x_ref[...].astype(f32) + dot_rows(mixed, w_output[...]) + b_output[...]
        middle_ref[...] = middle
        hat, _ = hat_rows(middle)
        normed_ref[...] = (hat * gain[...] + shift[...]).astype(bf16)
        y_acc[...] = middle + b_reduce[...]
        grad_acc[...] = jnp.zeros_like(grad_acc)
        line_ref[...] = jnp.zeros_like(line_ref)
        line_ref[1:2, :] = column_sums(dy_ref[...].astype(f32))

    normed = normed_ref[...]
    upper = dot_rows(normed, w_expand[...]) + b_expand[...]
    cumulative = 0.5 * lax.erf(upper * math.sqrt(0.5)) + 0.5
    density = jnp.exp(upper * upper * -0.5) * (1.0 / math.sqrt(2.0 * math.pi))
    active = (upper * cumulative).astype(bf16)
    slope = cumulative + upper * density
    y_acc[...] += dot_rows(active, w_reduce[...])
    put(1 + 2 * part, dot_left(active, dy_ref[...]))
    grad_upper = (dot_right(dy_ref[...], w_reduce[...]) * slope).astype(bf16)
    line_ref[pl.ds(4 + part, 1), :] = column_sums(grad_upper.astype(f32))
    put(2 + 2 * part, dot_left(normed, grad_upper))
    grad_acc[...] += dot_right(grad_upper, w_expand[...])

    @pl.when(part == pl.num_programs(0) - 1)
    def _():
        y_ref[...] = y_acc[...].astype(bf16)
        grad = grad_acc[...]
        hat, inverse = hat_rows(middle_ref[...])
        line_ref[2:3, :] = column_sums(grad * hat)
        line_ref[3:4, :] = column_sums(grad)
        dmid = hat_back(grad * gain[...], hat, inverse) + dy_ref[...].astype(f32)
        dmid_ref[...] = dmid
        branch = dmid.astype(bf16)
        line_ref[0:1, :] = column_sums(branch.astype(f32))
        put(0, dot_left(mix_ref[...].astype(bf16), branch))
        end = slice(keep_ref.shape[0] - line_ref.shape[0] // 2, None)
        keep_ref[end, :], send_ref[end, :] = halves(core[0], line_ref[...])
        dmix_ref[...] = dot_right(branch, w_output[...]).astype(bf16)


def feed(core, spare, x, mixed, dy, w_output, w_expand, w_reduce, b_output, b_expand, b_reduce, gain, shift):
    rows, width = x.shape
    hidden = w_expand.shape[1]
    parts = hidden // width
    row = whole((rows, width))
    line = whole((1, width))
    expand = pl.BlockSpec((width, width), lambda i, *_: (0, i))
    reduce = pl.BlockSpec((width, width), lambda i, *_: (i, 0))
    hidden_line = pl.BlockSpec((1, width), lambda i, *_: (0, i))
    weights = ((1 + 2 * parts) * width // 2 + spare, width)
    shape = jax.ShapeDtypeStruct
    return pl.pallas_call(
        feed_kernel,
        grid_spec=pltpu.PrefetchScalarGridSpec(
            num_scalar_prefetch=1,
            grid=(parts,),
            in_specs=[row, row, row, whole((width, width)), expand, reduce, line, hidden_line, line, line, line],
            out_specs=[row, row, row, whole(weights), whole(weights)],
            scratch_shapes=[
                pltpu.VMEM((rows, width), f32),
                pltpu.VMEM((rows, width), bf16),
                pltpu.VMEM((rows, width), f32),
                pltpu.VMEM((rows, width), f32),
                pltpu.VMEM((2 * spare, width), f32),
            ],
        ),
        out_shape=[
            shape((rows, width), bf16),
            shape((rows, width), f32),
            shape((rows, width), bf16),
            shape(weights, bf16),
            shape(weights, bf16),
        ],
        compiler_params=params(1),
        cost_estimate=cost(12 * rows * width * hidden + 6 * rows * width * width, 20 * rows * width, 2 * rows * hidden),
        name="feed",
    )(core, x, mixed, dy, w_output, w_expand, w_reduce, b_output, b_expand, b_reduce, gain, shift)


def gather_parts(refs, part, parts):
    blocks = []
    for ref in refs:
        pairs = ref.shape[1] // (parts * PAIR)
        for pair in range(pairs):
            start = (pair * parts + part) * PAIR
            blocks.append(ref[:, start:start + PAIR])
    return jnp.concatenate(blocks, axis=1)


def other_kernel(cats, w_key, w_value, *rest):
    cat_refs, send_ref = rest[:cats], rest[-1]
    dk = gather_parts(cat_refs, 0, 2)
    dv = gather_parts(cat_refs, 1, 2)
    send_ref[...] = (dot_right(dk, w_key[...]) + dot_right(dv, w_value[...])).astype(bf16)


def other_grads(cats, w_key, w_value, rows, after):
    total, width = cats[0].shape[0], w_key.shape[0]
    step = chunk_of(rows, 272)
    return pl.pallas_call(
        functools.partial(other_kernel, len(cats)),
        grid=(total // step,),
        in_specs=[whole((width, width))] * 2
        + [pl.BlockSpec((step, c.shape[1]), lambda i: (i, 0)) for c in cats]
        + [ANYWHERE] * len(after),
        out_specs=pl.BlockSpec((step, width), lambda i: (i, 0)),
        out_shape=jax.ShapeDtypeStruct((total, width), bf16),
        compiler_params=params(1),
        cost_estimate=cost(4 * total * width * width, 8 * total * width),
        name="other_grads",
    )(w_key, w_value, *cats, *after)


def own_kernel(cats, x_ref, recv_ref, dmid_ref, w_query, w_key, w_value, gain, *rest):
    cat_refs, dx_ref = rest[:cats], rest[-1]
    dk = gather_parts(cat_refs, 0, 3)
    dv = gather_parts(cat_refs, 1, 3)
    dq = gather_parts(cat_refs, 2, 3)
    grad = dot_right(dq, w_query[...]) + dot_right(dk, w_key[...]) + dot_right(dv, w_value[...])
    for index in range(recv_ref.shape[0]):
        grad = grad + recv_ref[index].astype(f32)
    hat, inverse = hat_rows(x_ref[...].astype(f32))
    dx_ref[...] = hat_back(grad * gain[...], hat, inverse) + dmid_ref[...]


def own_grads(x, cats, recv, dmid, w_query, w_key, w_value, gain, after):
    rows, width = x.shape
    step = chunk_of(rows, 272)
    row = pl.BlockSpec((step, width), lambda i: (i, 0))
    return pl.pallas_call(
        functools.partial(own_kernel, len(cats)),
        grid=(rows // step,),
        in_specs=[row, pl.BlockSpec((recv.shape[0], step, width), lambda i: (0, i, 0)), row]
        + [whole((width, width))] * 3
        + [whole((1, width))]
        + [pl.BlockSpec((step, c.shape[1]), lambda i: (i, 0)) for c in cats]
        + [ANYWHERE] * len(after),
        out_specs=row,
        out_shape=jax.ShapeDtypeStruct((rows, width), f32),
        compiler_params=params(1),
        cost_estimate=cost(6 * rows * width * width, 16 * rows * width),
        name="own_grads",
    )(x, recv, dmid, w_query, w_key, w_value, gain, *cats, *after)


class Slice:
    def __init__(self):
        group, rest = lax.axis_size("grp"), lax.axis_size("rest")
        batch = rest * lax.axis_size("core")
        side = 2 if rest % 2 == 0 else 1
        rest //= side
        high = 2 if rest % 2 == 0 else 1
        self.sizes = {"core": 2, "side": side, "member": group, "high": high, "low": rest // high}
        self.count = group * batch
        self.here = self.coords(lax.axis_index(ALL))

    def coords(self, linear):
        out = {}
        for name in ("member", "core", "side", "low", "high"):
            out[name] = linear % self.sizes[name]
            linear = linear // self.sizes[name]
        return out

    def linear(self, coords):
        total = 0
        for name in ("high", "low", "side", "core", "member"):
            total = total * self.sizes[name] + coords[name]
        return total

    def size(self, stage):
        return math.prod(self.sizes[name] for name in stage)

    def place(self, stage, coords=None):
        coords = self.here if coords is None else coords
        total = 0
        for name in stage:
            total = total * self.sizes[name] + coords[name]
        return total

    def send(self, array, stage, shift):
        pairs = []
        for source in range(self.count):
            coords = self.coords(source)
            place = (self.place(stage, coords) + shift) % self.size(stage)
            for name in reversed(stage):
                coords[name] = place % self.sizes[name]
                place //= self.sizes[name]
            pairs.append((source, self.linear(coords)))
        return lax.ppermute(array, ALL, pairs)

    def spread(self, parts, stage):
        return [parts[0]] + [self.send(part, stage, s) for s, part in enumerate(parts) if s > 0]

    def share(self, array, stage):
        return self.spread([array] * self.size(stage), stage)

    def origins(self, stage):
        size = self.size(stage)
        return ((self.place(stage) - jnp.arange(size)) % size).astype(jnp.int32)

    def in_order(self, parts, stage):
        if len(parts) <= 2:
            return parts
        stack = jnp.stack(parts)
        order = self.origins(stage)
        return [lax.dynamic_index_in_dim(stack, order[i], 0, False) for i in range(len(parts))]


def behind(array, *others):
    return lax.optimization_barrier((array, *others))[0] if others else array


def cut_kernel(size, groups, place, *refs):
    ins, outs = refs[:2 * groups], refs[2 * groups:]
    for shift, out in enumerate(outs):
        start = 0
        for index in range(groups):
            keep, came = ins[2 * index], ins[2 * index + 1]
            rows = keep.shape[0] // size
            span = pl.ds(pl.multiple_of((place[0] + shift) % size * rows, 16), rows)
            total = keep[span, :].astype(f32) + came[span, :].astype(f32)
            out[start:start + rows, :] = total.astype(bf16)
            start += rows


def cut(pairs, place, size):
    arrays = [array for pair in pairs for array in pair]
    width = arrays[0].shape[1]
    part = (sum(keep.shape[0] for keep, _ in pairs) // size, width)
    return pl.pallas_call(
        functools.partial(cut_kernel, size, len(pairs)),
        grid_spec=pltpu.PrefetchScalarGridSpec(
            num_scalar_prefetch=1,
            grid=(1,),
            in_specs=[whole(a.shape) for a in arrays],
            out_specs=[whole(part)] * size,
        ),
        out_shape=[jax.ShapeDtypeStruct(part, bf16)] * size,
        compiler_params=params(1),
        cost_estimate=cost(size * part[0] * width, 6 * size * part[0] * width),
        name="cut",
    )(jnp.reshape(place, (1,)).astype(jnp.int32), *arrays)


def add_up(parts):
    total = parts[0].astype(f32)
    for part in parts[1:]:
        total = total + part.astype(f32)
    return total.astype(bf16)


def place_pieces(places, core, pieces, flats):
    size = len(pieces) // 2
    for which in range(2):
        target = core[0] if which == 0 else 1 - core[0]
        for index in range(size):
            piece, at = pieces[which * size + index], 0
            for flat in flats:
                rows = flat.shape[1] // size
                span = pl.ds(pl.multiple_of(places[index] * rows, 16), rows)
                flat[target, span, :] = piece[at:at + rows, :]
                at += rows


def feed_weights_kernel(size, places, core, *refs):
    pieces, (dwo_ref, dwe_ref, dwr_ref, *line_refs, dbe_ref, flat) = refs[:2 * size], refs[-9:]
    width = dwo_ref.shape[0]
    half = width // 2
    step = pl.program_id(0)
    parts = pl.num_programs(0) - 1

    @pl.when(step == 0)
    def _():
        place_pieces(places, core, pieces, [flat])

    @pl.when(step < parts)
    def _():
        start = pl.multiple_of((1 + 2 * step) * half, half)
        for side in range(2):
            rows = slice(side * half, (side + 1) * half)
            dwr_ref[rows, :] = flat[side, pl.ds(start, half), :].astype(f32)
            dwe_ref[rows, :] = flat[side, pl.ds(start + half, half), :].astype(f32)

    @pl.when(step == parts)
    def _():
        for side in range(2):
            dwo_ref[side * half:(side + 1) * half, :] = flat[side, :half, :].astype(f32)
        count = dbe_ref.shape[1] // width
        start = (1 + 2 * count) * half
        lines = flat[0, start:start + 16, :].astype(f32)
        for index, ref in enumerate(line_refs):
            ref[...] = lines[index:index + 1]
        for part in range(count):
            dbe_ref[:, part * width:(part + 1) * width] = lines[4 + part:5 + part]


def feed_weights(places, core, own, came, hidden, after):
    rows, width = own[0].shape
    parts = hidden // width
    shapes = [(width, width), (width, hidden), (hidden, width)] + [(1, width)] * 4 + [(1, hidden)]
    out_specs = [whole(s) for s in shapes]
    out_specs[1] = pl.BlockSpec((width, width), lambda p, *_: (0, jnp.minimum(p, parts - 1)))
    out_specs[2] = pl.BlockSpec((width, width), lambda p, *_: (jnp.minimum(p, parts - 1), 0))
    return pl.pallas_call(
        functools.partial(feed_weights_kernel, len(own)),
        grid_spec=pltpu.PrefetchScalarGridSpec(
            num_scalar_prefetch=2,
            grid=(parts + 1,),
            in_specs=[whole((rows, width))] * (2 * len(own)) + [ANYWHERE] * len(after),
            out_specs=out_specs,
            scratch_shapes=[pltpu.VMEM((2, len(own) * rows, width), bf16)],
        ),
        out_shape=[jax.ShapeDtypeStruct(s, f32) for s in shapes],
        compiler_params=params(1),
        cost_estimate=cost(0, 12 * len(own) * rows * width),
        name="feed_weights",
    )(places, core, *own, *came, *after)


def project_weights_kernel(calls, places, core, *refs):
    flats, refs = refs[len(refs) - len(calls):], refs[:len(refs) - len(calls)]
    pieces, refs = refs[:-16], refs[-16:]
    weights, (gain, shift), refs = refs[:3], refs[3:5], refs[5:]
    outs, (dgain_ref, dshift_ref, dbq_ref, dbv_ref), refs = refs[:3], refs[3:7], refs[7:]
    gains, shifts, cross_acc, plain_acc = refs
    pair = pl.program_id(0)
    width = gains.shape[0]
    half = width // 2

    @pl.when(pair == 0)
    def _():
        place_pieces(places, core, pieces, flats)
        gains[...] = jnp.broadcast_to(gain[...], (PAIR, width)).T
        shifts[...] = jnp.broadcast_to(shift[...], (PAIR, width)).T
        cross_acc[...] = jnp.zeros_like(cross_acc)
        plain_acc[...] = jnp.zeros_like(plain_acc)

    def put(flat, pairs, index):
        sums = flat[0, pairs * half:pairs * half + 16, :].astype(f32)[index:index + 1]
        dbv_ref[...] = sums[:, PAIR:2 * PAIR]
        dbq_ref[...] = sums[:, 2 * PAIR:]
        for side in range(2):
            down = slice(side * half, (side + 1) * half)
            block = flat[side, index * half:(index + 1) * half, :].astype(f32)
            for which, (out, weight) in enumerate(zip(outs, weights)):
                lanes = slice(which * PAIR, (which + 1) * PAIR)
                part, line = block[:, lanes], sums[:, lanes]
                out[down, :] = gains[down, :] * part + shifts[down, :] * line
                own = weight[down, :].astype(f32)
                cross_acc[down, :] += own * part
                plain_acc[down, :] += own * line

    first = 0
    for flat, pairs in zip(flats, calls):
        for index in range(pairs):
            pl.when(pair == first + index)(functools.partial(put, flat, pairs, index))
        first += pairs

    @pl.when(pair == PAIRS - 1)
    def _():
        for acc, out in ((cross_acc, dgain_ref), (plain_acc, dshift_ref)):
            column = jnp.broadcast_to(jnp.sum(acc[...], axis=1, keepdims=True), (width, PAIR))
            out[...] = column.T[:1]


def project_weights(places, core, own, came, w_key, w_value, w_query, gain, shift, calls, spare):
    width = w_query.shape[0]
    rows, cat = own[0].shape
    line = whole((1, width))
    column_block = pl.BlockSpec((width, PAIR), lambda p, *_: (0, p))
    line_block = pl.BlockSpec((1, PAIR), lambda p, *_: (0, p))
    return pl.pallas_call(
        functools.partial(project_weights_kernel, calls),
        grid_spec=pltpu.PrefetchScalarGridSpec(
            num_scalar_prefetch=2,
            grid=(PAIRS,),
            in_specs=[whole((rows, cat))] * (2 * len(own)) + [column_block] * 3 + [line] * 2,
            out_specs=[column_block] * 3 + [line] * 2 + [line_block] * 2,
            scratch_shapes=[pltpu.VMEM((width, PAIR), f32)] * 4
            + [pltpu.VMEM((2, count * width // 2 + spare, cat), bf16) for count in calls],
        ),
        out_shape=[jax.ShapeDtypeStruct((width, width), f32)] * 3
        + [jax.ShapeDtypeStruct((1, width), f32)] * 4,
        compiler_params=params(1),
        cost_estimate=cost(0, 20 * width * width),
        name="project_weights",
    )(places, core, *own, *came, w_key, w_value, w_query, gain, shift)


def body(
    layer_input,
    lang_counts,
    w_query,
    w_key,
    w_value,
    w_output,
    w_expand,
    w_reduce,
    b_query,
    b_value,
    b_output,
    b_expand,
    b_reduce,
    gain_attn,
    shift_attn,
    gain_mlp,
    shift_mlp,
    cotangent,
):
    items, own_rows, width = layer_input.shape
    group = lax.axis_size("grp")
    me = lax.axis_index("grp")
    rows = -(-own_rows // 16) * 16
    total = items * rows
    patch_rows = VIEWS * PATCH
    shifts = range(1, group)

    def padded(array):
        if rows != own_rows:
            array = jnp.pad(array, ((0, 0), (0, rows - own_rows), (0, 0)))
        return array.reshape(total, width)

    def unpadded(array):
        return array.reshape(items, rows, width)[:, :own_rows]

    def limit_of(owner):
        return jnp.clip(patch_rows + lang_counts - owner * own_rows, 0, own_rows)

    def line(vector):
        return vector.reshape(1, -1)

    def group_shift(array, shift):
        return lax.ppermute(array, "grp", [(i, (i + shift) % group) for i in range(group)])

    def joined(parts):
        if len(parts) == 1:
            return parts[0]
        return jnp.stack([p.reshape(items, rows, width) for p in parts], 1).reshape(-1, width)

    x = padded(layer_input)
    dy = padded(cotangent)
    others = [group_shift(x, -shift) for shift in shifts]
    own_limits = limit_of(me).reshape(items, 1)
    other_limits = jnp.stack([limit_of((me + shift) % group) for shift in shifts], 1)

    norms = (line(gain_attn), line(shift_attn))
    hat, keys, values, queries, *first = attend(
        own_limits, x, norms, w_key, w_value, line(b_value), (w_query, line(b_query)), rows, 1, None
    )
    hat_other, keys_other, values_other, mixed, lse = attend(
        other_limits, joined(others), norms, w_key, w_value, line(b_value), queries, rows, group - 1, first
    )

    devices = Slice()
    plane = ("side", "member")
    core = jnp.reshape(devices.here["core"], (1,)).astype(jnp.int32)
    plane_place, plane_size = devices.place(plane), devices.size(plane)
    spare = 16 * plane_size
    output, dmid, dmix, keep, give = feed(
        core, spare, x, mixed, dy, w_output, w_expand, w_reduce, line(b_output), line(b_expand),
        line(b_reduce), line(gain_mlp), line(shift_mlp),
    )

    def summed(value, stage, *after):
        own, *came = devices.share(value, (stage,))
        return add_up(devices.in_order([behind(own, *after), *came], (stage,)))

    def back_other(first, count, tokens):
        return attend_back(
            other_limits, core, queries, keys_other, values_other, dmix, mixed, lse, hat_other,
            rows, group - 1, first, count, None, spare, tokens,
        )

    def back_own(first, count, before, tokens):
        return attend_back(
            own_limits, core, queries, keys, values, dmix, mixed, lse, hat,
            rows, 1, first, count, before, spare, tokens,
        )

    feed_pair = devices.spread([keep, give], ("core",))
    other_first = back_other(0, 1, [])
    feed_pair = [behind(half, other_first[1]) for half in feed_pair]
    share_rows = feed_pair[0].shape[0] // plane_size
    parts = [
        add_up([
            lax.dynamic_slice_in_dim(half, (plane_place + s) % plane_size * share_rows, share_rows)
            for half in feed_pair
        ])
        for s in range(plane_size)
    ]
    other_rest = back_other(1, PAIRS - 1, parts[:1])
    own, *came = devices.spread(parts, plane)
    feed_sum = add_up([behind(own, other_rest[1]), *came])
    cat_first, *pair_first = back_own(0, 1, (other_first, 0), [feed_sum])
    feed_sum = summed(feed_sum, "low", cat_first)
    send = other_grads([other_first[1], other_rest[1]], w_key, w_value, rows, [feed_sum])
    send_rows = send.reshape(items, group - 1, rows, width)
    received = jnp.stack(
        [group_shift(send_rows[:, shift - 1].reshape(total, width), shift) for shift in shifts]
    )
    cat_rest, *pair_rest = back_own(1, PAIRS - 1, (other_rest, 0), [feed_sum, send])
    own, *came_high = devices.share(feed_sum, ("high",))
    keep, give = pair_rest
    pair_rest = [keep, behind(give, *came_high)]
    pairs = [devices.spread(pair, ("core",)) for pair in (pair_first, pair_rest)]
    parts = cut(pairs, plane_place, plane_size)
    feed_sum = add_up(devices.in_order([behind(own, parts[0]), *came_high], ("high",)))
    parts = devices.spread(parts, plane)
    feed_own = devices.share(feed_sum, plane)
    dx = own_grads(
        x, [cat_first, cat_rest], received, dmid, w_query, w_key, w_value, line(gain_attn), parts[:1]
    )
    own, *came = parts
    value = add_up([behind(own, dx), *came])
    value = summed(summed(value, "low"), "high")
    project_own = devices.share(value, plane)
    feed_came = [devices.send(behind(piece, value), ("core",), 1) for piece in feed_own]
    places = devices.origins(plane)
    dwo, dwe, dwr, dbo, dbr, dgain_mlp, dshift_mlp, dbe = feed_weights(
        places, core, feed_own, feed_came, w_expand.shape[1], []
    )
    project_own = [project_own[0]] + [behind(piece, dwo) for piece in project_own[1:]]
    project_came = [devices.send(piece, ("core",), 1) for piece in project_own]
    dwk, dwv, dwq, dgain, dshift, dbq, dbv = project_weights(
        places, core, project_own, project_came, w_key, w_value, w_query, *norms, (1, PAIRS - 1), spare
    )
    small = (dbq, dbv, dbo, dbe, dbr, dgain, dshift, dgain_mlp, dshift_mlp)
    return (
        unpadded(output),
        unpadded(dx),
        dwq, dwk, dwv, dwo, dwe, dwr,
        *(vector.reshape(-1) for vector in small),
    )


def solution(mesh):
    batch, group = mesh.shape["dp"], mesh.shape["grp"]
    mesh = jax.sharding.Mesh(mesh.devices.reshape(batch // 2, 2, group), ALL)
    items = ("rest", "core")
    rows = P(items, "grp", None)
    in_specs = (rows, P(items)) + (P(),) * 15 + (rows,)
    out_specs = (rows, rows) + (P(),) * 15
    return jax.shard_map(body, mesh=mesh, in_specs=in_specs, out_specs=out_specs, check_vma=False)
```
